32 devices in a mesh: seg: 2 (over x), genome: 16 (over z, y, core).
Axes of the slice: x: 2, y: 2, z: 4, core: 2. Of those that a mesh axis runs over, the one named last changes fastest.
Arguments:
- z_typed: float32 [256, 16384], P(None, ('seg', 'genome')), parts along dimension 1, may hold values from -8 to 8
- diag_inverse: float32 [32, 512, 512], P(('seg', 'genome')), parts along dimension 0
- coupling: float32 [32, 512, 256], P(('seg', 'genome')), parts along dimension 0
- impute_coef: bfloat16 [16384, 1024], P(('seg', 'genome')), parts along dimension 0, may hold values from -0.25 to 0.25
- anchor: int32 [16384], P(('seg', 'genome')), parts along dimension 0, may hold values from 0 to 8191, as said below
Outputs:
- imputed: float32 [256, 16384], P(None, ('seg', 'genome')), parts along dimension 1
The draws below stay inside these ranges and needn't reach their ends.
There are 2 independent parts, one for each index of `seg`. The reference program is written for one: setup_inputs(seed, part) draws one part's arguments, and reference() takes and returns one part's arrays. A program takes and returns all parts, laid end to end along the dimension named above; each array names one. Nothing has to cross between parts.
Inputs may be any that keep to these rules, and one draw needn't show every extreme that they name: The anchor of the untyped variant t lies in typed block t // 512, i.e. in columns (t // 512) * 512 to (t // 512 + 1) * 512 - 1.
All inputs are finite; a program needn't handle non-finite values.
Results may differ from the reference program's by a relative error of at most 0.002.
The reference program's roundings to bfloat16 on the way (of `alpha`) count: a program that leaves them out, or rounds other values in their place, can miss the bound.
Values may be sent and summed in bfloat16 or wider, within the bound.
No kernel may reach another device: no remote copies, remote signals or barrier semaphores. Data moves between devices by JAX's collectives and lax.ppermute only.
A program may use at most 192 MiB of HBM per device.

```python
import jax
import jax.numpy as jnp
from jax import lax

TRAITS = 256
TYP_DEV = 512
HALF = 256
UNT_DEV = 512
BLOCKS = 16
TYPED = 8192
UNTYPED = 8192


def draw_diag_inverse(key, part):
    first, second = jax.random.split(key)
    noise = jax.random.normal(first, (BLOCKS, TYP_DEV, TYP_DEV), jnp.float32)
    lower_part = jnp.tril(noise, -1) * (0.3 / TYP_DEV ** 0.5)
    diag_values = jax.random.uniform(second, (BLOCKS, TYP_DEV), jnp.float32, 0.9, 1.1)
    rows_idx = jnp.arange(TYP_DEV)[:, None]
    cols_idx = jnp.arange(TYP_DEV)[None, :]
    on_diag = (rows_idx == cols_idx).astype(jnp.float32)
    return 0.25 * (lower_part + on_diag[None, :, :] * diag_values[:, :, None])


def block_order(one_key):
    return jax.random.permutation(one_key, HALF)


def draw_coupling(key, part):
    first, second, third, fourth = jax.random.split(key, 4)
    block_keys = jax.random.split(first, BLOCKS)
    orders = jax.vmap(block_order)(block_keys).astype(jnp.int32)
    signs = jax.random.randint(second, (BLOCKS, HALF), 0, 2).astype(jnp.float32) * 2.0 - 1.0
    columns = jnp.arange(HALF, dtype=jnp.int32)
    placed = (orders[:, :, None] == columns[None, None, :]).astype(jnp.float32) * signs[:, :, None]
    bottom_noise = jax.random.normal(third, (BLOCKS, HALF, HALF), jnp.float32)
    top_noise = jax.random.normal(fourth, (BLOCKS, TYP_DEV - HALF, HALF), jnp.float32)
    bottom = placed + bottom_noise * (0.05 / HALF ** 0.5)
    top = top_noise * (0.1 / TYP_DEV ** 0.5)
    factor = 0.5 ** (1.0 / BLOCKS) * 0.976 / 0.25
    return jnp.concatenate([top, bottom], axis=1) * factor


def draw_anchor(key, part):
    offsets = jax.random.randint(key, (UNTYPED,), 0, TYP_DEV)
    owners = jnp.arange(UNTYPED, dtype=jnp.int32) // UNT_DEV
    anchors = owners * TYP_DEV + offsets
    anchors = anchors.at[0].set(0)
    anchors = anchors.at[UNTYPED - 1].set(TYPED - 1)
    return anchors.astype(jnp.int32)


def level_of(stream_key, dims, cuts, smallest, top_value):
    def one(dim, blocks):
        heights = jax.random.uniform(jax.random.fold_in(jax.random.fold_in(stream_key, 6), dim), (blocks,), jnp.float32, smallest / len(cuts), top_value / len(cuts))
        return jnp.repeat(jnp.exp(heights), dims[dim] // blocks).reshape((-1,) + (1,) * (len(dims) - dim - 1))

    loudness = one(*cuts[0])
    for cut in cuts[1:]:
        loudness = loudness * one(*cut)
    return loudness


def bell_draw(rng, shape, width, limit, pieces=(), kind=jnp.bfloat16):
    drawn = width * jax.random.normal(rng, shape, jnp.float32)
    if pieces:
        drawn = drawn * level_of(rng, shape, pieces, -0.22, 0.18)
    return jnp.clip(drawn, -limit, limit).astype(kind)


def setup_inputs(seed: int = 0, part: int = 0) -> dict:
    splits = jax.random.split(jax.random.key(seed), 6)
    part_splits = jax.random.split(jax.random.fold_in(splits[5], part), 6)
    return {
        "z_typed": bell_draw(part_splits[0], (TRAITS, TYPED), 1.0, 8.0, ((1, 16),), jnp.float32),
        "diag_inverse": draw_diag_inverse(jax.random.fold_in(jax.random.fold_in(splits[5], part), 71), part),
        "coupling": draw_coupling(jax.random.fold_in(jax.random.fold_in(splits[5], part), 71), part),
        "impute_coef": bell_draw(part_splits[3], (UNTYPED, TYP_DEV + 2 * HALF), (2 * HALF) ** -0.5, 0.25, ((0, 16),)),
        "anchor": draw_anchor(jax.random.fold_in(jax.random.fold_in(splits[5], part), 71), part),
    }


precise = lax.Precision.HIGHEST


def reference(z_typed, diag_inverse, coupling, impute_coef, anchor):
    z_blocks = z_typed.reshape(TRAITS, BLOCKS, TYP_DEV).transpose(1, 0, 2)

    def forward_step(tail_in, inputs):
        z_block, inverse_block, couple = inputs
        projected = jnp.dot(inverse_block, couple, precision=precise)
        rows_now = jnp.dot(z_block, inverse_block.T, precision=precise) - jnp.dot(tail_in, projected.T, precision=precise)
        return rows_now[:, TYP_DEV - HALF:], rows_now

    start_tail = jnp.zeros((TRAITS, HALF), jnp.float32)
    _, all_rows = lax.scan(forward_step, start_tail, (z_blocks, diag_inverse, coupling))

    def backward_step(upper_in, inputs):
        rows_now, inverse_block, couple = inputs
        padded = jnp.concatenate([jnp.zeros((TRAITS, TYP_DEV - HALF), jnp.float32), upper_in], axis=1)
        solved = jnp.dot(rows_now - padded, inverse_block, precision=precise)
        return jnp.dot(solved, couple, precision=precise), solved

    _, all_alpha = lax.scan(backward_step, start_tail, (all_rows, diag_inverse, coupling), reverse=True)
    alpha = all_alpha.transpose(1, 0, 2).reshape(TRAITS, TYPED).astype(jnp.bfloat16)
    alpha_pad = jnp.concatenate([jnp.zeros((TRAITS, HALF), jnp.bfloat16), alpha, jnp.zeros((TRAITS, HALF), jnp.bfloat16)], axis=1)
    span = TYP_DEV + 2 * HALF
    coef_blocks = impute_coef.reshape(BLOCKS, UNT_DEV, span)
    anchor_blocks = anchor.reshape(BLOCKS, UNT_DEV)

    def impute_block(inputs):
        index, coef_block, anchor_block = inputs
        start = (index * TYP_DEV).astype(jnp.int32)
        window = lax.dynamic_slice_in_dim(alpha_pad, start, span, 1)
        columns = start - HALF + jnp.arange(span, dtype=jnp.int32)
        within = jnp.abs(columns[None, :] - anchor_block[:, None]) <= HALF
        masked = jnp.where(within, coef_block, jnp.zeros_like(coef_block))
        return lax.dot_general(window, masked, (((1,), (1,)), ((), ())), preferred_element_type=jnp.float32)

    parts = lax.map(impute_block, (jnp.arange(BLOCKS, dtype=jnp.int32), coef_blocks, anchor_blocks))
    return parts.transpose(1, 0, 2).reshape(TRAITS, UNTYPED)
```

```python
import jax
import jax.numpy as jnp
from jax import lax
from jax.sharding import PartitionSpec as P

AXIS = "genome"
GROUP = 4


def dot(a, b, ca=1, cb=0):
    return lax.dot_general(
        a, b, (((ca,), (cb,)), ((), ())),
        precision=lax.Precision.HIGH, preferred_element_type=jnp.float32,
    )


def swap(block, distance):
    n = lax.axis_size(AXIS)
    return lax.ppermute(block, AXIS, [(i, i ^ distance) for i in range(n)])


def shift(block, pairs):
    return lax.ppermute(block, AXIS, pairs)


def hop(block, step, up):
    lower = [step * GROUP + i for i in range(GROUP)]
    pairs = [(i, i + GROUP) if up else (i + GROUP, i) for i in lower]
    return shift(block, pairs)


def ordered(first, own, other):
    return jnp.where(first, own, other), jnp.where(first, other, own)


def half_of(block, which):
    rows = block.shape[0] // 2
    return lax.dynamic_slice_in_dim(block, which * rows, rows, 0)


def joined(first, own, other):
    return jnp.concatenate(ordered(first, own, other), axis=0)


def per_device(z_typed, diag_inverse, coupling, impute_coef, anchor):
    d = diag_inverse[0]
    c = coupling[0]
    typed = d.shape[0]
    half = c.shape[1]
    traits = z_typed.shape[0]
    n = lax.axis_size(AXIS)
    place = lax.axis_index(AXIS)
    core = place % 2
    pair = (place // 2) % 2
    first_core = core == 0
    first_pair = pair == 0

    p = dot(d, c)
    m = -p[typed - half :]
    solved = dot(z_typed, d, 1, 1)
    s = solved[:, typed - half :]

    got = swap(jnp.concatenate([m, half_of(s, 1 - core)], axis=0), 1)
    m0, m1 = ordered(first_core, m, got[:half])
    s0, s1 = ordered(first_core, half_of(s, core), got[half:])
    n_pair = dot(m1, m0)
    s_pair = dot(s0, m1, 1, 1) + s1

    got = swap(jnp.concatenate([n_pair, half_of(s_pair, 1 - pair)], axis=0), 2)
    n0, n1 = ordered(first_pair, n_pair, got[:half])
    sp0, sp1 = ordered(first_pair, half_of(s_pair, pair), got[half:])
    s_group = dot(sp0, n1, 1, 1) + sp1
    n_group = dot(n1, n0)

    g = dot(solved, p)
    gg = dot(p, p, 0, 0)
    got = swap(jnp.concatenate([gg, half_of(g, 1 - core)], axis=0), 1)
    gg0, gg1 = ordered(first_core, gg, got[:half])
    g0, g1 = ordered(first_core, half_of(g, core), got[half:])
    g_pair = dot(g1 - dot(s0, gg1), m0) + g0
    gg_pair = dot(m0, dot(gg1, m0), 0, 0) + gg0
    got = swap(jnp.concatenate([gg_pair, half_of(g_pair, 1 - pair)], axis=0), 2)
    ggp0, ggp1 = ordered(first_pair, gg_pair, got[:half])
    gp0, gp1 = ordered(first_pair, half_of(g_pair, pair), got[half:])
    g_group = dot(gp1 - dot(sp0, ggp1), n0) + gp0
    gg_group = dot(n0, dot(ggp1, n0), 0, 0) + ggp0

    groups = n // GROUP
    t_in = jnp.zeros_like(s_group)
    out = s_group
    for step in range(groups - 1):
        t_in = t_in + hop(out, step, True)
        out = dot(t_in, n_group, 1, 1) + s_group
    local = g_group - dot(t_in, gg_group)
    u_in = jnp.zeros_like(s_group)
    out = local
    for step in reversed(range(groups - 1)):
        u_in = u_in + hop(out, step, False)
        out = dot(u_in, n_group) + local

    t_mid = dot(t_in, n0, 1, 1) + sp0
    got = swap(jnp.where(first_pair, t_mid, t_in), 2)
    t_pair = joined(first_pair, jnp.where(first_pair, t_in, t_mid), got)
    t_in_mid = dot(t_pair, m0, 1, 1) + s0
    got = swap(jnp.where(first_core, t_in_mid, t_pair), 1)
    t_block = joined(first_core, jnp.where(first_core, t_pair, t_in_mid), got)
    rows = solved - dot(t_block, p, 1, 1)
    early = dot(rows, d)

    u_mid = dot(u_in, n1) + (gp1 - dot(t_mid, ggp1))
    got = swap(jnp.where(first_pair, u_in, u_mid), 2)
    u_pair = joined(first_pair, jnp.where(first_pair, u_mid, u_in), got)
    u_in_mid = dot(u_pair, m1) + (g1 - dot(t_in_mid, gg1))
    got = swap(jnp.where(first_core, u_pair, u_in_mid), 1)
    u_block = joined(first_core, jnp.where(first_core, u_in_mid, u_pair), got)
    weights = (early - dot(u_block, d[typed - half :])).astype(jnp.bfloat16)

    span = typed + 2 * half
    columns = place * typed - half + jnp.arange(span, dtype=jnp.int32)
    within = jnp.abs(columns[None, :] - anchor[:, None]) <= half
    masked = jnp.where(within, impute_coef, jnp.zeros_like(impute_coef))
    left = shift(weights[:, typed - half :], [(i, i + 1) for i in range(n - 1)])
    right = shift(weights[:, :half], [(i + 1, i) for i in range(n - 1)])
    imputed = contract(weights, masked[:, half : half + typed])
    imputed = imputed + contract(left, masked[:, :half])
    return imputed + contract(right, masked[:, half + typed :])


def contract(values, coefs):
    return lax.dot_general(
        values, coefs, (((1,), (1,)), ((), ())), preferred_element_type=jnp.float32
    )


def solution(mesh):
    in_specs = (
        P(None, ("seg", AXIS)),
        P(("seg", AXIS), None, None),
        P(("seg", AXIS), None, None),
        P(("seg", AXIS), None),
        P(("seg", AXIS)),
    )
    return jax.shard_map(
        per_device, mesh=mesh, in_specs=in_specs, out_specs=P(None, ("seg", AXIS)), check_vma=False
    )
```

```python
import functools

import jax
import jax.numpy as jnp
from jax import lax
from jax.experimental import pallas as pl
from jax.experimental.pallas import tpu as pltpu
from jax.sharding import PartitionSpec as P

AXIS = "genome"
GROUP = 4
f32 = jnp.float32
bf16 = jnp.bfloat16


def parts(x):
    high = x.astype(bf16)
    return high, (x - high.astype(f32)).astype(bf16)


def dot(a, b, ca=1, cb=0):
    ah, al = parts(a)
    bh, bl = parts(b)
    return lax.dot_general(
        jnp.concatenate([al, ah, ah], axis=ca),
        jnp.concatenate([bh, bl, bh], axis=cb),
        (((ca,), (cb,)), ((), ())),
        preferred_element_type=f32,
    )


def where_am_i():
    place = lax.axis_index(AXIS)
    return place % 2 == 0, (place // 2) % 2 == 0, place // GROUP


def ordered(first, own, other):
    return jnp.where(first, own, other), jnp.where(first, other, own)


def call(kernel, outs, *args, after=()):
    n_in, n_after = len(args), len(after)

    def body(*refs):
        kernel(*refs[:n_in], *refs[n_in + n_after :])

    single = not isinstance(outs, list)
    shapes = [outs] if single else outs
    vmem = pl.BlockSpec(memory_space=pltpu.VMEM)
    got = pl.pallas_call(
        body,
        out_shape=[jax.ShapeDtypeStruct(s, t) for s, t in shapes],
        in_specs=[vmem] * n_in + [pl.BlockSpec(memory_space=pl.ANY)] * n_after,
        out_specs=[vmem] * len(shapes),
        compiler_params=pltpu.CompilerParams(vmem_limit_bytes=24 * 2**20),
        name=kernel.__name__ if hasattr(kernel, "__name__") else kernel.func.__name__,
    )(*args, *after)
    return got[0] if single else got


def tail_part(z, d, c, x1, s_own):
    half = c.shape[1]
    rows = z.shape[0] // 2
    typed = d.shape[0]
    first, _, _ = where_am_i()
    tail = d[typed - half :]
    x1[:half] = -dot(tail, c[...])
    s = dot(z[...], tail, 1, 1)
    keep, send = ordered(first, s[:rows], s[rows:])
    x1[half:] = send
    s_own[...] = keep


def head_part(z, d, c, x1, s_own, x3, g_own, solved, p):
    half = c.shape[1]
    rows = z.shape[0] // 2
    head = d.shape[0] - half
    first, _, _ = where_am_i()
    p[:head] = dot(d[:head], c[...])
    p[head:] = -x1[:half]
    solved[:, :head] = dot(z[...], d[:head], 1, 1)
    low, high = ordered(first, s_own[...], x1[half:])
    solved[:rows, head:] = low
    solved[rows:, head:] = high
    g = dot(solved[...], p[...])
    keep, send = ordered(first, g[:rows], g[rows:])
    x3[:half] = dot(p[...], p[...], 0, 0)
    x3[half:] = send
    g_own[...] = keep


def pair_forward(x1, got1, s_own, x2, s_pair, sp_own):
    half = x1.shape[1]
    first, first_pair, _ = where_am_i()
    m0, m1 = ordered(first, x1[:half], got1[:half])
    s0, s1 = ordered(first, s_own[...], got1[half:])
    x2[:half] = dot(m1, m0)
    s = dot(s0, m1, 1, 1) + s1
    s_pair[...] = s
    rows = s.shape[0] // 2
    keep, send = ordered(first_pair, s[:rows], s[rows:])
    x2[half:] = send
    sp_own[...] = keep


def pair_backward(x1, got1, s_own, x3, got3, g_own, x4, gp_own):
    half = x1.shape[1]
    first, first_pair, _ = where_am_i()
    m0, _ = ordered(first, x1[:half], got1[:half])
    s0, _ = ordered(first, s_own[...], got1[half:])
    gg0, gg1 = ordered(first, x3[:half], got3[:half])
    g0, g1 = ordered(first, g_own[...], got3[half:])
    both = dot(jnp.concatenate([gg1, g1 - dot(s0, gg1)], axis=0), m0)
    x4[:half] = dot(m0, both[:half], 0, 0) + gg0
    g = both[half:] + g0
    rows = g.shape[0] // 2
    keep, send = ordered(first_pair, g[:rows], g[rows:])
    x4[half:] = send
    gp_own[...] = keep


def group_forward(x2, got2, sp_own, s_group):
    half = x2.shape[1]
    _, first_pair, _ = where_am_i()
    _, n1 = ordered(first_pair, x2[:half], got2[:half])
    s0, s1 = ordered(first_pair, sp_own[...], got2[half:])
    s_group[...] = dot(s0, n1, 1, 1) + s1


def group_map(x2, got2, n_group):
    half = x2.shape[1]
    _, first_pair, _ = where_am_i()
    n0, n1 = ordered(first_pair, x2[:half], got2[:half])
    n_group[...] = dot(n1, n0)


def group_backward(x2, got2, sp_own, x4, got4, gp_own, gg_group, g_group):
    half = x2.shape[1]
    _, first_pair, _ = where_am_i()
    n0, _ = ordered(first_pair, x2[:half], got2[:half])
    s0, _ = ordered(first_pair, sp_own[...], got2[half:])
    gg0, gg1 = ordered(first_pair, x4[:half], got4[:half])
    g0, g1 = ordered(first_pair, gp_own[...], got4[half:])
    both = dot(jnp.concatenate([gg1, g1 - dot(s0, gg1)], axis=0), n0)
    gg_group[...] = dot(n0, both[:half], 0, 0) + gg0
    g_group[...] = both[half:] + g0


def forward_hop(step, got, t_in, n_group, s_group, t_out, out):
    _, _, group = where_am_i()
    t = jnp.where(group == step + 1, got[...], t_in[...])
    t_out[...] = t
    out[...] = dot(t, n_group[...], 1, 1) + s_group[...]


def turn(step, got, t_in, gg_group, g_group, t_out, local):
    _, _, group = where_am_i()
    t = jnp.where(group == step + 1, got[...], t_in[...])
    t_out[...] = t
    local[...] = g_group[...] - dot(t, gg_group[...])


def backward_hop(step, got, u_in, n_group, local, u_out, out):
    _, _, group = where_am_i()
    u = jnp.where(group == step, got[...], u_in[...])
    u_out[...] = u
    out[...] = dot(u, n_group[...]) + local[...]


def spread_forward(t_in, x2, got2, sp_own, x4, got4, gp_own, x5, kept):
    half = x2.shape[1]
    rows = t_in.shape[0]
    _, first_pair, _ = where_am_i()
    n0, _ = ordered(first_pair, x2[:half], got2[:half])
    s0, _ = ordered(first_pair, sp_own[...], got2[half:])
    _, gg1 = ordered(first_pair, x4[:half], got4[:half])
    _, g1 = ordered(first_pair, gp_own[...], got4[half:])
    t_mid = dot(t_in[...], n0, 1, 1) + s0
    rest = g1 - dot(t_mid, gg1)
    keep, send = ordered(first_pair, t_in[...], t_mid)
    x5[:rows] = send
    x5[rows:] = rest
    kept[:rows] = keep
    kept[rows:] = rest


def pair_states(kept, got5, x1, got1, s_own, x3, got3, g_own, x6, t_own, rest_pair, rest_block):
    half = x1.shape[1]
    rows = kept.shape[0] // 2
    first, first_pair, _ = where_am_i()
    t = jnp.concatenate(ordered(first_pair, kept[:rows], got5[:rows]), axis=0)
    rest_pair[...] = jnp.concatenate(ordered(first_pair, kept[rows:], got5[rows:]), axis=0)
    m0, _ = ordered(first, x1[:half], got1[:half])
    s0, _ = ordered(first, s_own[...], got1[half:])
    _, gg1 = ordered(first, x3[:half], got3[:half])
    _, g1 = ordered(first, g_own[...], got3[half:])
    t_mid = dot(t, m0, 1, 1) + s0
    rest_block[...] = g1 - dot(t_mid, gg1)
    keep, send = ordered(first, t, t_mid)
    x6[...] = send
    t_own[...] = keep


def block_rows(t_own, got6, solved, p, d, early):
    first, _, _ = where_am_i()
    t = jnp.concatenate(ordered(first, t_own[...], got6[...]), axis=0)
    early[...] = dot(solved[...] - dot(t, p[...], 1, 1), d[...])


def spread_backward(*refs):
    u_in, x2, got2, rest_pair, x1, got1, rest_block = refs[:7]
    extra = refs[7:-2]
    x7, u_own = refs[-2:]
    half = x1.shape[1]
    first, first_pair, group = where_am_i()
    other = jnp.zeros_like(u_in)
    for step, ref in enumerate(extra):
        other = jnp.where(group == step, ref[...], other)
    u = jnp.concatenate(ordered(first_pair, u_in[...], other), axis=0)
    _, n1 = ordered(first_pair, x2[:half], got2[:half])
    u = jnp.where(first_pair, dot(u, n1) + rest_pair[...], u)
    _, m1 = ordered(first, x1[:half], got1[:half])
    keep, send = ordered(first, dot(u, m1) + rest_block[...], u)
    x7[...] = send
    u_own[...] = keep


def block_weights(u_own, got7, early, d, xa, xb, weights):
    first, _, _ = where_am_i()
    typed = d.shape[0]
    half = u_own.shape[1]
    u = jnp.concatenate(ordered(first, u_own[...], got7[...]), axis=0)
    w = (early[...] - dot(u, d[typed - half :])).astype(bf16)
    weights[...] = w
    a, b = ordered(first, w[:, :half], w[:, typed - half :])
    xa[...] = a
    xb[...] = b


def contract(values, coefs):
    return lax.dot_general(values, coefs, (((1,), (1,)), ((), ())), preferred_element_type=f32)


def mask_coefs(coefs, anchor, masked):
    untyped, span = coefs.shape
    half = span // 4
    typed = span - 2 * half
    place = lax.axis_index(AXIS)
    total = lax.axis_size(AXIS) * typed
    columns = place * typed - half + lax.broadcasted_iota(jnp.int32, (untyped, span), 1)
    within = (jnp.abs(columns - anchor[...]) <= half) & (columns >= 0) & (columns < total)
    masked[...] = jnp.where(within, coefs[...].astype(f32), 0.0).astype(bf16)


def impute_own(weights, masked, out):
    half = masked.shape[1] // 4
    typed = weights.shape[1]
    out[...] = contract(weights[...], masked[:, half : half + typed])


def impute_edges(acc, got_a, got_b, masked, out):
    first, _, _ = where_am_i()
    half = got_a.shape[1]
    span = masked.shape[1]
    left, right = ordered(first, got_a[...], got_b[...])
    out[...] = acc[...] + contract(left, masked[:, :half]) + contract(right, masked[:, span - half :])


def swap(block, distance):
    n = lax.axis_size(AXIS)
    return lax.ppermute(block, AXIS, [(i, i ^ distance) for i in range(n)])


def hop_pairs(n, step, across):
    groups = n // GROUP
    pairs = []
    for i in range(n):
        g = i // GROUP
        to = g + 1 if g % 2 == step % 2 else g - 1
        if 0 <= to < groups:
            pairs.append((i, (i + (to - g) * GROUP) ^ across))
        else:
            pairs.append((i, i))
    return pairs


def hop(block, step, across=0):
    return lax.ppermute(block, AXIS, hop_pairs(lax.axis_size(AXIS), step, across))


def swap_chips(block):
    n = lax.axis_size(AXIS)
    pairs = []
    for i in range(n):
        to = i + 1 if i % 2 else i - 1
        pairs.append((i, to if 0 <= to < n else i))
    return lax.ppermute(block, AXIS, pairs)


def per_device(z, diag_inverse, coupling, impute_coef, anchor):
    d = diag_inverse[0]
    c = coupling[0]
    typed = d.shape[0]
    half = c.shape[1]
    traits = z.shape[0]
    untyped, span = impute_coef.shape
    assert span == typed + 2 * half and typed == 2 * half
    groups = lax.axis_size(AXIS) // GROUP
    two, four = traits // 2, traits // 4
    square = (half, half)
    sq, h2, h4 = (square, f32), ((two, half), f32), ((four, half), f32)
    x2_shape, x4_shape = ((half + two, half), f32), ((half + four, half), f32)

    x1, s_own = call(tail_part, [x2_shape, h2], z, d, c)
    got1 = swap(x1, 1)
    x3, g_own, solved, p = call(
        head_part, [x2_shape, h2, ((traits, typed), f32), ((typed, half), f32)], z, d, c, x1, s_own
    )
    x2, s_pair, sp_own = call(pair_forward, [x4_shape, h2, h4], x1, got1, s_own, after=(p,))
    got2 = swap(x2, 2)
    got3 = swap(x3, 1)
    masked = call(mask_coefs, ((untyped, span), bf16), impute_coef, anchor[:, None], after=(x2,))
    x4, gp_own = call(pair_backward, [x4_shape, h4], x1, got1, s_own, x3, got3, g_own, after=(x2,))
    s_group = call(group_forward, h4, x2, got2, sp_own, after=(x4, masked))
    n_group = call(group_map, sq, x2, got2, after=(s_group,))

    t_in = jnp.zeros((four, half), f32)
    out = s_group
    got4 = swap(x4, 2)
    for step in range(groups - 2):
        got = hop(out, step)
        t_in, out = call(
            functools.partial(forward_hop, step), [h4, h4], got, t_in, n_group, s_group
        )
    gg_group, g_group = call(
        group_backward, [sq, h4], x2, got2, sp_own, x4, got4, gp_own, after=(out,)
    )
    step = groups - 2
    got = hop(out, step)
    t_in, local = call(functools.partial(turn, step), [h4, h4], got, t_in, gg_group, g_group)

    got = hop(local, step)
    extra = [hop(local, step, 2)]
    x5, kept = call(
        spread_forward, [h2, h2], t_in, x2, got2, sp_own, x4, got4, gp_own, after=(local,)
    )
    got5 = swap(x5, 2)
    x6, t_own, rest_pair, rest_block = call(
        pair_states, [h2] * 4, kept, got5, x1, got1, s_own, x3, got3, g_own
    )
    got6 = swap(x6, 1)
    u_in = jnp.zeros((four, half), f32)
    for step in reversed(range(groups - 1)):
        if step < groups - 2:
            got = hop(out, step)
            extra.insert(0, hop(out, step, 2))
        u_in, out = call(
            functools.partial(backward_hop, step), [h4, h4], got, u_in, n_group, local,
            after=(x6,) if step == groups - 2 else (),
        )
    early = call(block_rows, ((traits, typed), f32), t_own, got6, solved, p, d)
    x7, u_own = call(
        spread_backward, [h2, h2], u_in, x2, got2, rest_pair, x1, got1, rest_block, *extra
    )
    got7 = swap(x7, 1)
    xa, xb, weights = call(
        block_weights, [(square, bf16), (square, bf16), ((traits, typed), bf16)], u_own, got7, early, d
    )
    got_a = swap_chips(xa)
    got_b = swap(xb, 1)
    acc = call(impute_own, ((traits, untyped), f32), weights, masked)
    return call(impute_edges, ((traits, untyped), f32), acc, got_a, got_b, masked)


def solution(mesh):
    in_specs = (
        P(None, ("seg", AXIS)),
        P(("seg", AXIS), None, None),
        P(("seg", AXIS), None, None),
        P(("seg", AXIS), None),
        P(("seg", AXIS)),
    )
    return jax.shard_map(
        per_device, mesh=mesh, in_specs=in_specs, out_specs=P(None, ("seg", AXIS)), check_vma=False
    )
```

```python
import functools

import jax
import jax.numpy as jnp
from jax import lax
from jax.experimental import pallas as pl
from jax.experimental.pallas import tpu as pltpu
from jax.sharding import PartitionSpec as P

AXIS = "genome"
GROUP = 4
f32 = jnp.float32
bf16 = jnp.bfloat16


def parts(x):
    high = x.astype(bf16)
    return high, (x - high.astype(f32)).astype(bf16)


def dot(a, b, ca=1, cb=0):
    ah, al = parts(a)
    bh, bl = parts(b)
    return lax.dot_general(
        jnp.concatenate([al, ah, ah], axis=ca),
        jnp.concatenate([bh, bl, bh], axis=cb),
        (((ca,), (cb,)), ((), ())),
        preferred_element_type=f32,
    )


def where_am_i():
    place = lax.axis_index(AXIS)
    return place % 2 == 0, (place // 2) % 2 == 0, place // GROUP


def ordered(first, own, other):
    return jnp.where(first, own, other), jnp.where(first, other, own)


def call(kernel, outs, *args, after=(), hbm=False, scratch=()):
    n_in, n_after = len(args), len(after)

    def body(*refs):
        kernel(*refs[:n_in], *refs[n_in + n_after :])

    single = not isinstance(outs, list)
    shapes = [outs] if single else outs
    vmem = pl.BlockSpec(memory_space=pltpu.VMEM)
    anywhere = pl.BlockSpec(memory_space=pl.ANY)
    if hbm:
        args = [pltpu.with_memory_space_constraint(a, pltpu.HBM) for a in args]
    got = pl.pallas_call(
        body,
        out_shape=[jax.ShapeDtypeStruct(s, t) for s, t in shapes],
        in_specs=[anywhere if hbm else vmem] * n_in + [anywhere] * n_after,
        out_specs=[vmem] * len(shapes),
        scratch_shapes=scratch,
        compiler_params=pltpu.CompilerParams(vmem_limit_bytes=8 * 2**20),
        name=kernel.__name__ if hasattr(kernel, "__name__") else kernel.func.__name__,
    )(*args, *after)
    return got[0] if single else got


def tail_part(z_in, d_in, c_in, x1, s_own, z, d, c, sems):
    half = c.shape[1]
    rows = z.shape[0] // 2
    head = d.shape[0] - half
    first, _, _ = where_am_i()
    pieces = [
        (d_in.at[pl.ds(head, half)], d.at[pl.ds(head, half)]),
        (c_in, c),
        (z_in, z),
        (d_in.at[pl.ds(0, head)], d.at[pl.ds(0, head)]),
    ]
    copies = [pltpu.make_async_copy(src, dst, sems.at[i]) for i, (src, dst) in enumerate(pieces)]
    for copy in copies:
        copy.start()
    copies[0].wait()
    copies[1].wait()
    tail = d[head:]
    x1[:half] = -dot(tail, c[...])
    copies[2].wait()
    s = dot(z[...], tail, 1, 1)
    keep, send = ordered(first, s[:rows], s[rows:])
    x1[half:] = send
    s_own[...] = keep
    copies[3].wait()


def head_part(z, d, c, x1, s_own, x3, g_own, solved, p):
    half = c.shape[1]
    rows = z.shape[0] // 2
    head = d.shape[0] - half
    first, _, _ = where_am_i()
    p[:head] = dot(d[:head], c[...])
    p[head:] = -x1[:half]
    solved[:, :head] = dot(z[...], d[:head], 1, 1)
    low, high = ordered(first, s_own[...], x1[half:])
    solved[:rows, head:] = low
    solved[rows:, head:] = high
    g = dot(solved[...], p[...])
    keep, send = ordered(first, g[:rows], g[rows:])
    x3[:half] = dot(p[...], p[...], 0, 0)
    x3[half:] = send
    g_own[...] = keep


def pair_forward(x1, got1, s_own, x2, sp_own):
    half = x1.shape[1]
    first, first_pair, _ = where_am_i()
    m0, m1 = ordered(first, x1[:half], got1[:half])
    s0, s1 = ordered(first, s_own[...], got1[half:])
    x2[:half] = dot(m1, m0)
    s = dot(s0, m1, 1, 1) + s1
    rows = s.shape[0] // 2
    keep, send = ordered(first_pair, s[:rows], s[rows:])
    x2[half:] = send
    sp_own[...] = keep


def pair_backward(x1, got1, s_own, x3, got3, g_own, x4, gp_own):
    half = x1.shape[1]
    first, first_pair, _ = where_am_i()
    m0, _ = ordered(first, x1[:half], got1[:half])
    s0, _ = ordered(first, s_own[...], got1[half:])
    gg0, gg1 = ordered(first, x3[:half], got3[:half])
    g0, g1 = ordered(first, g_own[...], got3[half:])
    both = dot(jnp.concatenate([gg1, g1 - dot(s0, gg1)], axis=0), m0)
    x4[:half] = dot(m0, both[:half], 0, 0) + gg0
    g = both[half:] + g0
    rows = g.shape[0] // 2
    keep, send = ordered(first_pair, g[:rows], g[rows:])
    x4[half:] = send
    gp_own[...] = keep


def group_forward(x2, got2, sp_own, s_group):
    half = x2.shape[1]
    _, first_pair, _ = where_am_i()
    _, n1 = ordered(first_pair, x2[:half], got2[:half])
    s0, s1 = ordered(first_pair, sp_own[...], got2[half:])
    s_group[...] = dot(s0, n1, 1, 1) + s1


def group_map(x2, got2, n_group):
    half = x2.shape[1]
    _, first_pair, _ = where_am_i()
    n0, n1 = ordered(first_pair, x2[:half], got2[:half])
    n_group[...] = dot(n1, n0)


def group_backward(x2, got2, sp_own, x4, got4, gp_own, gg_group, g_group):
    half = x2.shape[1]
    _, first_pair, _ = where_am_i()
    n0, _ = ordered(first_pair, x2[:half], got2[:half])
    s0, _ = ordered(first_pair, sp_own[...], got2[half:])
    gg0, gg1 = ordered(first_pair, x4[:half], got4[:half])
    g0, g1 = ordered(first_pair, gp_own[...], got4[half:])
    both = dot(jnp.concatenate([gg1, g1 - dot(s0, gg1)], axis=0), n0)
    gg_group[...] = dot(n0, both[:half], 0, 0) + gg0
    g_group[...] = both[half:] + g0


def forward_hop(step, got, t_in, n_group, s_group, t_out, out):
    _, _, group = where_am_i()
    t = jnp.where(group == step + 1, got[...], t_in[...])
    t_out[...] = t
    out[...] = dot(t, n_group[...], 1, 1) + s_group[...]


def turn(step, got, t_in, gg_group, g_group, t_out, local):
    _, _, group = where_am_i()
    t = jnp.where(group == step + 1, got[...], t_in[...])
    t_out[...] = t
    local[...] = g_group[...] - dot(t, gg_group[...])


def backward_hop(step, got, u_in, n_group, local, u_out, out):
    _, _, group = where_am_i()
    u = jnp.where(group == step, got[...], u_in[...])
    u_out[...] = u
    out[...] = dot(u, n_group[...]) + local[...]


def arrive(step, got, u_in, u_out):
    _, _, group = where_am_i()
    u_out[...] = jnp.where(group == step, got[...], u_in[...])


def spread_forward(t_in, x2, got2, sp_own, x4, got4, gp_own, x5, kept):
    half = x2.shape[1]
    rows = t_in.shape[0]
    _, first_pair, _ = where_am_i()
    n0, _ = ordered(first_pair, x2[:half], got2[:half])
    s0, _ = ordered(first_pair, sp_own[...], got2[half:])
    _, gg1 = ordered(first_pair, x4[:half], got4[:half])
    _, g1 = ordered(first_pair, gp_own[...], got4[half:])
    t_mid = dot(t_in[...], n0, 1, 1) + s0
    rest = g1 - dot(t_mid, gg1)
    keep, send = ordered(first_pair, t_in[...], t_mid)
    x5[:rows] = send
    x5[rows:] = rest
    kept[:rows] = keep
    kept[rows:] = rest


def pair_states(kept, got5, x1, got1, s_own, x3, got3, g_own, x6, t_own, rest_pair, rest_block):
    half = x1.shape[1]
    rows = kept.shape[0] // 2
    first, first_pair, _ = where_am_i()
    t = jnp.concatenate(ordered(first_pair, kept[:rows], got5[:rows]), axis=0)
    rest_pair[...] = jnp.concatenate(ordered(first_pair, kept[rows:], got5[rows:]), axis=0)
    m0, _ = ordered(first, x1[:half], got1[:half])
    s0, _ = ordered(first, s_own[...], got1[half:])
    _, gg1 = ordered(first, x3[:half], got3[:half])
    _, g1 = ordered(first, g_own[...], got3[half:])
    t_mid = dot(t, m0, 1, 1) + s0
    rest_block[...] = g1 - dot(t_mid, gg1)
    keep, send = ordered(first, t, t_mid)
    x6[...] = send
    t_own[...] = keep


def block_rows(t_own, got6, solved, p, d, early):
    first, _, _ = where_am_i()
    t = jnp.concatenate(ordered(first, t_own[...], got6[...]), axis=0)
    early[...] = dot(solved[...] - dot(t, p[...], 1, 1), d[...])


def spread_backward(u_in, got_u, x2, got2, rest_pair, x1, got1, rest_block, x7, u_own):
    half = x1.shape[1]
    first, first_pair, _ = where_am_i()
    u = jnp.concatenate(ordered(first_pair, u_in[...], got_u[...]), axis=0)
    _, n1 = ordered(first_pair, x2[:half], got2[:half])
    u = jnp.where(first_pair, dot(u, n1) + rest_pair[...], u)
    _, m1 = ordered(first, x1[:half], got1[:half])
    keep, send = ordered(first, dot(u, m1) + rest_block[...], u)
    x7[...] = send
    u_own[...] = keep


def block_weights(u_own, got7, early, d, xa, xb, weights):
    first, _, _ = where_am_i()
    typed = d.shape[0]
    half = u_own.shape[1]
    u = jnp.concatenate(ordered(first, u_own[...], got7[...]), axis=0)
    w = (early[...] - dot(u, d[typed - half :])).astype(bf16)
    weights[...] = w
    a, b = ordered(first, w[:, :half], w[:, typed - half :])
    xa[...] = a
    xb[...] = b


def contract(values, coefs):
    return lax.dot_general(values, coefs, (((1,), (1,)), ((), ())), preferred_element_type=f32)


def mask_coefs(coefs, anchor, masked):
    untyped, span = coefs.shape
    half = span // 4
    typed = span - 2 * half
    place = lax.axis_index(AXIS)
    total = lax.axis_size(AXIS) * typed
    columns = place * typed - half + lax.broadcasted_iota(jnp.int32, (untyped, span), 1)
    within = (jnp.abs(columns - anchor[...]) <= half) & (columns >= 0) & (columns < total)
    masked[...] = jnp.where(within, coefs[...].astype(f32), 0.0).astype(bf16)


def impute_own(weights, masked, out):
    half = masked.shape[1] // 4
    typed = weights.shape[1]
    out[...] = contract(weights[...], masked[:, half : half + typed])


def impute_edges(acc, got_a, got_b, masked, out):
    first, _, _ = where_am_i()
    half = got_a.shape[1]
    span = masked.shape[1]
    left, right = ordered(first, got_a[...], got_b[...])
    out[...] = acc[...] + contract(left, masked[:, :half]) + contract(right, masked[:, span - half :])


def swap(block, distance):
    n = lax.axis_size(AXIS)
    return lax.ppermute(block, AXIS, [(i, i ^ distance) for i in range(n)])


def hop(block, step):
    pairs = []
    for i in range(lax.axis_size(AXIS)):
        g = i // GROUP
        pairs.append((i, i + GROUP if g == step else i - GROUP if g == step + 1 else i))
    return lax.ppermute(block, AXIS, pairs)


def swap_chips(block):
    n = lax.axis_size(AXIS)
    pairs = []
    for i in range(n):
        to = i + 1 if i % 2 else i - 1
        pairs.append((i, to if 0 <= to < n else i))
    return lax.ppermute(block, AXIS, pairs)


def per_device(z, diag_inverse, coupling, impute_coef, anchor):
    d = diag_inverse[0]
    c = coupling[0]
    typed = d.shape[0]
    half = c.shape[1]
    traits = z.shape[0]
    untyped, span = impute_coef.shape
    assert span == typed + 2 * half and typed == 2 * half
    groups = lax.axis_size(AXIS) // GROUP
    two, four = traits // 2, traits // 4
    square = (half, half)
    sq, h2, h4 = (square, f32), ((two, half), f32), ((four, half), f32)
    x2_shape, x4_shape = ((half + two, half), f32), ((half + four, half), f32)

    solved_shape, p_shape = ((traits, typed), f32), ((typed, half), f32)
    x1, s_own, z, d, c = call(
        tail_part, [x2_shape, h2, solved_shape, ((typed, typed), f32), p_shape], z, d, c,
        hbm=True, scratch=[pltpu.SemaphoreType.DMA((4,))],
    )
    got1 = swap(x1, 1)
    x3, g_own, solved, p = call(
        head_part, [x2_shape, h2, solved_shape, p_shape], z, d, c, x1, s_own
    )
    x2, sp_own = call(pair_forward, [x4_shape, h4], x1, got1, s_own, after=(p,))
    got2 = swap(x2, 2)
    got3 = swap(x3, 1)
    masked = call(mask_coefs, ((untyped, span), bf16), impute_coef, anchor[:, None], after=(x2,))
    x4, gp_own = call(
        pair_backward, [x4_shape, h4], x1, got1, s_own, x3, got3, g_own, after=(x2,)
    )
    s_group = call(group_forward, h4, x2, got2, sp_own, after=(x4, masked))
    n_group = call(group_map, sq, x2, got2, after=(s_group,))

    t_in = jnp.zeros((four, half), f32)
    out = s_group
    got4 = swap(x4, 2)
    for step in range(groups - 2):
        got = hop(out, step)
        t_in, out = call(
            functools.partial(forward_hop, step), [h4, h4], got, t_in, n_group, s_group
        )
    gg_group, g_group = call(
        group_backward, [sq, h4], x2, got2, sp_own, x4, got4, gp_own, after=(out,)
    )
    last = groups - 2
    got = hop(out, last)
    t_in, local = call(functools.partial(turn, last), [h4, h4], got, t_in, gg_group, g_group)

    u_in = jnp.zeros((four, half), f32)
    out = local
    for step in reversed(range(groups - 1)):
        got = hop(out, step)
        if step == last:
            x5, kept = call(
                spread_forward, [h2, h2], t_in, x2, got2, sp_own, x4, got4, gp_own, after=(local,)
            )
            got5 = swap(x5, 2)
            x6, t_own, rest_pair, rest_block = call(
                pair_states, [h2] * 4, kept, got5, x1, got1, s_own, x3, got3, g_own
            )
            got6 = swap(x6, 1)
            early = call(block_rows, solved_shape, t_own, got6, solved, p, d)
        if step:
            u_in, out = call(
                functools.partial(backward_hop, step), [h4, h4], got, u_in, n_group, local
            )
        else:
            u_in = call(functools.partial(arrive, step), h4, got, u_in)
    got_u = swap(u_in, 2)
    x7, u_own = call(
        spread_backward, [h2, h2], u_in, got_u, x2, got2, rest_pair, x1, got1, rest_block
    )
    got7 = swap(x7, 1)
    xa, xb, weights = call(
        block_weights, [(square, bf16), (square, bf16), ((traits, typed), bf16)], u_own, got7, early, d
    )
    got_a = swap_chips(xa)
    got_b = swap(xb, 1)
    acc = call(impute_own, ((traits, untyped), f32), weights, masked)
    return call(impute_edges, ((traits, untyped), f32), acc, got_a, got_b, masked)


def solution(mesh):
    in_specs = (
        P(None, ("seg", AXIS)),
        P(("seg", AXIS), None, None),
        P(("seg", AXIS), None, None),
        P(("seg", AXIS), None),
        P(("seg", AXIS)),
    )
    return jax.shard_map(
        per_device, mesh=mesh, in_specs=in_specs, out_specs=P(None, ("seg", AXIS)), check_vma=False
    )
```

```python
import functools

import jax
import jax.numpy as jnp
from jax import lax
from jax.experimental import pallas as pl
from jax.experimental.pallas import tpu as pltpu
from jax.sharding import PartitionSpec as P

AXIS = "genome"
GROUP = 4
f32 = jnp.float32
bf16 = jnp.bfloat16


def parts(x):
    high = x.astype(bf16)
    return high, (x - high.astype(f32)).astype(bf16)


def dot(a, b, ca=1, cb=0):
    ah, al = parts(a)
    bh, bl = parts(b)
    return lax.dot_general(
        jnp.concatenate([al, ah, ah], axis=ca),
        jnp.concatenate([bh, bl, bh], axis=cb),
        (((ca,), (cb,)), ((), ())),
        preferred_element_type=f32,
    )


def where_am_i():
    place = lax.axis_index(AXIS)
    return place % 2 == 0, (place // 2) % 2 == 0, place // GROUP


def ordered(first, own, other):
    return jnp.where(first, own, other), jnp.where(first, other, own)


def call(kernel, outs, *args, after=(), hbm=False, last=False, scratch=()):
    n_in, n_after = len(args), len(after)

    def body(*refs):
        kernel(*refs[:n_in], *refs[n_in + n_after :])

    single = not isinstance(outs, list)
    shapes = [outs] if single else outs
    vmem = pl.BlockSpec(memory_space=pltpu.VMEM)
    anywhere = pl.BlockSpec(memory_space=pl.ANY)
    if hbm:
        args = [pltpu.with_memory_space_constraint(a, pltpu.HBM) for a in args]
    got = pl.pallas_call(
        body,
        out_shape=[jax.ShapeDtypeStruct(s, t) if last else pltpu.VMEM(s, t) for s, t in shapes],
        in_specs=[anywhere if hbm else vmem] * n_in + [anywhere] * n_after,
        out_specs=[vmem] * len(shapes),
        scratch_shapes=scratch,
        compiler_params=pltpu.CompilerParams(vmem_limit_bytes=8 * 2**20),
        name=kernel.__name__ if hasattr(kernel, "__name__") else kernel.func.__name__,
    )(*args, *after)
    return got[0] if single else got


def tail_part(z_in, d_in, c_in, x1, s_own, z, d, c, sems):
    half = c.shape[1]
    rows = z.shape[0] // 2
    head = d.shape[0] - half
    first, _, _ = where_am_i()
    pieces = [
        (d_in.at[pl.ds(head, half)], d.at[pl.ds(head, half)]),
        (c_in, c),
        (z_in, z),
        (d_in.at[pl.ds(0, head)], d.at[pl.ds(0, head)]),
    ]
    copies = [pltpu.make_async_copy(src, dst, sems.at[i]) for i, (src, dst) in enumerate(pieces)]
    for copy in copies[:3]:
        copy.start()
    copies[0].wait()
    copies[1].wait()
    copies[3].start()
    tail = d[head:]
    x1[:half] = -dot(tail, c[...])
    copies[2].wait()
    s = dot(z[...], tail, 1, 1)
    keep, send = ordered(first, s[:rows], s[rows:])
    x1[half:] = send
    s_own[...] = keep
    copies[3].wait()


def head_part(z, d, c, x1, s_own, x3, g_own, solved, p):
    half = c.shape[1]
    rows = z.shape[0] // 2
    head = d.shape[0] - half
    first, _, _ = where_am_i()
    p[:head] = dot(d[:head], c[...])
    p[head:] = -x1[:half]
    solved[:, :head] = dot(z[...], d[:head], 1, 1)
    low, high = ordered(first, s_own[...], x1[half:])
    solved[:rows, head:] = low
    solved[rows:, head:] = high
    g = dot(solved[...], p[...])
    keep, send = ordered(first, g[:rows], g[rows:])
    x3[:half] = dot(p[...], p[...], 0, 0)
    x3[half:] = send
    g_own[...] = keep


def pair_forward(x1, got1, s_own, x2, n_own, sp_own):
    half = x1.shape[1]
    first, first_pair, _ = where_am_i()
    m0, m1 = ordered(first, x1[:half], got1[:half])
    s0, s1 = ordered(first, s_own[...], got1[half:])
    n = dot(m1, m0)
    n_own[...] = n
    x2[: half // 2] = jnp.where(first, n[: half // 2], n[half // 2 :])
    s = dot(s0, m1, 1, 1) + s1
    rows = s.shape[0] // 2
    keep, send = ordered(first_pair, s[:rows], s[rows:])
    x2[half // 2 :] = send
    sp_own[...] = keep


def pair_backward(x1, got1, s_own, x3, got3, g_own, x4, gg_own, gp_own):
    half = x1.shape[1]
    first, first_pair, _ = where_am_i()
    m0, _ = ordered(first, x1[:half], got1[:half])
    s0, _ = ordered(first, s_own[...], got1[half:])
    gg0, gg1 = ordered(first, x3[:half], got3[:half])
    g0, g1 = ordered(first, g_own[...], got3[half:])
    both = dot(jnp.concatenate([gg1, g1 - dot(s0, gg1)], axis=0), m0)
    gg = dot(m0, both[:half], 0, 0) + gg0
    gg_own[...] = gg
    x4[: half // 2] = jnp.where(first, gg[: half // 2], gg[half // 2 :])
    g = both[half:] + g0
    rows = g.shape[0] // 2
    keep, send = ordered(first_pair, g[:rows], g[rows:])
    x4[half // 2 :] = send
    gp_own[...] = keep


def pair_matrices(own, got, got_core):
    half = own.shape[1]
    first, first_pair, _ = where_am_i()
    other = jnp.concatenate(ordered(first, got[: half // 2], got_core[: half // 2]), axis=0)
    return ordered(first_pair, own[...], other)


def pair_vectors(own, got):
    _, first_pair, _ = where_am_i()
    return ordered(first_pair, own[...], got[got.shape[1] // 2 :])


def relay(got, out):
    out[...] = got[: out.shape[0]]


def group_forward(n_own, got2, got2_core, sp_own, s_group):
    _, n1 = pair_matrices(n_own, got2, got2_core)
    s0, s1 = pair_vectors(sp_own, got2)
    s_group[...] = dot(s0, n1, 1, 1) + s1


def group_map(n_own, got2, got2_core, n_group, n_first, n_second):
    n0, n1 = pair_matrices(n_own, got2, got2_core)
    n_first[...] = n0
    n_second[...] = n1
    n_group[...] = dot(n1, n0)


def group_backward(n_first, got2, sp_own, gg_own, got4, got4_core, gp_own, gg_group, g_group, gg_second, g_second):
    n0 = n_first[...]
    s0, _ = pair_vectors(sp_own, got2)
    gg0, gg1 = pair_matrices(gg_own, got4, got4_core)
    g0, g1 = pair_vectors(gp_own, got4)
    gg_second[...] = gg1
    g_second[...] = g1
    both = dot(jnp.concatenate([gg1, g1 - dot(s0, gg1)], axis=0), n0)
    gg_group[...] = dot(n0, both[: gg1.shape[0]], 0, 0) + gg0
    g_group[...] = both[gg1.shape[0] :] + g0


def forward_hop(step, got, t_in, n_group, s_group, t_out, out):
    _, _, group = where_am_i()
    t = jnp.where(group == step + 1, got[...], t_in[...])
    t_out[...] = t
    out[...] = dot(t, n_group[...], 1, 1) + s_group[...]


def turn(step, got, t_in, gg_group, g_group, t_out, local):
    _, _, group = where_am_i()
    t = jnp.where(group == step + 1, got[...], t_in[...])
    t_out[...] = t
    local[...] = g_group[...] - dot(t, gg_group[...])


def backward_hop(step, got, u_in, n_group, local, u_out, out):
    _, _, group = where_am_i()
    u = jnp.where(group == step, got[...], u_in[...])
    u_out[...] = u
    out[...] = dot(u, n_group[...]) + local[...]


def arrive(step, got, u_in, u_out):
    _, _, group = where_am_i()
    u_out[...] = jnp.where(group == step, got[...], u_in[...])


def spread_forward(t_in, n_first, got2, sp_own, gg_second, g_second, x5, kept):
    rows = t_in.shape[0]
    _, first_pair, _ = where_am_i()
    s0, _ = pair_vectors(sp_own, got2)
    t_mid = dot(t_in[...], n_first[...], 1, 1) + s0
    rest = g_second[...] - dot(t_mid, gg_second[...])
    keep, send = ordered(first_pair, t_in[...], t_mid)
    x5[:rows] = send
    x5[rows:] = rest
    kept[:rows] = keep
    kept[rows:] = rest


def pair_states(kept, got5, x1, got1, s_own, x3, got3, g_own, x6, t_own, rest_pair, rest_block):
    half = x1.shape[1]
    rows = kept.shape[0] // 2
    first, first_pair, _ = where_am_i()
    t = jnp.concatenate(ordered(first_pair, kept[:rows], got5[:rows]), axis=0)
    rest_pair[...] = jnp.concatenate(ordered(first_pair, kept[rows:], got5[rows:]), axis=0)
    m0, _ = ordered(first, x1[:half], got1[:half])
    s0, _ = ordered(first, s_own[...], got1[half:])
    _, gg1 = ordered(first, x3[:half], got3[:half])
    _, g1 = ordered(first, g_own[...], got3[half:])
    t_mid = dot(t, m0, 1, 1) + s0
    rest_block[...] = g1 - dot(t_mid, gg1)
    keep, send = ordered(first, t, t_mid)
    x6[...] = send
    t_own[...] = keep


def block_rows(t_own, got6, solved, p, d, early):
    first, _, _ = where_am_i()
    t = jnp.concatenate(ordered(first, t_own[...], got6[...]), axis=0)
    early[...] = dot(solved[...] - dot(t, p[...], 1, 1), d[...])


def spread_backward(u_in, got_u, n_second, rest_pair, x1, got1, rest_block, x7, u_own):
    half = x1.shape[1]
    first, first_pair, _ = where_am_i()
    u = jnp.concatenate(ordered(first_pair, u_in[...], got_u[...]), axis=0)
    u = jnp.where(first_pair, dot(u, n_second[...]) + rest_pair[...], u)
    _, m1 = ordered(first, x1[:half], got1[:half])
    keep, send = ordered(first, dot(u, m1) + rest_block[...], u)
    x7[...] = send
    u_own[...] = keep


def block_weights(u_own, got7, early, d, xa, xb, weights):
    first, _, _ = where_am_i()
    typed = d.shape[0]
    half = u_own.shape[1]
    u = jnp.concatenate(ordered(first, u_own[...], got7[...]), axis=0)
    w = (early[...] - dot(u, d[typed - half :])).astype(bf16)
    weights[...] = w
    a, b = ordered(first, w[:, :half], w[:, typed - half :])
    xa[...] = a
    xb[...] = b


def contract(values, coefs):
    return lax.dot_general(values, coefs, (((1,), (1,)), ((), ())), preferred_element_type=f32)


def mask_coefs(coefs_in, anchor_in, masked, coefs, anchor, sems):
    untyped, span = coefs.shape
    half = span // 4
    typed = span - 2 * half
    tile = 128
    place = lax.axis_index(AXIS)
    total = lax.axis_size(AXIS) * typed
    copies = [pltpu.make_async_copy(anchor_in, anchor, sems.at[0])]
    for i in range(untyped // tile):
        rows = pl.ds(i * tile, tile)
        copies.append(pltpu.make_async_copy(coefs_in.at[rows], coefs.at[rows], sems.at[i + 1]))
    for copy in copies:
        copy.start()
    copies[0].wait()
    first_column = place * typed - half
    for i in range(untyped // tile):
        rows = pl.ds(i * tile, tile)
        nearest = jnp.broadcast_to(anchor[:, i * tile : (i + 1) * tile], (tile, tile)).T
        copies[i + 1].wait()
        for j in range(span // tile):
            lanes = pl.ds(j * tile, tile)
            columns = first_column + j * tile + lax.broadcasted_iota(jnp.int32, (tile, tile), 1)
            within = (jnp.abs(columns - nearest) <= half) & (columns >= 0) & (columns < total)
            masked[rows, lanes] = jnp.where(within, coefs[rows, lanes].astype(f32), 0.0).astype(bf16)


def impute_own(weights, masked, out):
    half = masked.shape[1] // 4
    typed = weights.shape[1]
    out[...] = contract(weights[...], masked[:, half : half + typed])


def impute_edges(acc, got_a, got_b, masked, out):
    first, _, _ = where_am_i()
    half = got_a.shape[1]
    span = masked.shape[1]
    left, right = ordered(first, got_a[...], got_b[...])
    out[...] = acc[...] + contract(left, masked[:, :half]) + contract(right, masked[:, span - half :])


def swap(block, distance):
    n = lax.axis_size(AXIS)
    return lax.ppermute(block, AXIS, [(i, i ^ distance) for i in range(n)])


def hop(block, step):
    pairs = []
    for i in range(lax.axis_size(AXIS)):
        g = i // GROUP
        pairs.append((i, i + GROUP if g == step else i - GROUP if g == step + 1 else i ^ 1))
    return lax.ppermute(block, AXIS, pairs)


def swap_chips(block):
    n = lax.axis_size(AXIS)
    return lax.ppermute(block, AXIS, [(i, (i + 1 if i % 2 else i - 1) % n) for i in range(n)])


def per_device(z, diag_inverse, coupling, impute_coef, anchor):
    d = diag_inverse[0]
    c = coupling[0]
    typed = d.shape[0]
    half = c.shape[1]
    traits = z.shape[0]
    untyped, span = impute_coef.shape
    assert span == typed + 2 * half and typed == 2 * half
    groups = lax.axis_size(AXIS) // GROUP
    two, four = traits // 2, traits // 4
    square = (half, half)
    sq, h2, h4 = (square, f32), ((two, half), f32), ((four, half), f32)
    x2_shape, x4_shape = ((half + two, half), f32), ((half // 2 + four, half), f32)

    solved_shape, p_shape = ((traits, typed), f32), ((typed, half), f32)
    x1, s_own, z, d, c = call(
        tail_part, [x2_shape, h2, solved_shape, ((typed, typed), f32), p_shape], z, d, c,
        hbm=True, scratch=[pltpu.SemaphoreType.DMA((4,))],
    )
    got1 = swap(x1, 1)
    x3, g_own, solved, p = call(
        head_part, [x2_shape, h2, solved_shape, p_shape], z, d, c, x1, s_own
    )
    x2, n_own, sp_own = call(pair_forward, [x4_shape, sq, h4], x1, got1, s_own, after=(p,))
    got2 = swap(x2, 2)
    got3 = swap(x3, 1)
    masked = call(
        mask_coefs, ((untyped, span), bf16), impute_coef, anchor[None, :], after=(x2,), hbm=True,
        scratch=[
            pltpu.VMEM((untyped, span), bf16),
            pltpu.VMEM((1, untyped), jnp.int32),
            pltpu.SemaphoreType.DMA((untyped // 128 + 1,)),
        ],
    )
    x4, gg_own, gp_own = call(
        pair_backward, [x4_shape, sq, h4], x1, got1, s_own, x3, got3, g_own, after=(x2,)
    )
    rows_half = ((half // 2, half), f32)
    got2_core = swap(call(relay, rows_half, got2, after=(x4, masked)), 1)
    s_group = call(group_forward, h4, n_own, got2, got2_core, sp_own)
    n_group, n_first, n_second = call(
        group_map, [sq] * 3, n_own, got2, got2_core, after=(s_group,)
    )

    t_in = jnp.zeros((four, half), f32)
    out = s_group
    got4 = swap(x4, 2)
    for step in range(groups - 2):
        got = hop(out, step)
        t_in, out = call(
            functools.partial(forward_hop, step), [h4, h4], got, t_in, n_group, s_group
        )
    got4_core = swap(call(relay, rows_half, got4, after=(out,)), 1)
    gg_group, g_group, gg_second, g_second = call(
        group_backward, [sq, h4, sq, h4],
        n_first, got2, sp_own, gg_own, got4, got4_core, gp_own, after=(out,),
    )
    last = groups - 2
    got = hop(out, last)
    t_in, local = call(functools.partial(turn, last), [h4, h4], got, t_in, gg_group, g_group)

    u_in = jnp.zeros((four, half), f32)
    out = local
    for step in reversed(range(groups - 1)):
        got = hop(out, step)
        if step == last:
            x5, kept = call(
                spread_forward, [h2, h2], t_in, n_first, got2, sp_own, gg_second, g_second,
                after=(local,),
            )
            got5 = swap(x5, 2)
            x6, t_own, rest_pair, rest_block = call(
                pair_states, [h2] * 4, kept, got5, x1, got1, s_own, x3, got3, g_own
            )
            got6 = swap(x6, 1)
            early = call(block_rows, solved_shape, t_own, got6, solved, p, d)
        if step:
            u_in, out = call(
                functools.partial(backward_hop, step), [h4, h4], got, u_in, n_group, local
            )
        else:
            u_in = call(functools.partial(arrive, step), h4, got, u_in)
    got_u = swap(u_in, 2)
    x7, u_own = call(
        spread_backward, [h2, h2], u_in, got_u, n_second, rest_pair, x1, got1, rest_block
    )
    got7 = swap(x7, 1)
    xa, xb, weights = call(
        block_weights, [(square, bf16), (square, bf16), ((traits, typed), bf16)], u_own, got7, early, d
    )
    got_a = swap_chips(xa)
    got_b = swap(xb, 1)
    acc = call(impute_own, ((traits, untyped), f32), weights, masked)
    return call(impute_edges, ((traits, untyped), f32), acc, got_a, got_b, masked, last=True)


def solution(mesh):
    in_specs = (
        P(None, ("seg", AXIS)),
        P(("seg", AXIS), None, None),
        P(("seg", AXIS), None, None),
        P(("seg", AXIS), None),
        P(("seg", AXIS)),
    )
    return jax.shard_map(
        per_device, mesh=mesh, in_specs=in_specs, out_specs=P(None, ("seg", AXIS)), check_vma=False
    )
```

```python
import functools

import jax
import jax.numpy as jnp
from jax import lax
from jax.experimental import pallas as pl
from jax.experimental.pallas import tpu as pltpu
from jax.sharding import PartitionSpec as P

AXIS = "genome"
SEGMENTS = "seg"
GROUP = 4
f32 = jnp.float32
bf16 = jnp.bfloat16


def parts(x):
    high = x.astype(bf16)
    return high, (x - high.astype(f32)).astype(bf16)


def dot(a, b, ca=1, cb=0):
    ah, al = parts(a)
    bh, bl = parts(b)
    return lax.dot_general(
        jnp.concatenate([al, ah, ah], axis=ca),
        jnp.concatenate([bh, bl, bh], axis=cb),
        (((ca,), (cb,)), ((), ())),
        preferred_element_type=f32,
    )


def where_am_i():
    place = lax.axis_index(AXIS)
    return place % 2 == 0, (place // 2) % 2 == 0, place // GROUP


def ordered(first, own, other):
    return jnp.where(first, own, other), jnp.where(first, other, own)


def call(kernel, outs, *args, after=(), hbm=False, last=False, scratch=()):
    n_in, n_after = len(args), len(after)

    def body(*refs):
        kernel(*refs[:n_in], *refs[n_in + n_after :])

    single = not isinstance(outs, list)
    shapes = [outs] if single else outs
    vmem = pl.BlockSpec(memory_space=pltpu.VMEM)
    anywhere = pl.BlockSpec(memory_space=pl.ANY)
    if hbm:
        args = [pltpu.with_memory_space_constraint(a, pltpu.HBM) for a in args]
    got = pl.pallas_call(
        body,
        out_shape=[jax.ShapeDtypeStruct(s, t) if last else pltpu.VMEM(s, t) for s, t in shapes],
        in_specs=[anywhere if hbm else vmem] * n_in + [anywhere] * n_after,
        out_specs=[anywhere if last else vmem] * len(shapes),
        scratch_shapes=scratch,
        compiler_params=pltpu.CompilerParams(vmem_limit_bytes=8 * 2**20),
        name=kernel.__name__ if hasattr(kernel, "__name__") else kernel.func.__name__,
    )(*args, *after)
    return got[0] if single else got


def tail_part(z_in, d_in, c_in, x1, s_own, z, d, c, sems):
    half = c.shape[1]
    rows = z.shape[0] // 2
    head = d.shape[0] - half
    first, _, _ = where_am_i()
    def fetch(src, dst, start, stop, index):
        middle = (start + stop) // 2
        both = []
        for k, (low, high) in enumerate(((start, middle), (middle, stop))):
            rows_here = pl.ds(low, high - low)
            both.append(
                pltpu.make_async_copy(src.at[rows_here], dst.at[rows_here], sems.at[2 * index + k])
            )
        return both

    typed = d.shape[0]
    needed = fetch(d_in, d, head, typed, 0) + fetch(c_in, c, 0, typed, 1)
    traits = fetch(z_in, z, 0, z.shape[0], 2)
    rest = fetch(d_in, d, 0, head, 3)
    for copy in needed + traits:
        copy.start()
    for copy in needed:
        copy.wait()
    for copy in rest:
        copy.start()
    tail = d[head:]
    x1[:half] = -dot(tail, c[...])
    for copy in traits:
        copy.wait()
    s = dot(z[...], tail, 1, 1)
    keep, send = ordered(first, s[:rows], s[rows:])
    x1[half:] = send
    s_own[...] = keep
    for copy in rest:
        copy.wait()


def head_part(z, d, c, x1, s_own, x3, g_own, solved, p):
    half = c.shape[1]
    rows = z.shape[0] // 2
    head = d.shape[0] - half
    first, _, _ = where_am_i()
    p[:head] = dot(d[:head], c[...])
    p[head:] = -x1[:half]
    solved[:, :head] = dot(z[...], d[:head], 1, 1)
    low, high = ordered(first, s_own[...], x1[half:])
    solved[:rows, head:] = low
    solved[rows:, head:] = high
    g = dot(solved[...], p[...])
    keep, send = ordered(first, g[:rows], g[rows:])
    x3[:half] = dot(p[...], p[...], 0, 0)
    x3[half:] = send
    g_own[...] = keep


def pair_forward(x1, got1, s_own, x2, n_own, sp_own):
    half = x1.shape[1]
    first, first_pair, _ = where_am_i()
    m0, m1 = ordered(first, x1[:half], got1[:half])
    s0, s1 = ordered(first, s_own[...], got1[half:])
    n = dot(m1, m0)
    n_own[...] = n
    x2[: half // 2] = jnp.where(first, n[: half // 2], n[half // 2 :])
    s = dot(s0, m1, 1, 1) + s1
    rows = s.shape[0] // 2
    keep, send = ordered(first_pair, s[:rows], s[rows:])
    x2[half // 2 :] = send
    sp_own[...] = keep


def pair_backward(x1, got1, s_own, x3, got3, g_own, x4, gg_own, gp_own):
    half = x1.shape[1]
    first, first_pair, _ = where_am_i()
    m0, _ = ordered(first, x1[:half], got1[:half])
    s0, _ = ordered(first, s_own[...], got1[half:])
    gg0, gg1 = ordered(first, x3[:half], got3[:half])
    g0, g1 = ordered(first, g_own[...], got3[half:])
    both = dot(jnp.concatenate([gg1, g1 - dot(s0, gg1)], axis=0), m0)
    gg = dot(m0, both[:half], 0, 0) + gg0
    gg_own[...] = gg
    x4[: half // 2] = jnp.where(first, gg[: half // 2], gg[half // 2 :])
    g = both[half:] + g0
    rows = g.shape[0] // 2
    keep, send = ordered(first_pair, g[:rows], g[rows:])
    x4[half // 2 :] = send
    gp_own[...] = keep


def pair_matrices(own, got, got_core):
    half = own.shape[1]
    first, first_pair, _ = where_am_i()
    other = jnp.concatenate(ordered(first, got[: half // 2], got_core[: half // 2]), axis=0)
    return ordered(first_pair, own[...], other)


def pair_vectors(own, got):
    _, first_pair, _ = where_am_i()
    return ordered(first_pair, own[...], got[got.shape[1] // 2 :])


def relay(got, out):
    out[...] = got[: out.shape[0]]


def group_forward(n_own, got2, got2_core, sp_own, s_group):
    _, n1 = pair_matrices(n_own, got2, got2_core)
    s0, s1 = pair_vectors(sp_own, got2)
    s_group[...] = dot(s0, n1, 1, 1) + s1


def group_map(n_own, got2, got2_core, n_group, n_first, n_second):
    n0, n1 = pair_matrices(n_own, got2, got2_core)
    n_first[...] = n0
    n_second[...] = n1
    n_group[...] = dot(n1, n0)


def group_backward(n_first, got2, sp_own, gg_own, got4, got4_core, gp_own, gg_group, g_group, gg_second, g_second):
    n0 = n_first[...]
    s0, _ = pair_vectors(sp_own, got2)
    gg0, gg1 = pair_matrices(gg_own, got4, got4_core)
    g0, g1 = pair_vectors(gp_own, got4)
    gg_second[...] = gg1
    g_second[...] = g1
    both = dot(jnp.concatenate([gg1, g1 - dot(s0, gg1)], axis=0), n0)
    gg_group[...] = dot(n0, both[: gg1.shape[0]], 0, 0) + gg0
    g_group[...] = both[gg1.shape[0] :] + g0


def forward_hop(step, got, t_in, n_group, s_group, t_out, out):
    _, _, group = where_am_i()
    t = jnp.where(group == step + 1, got[...], t_in[...])
    t_out[...] = t
    out[...] = dot(t, n_group[...], 1, 1) + s_group[...]


def turn(step, got, t_in, gg_group, g_group, t_out, local):
    _, _, group = where_am_i()
    t = jnp.where(group == step + 1, got[...], t_in[...])
    t_out[...] = t
    local[...] = g_group[...] - dot(t, gg_group[...])


def backward_hop(step, got, u_in, n_group, local, u_out, out):
    _, _, group = where_am_i()
    u = jnp.where(group == step, got[...], u_in[...])
    u_out[...] = u
    out[...] = dot(u, n_group[...]) + local[...]


def arrive(step, got, u_in, u_out):
    _, _, group = where_am_i()
    u_out[...] = jnp.where(group == step, got[...], u_in[...])


def spread_forward(t_in, n_first, got2, sp_own, gg_second, g_second, x5, kept):
    rows = t_in.shape[0]
    _, first_pair, _ = where_am_i()
    s0, _ = pair_vectors(sp_own, got2)
    t_mid = dot(t_in[...], n_first[...], 1, 1) + s0
    rest = g_second[...] - dot(t_mid, gg_second[...])
    keep, send = ordered(first_pair, t_in[...], t_mid)
    x5[:rows] = send
    x5[rows:] = rest
    kept[:rows] = keep
    kept[rows:] = rest


def pair_states(kept, got5, x1, got1, s_own, x3, got3, g_own, x6, t_own, rest_pair, rest_block):
    half = x1.shape[1]
    rows = kept.shape[0] // 2
    first, first_pair, _ = where_am_i()
    t = jnp.concatenate(ordered(first_pair, kept[:rows], got5[:rows]), axis=0)
    rest_pair[...] = jnp.concatenate(ordered(first_pair, kept[rows:], got5[rows:]), axis=0)
    m0, _ = ordered(first, x1[:half], got1[:half])
    s0, _ = ordered(first, s_own[...], got1[half:])
    _, gg1 = ordered(first, x3[:half], got3[:half])
    _, g1 = ordered(first, g_own[...], got3[half:])
    t_mid = dot(t, m0, 1, 1) + s0
    rest_block[...] = g1 - dot(t_mid, gg1)
    keep, send = ordered(first, t, t_mid)
    x6[...] = send
    t_own[...] = keep


def block_rows(t_own, got6, solved, p, d, early):
    first, _, _ = where_am_i()
    t = jnp.concatenate(ordered(first, t_own[...], got6[...]), axis=0)
    early[...] = dot(solved[...] - dot(t, p[...], 1, 1), d[...])


def spread_backward(u_in, got_u, n_second, rest_pair, x1, got1, rest_block, x7, u_own):
    half = x1.shape[1]
    first, first_pair, _ = where_am_i()
    u = jnp.concatenate(ordered(first_pair, u_in[...], got_u[...]), axis=0)
    u = jnp.where(first_pair, dot(u, n_second[...]) + rest_pair[...], u)
    _, m1 = ordered(first, x1[:half], got1[:half])
    keep, send = ordered(first, dot(u, m1) + rest_block[...], u)
    x7[...] = send
    u_own[...] = keep


def block_weights(u_own, got7, early, d, xa, xb, weights):
    first, _, _ = where_am_i()
    typed = d.shape[0]
    half = u_own.shape[1]
    u = jnp.concatenate(ordered(first, u_own[...], got7[...]), axis=0)
    w = (early[...] - dot(u, d[typed - half :])).astype(bf16)
    weights[...] = w
    a, b = ordered(first, w[:, :half], w[:, typed - half :])
    xa[...] = a
    xb[...] = b


def contract(values, coefs):
    return lax.dot_general(values, coefs, (((1,), (1,)), ((), ())), preferred_element_type=f32)


def mask_coefs(coefs_in, anchor_in, masked, coefs, anchor, sems):
    untyped, span = coefs.shape
    half = span // 4
    typed = span - 2 * half
    tile = 128
    place = lax.axis_index(AXIS)
    total = lax.axis_size(AXIS) * typed
    copies = [pltpu.make_async_copy(anchor_in, anchor, sems.at[0])]
    for i in range(untyped // tile):
        rows = pl.ds(i * tile, tile)
        copies.append(pltpu.make_async_copy(coefs_in.at[rows], coefs.at[rows], sems.at[i + 1]))
    for copy in copies:
        copy.start()
    copies[0].wait()
    first_column = place * typed - half
    for i in range(untyped // tile):
        rows = pl.ds(i * tile, tile)
        nearest = jnp.broadcast_to(anchor[:, i * tile : (i + 1) * tile], (tile, tile)).T
        copies[i + 1].wait()
        for j in range(span // tile):
            lanes = pl.ds(j * tile, tile)
            columns = first_column + j * tile + lax.broadcasted_iota(jnp.int32, (tile, tile), 1)
            within = (jnp.abs(columns - nearest) <= half) & (columns >= 0) & (columns < total)
            masked[rows, lanes] = jnp.where(within, coefs[rows, lanes].astype(f32), 0.0).astype(bf16)


def impute_own(weights, masked, out):
    half = masked.shape[1] // 4
    typed = weights.shape[1]
    out[...] = contract(weights[...], masked[:, half : half + typed])


def impute_edges(acc, got_a, got_b, masked, out, result, sems):
    first, _, _ = where_am_i()
    half = got_a.shape[1]
    span = masked.shape[1]
    left, right = ordered(first, got_a[...], got_b[...])
    edges = jnp.concatenate([left, right], axis=1)
    coefs = jnp.concatenate([masked[:, :half], masked[:, span - half :]], axis=1)
    pieces = sems.shape[0]
    rows = acc.shape[0] // pieces
    copies = []
    for i in range(pieces):
        here = pl.ds(i * rows, rows)
        result[here] = acc[here] + contract(edges[i * rows : (i + 1) * rows], coefs)
        copies.append(pltpu.make_async_copy(result.at[here], out.at[here], sems.at[i]))
        copies[-1].start()
    for copy in copies:
        copy.wait()


def swap(block, distance):
    n = lax.axis_size(AXIS)
    return lax.ppermute(block, AXIS, [(i, i ^ distance) for i in range(n)])


def hop(block, step):
    pairs = []
    for i in range(lax.axis_size(AXIS)):
        g = i // GROUP
        pairs.append((i, i + GROUP if g == step else i - GROUP if g == step + 1 else i ^ 1))
    return lax.ppermute(block, AXIS, pairs)


def swap_chips(block):
    n, segments = lax.axis_size(AXIS), lax.axis_size(SEGMENTS)
    pairs = []
    for seg in range(segments):
        for i in range(n):
            to, to_seg = i + 1 if i % 2 else i - 1, seg
            if not 0 <= to < n:
                to, to_seg = (i, seg ^ 1) if segments % 2 == 0 else (to % n, seg)
            pairs.append((seg * n + i, to_seg * n + to))
    return lax.ppermute(block, (SEGMENTS, AXIS), pairs)


def per_device(z, diag_inverse, coupling, impute_coef, anchor):
    d = diag_inverse[0]
    c = coupling[0]
    typed = d.shape[0]
    half = c.shape[1]
    traits = z.shape[0]
    untyped, span = impute_coef.shape
    assert span == typed + 2 * half and typed == 2 * half
    groups = lax.axis_size(AXIS) // GROUP
    two, four = traits // 2, traits // 4
    square = (half, half)
    sq, h2, h4 = (square, f32), ((two, half), f32), ((four, half), f32)
    x2_shape, x4_shape = ((half + two, half), f32), ((half // 2 + four, half), f32)

    solved_shape, p_shape = ((traits, typed), f32), ((typed, half), f32)
    x1, s_own, z, d, c = call(
        tail_part, [x2_shape, h2, solved_shape, ((typed, typed), f32), p_shape], z, d, c,
        hbm=True, scratch=[pltpu.SemaphoreType.DMA((8,))],
    )
    got1 = swap(x1, 1)
    x3, g_own, solved, p = call(
        head_part, [x2_shape, h2, solved_shape, p_shape], z, d, c, x1, s_own
    )
    x2, n_own, sp_own = call(pair_forward, [x4_shape, sq, h4], x1, got1, s_own, after=(p,))
    got2 = swap(x2, 2)
    got3 = swap(x3, 1)
    masked = call(
        mask_coefs, ((untyped, span), bf16), impute_coef, anchor[None, :], after=(x2,), hbm=True,
        scratch=[
            pltpu.VMEM((untyped, span), bf16),
            pltpu.VMEM((1, untyped), jnp.int32),
            pltpu.SemaphoreType.DMA((untyped // 128 + 1,)),
        ],
    )
    x4, gg_own, gp_own = call(
        pair_backward, [x4_shape, sq, h4], x1, got1, s_own, x3, got3, g_own, after=(x2,)
    )
    rows_half = ((half // 2, half), f32)
    got2_core = swap(call(relay, rows_half, got2, after=(x4, masked)), 1)
    s_group = call(group_forward, h4, n_own, got2, got2_core, sp_own)
    n_group, n_first, n_second = call(
        group_map, [sq] * 3, n_own, got2, got2_core, after=(s_group,)
    )

    t_in = jnp.zeros((four, half), f32)
    out = s_group
    got4 = swap(x4, 2)
    for step in range(groups - 2):
        got = hop(out, step)
        t_in, out = call(
            functools.partial(forward_hop, step), [h4, h4], got, t_in, n_group, s_group
        )
    got4_core = swap(call(relay, rows_half, got4, after=(out,)), 1)
    gg_group, g_group, gg_second, g_second = call(
        group_backward, [sq, h4, sq, h4],
        n_first, got2, sp_own, gg_own, got4, got4_core, gp_own, after=(out,),
    )
    last = groups - 2
    got = hop(out, last)
    t_in, local = call(functools.partial(turn, last), [h4, h4], got, t_in, gg_group, g_group)

    u_in = jnp.zeros((four, half), f32)
    out = local
    for step in reversed(range(groups - 1)):
        got = hop(out, step)
        if step == last:
            x5, kept = call(
                spread_forward, [h2, h2], t_in, n_first, got2, sp_own, gg_second, g_second,
                after=(local,),
            )
            got5 = swap(x5, 2)
            x6, t_own, rest_pair, rest_block = call(
                pair_states, [h2] * 4, kept, got5, x1, got1, s_own, x3, got3, g_own
            )
            got6 = swap(x6, 1)
            early = call(block_rows, solved_shape, t_own, got6, solved, p, d)
        if step:
            u_in, out = call(
                functools.partial(backward_hop, step), [h4, h4], got, u_in, n_group, local
            )
        else:
            u_in = call(functools.partial(arrive, step), h4, got, u_in)
    got_u = swap(u_in, 2)
    x7, u_own = call(
        spread_backward, [h2, h2], u_in, got_u, n_second, rest_pair, x1, got1, rest_block
    )
    got7 = swap(x7, 1)
    xa, xb, weights = call(
        block_weights, [(square, bf16), (square, bf16), ((traits, typed), bf16)], u_own, got7, early, d
    )
    got_a = swap_chips(xa)
    got_b = swap(xb, 1)
    acc = call(impute_own, ((traits, untyped), f32), weights, masked)
    return call(
        impute_edges, ((traits, untyped), f32), acc, got_a, got_b, masked, last=True,
        scratch=[pltpu.VMEM((traits, untyped), f32), pltpu.SemaphoreType.DMA((2,))],
    )


def solution(mesh):
    in_specs = (
        P(None, (SEGMENTS, AXIS)),
        P((SEGMENTS, AXIS), None, None),
        P((SEGMENTS, AXIS), None, None),
        P((SEGMENTS, AXIS), None),
        P((SEGMENTS, AXIS)),
    )
    return jax.shard_map(
        per_device, mesh=mesh, in_specs=in_specs, out_specs=P(None, (SEGMENTS, AXIS)), check_vma=False
    )
```

```python
import functools

import jax
import jax.numpy as jnp
from jax import lax
from jax.experimental import pallas as pl
from jax.experimental.pallas import tpu as pltpu
from jax.sharding import PartitionSpec as P

AXIS = "genome"
SEGMENTS = "seg"
GROUP = 4
f32 = jnp.float32
bf16 = jnp.bfloat16


def parts(x):
    high = x.astype(bf16)
    return high, (x - high.astype(f32)).astype(bf16)


def dot(a, b, ca=1, cb=0):
    ah, al = parts(a)
    bh, bl = parts(b)
    return lax.dot_general(
        jnp.concatenate([al, ah, ah], axis=ca),
        jnp.concatenate([bh, bl, bh], axis=cb),
        (((ca,), (cb,)), ((), ())),
        preferred_element_type=f32,
    )


def where_am_i():
    place = lax.axis_index(AXIS)
    return place % 2 == 0, (place // 2) % 2 == 0, place // GROUP


def low_traits():
    place = lax.axis_index(AXIS)
    return (place + place // 2 + place // GROUP) % 2 == 0


def ordered(first, own, other):
    return jnp.where(first, own, other), jnp.where(first, other, own)


def call(kernel, outs, *args, after=(), hbm=False, last=False, scratch=()):
    n_in, n_after = len(args), len(after)

    def body(*refs):
        kernel(*refs[:n_in], *refs[n_in + n_after :])

    single = not isinstance(outs, list)
    shapes = [outs] if single else outs
    vmem = pl.BlockSpec(memory_space=pltpu.VMEM)
    anywhere = pl.BlockSpec(memory_space=pl.ANY)
    if hbm:
        args = [pltpu.with_memory_space_constraint(a, pltpu.HBM) for a in args]
    got = pl.pallas_call(
        body,
        out_shape=[jax.ShapeDtypeStruct(s, t) if last else pltpu.VMEM(s, t) for s, t in shapes],
        in_specs=[anywhere if hbm else vmem] * n_in + [anywhere] * n_after,
        out_specs=[vmem] * len(shapes),
        scratch_shapes=scratch,
        compiler_params=pltpu.CompilerParams(vmem_limit_bytes=8 * 2**20),
        name=kernel.__name__ if hasattr(kernel, "__name__") else kernel.func.__name__,
    )(*args, *after)
    return got[0] if single else got


def tail_part(z_in, d_in, c_in, x1, s_own, z, d, c, sems):
    half = c.shape[1]
    rows = z.shape[0] // 2
    head = d.shape[0] - half
    pieces = [
        (d_in.at[pl.ds(head, half)], d.at[pl.ds(head, half)]),
        (c_in, c),
        (z_in, z),
        (d_in.at[pl.ds(0, head)], d.at[pl.ds(0, head)]),
    ]
    copies = [pltpu.make_async_copy(src, dst, sems.at[i]) for i, (src, dst) in enumerate(pieces)]
    for copy in copies[:3]:
        copy.start()
    copies[0].wait()
    copies[1].wait()
    copies[3].start()
    tail = d[head:]
    x1[:half] = -dot(tail, c[...])
    copies[2].wait()
    s = dot(z[...], tail, 1, 1)
    keep, send = ordered(low_traits(), s[:rows], s[rows:])
    x1[half:] = send
    s_own[...] = keep
    copies[3].wait()


def head_part(z, d, c, x1, s_own, x3, g_own, solved, p):
    half = c.shape[1]
    rows = z.shape[0] // 2
    head = d.shape[0] - half
    first, _, _ = where_am_i()
    p[:head] = dot(d[:head], c[...])
    p[head:] = -x1[:half]
    solved[:, :head] = dot(z[...], d[:head], 1, 1)
    low, high = ordered(low_traits(), s_own[...], x1[half:])
    solved[:rows, head:] = low
    solved[rows:, head:] = high
    g = dot(solved[...], p[...])
    keep, send = ordered(low_traits(), g[:rows], g[rows:])
    x3[:half] = dot(p[...], p[...], 0, 0)
    x3[half:] = send
    g_own[...] = keep


def pair_forward(x1, got1, s_own, x2, n_own, sp_own):
    half = x1.shape[1]
    first, first_pair, _ = where_am_i()
    m0, m1 = ordered(first, x1[:half], got1[:half])
    s0, s1 = ordered(first, s_own[...], got1[half:])
    n = dot(m1, m0)
    n_own[...] = n
    x2[: half // 2] = jnp.where(first, n[: half // 2], n[half // 2 :])
    s = dot(s0, m1, 1, 1) + s1
    rows = s.shape[0] // 2
    keep, send = ordered(first_pair, s[:rows], s[rows:])
    x2[half // 2 :] = send
    sp_own[...] = keep


def pair_backward(x1, got1, s_own, x3, got3, g_own, x4, gg_own, gp_own):
    half = x1.shape[1]
    first, first_pair, _ = where_am_i()
    m0, _ = ordered(first, x1[:half], got1[:half])
    s0, _ = ordered(first, s_own[...], got1[half:])
    gg0, gg1 = ordered(first, x3[:half], got3[:half])
    g0, g1 = ordered(first, g_own[...], got3[half:])
    both = dot(jnp.concatenate([gg1, g1 - dot(s0, gg1)], axis=0), m0)
    gg = dot(m0, both[:half], 0, 0) + gg0
    gg_own[...] = gg
    x4[: half // 2] = jnp.where(first, gg[: half // 2], gg[half // 2 :])
    g = both[half:] + g0
    rows = g.shape[0] // 2
    keep, send = ordered(first_pair, g[:rows], g[rows:])
    x4[half // 2 :] = send
    gp_own[...] = keep


def pair_matrices(own, got, got_core):
    half = own.shape[1]
    first, first_pair, _ = where_am_i()
    other = jnp.concatenate(ordered(first, got_core[: half // 2], got[: half // 2]), axis=0)
    return ordered(first_pair, own[...], other)


def pair_vectors(own, got):
    _, first_pair, _ = where_am_i()
    return ordered(first_pair, own[...], got[got.shape[1] // 2 :])


def relay(got, out):
    out[...] = got[: out.shape[0]]


def group_forward(n_own, got2, got2_core, sp_own, s_group):
    _, n1 = pair_matrices(n_own, got2, got2_core)
    s0, s1 = pair_vectors(sp_own, got2)
    s_group[...] = dot(s0, n1, 1, 1) + s1


def group_map(n_own, got2, got2_core, n_group, n_first, n_second):
    n0, n1 = pair_matrices(n_own, got2, got2_core)
    n_first[...] = n0
    n_second[...] = n1
    n_group[...] = dot(n1, n0)


def group_backward(n_first, got2, sp_own, gg_own, got4, got4_core, gp_own, gg_group, g_group, gg_second, g_second):
    n0 = n_first[...]
    s0, _ = pair_vectors(sp_own, got2)
    gg0, gg1 = pair_matrices(gg_own, got4, got4_core)
    g0, g1 = pair_vectors(gp_own, got4)
    gg_second[...] = gg1
    g_second[...] = g1
    both = dot(jnp.concatenate([gg1, g1 - dot(s0, gg1)], axis=0), n0)
    gg_group[...] = dot(n0, both[: gg1.shape[0]], 0, 0) + gg0
    g_group[...] = both[gg1.shape[0] :] + g0


def forward_hop(step, got, t_in, n_group, s_group, t_out, out):
    _, _, group = where_am_i()
    t = jnp.where(group == step + 1, got[...], t_in[...])
    t_out[...] = t
    out[...] = dot(t, n_group[...], 1, 1) + s_group[...]


def turn(step, got, t_in, gg_group, g_group, t_out, local):
    _, _, group = where_am_i()
    t = jnp.where(group == step + 1, got[...], t_in[...])
    t_out[...] = t
    local[...] = g_group[...] - dot(t, gg_group[...])


def backward_hop(step, got, u_in, n_group, local, u_out, out):
    _, _, group = where_am_i()
    u = jnp.where(group == step, got[...], u_in[...])
    u_out[...] = u
    out[...] = dot(u, n_group[...]) + local[...]


def arrive(step, got, u_in, u_out):
    _, _, group = where_am_i()
    u_out[...] = jnp.where(group == step, got[...], u_in[...])


def spread_forward(t_in, n_first, got2, sp_own, gg_second, g_second, x5, kept):
    rows = t_in.shape[0]
    _, first_pair, _ = where_am_i()
    s0, _ = pair_vectors(sp_own, got2)
    t_mid = dot(t_in[...], n_first[...], 1, 1) + s0
    rest = g_second[...] - dot(t_mid, gg_second[...])
    keep, send = ordered(first_pair, t_in[...], t_mid)
    x5[:rows] = send
    x5[rows:] = rest
    kept[:rows] = keep
    kept[rows:] = rest


def pair_states(kept, got5, x1, got1, s_own, x3, got3, g_own, x6, t_own, rest_pair, rest_block):
    half = x1.shape[1]
    rows = kept.shape[0] // 2
    first, first_pair, _ = where_am_i()
    t = jnp.concatenate(ordered(first_pair, kept[:rows], got5[:rows]), axis=0)
    rest_pair[...] = jnp.concatenate(ordered(first_pair, kept[rows:], got5[rows:]), axis=0)
    m0, _ = ordered(first, x1[:half], got1[:half])
    s0, _ = ordered(first, s_own[...], got1[half:])
    _, gg1 = ordered(first, x3[:half], got3[:half])
    _, g1 = ordered(first, g_own[...], got3[half:])
    t_mid = dot(t, m0, 1, 1) + s0
    rest_block[...] = g1 - dot(t_mid, gg1)
    keep, send = ordered(first, t, t_mid)
    x6[...] = send
    t_own[...] = keep


def block_rows(t_own, got6, solved, p, d, early):
    first, _, _ = where_am_i()
    t = jnp.concatenate(ordered(low_traits(), t_own[...], got6[...]), axis=0)
    early[...] = dot(solved[...] - dot(t, p[...], 1, 1), d[...])


def spread_backward(u_in, got_u, n_second, rest_pair, x1, got1, rest_block, x7, u_own):
    half = x1.shape[1]
    first, first_pair, _ = where_am_i()
    u = jnp.concatenate(ordered(first_pair, u_in[...], got_u[...]), axis=0)
    u = jnp.where(first_pair, dot(u, n_second[...]) + rest_pair[...], u)
    _, m1 = ordered(first, x1[:half], got1[:half])
    keep, send = ordered(first, dot(u, m1) + rest_block[...], u)
    x7[...] = send
    u_own[...] = keep


def block_weights(u_own, got7, early, d, xa, xb, weights):
    first, _, _ = where_am_i()
    typed = d.shape[0]
    half = u_own.shape[1]
    u = jnp.concatenate(ordered(low_traits(), u_own[...], got7[...]), axis=0)
    w = (early[...] - dot(u, d[typed - half :])).astype(bf16)
    weights[...] = w
    a, b = ordered(first, w[:, :half], w[:, typed - half :])
    xa[...] = a
    xb[...] = b


def contract(values, coefs):
    return lax.dot_general(values, coefs, (((1,), (1,)), ((), ())), preferred_element_type=f32)


def mask_coefs(coefs_in, anchor_in, masked, coefs, anchor, sems):
    untyped, span = coefs.shape
    half = span // 4
    typed = span - 2 * half
    tile = 128
    place = lax.axis_index(AXIS)
    total = lax.axis_size(AXIS) * typed
    copies = [pltpu.make_async_copy(anchor_in, anchor, sems.at[0])]
    for i in range(untyped // tile):
        rows = pl.ds(i * tile, tile)
        copies.append(pltpu.make_async_copy(coefs_in.at[rows], coefs.at[rows], sems.at[i + 1]))
    for copy in copies:
        copy.start()
    copies[0].wait()
    first_column = place * typed - half
    for i in range(untyped // tile):
        rows = pl.ds(i * tile, tile)
        nearest = jnp.broadcast_to(anchor[:, i * tile : (i + 1) * tile], (tile, tile)).T
        copies[i + 1].wait()
        for j in range(span // tile):
            lanes = pl.ds(j * tile, tile)
            columns = first_column + j * tile + lax.broadcasted_iota(jnp.int32, (tile, tile), 1)
            within = (jnp.abs(columns - nearest) <= half) & (columns >= 0) & (columns < total)
            masked[rows, lanes] = jnp.where(within, coefs[rows, lanes].astype(f32), 0.0).astype(bf16)


def impute_own(weights, masked, out):
    half = masked.shape[1] // 4
    typed = weights.shape[1]
    out[...] = contract(weights[...], masked[:, half : half + typed])


def impute_edges(acc, got_a, got_b, masked, out):
    first, _, _ = where_am_i()
    half = got_a.shape[1]
    span = masked.shape[1]
    left, right = ordered(first, got_a[...], got_b[...])
    out[...] = acc[...] + contract(left, masked[:, :half]) + contract(right, masked[:, span - half :])


def swap(block, distance):
    n = lax.axis_size(AXIS)
    return lax.ppermute(block, AXIS, [(i, i ^ distance) for i in range(n)])


def hop(block, step):
    pairs = []
    for i in range(lax.axis_size(AXIS)):
        g = i // GROUP
        to = i + GROUP if g == step else i - GROUP if g == step + 1 else i
        pairs.append((i, to ^ 1))
    return lax.ppermute(block, AXIS, pairs)


def swap_chips(block):
    n, segments = lax.axis_size(AXIS), lax.axis_size(SEGMENTS)
    pairs = []
    for seg in range(segments):
        for i in range(n):
            to, to_seg = i + 1 if i % 2 else i - 1, seg
            if not 0 <= to < n:
                to, to_seg = (i, seg ^ 1) if segments % 2 == 0 else (to % n, seg)
            pairs.append((seg * n + i, to_seg * n + to))
    return lax.ppermute(block, (SEGMENTS, AXIS), pairs)


def per_device(z, diag_inverse, coupling, impute_coef, anchor):
    d = diag_inverse[0]
    c = coupling[0]
    typed = d.shape[0]
    half = c.shape[1]
    traits = z.shape[0]
    untyped, span = impute_coef.shape
    assert span == typed + 2 * half and typed == 2 * half
    groups = lax.axis_size(AXIS) // GROUP
    two, four = traits // 2, traits // 4
    square = (half, half)
    sq, h2, h4 = (square, f32), ((two, half), f32), ((four, half), f32)
    x2_shape, x4_shape = ((half + two, half), f32), ((half // 2 + four, half), f32)

    solved_shape, p_shape = ((traits, typed), f32), ((typed, half), f32)
    x1, s_own, z, d, c = call(
        tail_part, [x2_shape, h2, solved_shape, ((typed, typed), f32), p_shape], z, d, c,
        hbm=True, scratch=[pltpu.SemaphoreType.DMA((4,))],
    )
    got1 = swap(x1, 1)
    x3, g_own, solved, p = call(
        head_part, [x2_shape, h2, solved_shape, p_shape], z, d, c, x1, s_own
    )
    x2, n_own, sp_own = call(pair_forward, [x4_shape, sq, h4], x1, got1, s_own, after=(p,))
    got2 = swap(x2, 3)
    got3 = swap(x3, 1)
    masked = call(
        mask_coefs, ((untyped, span), bf16), impute_coef, anchor[None, :], after=(x2,), hbm=True,
        scratch=[
            pltpu.VMEM((untyped, span), bf16),
            pltpu.VMEM((1, untyped), jnp.int32),
            pltpu.SemaphoreType.DMA((untyped // 128 + 1,)),
        ],
    )
    x4, gg_own, gp_own = call(
        pair_backward, [x4_shape, sq, h4], x1, got1, s_own, x3, got3, g_own, after=(x2,)
    )
    rows_half = ((half // 2, half), f32)
    got2_core = swap(call(relay, rows_half, got2, after=(x4, masked)), 1)
    s_group = call(group_forward, h4, n_own, got2, got2_core, sp_own)
    n_group, n_first, n_second = call(
        group_map, [sq] * 3, n_own, got2, got2_core, after=(s_group,)
    )

    t_in = jnp.zeros((four, half), f32)
    out = s_group
    got4 = swap(x4, 3)
    for step in range(groups - 2):
        got = hop(out, step)
        t_in, out = call(
            functools.partial(forward_hop, step), [h4, h4], got, t_in, n_group, s_group
        )
    got4_core = swap(call(relay, rows_half, got4, after=(out,)), 1)
    gg_group, g_group, gg_second, g_second = call(
        group_backward, [sq, h4, sq, h4],
        n_first, got2, sp_own, gg_own, got4, got4_core, gp_own, after=(out,),
    )
    last = groups - 2
    got = hop(out, last)
    t_in, local = call(functools.partial(turn, last), [h4, h4], got, t_in, gg_group, g_group)

    u_in = jnp.zeros((four, half), f32)
    out = local
    for step in reversed(range(groups - 1)):
        got = hop(out, step)
        if step == last:
            x5, kept = call(
                spread_forward, [h2, h2], t_in, n_first, got2, sp_own, gg_second, g_second,
                after=(local,),
            )
            got5 = swap(x5, 3)
            x6, t_own, rest_pair, rest_block = call(
                pair_states, [h2] * 4, kept, got5, x1, got1, s_own, x3, got3, g_own
            )
            got6 = swap(x6, 1)
            early = call(block_rows, solved_shape, t_own, got6, solved, p, d)
        if step:
            u_in, out = call(
                functools.partial(backward_hop, step), [h4, h4], got, u_in, n_group, local
            )
        else:
            u_in = call(functools.partial(arrive, step), h4, got, u_in)
    got_u = swap(u_in, 3)
    x7, u_own = call(
        spread_backward, [h2, h2], u_in, got_u, n_second, rest_pair, x1, got1, rest_block
    )
    got7 = swap(x7, 1)
    xa, xb, weights = call(
        block_weights, [(square, bf16), (square, bf16), ((traits, typed), bf16)], u_own, got7, early, d
    )
    got_a = swap_chips(xa)
    got_b = swap(xb, 1)
    acc = call(impute_own, ((traits, untyped), f32), weights, masked)
    return call(impute_edges, ((traits, untyped), f32), acc, got_a, got_b, masked, last=True)


def solution(mesh):
    in_specs = (
        P(None, (SEGMENTS, AXIS)),
        P((SEGMENTS, AXIS), None, None),
        P((SEGMENTS, AXIS), None, None),
        P((SEGMENTS, AXIS), None),
        P((SEGMENTS, AXIS)),
    )
    return jax.shard_map(
        per_device, mesh=mesh, in_specs=in_specs, out_specs=P(None, (SEGMENTS, AXIS)), check_vma=False
    )
```

```python
import functools

import jax
import jax.numpy as jnp
from jax import lax
from jax.experimental import pallas as pl
from jax.experimental.pallas import tpu as pltpu
from jax.sharding import PartitionSpec as P

AXIS = "genome"
SEGMENTS = "seg"
GROUP = 4
f32 = jnp.float32
bf16 = jnp.bfloat16
i16 = jnp.int16
SCALES = 16
LIMIT = 32767.0


def parts(x):
    high = x.astype(bf16)
    return high, (x - high.astype(f32)).astype(bf16)


def dot(a, b, ca=1, cb=0):
    ah, al = parts(a)
    bh, bl = parts(b)
    return lax.dot_general(
        jnp.concatenate([al, ah, ah], axis=ca),
        jnp.concatenate([bh, bl, bh], axis=cb),
        (((ca,), (cb,)), ((), ())),
        preferred_element_type=f32,
    )


def code(x):
    top = jnp.maximum(jnp.max(jnp.abs(x), axis=0, keepdims=True), 1e-32)
    power = jnp.ceil(jnp.log2(top) * 4.0)
    root = jnp.exp2(power * -0.125)
    steps = jnp.floor(x * root * (root * LIMIT) + 0.5)
    steps = jnp.clip(steps, -LIMIT, LIMIT)
    powers = jnp.broadcast_to(power, (SCALES, x.shape[1]))
    return jnp.concatenate([steps, powers], axis=0).astype(jnp.int32).astype(i16)


def decode(coded):
    rows = coded.shape[0] - SCALES
    values = coded[...].astype(jnp.int32).astype(f32)
    root = jnp.exp2(values[rows : rows + 1] * 0.125)
    return values[:rows] * (root / LIMIT) * root


def where_am_i():
    place = lax.axis_index(AXIS)
    return place % 2 == 0, (place // 2) % 2 == 0, place // GROUP


def low_traits():
    place = lax.axis_index(AXIS)
    return (place + place // 2 + place // GROUP) % 2 == 0


def ordered(first, own, other):
    return jnp.where(first, own, other), jnp.where(first, other, own)


def call(kernel, outs, *args, after=(), hbm=False, last=False, scratch=()):
    n_in, n_after = len(args), len(after)

    def body(*refs):
        kernel(*refs[:n_in], *refs[n_in + n_after :])

    single = not isinstance(outs, list)
    shapes = [outs] if single else outs
    vmem = pl.BlockSpec(memory_space=pltpu.VMEM)
    anywhere = pl.BlockSpec(memory_space=pl.ANY)
    if hbm:
        args = [pltpu.with_memory_space_constraint(a, pltpu.HBM) for a in args]
    got = pl.pallas_call(
        body,
        out_shape=[jax.ShapeDtypeStruct(s, t) if last else pltpu.VMEM(s, t) for s, t in shapes],
        in_specs=[anywhere if hbm else vmem] * n_in + [anywhere] * n_after,
        out_specs=[vmem] * len(shapes),
        scratch_shapes=scratch,
        compiler_params=pltpu.CompilerParams(vmem_limit_bytes=8 * 2**20),
        name=kernel.__name__ if hasattr(kernel, "__name__") else kernel.func.__name__,
    )(*args, *after)
    return got[0] if single else got


def tail_part(z_in, d_in, c_in, x1, s_own, z, d, c, sems):
    half = c.shape[1]
    rows = z.shape[0] // 2
    head = d.shape[0] - half
    pieces = [
        (d_in.at[pl.ds(head, half)], d.at[pl.ds(head, half)]),
        (c_in, c),
        (z_in, z),
        (d_in.at[pl.ds(0, head)], d.at[pl.ds(0, head)]),
    ]
    copies = [pltpu.make_async_copy(src, dst, sems.at[i]) for i, (src, dst) in enumerate(pieces)]
    for copy in copies[:3]:
        copy.start()
    copies[0].wait()
    copies[1].wait()
    copies[3].start()
    tail = d[head:]
    x1[:half] = -dot(tail, c[...])
    copies[2].wait()
    s = dot(z[...], tail, 1, 1)
    keep, send = ordered(low_traits(), s[:rows], s[rows:])
    x1[half:] = send
    s_own[...] = keep
    copies[3].wait()


def head_part(z, d, c, x1, s_own, x3, g_own, solved, p):
    half = c.shape[1]
    rows = z.shape[0] // 2
    head = d.shape[0] - half
    first, _, _ = where_am_i()
    p[:head] = dot(d[:head], c[...])
    p[head:] = -x1[:half]
    solved[:, :head] = dot(z[...], d[:head], 1, 1)
    low, high = ordered(low_traits(), s_own[...], x1[half:])
    solved[:rows, head:] = low
    solved[rows:, head:] = high
    g = dot(solved[...], p[...])
    keep, send = ordered(low_traits(), g[:rows], g[rows:])
    x3[:half] = dot(p[...], p[...], 0, 0)
    x3[half:] = send
    g_own[...] = keep


def pair_forward(x1, got1, s_own, x2, n_own, sp_own):
    half = x1.shape[1]
    first, first_pair, _ = where_am_i()
    m0, m1 = ordered(first, x1[:half], got1[:half])
    s0, s1 = ordered(first, s_own[...], got1[half:])
    n = dot(m1, m0)
    n_own[...] = n
    x2[: half // 2] = jnp.where(first, n[: half // 2], n[half // 2 :])
    s = dot(s0, m1, 1, 1) + s1
    rows = s.shape[0] // 2
    keep, send = ordered(first_pair, s[:rows], s[rows:])
    x2[half // 2 :] = send
    sp_own[...] = keep


def pair_backward(x1, got1, s_own, x3, got3, g_own, x4, gg_own, gp_own):
    half = x1.shape[1]
    first, first_pair, _ = where_am_i()
    m0, _ = ordered(first, x1[:half], got1[:half])
    s0, _ = ordered(first, s_own[...], got1[half:])
    gg0, gg1 = ordered(first, x3[:half], got3[:half])
    g0, g1 = ordered(first, g_own[...], got3[half:])
    both = dot(jnp.concatenate([gg1, g1 - dot(s0, gg1)], axis=0), m0)
    gg = dot(m0, both[:half], 0, 0) + gg0
    gg_own[...] = gg
    split = half // 2 + SCALES
    x4[:split] = code(jnp.where(first, gg[: half // 2], gg[half // 2 :]))
    g = both[half:] + g0
    rows = g.shape[0] // 2
    keep, send = ordered(first_pair, g[:rows], g[rows:])
    x4[split:] = code(send)
    gp_own[...] = keep


def pair_matrices(own, got, got_core):
    first, first_pair, _ = where_am_i()
    other = jnp.concatenate(ordered(first, got_core, got), axis=0)
    return ordered(first_pair, own[...], other)


def pair_vectors(own, got):
    _, first_pair, _ = where_am_i()
    return ordered(first_pair, own[...], got)


def relay(got, out):
    out[...] = got[: out.shape[0]]


def group_forward(n_own, got2, got2_core, sp_own, s_group, out):
    half = n_own.shape[1]
    _, n1 = pair_matrices(n_own, got2[: half // 2], got2_core[...])
    s0, s1 = pair_vectors(sp_own, got2[half // 2 :])
    s = dot(s0, n1, 1, 1) + s1
    s_group[...] = s
    out[...] = code(s)


def group_map(n_own, got2, got2_core, n_group, n_first, n_second):
    half = n_own.shape[1]
    n0, n1 = pair_matrices(n_own, got2[: half // 2], got2_core[...])
    n_first[...] = n0
    n_second[...] = n1
    n_group[...] = dot(n1, n0)


def group_backward(
    n_first, got2, sp_own, gg_own, got4, got4_core, gp_own, gg_group, g_group, gg_second, g_second
):
    half = n_first.shape[1]
    split = half // 2 + SCALES
    n0 = n_first[...]
    s0, _ = pair_vectors(sp_own, got2[half // 2 :])
    gg0, gg1 = pair_matrices(gg_own, decode(got4[:split]), decode(got4_core))
    g0, g1 = pair_vectors(gp_own, decode(got4[split:]))
    gg_second[...] = gg1
    g_second[...] = g1
    both = dot(jnp.concatenate([gg1, g1 - dot(s0, gg1)], axis=0), n0)
    gg_group[...] = dot(n0, both[:half], 0, 0) + gg0
    g_group[...] = both[half:] + g0


def forward_hop(step, got, t_in, n_group, s_group, t_out, out):
    _, _, group = where_am_i()
    t = jnp.where(group == step + 1, decode(got), t_in[...])
    t_out[...] = t
    out[...] = code(dot(t, n_group[...], 1, 1) + s_group[...])


def turn(step, got, t_in, gg_group, g_group, t_out, local, out):
    _, _, group = where_am_i()
    t = jnp.where(group == step + 1, decode(got), t_in[...])
    t_out[...] = t
    u = g_group[...] - dot(t, gg_group[...])
    local[...] = u
    out[...] = code(u)


def backward_hop(step, got, u_in, n_group, local, u_out, out):
    _, _, group = where_am_i()
    u = jnp.where(group == step, decode(got), u_in[...])
    u_out[...] = u
    out[...] = code(dot(u, n_group[...]) + local[...])


def arrive(step, got, u_in, u_out, out):
    _, _, group = where_am_i()
    u = jnp.where(group == step, decode(got), u_in[...])
    u_out[...] = u
    out[...] = code(u)


def spread_forward(t_in, n_first, got2, sp_own, gg_second, g_second, x5, kept, rest_own):
    half = n_first.shape[1]
    rows = t_in.shape[0]
    _, first_pair, _ = where_am_i()
    s0, _ = pair_vectors(sp_own, got2[half // 2 :])
    t_mid = dot(t_in[...], n_first[...], 1, 1) + s0
    rest = g_second[...] - dot(t_mid, gg_second[...])
    keep, send = ordered(first_pair, t_in[...], t_mid)
    x5[: rows + SCALES] = code(send)
    x5[rows + SCALES :] = code(rest)
    kept[...] = keep
    rest_own[...] = rest


def pair_states(
    kept, rest_own, got5, x1, got1, s_own, x3, got3, g_own, x6, t_own, rest_pair, rest_block
):
    half = x1.shape[1]
    split = kept.shape[0] + SCALES
    first, first_pair, _ = where_am_i()
    t = jnp.concatenate(ordered(first_pair, kept[...], decode(got5[:split])), axis=0)
    rest_pair[...] = jnp.concatenate(
        ordered(first_pair, rest_own[...], decode(got5[split:])), axis=0
    )
    m0, _ = ordered(first, x1[:half], got1[:half])
    s0, _ = ordered(first, s_own[...], got1[half:])
    _, gg1 = ordered(first, x3[:half], got3[:half])
    _, g1 = ordered(first, g_own[...], got3[half:])
    t_mid = dot(t, m0, 1, 1) + s0
    rest_block[...] = g1 - dot(t_mid, gg1)
    keep, send = ordered(first, t, t_mid)
    x6[...] = send
    t_own[...] = keep


def block_rows(t_own, got6, solved, p, d, early):
    first, _, _ = where_am_i()
    t = jnp.concatenate(ordered(low_traits(), t_own[...], got6[...]), axis=0)
    early[...] = dot(solved[...] - dot(t, p[...], 1, 1), d[...])


def spread_backward(u_in, got_u, n_second, rest_pair, x1, got1, rest_block, x7, u_own):
    half = x1.shape[1]
    first, first_pair, _ = where_am_i()
    u = jnp.concatenate(ordered(first_pair, u_in[...], decode(got_u)), axis=0)
    u = jnp.where(first_pair, dot(u, n_second[...]) + rest_pair[...], u)
    _, m1 = ordered(first, x1[:half], got1[:half])
    keep, send = ordered(first, dot(u, m1) + rest_block[...], u)
    x7[...] = send
    u_own[...] = keep


def block_weights(u_own, got7, early, d, xa, xb, weights):
    first, _, _ = where_am_i()
    typed = d.shape[0]
    half = u_own.shape[1]
    u = jnp.concatenate(ordered(low_traits(), u_own[...], got7[...]), axis=0)
    w = (early[...] - dot(u, d[typed - half :])).astype(bf16)
    weights[...] = w
    a, b = ordered(first, w[:, :half], w[:, typed - half :])
    xa[...] = a
    xb[...] = b


def contract(values, coefs):
    return lax.dot_general(values, coefs, (((1,), (1,)), ((), ())), preferred_element_type=f32)


def mask_coefs(coefs_in, anchor_in, masked, coefs, anchor, sems):
    untyped, span = coefs.shape
    half = span // 4
    typed = span - 2 * half
    tile = 128
    place = lax.axis_index(AXIS)
    total = lax.axis_size(AXIS) * typed
    copies = [pltpu.make_async_copy(anchor_in, anchor, sems.at[0])]
    for i in range(untyped // tile):
        rows = pl.ds(i * tile, tile)
        copies.append(pltpu.make_async_copy(coefs_in.at[rows], coefs.at[rows], sems.at[i + 1]))
    for copy in copies:
        copy.start()
    copies[0].wait()
    first_column = place * typed - half
    for i in range(untyped // tile):
        rows = pl.ds(i * tile, tile)
        nearest = jnp.broadcast_to(anchor[:, i * tile : (i + 1) * tile], (tile, tile)).T
        copies[i + 1].wait()
        for j in range(span // tile):
            lanes = pl.ds(j * tile, tile)
            columns = first_column + j * tile + lax.broadcasted_iota(jnp.int32, (tile, tile), 1)
            within = (jnp.abs(columns - nearest) <= half) & (columns >= 0) & (columns < total)
            masked[rows, lanes] = jnp.where(within, coefs[rows, lanes].astype(f32), 0.0).astype(bf16)


def impute_own(weights, masked, out):
    half = masked.shape[1] // 4
    typed = weights.shape[1]
    out[...] = contract(weights[...], masked[:, half : half + typed])


def impute_edges(acc, got_a, got_b, masked, out):
    first, _, _ = where_am_i()
    half = got_a.shape[1]
    span = masked.shape[1]
    left, right = ordered(first, got_a[...], got_b[...])
    out[...] = acc[...] + contract(left, masked[:, :half]) + contract(right, masked[:, span - half :])


def swap(block, distance):
    n = lax.axis_size(AXIS)
    return lax.ppermute(block, AXIS, [(i, i ^ distance) for i in range(n)])


def hop(block, step):
    pairs = []
    for i in range(lax.axis_size(AXIS)):
        g = i // GROUP
        to = i + GROUP if g == step else i - GROUP if g == step + 1 else i
        pairs.append((i, to ^ 1))
    return lax.ppermute(block, AXIS, pairs)


def swap_chips(block):
    n, segments = lax.axis_size(AXIS), lax.axis_size(SEGMENTS)
    pairs = []
    for seg in range(segments):
        for i in range(n):
            to, to_seg = i + 1 if i % 2 else i - 1, seg
            if not 0 <= to < n:
                to, to_seg = (i, seg ^ 1) if segments % 2 == 0 else (to % n, seg)
            pairs.append((seg * n + i, to_seg * n + to))
    return lax.ppermute(block, (SEGMENTS, AXIS), pairs)


def per_device(z, diag_inverse, coupling, impute_coef, anchor):
    d = diag_inverse[0]
    c = coupling[0]
    typed = d.shape[0]
    half = c.shape[1]
    traits = z.shape[0]
    untyped, span = impute_coef.shape
    assert span == typed + 2 * half and typed == 2 * half
    groups = lax.axis_size(AXIS) // GROUP
    two, four = traits // 2, traits // 4
    square = (half, half)
    sq, h2, h4 = (square, f32), ((two, half), f32), ((four, half), f32)
    x1_shape, x2_shape = ((half + two, half), f32), ((half // 2 + four, half), f32)
    x4_shape = ((half // 2 + four + 2 * SCALES, half), i16)
    coded, coded_pair = ((four + SCALES, half), i16), ((two + 2 * SCALES, half), i16)

    solved_shape, p_shape = ((traits, typed), f32), ((typed, half), f32)
    x1, s_own, z, d, c = call(
        tail_part, [x1_shape, h2, solved_shape, ((typed, typed), f32), p_shape], z, d, c,
        hbm=True, scratch=[pltpu.SemaphoreType.DMA((4,))],
    )
    got1 = swap(x1, 1)
    x3, g_own, solved, p = call(
        head_part, [x1_shape, h2, solved_shape, p_shape], z, d, c, x1, s_own
    )
    x2, n_own, sp_own = call(pair_forward, [x2_shape, sq, h4], x1, got1, s_own, after=(p,))
    got2 = swap(x2, 3)
    got3 = swap(x3, 1)
    masked = call(
        mask_coefs, ((untyped, span), bf16), impute_coef, anchor[None, :], after=(x2,), hbm=True,
        scratch=[
            pltpu.VMEM((untyped, span), bf16),
            pltpu.VMEM((1, untyped), jnp.int32),
            pltpu.SemaphoreType.DMA((untyped // 128 + 1,)),
        ],
    )
    x4, gg_own, gp_own = call(
        pair_backward, [x4_shape, sq, h4], x1, got1, s_own, x3, got3, g_own, after=(x2,)
    )
    rows_half = ((half // 2, half), f32)
    got2_core = swap(call(relay, rows_half, got2, after=(x4, masked)), 1)
    s_group, out = call(group_forward, [h4, coded], n_own, got2, got2_core, sp_own)
    n_group, n_first, n_second = call(
        group_map, [sq] * 3, n_own, got2, got2_core, after=(s_group,)
    )

    t_in = jnp.zeros((four, half), f32)
    got4 = swap(x4, 3)
    for step in range(groups - 2):
        got = hop(out, step)
        t_in, out = call(
            functools.partial(forward_hop, step), [h4, coded], got, t_in, n_group, s_group
        )
    got4_core = swap(call(relay, ((half // 2 + SCALES, half), i16), got4, after=(out,)), 1)
    gg_group, g_group, gg_second, g_second = call(
        group_backward, [sq, h4, sq, h4],
        n_first, got2, sp_own, gg_own, got4, got4_core, gp_own, after=(out,),
    )
    last = groups - 2
    got = hop(out, last)
    t_in, local, out = call(
        functools.partial(turn, last), [h4, h4, coded], got, t_in, gg_group, g_group
    )

    u_in = jnp.zeros((four, half), f32)
    for step in reversed(range(groups - 1)):
        got = hop(out, step)
        if step == last:
            x5, kept, rest_own = call(
                spread_forward, [coded_pair, h4, h4], t_in, n_first, got2, sp_own, gg_second, g_second,
                after=(local,),
            )
            got5 = swap(x5, 3)
            x6, t_own, rest_pair, rest_block = call(
                pair_states, [h2] * 4, kept, rest_own, got5, x1, got1, s_own, x3, got3, g_own
            )
            got6 = swap(x6, 1)
            early = call(block_rows, solved_shape, t_own, got6, solved, p, d)
        if step:
            u_in, out = call(
                functools.partial(backward_hop, step), [h4, coded], got, u_in, n_group, local
            )
        else:
            u_in, out = call(functools.partial(arrive, step), [h4, coded], got, u_in)
    got_u = swap(out, 3)
    x7, u_own = call(
        spread_backward, [h2, h2], u_in, got_u, n_second, rest_pair, x1, got1, rest_block
    )
    got7 = swap(x7, 1)
    xa, xb, weights = call(
        block_weights, [(square, bf16), (square, bf16), ((traits, typed), bf16)], u_own, got7, early, d
    )
    got_a = swap_chips(xa)
    got_b = swap(xb, 1)
    acc = call(impute_own, ((traits, untyped), f32), weights, masked)
    return call(impute_edges, ((traits, untyped), f32), acc, got_a, got_b, masked, last=True)


def solution(mesh):
    in_specs = (
        P(None, (SEGMENTS, AXIS)),
        P((SEGMENTS, AXIS), None, None),
        P((SEGMENTS, AXIS), None, None),
        P((SEGMENTS, AXIS), None),
        P((SEGMENTS, AXIS)),
    )
    return jax.shard_map(
        per_device, mesh=mesh, in_specs=in_specs, out_specs=P(None, (SEGMENTS, AXIS)), check_vma=False
    )
```

```python
import functools

import jax
import jax.numpy as jnp
from jax import lax
from jax.experimental import pallas as pl
from jax.experimental.pallas import tpu as pltpu
from jax.sharding import PartitionSpec as P

AXIS = "genome"
SEGMENTS = "seg"
GROUP = 4
f32 = jnp.float32
bf16 = jnp.bfloat16
i16 = jnp.int16
SCALES = 16
LANES = 128
LIMIT = 32767.0


def parts(x):
    high = x.astype(bf16)
    return high, (x - high.astype(f32)).astype(bf16)


def dot(a, b, ca=1, cb=0):
    ah, al = parts(a)
    bh, bl = parts(b)
    return lax.dot_general(
        jnp.concatenate([al, ah, ah], axis=ca),
        jnp.concatenate([bh, bl, bh], axis=cb),
        (((ca,), (cb,)), ((), ())),
        preferred_element_type=f32,
    )


def code(x):
    top = jnp.maximum(jnp.max(jnp.abs(x), axis=0, keepdims=True), 1e-32)
    power = jnp.ceil(jnp.log2(top) * 4.0)
    root = jnp.exp2(power * -0.125)
    steps = jnp.floor(x * root * (root * LIMIT) + 0.5)
    steps = jnp.clip(steps, -LIMIT, LIMIT)
    tiles = x.shape[1] // LANES
    powers = jnp.broadcast_to(power, (SCALES // tiles, x.shape[1]))
    pieces = [v[:, i * LANES : (i + 1) * LANES] for v in (steps, powers) for i in range(tiles)]
    return jnp.concatenate(pieces, axis=0).astype(jnp.int32).astype(i16)


def decode(coded, tiles=2):
    rows = (coded.shape[0] - SCALES) // tiles
    values = coded[...].astype(jnp.int32).astype(f32)
    columns = []
    for i in range(tiles):
        at = tiles * rows + i * (SCALES // tiles)
        root = jnp.exp2(values[at : at + 1] * 0.125)
        columns.append(values[i * rows : (i + 1) * rows] * (root / LIMIT) * root)
    return jnp.concatenate(columns, axis=1)


def coded_rows(rows, columns):
    return rows * (columns // LANES) + SCALES


def where_am_i():
    place = lax.axis_index(AXIS)
    return place % 2 == 0, (place // 2) % 2 == 0, place // GROUP


def low_traits():
    place = lax.axis_index(AXIS)
    return (place + place // 2 + place // GROUP) % 2 == 0


def ordered(first, own, other):
    return jnp.where(first, own, other), jnp.where(first, other, own)


def call(kernel, outs, *args, after=(), hbm=False, last=False, scratch=()):
    n_in, n_after = len(args), len(after)

    def body(*refs):
        kernel(*refs[:n_in], *refs[n_in + n_after :])

    single = not isinstance(outs, list)
    shapes = [outs] if single else outs
    vmem = pl.BlockSpec(memory_space=pltpu.VMEM)
    anywhere = pl.BlockSpec(memory_space=pl.ANY)
    if hbm:
        args = [pltpu.with_memory_space_constraint(a, pltpu.HBM) for a in args]
    got = pl.pallas_call(
        body,
        out_shape=[jax.ShapeDtypeStruct(s, t) if last else pltpu.VMEM(s, t) for s, t in shapes],
        in_specs=[anywhere if hbm else vmem] * n_in + [anywhere] * n_after,
        out_specs=[vmem] * len(shapes),
        scratch_shapes=scratch,
        compiler_params=pltpu.CompilerParams(vmem_limit_bytes=8 * 2**20),
        name=kernel.__name__ if hasattr(kernel, "__name__") else kernel.func.__name__,
    )(*args, *after)
    return got[0] if single else got


def tail_part(z_in, d_in, c_in, x1, s_own, z, d, c, sems):
    half = c.shape[1]
    rows = z.shape[0] // 2
    head = d.shape[0] - half
    pieces = [
        (d_in.at[pl.ds(head, half)], d.at[pl.ds(head, half)]),
        (c_in, c),
        (z_in, z),
        (d_in.at[pl.ds(0, head)], d.at[pl.ds(0, head)]),
    ]
    copies = [pltpu.make_async_copy(src, dst, sems.at[i]) for i, (src, dst) in enumerate(pieces)]
    for copy in copies[:3]:
        copy.start()
    copies[0].wait()
    copies[1].wait()
    copies[3].start()
    tail = d[head:]
    x1[:half] = -dot(tail, c[...])
    copies[2].wait()
    s = dot(z[...], tail, 1, 1)
    keep, send = ordered(low_traits(), s[:rows], s[rows:])
    x1[half:] = send
    s_own[...] = keep
    copies[3].wait()


def head_part(z, d, c, x1, s_own, x3, g_own, solved, p):
    half = c.shape[1]
    rows = z.shape[0] // 2
    head = d.shape[0] - half
    first, _, _ = where_am_i()
    p[:head] = dot(d[:head], c[...])
    p[head:] = -x1[:half]
    solved[:, :head] = dot(z[...], d[:head], 1, 1)
    low, high = ordered(low_traits(), s_own[...], x1[half:])
    solved[:rows, head:] = low
    solved[rows:, head:] = high
    g = dot(solved[...], p[...])
    keep, send = ordered(low_traits(), g[:rows], g[rows:])
    x3[:half] = dot(p[...], p[...], 0, 0)
    x3[half:] = send
    g_own[...] = keep


def pair_forward(x1, got1, s_own, x2, n_own, sp_own):
    half = x1.shape[1]
    first, first_pair, _ = where_am_i()
    m0, m1 = ordered(first, x1[:half], got1[:half])
    s0, s1 = ordered(first, s_own[...], got1[half:])
    n = dot(m1, m0)
    n_own[...] = n
    split = coded_rows(half // 2, half)
    x2[:split] = code(jnp.where(first, n[: half // 2], n[half // 2 :]))
    s = dot(s0, m1, 1, 1) + s1
    rows = s.shape[0] // 2
    keep, send = ordered(first_pair, s[:rows], s[rows:])
    x2[split:] = code(send)
    sp_own[...] = keep


def pair_backward(x1, got1, s_own, x3, got3, g_own, x4, gg_own, gp_own):
    half = x1.shape[1]
    first, first_pair, _ = where_am_i()
    m0, _ = ordered(first, x1[:half], got1[:half])
    s0, _ = ordered(first, s_own[...], got1[half:])
    gg0, gg1 = ordered(first, x3[:half], got3[:half])
    g0, g1 = ordered(first, g_own[...], got3[half:])
    both = dot(jnp.concatenate([gg1, g1 - dot(s0, gg1)], axis=0), m0)
    gg = dot(m0, both[:half], 0, 0) + gg0
    gg_own[...] = gg
    split = coded_rows(half // 2, half)
    x4[:split] = code(jnp.where(first, gg[: half // 2], gg[half // 2 :]))
    g = both[half:] + g0
    rows = g.shape[0] // 2
    keep, send = ordered(first_pair, g[:rows], g[rows:])
    x4[split:] = code(send)
    gp_own[...] = keep


def pair_matrices(own, got, got_core):
    first, first_pair, _ = where_am_i()
    other = jnp.concatenate(ordered(first, got_core, got), axis=0)
    return ordered(first_pair, own[...], other)


def pair_vectors(own, got):
    _, first_pair, _ = where_am_i()
    return ordered(first_pair, own[...], got)


def relay(got, out):
    out[...] = got[: out.shape[0]]


def group_forward(n_own, got2, got2_core, sp_own, s_group, out):
    half = n_own.shape[1]
    split = coded_rows(half // 2, half)
    _, n1 = pair_matrices(n_own, decode(got2[:split]), decode(got2_core))
    s0, s1 = pair_vectors(sp_own, decode(got2[split:]))
    s = dot(s0, n1, 1, 1) + s1
    s_group[...] = s
    out[...] = code(s)


def group_map(n_own, got2, got2_core, n_group, n_first, n_second):
    half = n_own.shape[1]
    split = coded_rows(half // 2, half)
    n0, n1 = pair_matrices(n_own, decode(got2[:split]), decode(got2_core))
    n_first[...] = n0
    n_second[...] = n1
    n_group[...] = dot(n1, n0)


def group_backward(
    n_first, got2, sp_own, gg_own, got4, got4_core, gp_own, gg_group, g_group, gg_second, g_second
):
    half = n_first.shape[1]
    split = coded_rows(half // 2, half)
    n0 = n_first[...]
    s0, _ = pair_vectors(sp_own, decode(got2[split:]))
    gg0, gg1 = pair_matrices(gg_own, decode(got4[:split]), decode(got4_core))
    g0, g1 = pair_vectors(gp_own, decode(got4[split:]))
    gg_second[...] = gg1
    g_second[...] = g1
    both = dot(jnp.concatenate([gg1, g1 - dot(s0, gg1)], axis=0), n0)
    gg_group[...] = dot(n0, both[:half], 0, 0) + gg0
    g_group[...] = both[half:] + g0


def forward_hop(step, got, t_in, n_group, s_group, t_out, out):
    _, _, group = where_am_i()
    t = jnp.where(group == step + 1, decode(got), t_in[...])
    t_out[...] = t
    out[...] = code(dot(t, n_group[...], 1, 1) + s_group[...])


def turn(step, got, t_in, gg_group, g_group, t_out, local, out):
    _, _, group = where_am_i()
    t = jnp.where(group == step + 1, decode(got), t_in[...])
    t_out[...] = t
    u = g_group[...] - dot(t, gg_group[...])
    local[...] = u
    out[...] = code(u)


def backward_hop(step, got, u_in, n_group, local, u_out, out):
    _, _, group = where_am_i()
    u = jnp.where(group == step, decode(got), u_in[...])
    u_out[...] = u
    out[...] = code(dot(u, n_group[...]) + local[...])


def arrive(step, got, u_in, u_out, out):
    _, _, group = where_am_i()
    u = jnp.where(group == step, decode(got), u_in[...])
    u_out[...] = u
    out[...] = code(u)


def spread_forward(t_in, n_first, got2, sp_own, gg_second, g_second, x5, kept, rest_own):
    half = n_first.shape[1]
    rows = coded_rows(t_in.shape[0], half)
    _, first_pair, _ = where_am_i()
    s0, _ = pair_vectors(sp_own, decode(got2[coded_rows(half // 2, half) :]))
    t_mid = dot(t_in[...], n_first[...], 1, 1) + s0
    rest = g_second[...] - dot(t_mid, gg_second[...])
    keep, send = ordered(first_pair, t_in[...], t_mid)
    x5[:rows] = code(send)
    x5[rows:] = code(rest)
    kept[...] = keep
    rest_own[...] = rest


def pair_states(
    kept, rest_own, got5, x1, got1, s_own, x3, got3, g_own, x6, t_own, rest_pair, rest_block
):
    half = x1.shape[1]
    split = coded_rows(kept.shape[0], half)
    first, first_pair, _ = where_am_i()
    t = jnp.concatenate(ordered(first_pair, kept[...], decode(got5[:split])), axis=0)
    rest_pair[...] = jnp.concatenate(
        ordered(first_pair, rest_own[...], decode(got5[split:])), axis=0
    )
    m0, _ = ordered(first, x1[:half], got1[:half])
    s0, _ = ordered(first, s_own[...], got1[half:])
    _, gg1 = ordered(first, x3[:half], got3[:half])
    _, g1 = ordered(first, g_own[...], got3[half:])
    t_mid = dot(t, m0, 1, 1) + s0
    rest_block[...] = g1 - dot(t_mid, gg1)
    keep, send = ordered(first, t, t_mid)
    x6[...] = send
    t_own[...] = keep


def block_rows(t_own, got6, solved, p, d, early):
    first, _, _ = where_am_i()
    t = jnp.concatenate(ordered(low_traits(), t_own[...], got6[...]), axis=0)
    early[...] = dot(solved[...] - dot(t, p[...], 1, 1), d[...])


def spread_backward(u_in, got_u, n_second, rest_pair, x1, got1, rest_block, x7, u_own):
    half = x1.shape[1]
    first, first_pair, _ = where_am_i()
    u = jnp.concatenate(ordered(first_pair, u_in[...], decode(got_u)), axis=0)
    u = jnp.where(first_pair, dot(u, n_second[...]) + rest_pair[...], u)
    _, m1 = ordered(first, x1[:half], got1[:half])
    keep, send = ordered(first, dot(u, m1) + rest_block[...], u)
    x7[...] = send
    u_own[...] = keep


def block_weights(u_own, got7, early, d, xa, xb, weights):
    first, _, _ = where_am_i()
    typed = d.shape[0]
    half = u_own.shape[1]
    u = jnp.concatenate(ordered(low_traits(), u_own[...], got7[...]), axis=0)
    w = (early[...] - dot(u, d[typed - half :])).astype(bf16)
    weights[...] = w
    a, b = ordered(first, w[:, :half], w[:, typed - half :])
    xa[...] = a
    xb[...] = b


def contract(values, coefs):
    return lax.dot_general(values, coefs, (((1,), (1,)), ((), ())), preferred_element_type=f32)


def mask_coefs(coefs_in, anchor_in, masked, coefs, anchor, sems):
    untyped, span = coefs.shape
    half = span // 4
    typed = span - 2 * half
    tile = 128
    place = lax.axis_index(AXIS)
    total = lax.axis_size(AXIS) * typed
    copies = [pltpu.make_async_copy(anchor_in, anchor, sems.at[0])]
    for i in range(untyped // tile):
        rows = pl.ds(i * tile, tile)
        copies.append(pltpu.make_async_copy(coefs_in.at[rows], coefs.at[rows], sems.at[i + 1]))
    for copy in copies:
        copy.start()
    copies[0].wait()
    first_column = place * typed - half
    for i in range(untyped // tile):
        rows = pl.ds(i * tile, tile)
        nearest = jnp.broadcast_to(anchor[:, i * tile : (i + 1) * tile], (tile, tile)).T
        copies[i + 1].wait()
        for j in range(span // tile):
            lanes = pl.ds(j * tile, tile)
            columns = first_column + j * tile + lax.broadcasted_iota(jnp.int32, (tile, tile), 1)
            within = (jnp.abs(columns - nearest) <= half) & (columns >= 0) & (columns < total)
            masked[rows, lanes] = jnp.where(within, coefs[rows, lanes].astype(f32), 0.0).astype(bf16)


def impute_own(weights, got_b, masked, out):
    first, _, _ = where_am_i()
    half = got_b.shape[1]
    span = masked.shape[1]
    coefs = jnp.where(first, masked[:, span - half :], masked[:, :half])
    out[...] = contract(weights[...], masked[:, half : span - half]) + contract(got_b[...], coefs)


def impute_edge(acc, got_a, masked, out):
    first, _, _ = where_am_i()
    half = got_a.shape[1]
    span = masked.shape[1]
    coefs = jnp.where(first, masked[:, :half], masked[:, span - half :])
    out[...] = acc[...] + contract(got_a[...], coefs)


def swap(block, distance):
    n = lax.axis_size(AXIS)
    return lax.ppermute(block, AXIS, [(i, i ^ distance) for i in range(n)])


def hop(block, step):
    pairs = []
    for i in range(lax.axis_size(AXIS)):
        g = i // GROUP
        to = i + GROUP if g == step else i - GROUP if g == step + 1 else i
        pairs.append((i, to ^ 1))
    return lax.ppermute(block, AXIS, pairs)


def swap_chips(block):
    n, segments = lax.axis_size(AXIS), lax.axis_size(SEGMENTS)
    pairs = []
    for seg in range(segments):
        for i in range(n):
            to, to_seg = i + 1 if i % 2 else i - 1, seg
            if not 0 <= to < n:
                to, to_seg = (i, seg ^ 1) if segments % 2 == 0 else (to % n, seg)
            pairs.append((seg * n + i, to_seg * n + to))
    return lax.ppermute(block, (SEGMENTS, AXIS), pairs)


def per_device(z, diag_inverse, coupling, impute_coef, anchor):
    d = diag_inverse[0]
    c = coupling[0]
    typed = d.shape[0]
    half = c.shape[1]
    traits = z.shape[0]
    untyped, span = impute_coef.shape
    assert span == typed + 2 * half and typed == 2 * half
    groups = lax.axis_size(AXIS) // GROUP
    two, four = traits // 2, traits // 4
    square = (half, half)
    sq, h2, h4 = (square, f32), ((two, half), f32), ((four, half), f32)
    x1_shape = ((half + two, half), f32)
    coded = ((coded_rows(four, half), LANES), i16)
    coded_pair = ((2 * coded_rows(four, half), LANES), i16)
    coded_half = ((coded_rows(half // 2, half), LANES), i16)
    mixed = ((coded_rows(half // 2, half) + coded_rows(four, half), LANES), i16)

    solved_shape, p_shape = ((traits, typed), f32), ((typed, half), f32)
    x1, s_own, z, d, c = call(
        tail_part, [x1_shape, h2, solved_shape, ((typed, typed), f32), p_shape], z, d, c,
        hbm=True, scratch=[pltpu.SemaphoreType.DMA((4,))],
    )
    got1 = swap(x1, 1)
    x3, g_own, solved, p = call(
        head_part, [x1_shape, h2, solved_shape, p_shape], z, d, c, x1, s_own
    )
    x2, n_own, sp_own = call(pair_forward, [mixed, sq, h4], x1, got1, s_own, after=(p,))
    got2 = swap(x2, 3)
    got3 = swap(x3, 1)
    masked = call(
        mask_coefs, ((untyped, span), bf16), impute_coef, anchor[None, :], after=(x2,), hbm=True,
        scratch=[
            pltpu.VMEM((untyped, span), bf16),
            pltpu.VMEM((1, untyped), jnp.int32),
            pltpu.SemaphoreType.DMA((untyped // 128 + 1,)),
        ],
    )
    x4, gg_own, gp_own = call(
        pair_backward, [mixed, sq, h4], x1, got1, s_own, x3, got3, g_own, after=(x2,)
    )
    got2_core = swap(call(relay, coded_half, got2, after=(x4, masked)), 1)
    s_group, out = call(group_forward, [h4, coded], n_own, got2, got2_core, sp_own)
    n_group, n_first, n_second = call(
        group_map, [sq] * 3, n_own, got2, got2_core, after=(s_group,)
    )

    t_in = jnp.zeros((four, half), f32)
    got4 = swap(x4, 3)
    for step in range(groups - 2):
        got = hop(out, step)
        t_in, out = call(
            functools.partial(forward_hop, step), [h4, coded], got, t_in, n_group, s_group
        )
    got4_core = swap(call(relay, coded_half, got4, after=(out,)), 1)
    gg_group, g_group, gg_second, g_second = call(
        group_backward, [sq, h4, sq, h4],
        n_first, got2, sp_own, gg_own, got4, got4_core, gp_own, after=(out,),
    )
    last = groups - 2
    got = hop(out, last)
    t_in, local, out = call(
        functools.partial(turn, last), [h4, h4, coded], got, t_in, gg_group, g_group
    )

    u_in = jnp.zeros((four, half), f32)
    for step in reversed(range(groups - 1)):
        got = hop(out, step)
        if step == last:
            x5, kept, rest_own = call(
                spread_forward, [coded_pair, h4, h4], t_in, n_first, got2, sp_own, gg_second, g_second,
                after=(local,),
            )
            got5 = swap(x5, 3)
            x6, t_own, rest_pair, rest_block = call(
                pair_states, [h2] * 4, kept, rest_own, got5, x1, got1, s_own, x3, got3, g_own
            )
            got6 = swap(x6, 1)
            early = call(block_rows, solved_shape, t_own, got6, solved, p, d)
        if step:
            u_in, out = call(
                functools.partial(backward_hop, step), [h4, coded], got, u_in, n_group, local
            )
        else:
            u_in, out = call(functools.partial(arrive, step), [h4, coded], got, u_in)
    got_u = swap(out, 3)
    x7, u_own = call(
        spread_backward, [h2, h2], u_in, got_u, n_second, rest_pair, x1, got1, rest_block
    )
    got7 = swap(x7, 1)
    xa, xb, weights = call(
        block_weights, [(square, bf16), (square, bf16), ((traits, typed), bf16)], u_own, got7, early, d
    )
    got_a = swap_chips(xa)
    got_b = swap(xb, 1)
    acc = call(impute_own, ((traits, untyped), f32), weights, got_b, masked)
    return call(impute_edge, ((traits, untyped), f32), acc, got_a, masked, last=True)


def solution(mesh):
    in_specs = (
        P(None, (SEGMENTS, AXIS)),
        P((SEGMENTS, AXIS), None, None),
        P((SEGMENTS, AXIS), None, None),
        P((SEGMENTS, AXIS), None),
        P((SEGMENTS, AXIS)),
    )
    return jax.shard_map(
        per_device, mesh=mesh, in_specs=in_specs, out_specs=P(None, (SEGMENTS, AXIS)), check_vma=False
    )
```

```python
import functools

import jax
import jax.numpy as jnp
from jax import lax
from jax.experimental import pallas as pl
from jax.experimental.pallas import tpu as pltpu
from jax.sharding import PartitionSpec as P

AXIS = "genome"
SEGMENTS = "seg"
GROUP = 4
f32 = jnp.float32
bf16 = jnp.bfloat16
i16 = jnp.int16
SCALES = 16
LANES = 128
LIMIT = 32767.0


def parts(x):
    high = x.astype(bf16)
    return high, (x - high.astype(f32)).astype(bf16)


def dot(a, b, ca=1, cb=0):
    ah, al = parts(a)
    bh, bl = parts(b)
    return lax.dot_general(
        jnp.concatenate([al, ah, ah], axis=ca),
        jnp.concatenate([bh, bl, bh], axis=cb),
        (((ca,), (cb,)), ((), ())),
        preferred_element_type=f32,
    )


def code(x):
    top = jnp.maximum(jnp.max(jnp.abs(x), axis=0, keepdims=True), 1e-32)
    power = jnp.ceil(jnp.log2(top) * 4.0)
    root = jnp.exp2(power * -0.125)
    steps = jnp.floor(x * root * (root * LIMIT) + 0.5)
    steps = jnp.clip(steps, -LIMIT, LIMIT)
    tiles = x.shape[1] // LANES
    powers = jnp.broadcast_to(power, (SCALES // tiles, x.shape[1]))
    pieces = [v[:, i * LANES : (i + 1) * LANES] for v in (steps, powers) for i in range(tiles)]
    return jnp.concatenate(pieces, axis=0).astype(jnp.int32).astype(i16)


def decode(coded, tiles=2):
    rows = (coded.shape[0] - SCALES) // tiles
    values = coded[...].astype(jnp.int32).astype(f32)
    columns = []
    for i in range(tiles):
        at = tiles * rows + i * (SCALES // tiles)
        root = jnp.exp2(values[at : at + 1] * 0.125)
        columns.append(values[i * rows : (i + 1) * rows] * (root / LIMIT) * root)
    return jnp.concatenate(columns, axis=1)


def coded_rows(rows, columns):
    return rows * (columns // LANES) + SCALES


def where_am_i():
    place = lax.axis_index(AXIS)
    return place % 2 == 0, (place // 2) % 2 == 0, place // GROUP


def low_traits():
    place = lax.axis_index(AXIS)
    return (place + place // 2 + place // GROUP) % 2 == 0


def ordered(first, own, other):
    return jnp.where(first, own, other), jnp.where(first, other, own)


def call(kernel, outs, *args, after=(), hbm=False, last=False, scratch=()):
    n_in, n_after = len(args), len(after)

    def body(*refs):
        kernel(*refs[:n_in], *refs[n_in + n_after :])

    single = not isinstance(outs, list)
    shapes = [outs] if single else outs
    vmem = pl.BlockSpec(memory_space=pltpu.VMEM)
    anywhere = pl.BlockSpec(memory_space=pl.ANY)
    if hbm:
        args = [pltpu.with_memory_space_constraint(a, pltpu.HBM) for a in args]
    got = pl.pallas_call(
        body,
        out_shape=[jax.ShapeDtypeStruct(s, t) if last else pltpu.VMEM(s, t) for s, t in shapes],
        in_specs=[anywhere if hbm else vmem] * n_in + [anywhere] * n_after,
        out_specs=[vmem] * len(shapes),
        scratch_shapes=scratch,
        compiler_params=pltpu.CompilerParams(vmem_limit_bytes=8 * 2**20),
        name=kernel.__name__ if hasattr(kernel, "__name__") else kernel.func.__name__,
    )(*args, *after)
    return got[0] if single else got


def tail_part(z_in, d_in, c_in, x1, s_own, z, d, c, sems):
    half = c.shape[1]
    rows = z.shape[0] // 2
    head = d.shape[0] - half
    pieces = [
        (d_in.at[pl.ds(head, half)], d.at[pl.ds(head, half)]),
        (c_in, c),
        (z_in, z),
        (d_in.at[pl.ds(0, head)], d.at[pl.ds(0, head)]),
    ]
    copies = [pltpu.make_async_copy(src, dst, sems.at[i]) for i, (src, dst) in enumerate(pieces)]
    for copy in copies[:3]:
        copy.start()
    copies[0].wait()
    copies[1].wait()
    copies[3].start()
    tail = d[head:]
    x1[:half] = -dot(tail, c[...])
    copies[2].wait()
    s = dot(z[...], tail, 1, 1)
    keep, send = ordered(low_traits(), s[:rows], s[rows:])
    x1[half:] = send
    s_own[...] = keep
    copies[3].wait()


def head_part(z, d, c, x1, s_own, x3, g_own, solved, p):
    half = c.shape[1]
    rows = z.shape[0] // 2
    head = d.shape[0] - half
    first, _, _ = where_am_i()
    p[:head] = dot(d[:head], c[...])
    p[head:] = -x1[:half]
    solved[:, :head] = dot(z[...], d[:head], 1, 1)
    low, high = ordered(low_traits(), s_own[...], x1[half:])
    solved[:rows, head:] = low
    solved[rows:, head:] = high
    g = dot(solved[...], p[...])
    keep, send = ordered(low_traits(), g[:rows], g[rows:])
    x3[:half] = dot(p[...], p[...], 0, 0)
    x3[half:] = send
    g_own[...] = keep


def pair_forward(x1, got1, s_own, x2, n_own, sp_own):
    half = x1.shape[1]
    first, first_pair, _ = where_am_i()
    m0, m1 = ordered(first, x1[:half], got1[:half])
    s0, s1 = ordered(first, s_own[...], got1[half:])
    n = dot(m1, m0)
    n_own[...] = n
    split = coded_rows(half // 2, half)
    x2[:split] = code(jnp.where(first, n[: half // 2], n[half // 2 :]))
    s = dot(s0, m1, 1, 1) + s1
    rows = s.shape[0] // 2
    keep, send = ordered(first_pair, s[:rows], s[rows:])
    x2[split:] = code(send)
    sp_own[...] = keep


def pair_backward(x1, got1, s_own, x3, got3, g_own, x4, gg_own, gp_own):
    half = x1.shape[1]
    first, first_pair, _ = where_am_i()
    m0, _ = ordered(first, x1[:half], got1[:half])
    s0, _ = ordered(first, s_own[...], got1[half:])
    gg0, gg1 = ordered(first, x3[:half], got3[:half])
    g0, g1 = ordered(first, g_own[...], got3[half:])
    both = dot(jnp.concatenate([gg1, g1 - dot(s0, gg1)], axis=0), m0)
    gg = dot(m0, both[:half], 0, 0) + gg0
    gg_own[...] = gg
    split = coded_rows(half // 2, half)
    x4[:split] = code(jnp.where(first, gg[: half // 2], gg[half // 2 :]))
    g = both[half:] + g0
    rows = g.shape[0] // 2
    keep, send = ordered(first_pair, g[:rows], g[rows:])
    x4[split:] = code(send)
    gp_own[...] = keep


def pair_matrices(own, got, got_core):
    first, first_pair, _ = where_am_i()
    other = jnp.concatenate(ordered(first, got_core, got), axis=0)
    return ordered(first_pair, own[...], other)


def pair_vectors(own, got):
    _, first_pair, _ = where_am_i()
    return ordered(first_pair, own[...], got)


def relay(got, out):
    out[...] = got[: out.shape[0]]


def group_forward(n_own, got2, got2_core, sp_own, s_group, out):
    half = n_own.shape[1]
    split = coded_rows(half // 2, half)
    _, n1 = pair_matrices(n_own, decode(got2[:split]), decode(got2_core))
    s0, s1 = pair_vectors(sp_own, decode(got2[split:]))
    s = dot(s0, n1, 1, 1) + s1
    s_group[...] = s
    out[...] = code(s)


def group_map(n_own, got2, got2_core, n_group, n_first, n_second):
    half = n_own.shape[1]
    split = coded_rows(half // 2, half)
    n0, n1 = pair_matrices(n_own, decode(got2[:split]), decode(got2_core))
    n_first[...] = n0
    n_second[...] = n1
    n_group[...] = dot(n1, n0)


def group_backward(
    n_first, got2, sp_own, gg_own, got4, got4_core, gp_own, gg_group, g_group, gg_second, g_second
):
    half = n_first.shape[1]
    split = coded_rows(half // 2, half)
    n0 = n_first[...]
    s0, _ = pair_vectors(sp_own, decode(got2[split:]))
    gg0, gg1 = pair_matrices(gg_own, decode(got4[:split]), decode(got4_core))
    g0, g1 = pair_vectors(gp_own, decode(got4[split:]))
    gg_second[...] = gg1
    g_second[...] = g1
    both = dot(jnp.concatenate([gg1, g1 - dot(s0, gg1)], axis=0), n0)
    gg_group[...] = dot(n0, both[:half], 0, 0) + gg0
    g_group[...] = both[half:] + g0


def forward_hop(step, got, t_in, n_group, s_group, t_out, out):
    _, _, group = where_am_i()
    t = jnp.where(group == step + 1, decode(got), t_in[...])
    t_out[...] = t
    out[...] = code(dot(t, n_group[...], 1, 1) + s_group[...])


def turn(step, got, t_in, gg_group, g_group, t_out, local, out):
    _, _, group = where_am_i()
    t = jnp.where(group == step + 1, decode(got), t_in[...])
    t_out[...] = t
    u = g_group[...] - dot(t, gg_group[...])
    local[...] = u
    out[...] = code(u)


def backward_hop(step, got, u_in, n_group, local, u_out, out):
    _, _, group = where_am_i()
    u = jnp.where(group == step, decode(got), u_in[...])
    u_out[...] = u
    out[...] = code(dot(u, n_group[...]) + local[...])


def arrive(step, got, u_in, out):
    _, _, group = where_am_i()
    out[...] = code(jnp.where(group == step, decode(got), u_in[...]))


def spread_forward(t_in, n_first, got2, sp_own, gg_second, g_second, x5, x5_rest, kept, rest_own):
    half = n_first.shape[1]
    _, first_pair, _ = where_am_i()
    s0, _ = pair_vectors(sp_own, decode(got2[coded_rows(half // 2, half) :]))
    t_mid = dot(t_in[...], n_first[...], 1, 1) + s0
    rest = g_second[...] - dot(t_mid, gg_second[...])
    keep, send = ordered(first_pair, t_in[...], t_mid)
    x5[...] = code(send)
    x5_rest[...] = code(rest)
    kept[...] = keep
    rest_own[...] = rest


def block_map(n_second, x1, got1, d, k):
    half = x1.shape[1]
    first, first_pair, _ = where_am_i()
    rows = lax.broadcasted_iota(jnp.int32, (half, half), 0)
    columns = lax.broadcasted_iota(jnp.int32, (half, half), 1)
    unit = (rows == columns).astype(f32)
    _, m1 = ordered(first, x1[:half], got1[:half])
    above = jnp.where(first_pair, n_second[...], unit)
    above = jnp.where(first, dot(above, m1), above)
    k[...] = dot(above, d[d.shape[0] - half :])


def pair_states(kept, rest_own, got5, got5_rest, x1, got1, s_own, x3, got3, g_own, x6, own):
    half = x1.shape[1]
    rows = s_own.shape[0]
    first, first_pair, _ = where_am_i()
    t = jnp.concatenate(ordered(first_pair, kept[...], decode(got5)), axis=0)
    rest = jnp.concatenate(ordered(first_pair, rest_own[...], decode(got5_rest)), axis=0)
    m0, m1 = ordered(first, x1[:half], got1[:half])
    s0, _ = ordered(first, s_own[...], got1[half:])
    _, gg1 = ordered(first, x3[:half], got3[:half])
    _, g1 = ordered(first, g_own[...], got3[half:])
    t_mid = dot(t, m0, 1, 1) + s0
    fixed = jnp.where(first_pair, rest, 0.0)
    fixed_mid = dot(fixed, m1) + g1 - dot(t_mid, gg1)
    split = coded_rows(rows, half)
    keep, send = ordered(first, t, t_mid)
    x6[:split] = code(send)
    own[:rows] = keep
    keep, send = ordered(first, fixed_mid, fixed)
    x6[split:] = code(send)
    own[rows:] = keep


def block_parts(solved, p, d, start, maps):
    half = p.shape[1]
    start[...] = dot(solved[...], d[...])
    maps[:half] = dot(p[...], d[...], 0, 0)
    maps[half:] = d[d.shape[0] - half :]


def block_fixed(own, got6, start, maps, fixed_weights):
    rows = own.shape[0] // 2
    split = coded_rows(rows, own.shape[1])
    low = low_traits()
    t = jnp.concatenate(ordered(low, own[:rows], decode(got6[:split])), axis=0)
    above = jnp.concatenate(ordered(low, own[rows:], decode(got6[split:])), axis=0)
    fixed_weights[...] = start[...] - dot(jnp.concatenate([t, above], axis=1), maps[...])


def block_weights(mine, got_u, theirs, their_got, fixed_weights, k, xa, xb):
    half = k.shape[0]
    first, first_pair, _ = where_am_i()
    near = jnp.concatenate(ordered(first_pair, decode(mine), decode(got_u)), axis=0)
    far = jnp.concatenate(ordered(first_pair, decode(theirs), decode(their_got)), axis=0)
    u = jnp.concatenate(ordered(low_traits(), near, far), axis=0)
    weights = (fixed_weights[...] - dot(u, k[...])).astype(bf16)
    a, b = ordered(first, weights[:, :half], weights[:, half:])
    xa[...] = a
    xb[...] = b


def contract(values, coefs):
    return lax.dot_general(values, coefs, (((1,), (1,)), ((), ())), preferred_element_type=f32)


def mask_coefs(coefs_in, anchor_in, masked, coefs, anchor, sems):
    untyped, span = coefs.shape
    half = span // 4
    typed = span - 2 * half
    tile = 128
    place = lax.axis_index(AXIS)
    total = lax.axis_size(AXIS) * typed
    copies = [pltpu.make_async_copy(anchor_in, anchor, sems.at[0])]
    for i in range(untyped // tile):
        rows = pl.ds(i * tile, tile)
        copies.append(pltpu.make_async_copy(coefs_in.at[rows], coefs.at[rows], sems.at[i + 1]))
    for copy in copies:
        copy.start()
    copies[0].wait()
    first_column = place * typed - half
    for i in range(untyped // tile):
        rows = pl.ds(i * tile, tile)
        nearest = jnp.broadcast_to(anchor[:, i * tile : (i + 1) * tile], (tile, tile)).T
        copies[i + 1].wait()
        for j in range(span // tile):
            lanes = pl.ds(j * tile, tile)
            columns = first_column + j * tile + lax.broadcasted_iota(jnp.int32, (tile, tile), 1)
            within = (jnp.abs(columns - nearest) <= half) & (columns >= 0) & (columns < total)
            masked[rows, lanes] = jnp.where(within, coefs[rows, lanes].astype(f32), 0.0).astype(bf16)


def impute_own(xa, xb, masked, out):
    first, _, _ = where_am_i()
    half = xa.shape[1]
    span = masked.shape[1]
    weights = jnp.concatenate(ordered(first, xa[...], xb[...]), axis=1)
    out[...] = contract(weights, masked[:, half : span - half])


def impute_edges(acc, got_a, got_b, masked, out):
    first, _, _ = where_am_i()
    half = got_a.shape[1]
    span = masked.shape[1]
    left, right = ordered(first, got_a[...], got_b[...])
    out[...] = acc[...] + contract(left, masked[:, :half]) + contract(right, masked[:, span - half :])


def swap(block, distance):
    n = lax.axis_size(AXIS)
    return lax.ppermute(block, AXIS, [(i, i ^ distance) for i in range(n)])


def hop(block, step):
    pairs = []
    for i in range(lax.axis_size(AXIS)):
        g = i // GROUP
        to = i + GROUP if g == step else i - GROUP if g == step + 1 else i
        pairs.append((i, to ^ 1))
    return lax.ppermute(block, AXIS, pairs)


def swap_chips(block):
    n, segments = lax.axis_size(AXIS), lax.axis_size(SEGMENTS)
    pairs = []
    for seg in range(segments):
        for i in range(n):
            to, to_seg = i + 1 if i % 2 else i - 1, seg
            if not 0 <= to < n:
                to, to_seg = (i, seg ^ 1) if segments % 2 == 0 else (to % n, seg)
            pairs.append((seg * n + i, to_seg * n + to))
    return lax.ppermute(block, (SEGMENTS, AXIS), pairs)


def per_device(z, diag_inverse, coupling, impute_coef, anchor):
    d = diag_inverse[0]
    c = coupling[0]
    typed = d.shape[0]
    half = c.shape[1]
    traits = z.shape[0]
    untyped, span = impute_coef.shape
    assert span == typed + 2 * half and typed == 2 * half
    assert lax.axis_size(AXIS) >= 3 * GROUP
    groups = lax.axis_size(AXIS) // GROUP
    two, four = traits // 2, traits // 4
    square = (half, half)
    sq, h2, h4 = (square, f32), ((two, half), f32), ((four, half), f32)
    x1_shape, x6_shape = ((half + two, half), f32), ((2 * two, half), f32)
    x6_coded = ((2 * coded_rows(two, half), LANES), i16)
    coded = ((coded_rows(four, half), LANES), i16)
    coded_half = ((coded_rows(half // 2, half), LANES), i16)
    mixed = ((coded_rows(half // 2, half) + coded_rows(four, half), LANES), i16)

    solved_shape, p_shape = ((traits, typed), f32), ((typed, half), f32)
    x1, s_own, z, d, c = call(
        tail_part, [x1_shape, h2, solved_shape, ((typed, typed), f32), p_shape], z, d, c,
        hbm=True, scratch=[pltpu.SemaphoreType.DMA((4,))],
    )
    got1 = swap(x1, 1)
    x3, g_own, solved, p = call(
        head_part, [x1_shape, h2, solved_shape, p_shape], z, d, c, x1, s_own
    )
    x2, n_own, sp_own = call(pair_forward, [mixed, sq, h4], x1, got1, s_own, after=(p,))
    got2 = swap(x2, 3)
    got3 = swap(x3, 1)
    masked = call(
        mask_coefs, ((untyped, span), bf16), impute_coef, anchor[None, :], after=(x2,), hbm=True,
        scratch=[
            pltpu.VMEM((untyped, span), bf16),
            pltpu.VMEM((1, untyped), jnp.int32),
            pltpu.SemaphoreType.DMA((untyped // 128 + 1,)),
        ],
    )
    x4, gg_own, gp_own = call(
        pair_backward, [mixed, sq, h4], x1, got1, s_own, x3, got3, g_own, after=(x2,)
    )
    got2_core = swap(call(relay, coded_half, got2, after=(x4, masked)), 1)
    s_group, out = call(group_forward, [h4, coded], n_own, got2, got2_core, sp_own)
    n_group, n_first, n_second = call(
        group_map, [sq] * 3, n_own, got2, got2_core, after=(s_group,)
    )

    k = call(block_map, ((half, typed), f32), n_second, x1, got1, d)
    t_in = jnp.zeros((four, half), f32)
    got4 = swap(x4, 3)
    for step in range(groups - 2):
        got = hop(out, step)
        t_in, out = call(
            functools.partial(forward_hop, step), [h4, coded], got, t_in, n_group, s_group,
            after=(k,) if step == 0 else (maps,) if step == 1 else (),
        )
        if step == 0:
            start, maps = call(
                block_parts, [solved_shape, ((2 * half, typed), f32)], solved, p, d, after=(out,)
            )
    got4_core = swap(call(relay, coded_half, got4, after=(out,)), 1)
    gg_group, g_group, gg_second, g_second = call(
        group_backward, [sq, h4, sq, h4],
        n_first, got2, sp_own, gg_own, got4, got4_core, gp_own, after=(out,),
    )
    last = groups - 2
    got = hop(out, last)
    t_in, local, out = call(
        functools.partial(turn, last), [h4, h4, coded], got, t_in, gg_group, g_group
    )

    u_in = jnp.zeros((four, half), f32)
    for step in reversed(range(groups - 1)):
        got = hop(out, step)
        if step == last:
            x5, x5_rest, kept, rest_own = call(
                spread_forward, [coded, coded, h4, h4], t_in, n_first, got2, sp_own, gg_second, g_second,
                after=(local,),
            )
            got5, got5_rest = swap(x5, 3), swap(x5_rest, 3)
        if step:
            u_in, out = call(
                functools.partial(backward_hop, step), [h4, coded], got, u_in, n_group, local
            )
        else:
            out = call(functools.partial(arrive, step), coded, got, u_in)
    x6, own = call(
        pair_states, [x6_coded, x6_shape], kept, rest_own, got5, got5_rest, x1, got1, s_own, x3, got3, g_own
    )
    got6 = swap(x6, 1)
    fixed = call(block_fixed, solved_shape, own, got6, start, maps)
    theirs = swap(out, 1)
    got_u = swap(out, 3)
    their_got = swap(got_u, 1)
    edge = (square, bf16)
    xa, xb = call(block_weights, [edge, edge], out, got_u, theirs, their_got, fixed, k)
    got_a = swap_chips(xa)
    got_b = swap(xb, 1)
    acc = call(impute_own, ((traits, untyped), f32), xa, xb, masked)
    return call(
        impute_edges, ((traits, untyped), f32), acc, got_a, got_b, masked, last=True
    )


def solution(mesh):
    in_specs = (
        P(None, (SEGMENTS, AXIS)),
        P((SEGMENTS, AXIS), None, None),
        P((SEGMENTS, AXIS), None, None),
        P((SEGMENTS, AXIS), None),
        P((SEGMENTS, AXIS)),
    )
    return jax.shard_map(
        per_device, mesh=mesh, in_specs=in_specs, out_specs=P(None, (SEGMENTS, AXIS)), check_vma=False
    )
```

```python
import functools

import jax
import jax.numpy as jnp
from jax import lax
from jax.experimental import pallas as pl
from jax.experimental.pallas import tpu as pltpu
from jax.sharding import PartitionSpec as P

AXIS = "genome"
SEGMENTS = "seg"
GROUP = 4
f32 = jnp.float32
bf16 = jnp.bfloat16
i16 = jnp.int16
SCALES = 16
LANES = 128
LIMIT = 32767.0


def parts(x):
    high = x.astype(bf16)
    return high, (x - high.astype(f32)).astype(bf16)


def dot(a, b, ca=1, cb=0):
    ah, al = parts(a)
    bh, bl = parts(b)
    return lax.dot_general(
        jnp.concatenate([al, ah, ah], axis=ca),
        jnp.concatenate([bh, bl, bh], axis=cb),
        (((ca,), (cb,)), ((), ())),
        preferred_element_type=f32,
    )


def code(x):
    top = jnp.maximum(jnp.max(jnp.abs(x), axis=0, keepdims=True), 1e-32)
    power = jnp.ceil(jnp.log2(top) * 4.0)
    root = jnp.exp2(power * -0.125)
    steps = jnp.floor(x * root * (root * LIMIT) + 0.5)
    steps = jnp.clip(steps, -LIMIT, LIMIT)
    tiles = x.shape[1] // LANES
    powers = jnp.broadcast_to(power, (SCALES // tiles, x.shape[1]))
    pieces = [v[:, i * LANES : (i + 1) * LANES] for v in (steps, powers) for i in range(tiles)]
    return jnp.concatenate(pieces, axis=0).astype(jnp.int32).astype(i16)


def decode(coded, tiles=2):
    rows = (coded.shape[0] - SCALES) // tiles
    values = coded[...].astype(jnp.int32).astype(f32)
    columns = []
    for i in range(tiles):
        at = tiles * rows + i * (SCALES // tiles)
        root = jnp.exp2(values[at : at + 1] * 0.125)
        columns.append(values[i * rows : (i + 1) * rows] * (root / LIMIT) * root)
    return jnp.concatenate(columns, axis=1)


def coded_rows(rows, columns):
    return rows * (columns // LANES) + SCALES


def where_am_i():
    place = lax.axis_index(AXIS)
    return place % 2 == 0, (place // 2) % 2 == 0, place // GROUP


def low_traits():
    place = lax.axis_index(AXIS)
    return (place + place // 2 + place // GROUP) % 2 == 0


def ordered(first, own, other):
    return jnp.where(first, own, other), jnp.where(first, other, own)


def call(kernel, outs, *args, after=(), hbm=False, last=False, scratch=()):
    n_in, n_after = len(args), len(after)

    def body(*refs):
        kernel(*refs[:n_in], *refs[n_in + n_after :])

    single = not isinstance(outs, list)
    shapes = [outs] if single else outs
    vmem = pl.BlockSpec(memory_space=pltpu.VMEM)
    anywhere = pl.BlockSpec(memory_space=pl.ANY)
    if hbm:
        args = [pltpu.with_memory_space_constraint(a, pltpu.HBM) for a in args]
    got = pl.pallas_call(
        body,
        out_shape=[jax.ShapeDtypeStruct(s, t) if last else pltpu.VMEM(s, t) for s, t in shapes],
        in_specs=[anywhere if hbm else vmem] * n_in + [anywhere] * n_after,
        out_specs=[vmem] * len(shapes),
        scratch_shapes=scratch,
        compiler_params=pltpu.CompilerParams(vmem_limit_bytes=8 * 2**20),
        name=kernel.__name__ if hasattr(kernel, "__name__") else kernel.func.__name__,
    )(*args, *after)
    return got[0] if single else got


def tail_part(z_in, d_in, c_in, x1, s_own, z, d, c, sems):
    half = c.shape[1]
    rows = z.shape[0] // 2
    head = d.shape[0] - half
    pieces = [
        (d_in.at[pl.ds(head, half)], d.at[pl.ds(head, half)]),
        (c_in, c),
        (z_in, z),
        (d_in.at[pl.ds(0, head)], d.at[pl.ds(0, head)]),
    ]
    copies = [pltpu.make_async_copy(src, dst, sems.at[i]) for i, (src, dst) in enumerate(pieces)]
    for copy in copies[:3]:
        copy.start()
    copies[0].wait()
    copies[1].wait()
    copies[3].start()
    tail = d[head:]
    x1[:half] = -dot(tail, c[...])
    copies[2].wait()
    s = dot(z[...], tail, 1, 1)
    keep, send = ordered(low_traits(), s[:rows], s[rows:])
    x1[half:] = send
    s_own[...] = keep
    copies[3].wait()


def head_part(z, d, c, x1, s_own, x3, g_own, solved, p):
    half = c.shape[1]
    rows = z.shape[0] // 2
    head = d.shape[0] - half
    first, _, _ = where_am_i()
    p[:head] = dot(d[:head], c[...])
    p[head:] = -x1[:half]
    solved[:, :head] = dot(z[...], d[:head], 1, 1)
    low, high = ordered(low_traits(), s_own[...], x1[half:])
    solved[:rows, head:] = low
    solved[rows:, head:] = high
    g = dot(solved[...], p[...])
    keep, send = ordered(low_traits(), g[:rows], g[rows:])
    x3[:half] = dot(p[...], p[...], 0, 0)
    x3[half:] = send
    g_own[...] = keep


def pair_forward(x1, got1, s_own, x2, n_own, sp_own):
    half = x1.shape[1]
    first, first_pair, _ = where_am_i()
    m0, m1 = ordered(first, x1[:half], got1[:half])
    s0, s1 = ordered(first, s_own[...], got1[half:])
    n = dot(m1, m0)
    n_own[...] = n
    split = coded_rows(half // 2, half)
    x2[:split] = code(jnp.where(first, n[: half // 2], n[half // 2 :]))
    s = dot(s0, m1, 1, 1) + s1
    rows = s.shape[0] // 2
    keep, send = ordered(first_pair, s[:rows], s[rows:])
    x2[split:] = code(send)
    sp_own[...] = keep


def pair_backward(x1, got1, s_own, x3, got3, g_own, x4, gg_own, gp_own):
    half = x1.shape[1]
    first, first_pair, _ = where_am_i()
    m0, _ = ordered(first, x1[:half], got1[:half])
    s0, _ = ordered(first, s_own[...], got1[half:])
    gg0, gg1 = ordered(first, x3[:half], got3[:half])
    g0, g1 = ordered(first, g_own[...], got3[half:])
    both = dot(jnp.concatenate([gg1, g1 - dot(s0, gg1)], axis=0), m0)
    gg = dot(m0, both[:half], 0, 0) + gg0
    gg_own[...] = gg
    split = coded_rows(half // 2, half)
    x4[:split] = code(jnp.where(first, gg[: half // 2], gg[half // 2 :]))
    g = both[half:] + g0
    rows = g.shape[0] // 2
    keep, send = ordered(first_pair, g[:rows], g[rows:])
    x4[split:] = code(send)
    gp_own[...] = keep


def pair_matrices(own, got, got_core):
    first, first_pair, _ = where_am_i()
    other = jnp.concatenate(ordered(first, got_core, got), axis=0)
    return ordered(first_pair, own[...], other)


def pair_vectors(own, got):
    _, first_pair, _ = where_am_i()
    return ordered(first_pair, own[...], got)


def relay(got, out):
    out[...] = got[: out.shape[0]]


def relay_halves(got, low, high):
    rows = low.shape[0] - SCALES
    low[:rows] = got[:rows]
    high[:rows] = got[rows : 2 * rows]
    low[rows:] = got[2 * rows : 2 * rows + SCALES]
    high[rows:] = got[2 * rows : 2 * rows + SCALES]


def above_map(n_second, x1, got1, d, k):
    half = x1.shape[1]
    first, first_pair, _ = where_am_i()
    rows = lax.broadcasted_iota(jnp.int32, (half, half), 0)
    columns = lax.broadcasted_iota(jnp.int32, (half, half), 1)
    unit = (rows == columns).astype(f32)
    _, m1 = ordered(first, x1[:half], got1[:half])
    above = jnp.where(first_pair, n_second, unit)
    above = jnp.where(first, dot(above, m1), above)
    k[...] = dot(above, d[d.shape[0] - half :])


def group_forward(n_own, got2, got2_core, sp_own, x1, got1, d, s_group, out, k_high):
    half = n_own.shape[1]
    split = coded_rows(half // 2, half)
    _, n1 = pair_matrices(n_own, decode(got2[:split]), decode(got2_core))

    @pl.when(jnp.logical_not(low_traits()))
    def _():
        above_map(n1, x1, got1, d, k_high)

    s0, s1 = pair_vectors(sp_own, decode(got2[split:]))
    s = dot(s0, n1, 1, 1) + s1
    s_group[...] = s
    out[...] = code(s)


def group_map(n_own, got2, got2_core, x1, got1, d, n_group, n_first, k_low):
    half = n_own.shape[1]
    split = coded_rows(half // 2, half)
    n0, n1 = pair_matrices(n_own, decode(got2[:split]), decode(got2_core))
    n_first[...] = n0
    n_group[...] = dot(n1, n0)

    @pl.when(low_traits())
    def _():
        above_map(n1, x1, got1, d, k_low)


def group_backward(
    n_first, got2, sp_own, gg_own, got4, got4_low, got4_high, gp_own,
    gg_group, g_group, gg_second, g_second,
):
    half = n_first.shape[1]
    split = coded_rows(half // 2, half)
    n0 = n_first[...]
    s0, _ = pair_vectors(sp_own, decode(got2[split:]))
    rows = got4_low.shape[0] - SCALES
    got4_core = jnp.concatenate([got4_low[:rows], got4_high[...]], axis=0)
    gg0, gg1 = pair_matrices(gg_own, decode(got4[:split]), decode(got4_core))
    g0, g1 = pair_vectors(gp_own, decode(got4[split:]))
    gg_second[...] = gg1
    g_second[...] = g1
    both = dot(jnp.concatenate([gg1, g1 - dot(s0, gg1)], axis=0), n0)
    gg_group[...] = dot(n0, both[:half], 0, 0) + gg0
    g_group[...] = both[half:] + g0


def forward_hop(step, got, t_in, n_group, s_group, t_out, out):
    _, _, group = where_am_i()
    t = jnp.where(group == step + 1, decode(got), t_in[...])
    t_out[...] = t
    out[...] = code(dot(t, n_group[...], 1, 1) + s_group[...])


def turn(step, got, t_in, gg_group, g_group, t_out, local, out):
    _, _, group = where_am_i()
    t = jnp.where(group == step + 1, decode(got), t_in[...])
    t_out[...] = t
    u = g_group[...] - dot(t, gg_group[...])
    local[...] = u
    out[...] = code(u)


def backward_hop(step, got, u_in, n_group, local, u_out, out):
    _, _, group = where_am_i()
    u = jnp.where(group == step, decode(got), u_in[...])
    u_out[...] = u
    out[...] = code(dot(u, n_group[...]) + local[...])


def arrive(step, got, u_in, out):
    _, _, group = where_am_i()
    out[...] = code(jnp.where(group == step, decode(got), u_in[...]))


def spread_forward(t_in, n_first, got2, sp_own, gg_second, g_second, x5, x5_rest, kept, rest_own):
    half = n_first.shape[1]
    _, first_pair, _ = where_am_i()
    s0, _ = pair_vectors(sp_own, decode(got2[coded_rows(half // 2, half) :]))
    t_mid = dot(t_in[...], n_first[...], 1, 1) + s0
    rest = g_second[...] - dot(t_mid, gg_second[...])
    keep, send = ordered(first_pair, t_in[...], t_mid)
    x5[...] = code(send)
    x5_rest[...] = code(rest)
    kept[...] = keep
    rest_own[...] = rest


def pair_states(kept, rest_own, got5, got5_rest, x1, got1, s_own, x3, got3, g_own, x6, own):
    half = x1.shape[1]
    rows = s_own.shape[0]
    first, first_pair, _ = where_am_i()
    t = jnp.concatenate(ordered(first_pair, kept[...], decode(got5)), axis=0)
    rest = jnp.concatenate(ordered(first_pair, rest_own[...], decode(got5_rest)), axis=0)
    m0, m1 = ordered(first, x1[:half], got1[:half])
    s0, _ = ordered(first, s_own[...], got1[half:])
    _, gg1 = ordered(first, x3[:half], got3[:half])
    _, g1 = ordered(first, g_own[...], got3[half:])
    t_mid = dot(t, m0, 1, 1) + s0
    fixed = jnp.where(first_pair, rest, 0.0)
    fixed_mid = dot(fixed, m1) + g1 - dot(t_mid, gg1)
    split = coded_rows(rows, half)
    keep, send = ordered(first, t, t_mid)
    x6[:split] = code(send)
    own[:rows] = keep
    keep, send = ordered(first, fixed_mid, fixed)
    x6[split:] = code(send)
    own[rows:] = keep


def block_parts(solved, p, d, start, maps):
    half = p.shape[1]
    start[...] = dot(solved[...], d[...])
    maps[:half] = dot(p[...], d[...], 0, 0)
    maps[half:] = d[d.shape[0] - half :]


def block_fixed(own, got6, start, maps, fixed_weights):
    rows = own.shape[0] // 2
    split = coded_rows(rows, own.shape[1])
    low = low_traits()
    t = jnp.concatenate(ordered(low, own[:rows], decode(got6[:split])), axis=0)
    above = jnp.concatenate(ordered(low, own[rows:], decode(got6[split:])), axis=0)
    fixed_weights[...] = start[...] - dot(jnp.concatenate([t, above], axis=1), maps[...])


def block_weights(mine, got_u, theirs, their_got, fixed_weights, k_low, k_high, xa, xb):
    half = k_low.shape[0]
    first, first_pair, _ = where_am_i()
    k = jnp.where(low_traits(), k_low[...], k_high[...])
    near = jnp.concatenate(ordered(first_pair, decode(mine), decode(got_u)), axis=0)
    far = jnp.concatenate(ordered(first_pair, decode(theirs), decode(their_got)), axis=0)
    u = jnp.concatenate(ordered(low_traits(), near, far), axis=0)
    weights = (fixed_weights[...] - dot(u, k)).astype(bf16)
    a, b = ordered(first, weights[:, :half], weights[:, half:])
    xa[...] = a
    xb[...] = b


def contract(values, coefs):
    return lax.dot_general(values, coefs, (((1,), (1,)), ((), ())), preferred_element_type=f32)


def mask_coefs(coefs_in, anchor_in, masked, coefs, anchor, sems):
    untyped, span = coefs.shape
    half = span // 4
    typed = span - 2 * half
    tile = 128
    place = lax.axis_index(AXIS)
    total = lax.axis_size(AXIS) * typed
    copies = [pltpu.make_async_copy(anchor_in, anchor, sems.at[0])]
    for i in range(untyped // tile):
        rows = pl.ds(i * tile, tile)
        copies.append(pltpu.make_async_copy(coefs_in.at[rows], coefs.at[rows], sems.at[i + 1]))
    for copy in copies:
        copy.start()
    copies[0].wait()
    first_column = place * typed - half
    for i in range(untyped // tile):
        rows = pl.ds(i * tile, tile)
        nearest = jnp.broadcast_to(anchor[:, i * tile : (i + 1) * tile], (tile, tile)).T
        copies[i + 1].wait()
        for j in range(span // tile):
            lanes = pl.ds(j * tile, tile)
            columns = first_column + j * tile + lax.broadcasted_iota(jnp.int32, (tile, tile), 1)
            within = (jnp.abs(columns - nearest) <= half) & (columns >= 0) & (columns < total)
            masked[rows, lanes] = jnp.where(within, coefs[rows, lanes].astype(f32), 0.0).astype(bf16)


def impute_own(xa, xb, masked, out):
    first, _, _ = where_am_i()
    half = xa.shape[1]
    span = masked.shape[1]
    weights = jnp.concatenate(ordered(first, xa[...], xb[...]), axis=1)
    out[...] = contract(weights, masked[:, half : span - half])


def impute_edges(acc, got_a, got_b, masked, out):
    first, _, _ = where_am_i()
    half = got_a.shape[1]
    span = masked.shape[1]
    left, right = ordered(first, got_a[...], got_b[...])
    out[...] = acc[...] + contract(left, masked[:, :half]) + contract(right, masked[:, span - half :])


def swap(block, distance):
    n = lax.axis_size(AXIS)
    return lax.ppermute(block, AXIS, [(i, i ^ distance) for i in range(n)])


def hop(block, step):
    pairs = []
    for i in range(lax.axis_size(AXIS)):
        g = i // GROUP
        to = i + GROUP if g == step else i - GROUP if g == step + 1 else i
        pairs.append((i, to ^ 1))
    return lax.ppermute(block, AXIS, pairs)


def swap_chips(block):
    n, segments = lax.axis_size(AXIS), lax.axis_size(SEGMENTS)
    pairs = []
    for seg in range(segments):
        for i in range(n):
            to, to_seg = i + 1 if i % 2 else i - 1, seg
            if not 0 <= to < n:
                to, to_seg = (i, seg ^ 1) if segments % 2 == 0 else (to % n, seg)
            pairs.append((seg * n + i, to_seg * n + to))
    return lax.ppermute(block, (SEGMENTS, AXIS), pairs)


def per_device(z, diag_inverse, coupling, impute_coef, anchor):
    d = diag_inverse[0]
    c = coupling[0]
    typed = d.shape[0]
    half = c.shape[1]
    traits = z.shape[0]
    untyped, span = impute_coef.shape
    assert span == typed + 2 * half and typed == 2 * half
    assert lax.axis_size(AXIS) >= 3 * GROUP
    groups = lax.axis_size(AXIS) // GROUP
    two, four = traits // 2, traits // 4
    square = (half, half)
    sq, h2, h4 = (square, f32), ((two, half), f32), ((four, half), f32)
    x1_shape, x6_shape = ((half + two, half), f32), ((2 * two, half), f32)
    x6_coded = ((2 * coded_rows(two, half), LANES), i16)
    coded = ((coded_rows(four, half), LANES), i16)
    coded_half = ((coded_rows(half // 2, half), LANES), i16)
    mixed = ((coded_rows(half // 2, half) + coded_rows(four, half), LANES), i16)

    solved_shape, p_shape = ((traits, typed), f32), ((typed, half), f32)
    x1, s_own, z, d, c = call(
        tail_part, [x1_shape, h2, solved_shape, ((typed, typed), f32), p_shape], z, d, c,
        hbm=True, scratch=[pltpu.SemaphoreType.DMA((4,))],
    )
    got1 = swap(x1, 1)
    x3, g_own, solved, p = call(
        head_part, [x1_shape, h2, solved_shape, p_shape], z, d, c, x1, s_own
    )
    x2, n_own, sp_own = call(pair_forward, [mixed, sq, h4], x1, got1, s_own, after=(p,))
    got2 = swap(x2, 3)
    got3 = swap(x3, 1)
    masked = call(
        mask_coefs, ((untyped, span), bf16), impute_coef, anchor[None, :], after=(x2,), hbm=True,
        scratch=[
            pltpu.VMEM((untyped, span), bf16),
            pltpu.VMEM((1, untyped), jnp.int32),
            pltpu.SemaphoreType.DMA((untyped // 128 + 1,)),
        ],
    )
    x4, gg_own, gp_own = call(
        pair_backward, [mixed, sq, h4], x1, got1, s_own, x3, got3, g_own, after=(x2,)
    )
    got2_core = swap(call(relay, coded_half, got2, after=(x4, masked)), 1)
    k_shape = ((half, typed), f32)
    s_group, out, k_high = call(
        group_forward, [h4, coded, k_shape], n_own, got2, got2_core, sp_own, x1, got1, d
    )
    n_group, n_first, k_low = call(
        group_map, [sq, sq, k_shape], n_own, got2, got2_core, x1, got1, d, after=(s_group,)
    )

    t_in = jnp.zeros((four, half), f32)
    got4 = swap(x4, 3)
    for step in range(groups - 2):
        got = hop(out, step)
        t_in, out = call(
            functools.partial(forward_hop, step), [h4, coded], got, t_in, n_group, s_group,
        )
        if step == 0:
            pieces = [((half // 2 + SCALES, LANES), i16)] * 2
            low, high = call(relay_halves, pieces, got4, after=(out,))
            got4_low, got4_high = swap(low, 1), swap(high, 1)
    gg_group, g_group, gg_second, g_second = call(
        group_backward, [sq, h4, sq, h4],
        n_first, got2, sp_own, gg_own, got4, got4_low, got4_high, gp_own, after=(out,),
    )
    last = groups - 2
    got = hop(out, last)
    t_in, local, out = call(
        functools.partial(turn, last), [h4, h4, coded], got, t_in, gg_group, g_group
    )

    u_in = jnp.zeros((four, half), f32)
    for step in reversed(range(groups - 1)):
        got = hop(out, step)
        if step == last:
            x5, x5_rest, kept, rest_own = call(
                spread_forward, [coded, coded, h4, h4], t_in, n_first, got2, sp_own, gg_second, g_second,
                after=(local,),
            )
            got5, got5_rest = swap(x5, 3), swap(x5_rest, 3)
        if step:
            u_in, out = call(
                functools.partial(backward_hop, step), [h4, coded], got, u_in, n_group, local
            )
        else:
            start, maps = call(
                block_parts, [solved_shape, ((2 * half, typed), f32)], solved, p, d, after=(out,)
            )
            out = call(functools.partial(arrive, step), coded, got, u_in, after=(maps,))
    x6, own = call(
        pair_states, [x6_coded, x6_shape], kept, rest_own, got5, got5_rest, x1, got1, s_own, x3, got3, g_own
    )
    got6 = swap(x6, 1)
    fixed = call(block_fixed, solved_shape, own, got6, start, maps)
    theirs = swap(out, 1)
    got_u = swap(out, 3)
    their_got = swap(got_u, 1)
    edge = (square, bf16)
    xa, xb = call(block_weights, [edge, edge], out, got_u, theirs, their_got, fixed, k_low, k_high)
    got_a = swap_chips(xa)
    got_b = swap(xb, 1)
    acc = call(impute_own, ((traits, untyped), f32), xa, xb, masked)
    return call(
        impute_edges, ((traits, untyped), f32), acc, got_a, got_b, masked, last=True
    )


def solution(mesh):
    in_specs = (
        P(None, (SEGMENTS, AXIS)),
        P((SEGMENTS, AXIS), None, None),
        P((SEGMENTS, AXIS), None, None),
        P((SEGMENTS, AXIS), None),
        P((SEGMENTS, AXIS)),
    )
    return jax.shard_map(
        per_device, mesh=mesh, in_specs=in_specs, out_specs=P(None, (SEGMENTS, AXIS)), check_vma=False
    )
```

```python
import functools

import jax
import jax.numpy as jnp
from jax import lax
from jax.experimental import pallas as pl
from jax.experimental.pallas import tpu as pltpu
from jax.sharding import PartitionSpec as P

AXIS = "genome"
SEGMENTS = "seg"
GROUP = 4
f32 = jnp.float32
bf16 = jnp.bfloat16
i16 = jnp.int16
SCALES = 16
LANES = 128
LIMIT = 32767.0


def parts(x):
    high = x.astype(bf16)
    return high, (x - high.astype(f32)).astype(bf16)


def dot(a, b, ca=1, cb=0):
    ah, al = parts(a)
    bh, bl = parts(b)
    return lax.dot_general(
        jnp.concatenate([al, ah, ah], axis=ca),
        jnp.concatenate([bh, bl, bh], axis=cb),
        (((ca,), (cb,)), ((), ())),
        preferred_element_type=f32,
    )


def code(x):
    top = jnp.maximum(jnp.max(jnp.abs(x), axis=0, keepdims=True), 1e-32)
    power = jnp.ceil(jnp.log2(top) * 4.0)
    root = jnp.exp2(power * -0.125)
    steps = jnp.floor(x * root * (root * LIMIT) + 0.5)
    steps = jnp.clip(steps, -LIMIT, LIMIT)
    tiles = x.shape[1] // LANES
    powers = jnp.broadcast_to(power, (SCALES // tiles, x.shape[1]))
    pieces = [v[:, i * LANES : (i + 1) * LANES] for v in (steps, powers) for i in range(tiles)]
    return jnp.concatenate(pieces, axis=0).astype(jnp.int32).astype(i16)


def decode(coded, tiles=2):
    rows = (coded.shape[0] - SCALES) // tiles
    values = coded[...].astype(jnp.int32).astype(f32)
    columns = []
    for i in range(tiles):
        at = tiles * rows + i * (SCALES // tiles)
        root = jnp.exp2(values[at : at + 1] * 0.125)
        columns.append(values[i * rows : (i + 1) * rows] * (root / LIMIT) * root)
    return jnp.concatenate(columns, axis=1)


def coded_rows(rows, columns):
    return rows * (columns // LANES) + SCALES


def where_am_i():
    place = lax.axis_index(AXIS)
    return place % 2 == 0, (place // 2) % 2 == 0, place // GROUP


def low_traits():
    place = lax.axis_index(AXIS)
    return (place + place // 2 + place // GROUP) % 2 == 0


def ordered(first, own, other):
    return jnp.where(first, own, other), jnp.where(first, other, own)


def call(kernel, outs, *args, after=(), hbm=False, last=False, scratch=()):
    n_in, n_after = len(args), len(after)

    def body(*refs):
        kernel(*refs[:n_in], *refs[n_in + n_after :])

    single = not isinstance(outs, list)
    shapes = [outs] if single else outs
    vmem = pl.BlockSpec(memory_space=pltpu.VMEM)
    anywhere = pl.BlockSpec(memory_space=pl.ANY)
    if hbm:
        args = [pltpu.with_memory_space_constraint(a, pltpu.HBM) for a in args]
    got = pl.pallas_call(
        body,
        out_shape=[jax.ShapeDtypeStruct(s, t) if last else pltpu.VMEM(s, t) for s, t in shapes],
        in_specs=[anywhere if hbm else vmem] * n_in + [anywhere] * n_after,
        out_specs=[vmem] * len(shapes),
        scratch_shapes=scratch,
        compiler_params=pltpu.CompilerParams(vmem_limit_bytes=8 * 2**20),
        name=kernel.__name__ if hasattr(kernel, "__name__") else kernel.func.__name__,
    )(*args, *after)
    return got[0] if single else got


def tail_part(z_in, d_in, c_in, x1, s_own, z, d, c, sems):
    half = c.shape[1]
    rows = z.shape[0] // 2
    head = d.shape[0] - half
    pieces = [
        (d_in.at[pl.ds(head, half)], d.at[pl.ds(head, half)]),
        (c_in, c),
        (z_in, z),
        (d_in.at[pl.ds(0, head)], d.at[pl.ds(0, head)]),
    ]
    copies = [pltpu.make_async_copy(src, dst, sems.at[i]) for i, (src, dst) in enumerate(pieces)]
    for copy in copies[:3]:
        copy.start()
    copies[0].wait()
    copies[1].wait()
    copies[3].start()
    tail = d[head:]
    x1[:half] = -dot(tail, c[...])
    copies[2].wait()
    s = dot(z[...], tail, 1, 1)
    keep, send = ordered(low_traits(), s[:rows], s[rows:])
    x1[half:] = send
    s_own[...] = keep
    copies[3].wait()


def head_part(z, d, c, x1, s_own, x3, g_own, solved, p):
    half = c.shape[1]
    rows = z.shape[0] // 2
    head = d.shape[0] - half
    first, _, _ = where_am_i()
    p[:head] = dot(d[:head], c[...])
    p[head:] = -x1[:half]
    solved[:, :head] = dot(z[...], d[:head], 1, 1)
    low, high = ordered(low_traits(), s_own[...], x1[half:])
    solved[:rows, head:] = low
    solved[rows:, head:] = high
    g = dot(solved[...], p[...])
    keep, send = ordered(low_traits(), g[:rows], g[rows:])
    x3[:half] = dot(p[...], p[...], 0, 0)
    x3[half:] = send
    g_own[...] = keep


def pair_forward(x1, got1, s_own, x2, n_own, sp_own):
    half = x1.shape[1]
    first, first_pair, _ = where_am_i()
    m0, m1 = ordered(first, x1[:half], got1[:half])
    s0, s1 = ordered(first, s_own[...], got1[half:])
    n = dot(m1, m0)
    n_own[...] = n
    split = coded_rows(half // 2, half)
    x2[:split] = code(jnp.where(first, n[: half // 2], n[half // 2 :]))
    s = dot(s0, m1, 1, 1) + s1
    rows = s.shape[0] // 2
    keep, send = ordered(first_pair, s[:rows], s[rows:])
    x2[split:] = code(send)
    sp_own[...] = keep


def pair_backward(x1, got1, s_own, x3, got3, g_own, x4, gg_own, gp_own):
    half = x1.shape[1]
    first, first_pair, _ = where_am_i()
    m0, _ = ordered(first, x1[:half], got1[:half])
    s0, _ = ordered(first, s_own[...], got1[half:])
    gg0, gg1 = ordered(first, x3[:half], got3[:half])
    g0, g1 = ordered(first, g_own[...], got3[half:])
    both = dot(jnp.concatenate([gg1, g1 - dot(s0, gg1)], axis=0), m0)
    gg = dot(m0, both[:half], 0, 0) + gg0
    gg_own[...] = gg
    split = coded_rows(half // 2, half)
    x4[:split] = code(jnp.where(first, gg[: half // 2], gg[half // 2 :]))
    g = both[half:] + g0
    rows = g.shape[0] // 2
    keep, send = ordered(first_pair, g[:rows], g[rows:])
    x4[split:] = code(send)
    gp_own[...] = keep


def pair_matrices(own, got, got_core):
    first, first_pair, _ = where_am_i()
    other = jnp.concatenate(ordered(first, got_core, got), axis=0)
    return ordered(first_pair, own[...], other)


def pair_vectors(own, got):
    _, first_pair, _ = where_am_i()
    return ordered(first_pair, own[...], got)


def relay(got, out):
    out[...] = got[: out.shape[0]]


def relay_halves(got, low, high):
    rows = low.shape[0] - SCALES
    low[:rows] = got[:rows]
    high[:rows] = got[rows : 2 * rows]
    low[rows:] = got[2 * rows : 2 * rows + SCALES]
    high[rows:] = got[2 * rows : 2 * rows + SCALES]


def group_forward(n_own, got2, got2_core, sp_own, out):
    _, _, group = where_am_i()
    out[...] = jnp.zeros_like(out)

    @pl.when(group == 0)
    def _():
        split = coded_rows(n_own.shape[1] // 2, n_own.shape[1])
        _, n1 = pair_matrices(n_own, decode(got2[:split]), decode(got2_core))
        s0, s1 = pair_vectors(sp_own, decode(got2[split:]))
        out[...] = code(dot(s0, n1, 1, 1) + s1)


def group_map(n_own, got2, got2_core, sp_own, s_group, n_group, n_first, n_second):
    split = coded_rows(n_own.shape[1] // 2, n_own.shape[1])
    n0, n1 = pair_matrices(n_own, decode(got2[:split]), decode(got2_core))
    s0, s1 = pair_vectors(sp_own, decode(got2[split:]))
    s_group[...] = dot(s0, n1, 1, 1) + s1
    n_first[...] = n0
    n_second[...] = n1
    n_group[...] = dot(n1, n0)


def block_map(n_second, x1, got1, d, k):
    half = x1.shape[1]
    first, first_pair, _ = where_am_i()
    rows = lax.broadcasted_iota(jnp.int32, (half, half), 0)
    columns = lax.broadcasted_iota(jnp.int32, (half, half), 1)
    unit = (rows == columns).astype(f32)
    _, m1 = ordered(first, x1[:half], got1[:half])
    above = jnp.where(first_pair, n_second[...], unit)
    above = jnp.where(first, dot(above, m1), above)
    k[...] = dot(above, d[d.shape[0] - half :])


def group_backward(
    n_first, got2, sp_own, gg_own, got4, got4_low, got4_high, gp_own,
    gg_group, g_group, gg_second, g_second,
):
    half = n_first.shape[1]
    split = coded_rows(half // 2, half)
    n0 = n_first[...]
    s0, _ = pair_vectors(sp_own, decode(got2[split:]))
    rows = got4_low.shape[0] - SCALES
    got4_core = jnp.concatenate([got4_low[:rows], got4_high[...]], axis=0)
    gg0, gg1 = pair_matrices(gg_own, decode(got4[:split]), decode(got4_core))
    g0, g1 = pair_vectors(gp_own, decode(got4[split:]))
    gg_second[...] = gg1
    g_second[...] = g1
    both = dot(jnp.concatenate([gg1, g1 - dot(s0, gg1)], axis=0), n0)
    gg_group[...] = dot(n0, both[:half], 0, 0) + gg0
    g_group[...] = both[half:] + g0


def forward_hop(step, got, t_in, n_group, s_group, t_out, out):
    _, _, group = where_am_i()
    t = jnp.where(group == step + 1, decode(got), t_in[...])
    t_out[...] = t
    out[...] = code(dot(t, n_group[...], 1, 1) + s_group[...])


def turn(step, got, t_in, gg_group, g_group, t_out, out):
    _, _, group = where_am_i()
    t = jnp.where(group == step + 1, decode(got), t_in[...])
    t_out[...] = t
    out[...] = jnp.zeros_like(out)

    @pl.when(group == step + 1)
    def _():
        out[...] = code(g_group[...] - dot(t, gg_group[...]))


def backward_hop(step, got, u_in, n_group, local, u_out, out):
    _, _, group = where_am_i()
    u = jnp.where(group == step, decode(got), u_in[...])
    u_out[...] = u
    out[...] = code(dot(u, n_group[...]) + local[...])


def arrive(step, got, u_in, out):
    _, _, group = where_am_i()
    out[...] = code(jnp.where(group == step, decode(got), u_in[...]))


def spread_forward(
    t_in, n_first, got2, sp_own, gg_second, g_second, gg_group, g_group, x5, x5_rest, kept, rest_own, local
):
    half = n_first.shape[1]
    _, first_pair, _ = where_am_i()
    s0, _ = pair_vectors(sp_own, decode(got2[coded_rows(half // 2, half) :]))
    t_mid = dot(t_in[...], n_first[...], 1, 1) + s0
    rest = g_second[...] - dot(t_mid, gg_second[...])
    keep, send = ordered(first_pair, t_in[...], t_mid)
    x5[...] = code(send)
    x5_rest[...] = code(rest)
    kept[...] = keep
    rest_own[...] = rest
    local[...] = g_group[...] - dot(t_in[...], gg_group[...])


def pair_states(kept, rest_own, got5, got5_rest, x1, got1, s_own, x3, got3, g_own, x6, own):
    half = x1.shape[1]
    rows = s_own.shape[0]
    first, first_pair, _ = where_am_i()
    t = jnp.concatenate(ordered(first_pair, kept[...], decode(got5)), axis=0)
    rest = jnp.concatenate(ordered(first_pair, rest_own[...], decode(got5_rest)), axis=0)
    m0, m1 = ordered(first, x1[:half], got1[:half])
    s0, _ = ordered(first, s_own[...], got1[half:])
    _, gg1 = ordered(first, x3[:half], got3[:half])
    _, g1 = ordered(first, g_own[...], got3[half:])
    t_mid = dot(t, m0, 1, 1) + s0
    fixed = jnp.where(first_pair, rest, 0.0)
    fixed_mid = dot(fixed, m1) + g1 - dot(t_mid, gg1)
    split = coded_rows(rows, half)
    keep, send = ordered(first, t, t_mid)
    x6[:split] = code(send)
    own[:rows] = keep
    keep, send = ordered(first, fixed_mid, fixed)
    x6[split:] = code(send)
    own[rows:] = keep


def block_parts(solved, p, d, start, maps):
    half = p.shape[1]
    start[...] = dot(solved[...], d[...])
    maps[:half] = dot(p[...], d[...], 0, 0)
    maps[half:] = d[d.shape[0] - half :]


def block_fixed(own, got6, start, maps, fixed_weights):
    rows = own.shape[0] // 2
    split = coded_rows(rows, own.shape[1])
    low = low_traits()
    t = jnp.concatenate(ordered(low, own[:rows], decode(got6[:split])), axis=0)
    above = jnp.concatenate(ordered(low, own[rows:], decode(got6[split:])), axis=0)
    fixed_weights[...] = start[...] - dot(jnp.concatenate([t, above], axis=1), maps[...])


def block_weights(mine, got_u, theirs, their_got, fixed_weights, k, xa, xb):
    half = k.shape[0]
    first, first_pair, _ = where_am_i()
    near = jnp.concatenate(ordered(first_pair, decode(mine), decode(got_u)), axis=0)
    far = jnp.concatenate(ordered(first_pair, decode(theirs), decode(their_got)), axis=0)
    u = jnp.concatenate(ordered(low_traits(), near, far), axis=0)
    weights = (fixed_weights[...] - dot(u, k[...])).astype(bf16)
    a, b = ordered(first, weights[:, :half], weights[:, half:])
    xa[...] = a
    xb[...] = b


def contract(values, coefs):
    return lax.dot_general(values, coefs, (((1,), (1,)), ((), ())), preferred_element_type=f32)


def mask_coefs(coefs_in, anchor_in, masked, coefs, anchor, sems):
    untyped, span = coefs.shape
    half = span // 4
    typed = span - 2 * half
    tile = 128
    place = lax.axis_index(AXIS)
    total = lax.axis_size(AXIS) * typed
    copies = [pltpu.make_async_copy(anchor_in, anchor, sems.at[0])]
    for i in range(untyped // tile):
        rows = pl.ds(i * tile, tile)
        copies.append(pltpu.make_async_copy(coefs_in.at[rows], coefs.at[rows], sems.at[i + 1]))
    for copy in copies:
        copy.start()
    copies[0].wait()
    first_column = place * typed - half
    for i in range(untyped // tile):
        rows = pl.ds(i * tile, tile)
        nearest = jnp.broadcast_to(anchor[:, i * tile : (i + 1) * tile], (tile, tile)).T
        copies[i + 1].wait()
        for j in range(span // tile):
            lanes = pl.ds(j * tile, tile)
            columns = first_column + j * tile + lax.broadcasted_iota(jnp.int32, (tile, tile), 1)
            within = (jnp.abs(columns - nearest) <= half) & (columns >= 0) & (columns < total)
            masked[rows, lanes] = jnp.where(within, coefs[rows, lanes].astype(f32), 0.0).astype(bf16)


def impute_own(xa, xb, masked, out):
    first, _, _ = where_am_i()
    half = xa.shape[1]
    span = masked.shape[1]
    weights = jnp.concatenate(ordered(first, xa[...], xb[...]), axis=1)
    out[...] = contract(weights, masked[:, half : span - half])


def impute_edges(acc, got_a, got_b, masked, out):
    first, _, _ = where_am_i()
    half = got_a.shape[1]
    span = masked.shape[1]
    left, right = ordered(first, got_a[...], got_b[...])
    out[...] = acc[...] + contract(left, masked[:, :half]) + contract(right, masked[:, span - half :])


def swap(block, distance):
    n = lax.axis_size(AXIS)
    return lax.ppermute(block, AXIS, [(i, i ^ distance) for i in range(n)])


def hop(block, step):
    pairs = []
    for i in range(lax.axis_size(AXIS)):
        g = i // GROUP
        to = i + GROUP if g == step else i - GROUP if g == step + 1 else i
        pairs.append((i, to ^ 1))
    return lax.ppermute(block, AXIS, pairs)


def swap_chips(block):
    n, segments = lax.axis_size(AXIS), lax.axis_size(SEGMENTS)
    pairs = []
    for seg in range(segments):
        for i in range(n):
            to, to_seg = i + 1 if i % 2 else i - 1, seg
            if not 0 <= to < n:
                to, to_seg = (i, seg ^ 1) if segments % 2 == 0 else (to % n, seg)
            pairs.append((seg * n + i, to_seg * n + to))
    return lax.ppermute(block, (SEGMENTS, AXIS), pairs)


def per_device(z, diag_inverse, coupling, impute_coef, anchor):
    d = diag_inverse[0]
    c = coupling[0]
    typed = d.shape[0]
    half = c.shape[1]
    traits = z.shape[0]
    untyped, span = impute_coef.shape
    assert span == typed + 2 * half and typed == 2 * half
    assert lax.axis_size(AXIS) >= 3 * GROUP
    groups = lax.axis_size(AXIS) // GROUP
    two, four = traits // 2, traits // 4
    square = (half, half)
    sq, h2, h4 = (square, f32), ((two, half), f32), ((four, half), f32)
    x1_shape, x6_shape = ((half + two, half), f32), ((2 * two, half), f32)
    x6_coded = ((2 * coded_rows(two, half), LANES), i16)
    coded = ((coded_rows(four, half), LANES), i16)
    coded_half = ((coded_rows(half // 2, half), LANES), i16)
    mixed = ((coded_rows(half // 2, half) + coded_rows(four, half), LANES), i16)

    solved_shape, p_shape = ((traits, typed), f32), ((typed, half), f32)
    x1, s_own, z, d, c = call(
        tail_part, [x1_shape, h2, solved_shape, ((typed, typed), f32), p_shape], z, d, c,
        hbm=True, scratch=[pltpu.SemaphoreType.DMA((4,))],
    )
    got1 = swap(x1, 1)
    x3, g_own, solved, p = call(
        head_part, [x1_shape, h2, solved_shape, p_shape], z, d, c, x1, s_own
    )
    x2, n_own, sp_own = call(pair_forward, [mixed, sq, h4], x1, got1, s_own, after=(p,))
    got2 = swap(x2, 3)
    got3 = swap(x3, 1)
    masked = call(
        mask_coefs, ((untyped, span), bf16), impute_coef, anchor[None, :], after=(x2,), hbm=True,
        scratch=[
            pltpu.VMEM((untyped, span), bf16),
            pltpu.VMEM((1, untyped), jnp.int32),
            pltpu.SemaphoreType.DMA((untyped // 128 + 1,)),
        ],
    )
    x4, gg_own, gp_own = call(
        pair_backward, [mixed, sq, h4], x1, got1, s_own, x3, got3, g_own, after=(x2,)
    )
    got2_core = swap(call(relay, coded_half, got2, after=(x4, masked)), 1)
    out = call(group_forward, coded, n_own, got2, got2_core, sp_own)
    s_group, n_group, n_first, n_second = call(
        group_map, [h4, sq, sq, sq], n_own, got2, got2_core, sp_own, after=(out,)
    )
    k = call(block_map, ((half, typed), f32), n_second, x1, got1, d)
    t_in = jnp.zeros((four, half), f32)
    got4 = swap(x4, 3)
    for step in range(groups - 2):
        got = hop(out, step)
        t_in, out = call(
            functools.partial(forward_hop, step), [h4, coded], got, t_in, n_group, s_group,
            after=(k,) if step == 0 else (),
        )
        if step == 0:
            pieces = [((half // 2 + SCALES, LANES), i16)] * 2
            low, high = call(relay_halves, pieces, got4, after=(out,))
            got4_low, got4_high = swap(low, 1), swap(high, 1)
    gg_group, g_group, gg_second, g_second = call(
        group_backward, [sq, h4, sq, h4],
        n_first, got2, sp_own, gg_own, got4, got4_low, got4_high, gp_own, after=(out,),
    )
    last = groups - 2
    got = hop(out, last)
    t_in, out = call(
        functools.partial(turn, last), [h4, coded], got, t_in, gg_group, g_group
    )

    u_in = jnp.zeros((four, half), f32)
    for step in reversed(range(groups - 1)):
        got = hop(out, step)
        if step == last:
            x5, x5_rest, kept, rest_own, local = call(
                spread_forward, [coded, coded, h4, h4, h4],
                t_in, n_first, got2, sp_own, gg_second, g_second, gg_group, g_group, after=(out,),
            )
            got5, got5_rest = swap(x5, 3), swap(x5_rest, 3)
        if step:
            u_in, out = call(
                functools.partial(backward_hop, step), [h4, coded], got, u_in, n_group, local
            )
        else:
            start, maps = call(
                block_parts, [solved_shape, ((2 * half, typed), f32)], solved, p, d, after=(out,)
            )
            out = call(functools.partial(arrive, step), coded, got, u_in, after=(maps,))
    x6, own = call(
        pair_states, [x6_coded, x6_shape], kept, rest_own, got5, got5_rest, x1, got1, s_own, x3, got3, g_own
    )
    got6 = swap(x6, 1)
    fixed = call(block_fixed, solved_shape, own, got6, start, maps)
    theirs = swap(out, 1)
    got_u = swap(out, 3)
    their_got = swap(got_u, 1)
    edge = (square, bf16)
    xa, xb = call(block_weights, [edge, edge], out, got_u, theirs, their_got, fixed, k)
    got_a = swap_chips(xa)
    got_b = swap(xb, 1)
    acc = call(impute_own, ((traits, untyped), f32), xa, xb, masked)
    return call(
        impute_edges, ((traits, untyped), f32), acc, got_a, got_b, masked, last=True
    )


def solution(mesh):
    in_specs = (
        P(None, (SEGMENTS, AXIS)),
        P((SEGMENTS, AXIS), None, None),
        P((SEGMENTS, AXIS), None, None),
        P((SEGMENTS, AXIS), None),
        P((SEGMENTS, AXIS)),
    )
    return jax.shard_map(
        per_device, mesh=mesh, in_specs=in_specs, out_specs=P(None, (SEGMENTS, AXIS)), check_vma=False
    )
```

```python
import functools

import jax
import jax.numpy as jnp
from jax import lax
from jax.experimental import pallas as pl
from jax.experimental.pallas import tpu as pltpu
from jax.sharding import PartitionSpec as P

AXIS = "genome"
SEGMENTS = "seg"
GROUP = 4
f32 = jnp.float32
bf16 = jnp.bfloat16
i16 = jnp.int16
SCALES = 16
LANES = 128
LIMIT = 32767.0


def parts(x):
    high = x.astype(bf16)
    return high, (x - high.astype(f32)).astype(bf16)


def dot(a, b, ca=1, cb=0):
    ah, al = parts(a)
    bh, bl = parts(b)
    return lax.dot_general(
        jnp.concatenate([al, ah, ah], axis=ca),
        jnp.concatenate([bh, bl, bh], axis=cb),
        (((ca,), (cb,)), ((), ())),
        preferred_element_type=f32,
    )


def code(x):
    top = jnp.maximum(jnp.max(jnp.abs(x), axis=0, keepdims=True), 1e-32)
    power = jnp.ceil(jnp.log2(top) * 4.0)
    root = jnp.exp2(power * -0.125)
    steps = jnp.floor(x * root * (root * LIMIT) + 0.5)
    steps = jnp.clip(steps, -LIMIT, LIMIT)
    tiles = x.shape[1] // LANES
    powers = jnp.broadcast_to(power, (SCALES // tiles, x.shape[1]))
    pieces = [v[:, i * LANES : (i + 1) * LANES] for v in (steps, powers) for i in range(tiles)]
    return jnp.concatenate(pieces, axis=0).astype(jnp.int32).astype(i16)


def decode(coded, tiles=2):
    rows = (coded.shape[0] - SCALES) // tiles
    values = coded[...].astype(jnp.int32).astype(f32)
    columns = []
    for i in range(tiles):
        at = tiles * rows + i * (SCALES // tiles)
        root = jnp.exp2(values[at : at + 1] * 0.125)
        columns.append(values[i * rows : (i + 1) * rows] * (root / LIMIT) * root)
    return jnp.concatenate(columns, axis=1)


def coded_rows(rows, columns):
    return rows * (columns // LANES) + SCALES


def where_am_i():
    place = lax.axis_index(AXIS)
    return place % 2 == 0, (place // 2) % 2 == 0, place // GROUP


def low_traits():
    place = lax.axis_index(AXIS)
    return (place + place // 2 + place // GROUP) % 2 == 0


def ordered(first, own, other):
    return jnp.where(first, own, other), jnp.where(first, other, own)


def call(kernel, outs, *args, after=(), hbm=False, last=False, scratch=()):
    n_in, n_after = len(args), len(after)

    def body(*refs):
        kernel(*refs[:n_in], *refs[n_in + n_after :])

    single = not isinstance(outs, list)
    shapes = [outs] if single else outs
    vmem = pl.BlockSpec(memory_space=pltpu.VMEM)
    anywhere = pl.BlockSpec(memory_space=pl.ANY)
    if hbm:
        args = [pltpu.with_memory_space_constraint(a, pltpu.HBM) for a in args]
    got = pl.pallas_call(
        body,
        out_shape=[jax.ShapeDtypeStruct(s, t) if last else pltpu.VMEM(s, t) for s, t in shapes],
        in_specs=[anywhere if hbm else vmem] * n_in + [anywhere] * n_after,
        out_specs=[vmem] * len(shapes),
        scratch_shapes=scratch,
        compiler_params=pltpu.CompilerParams(vmem_limit_bytes=8 * 2**20),
        name=kernel.__name__ if hasattr(kernel, "__name__") else kernel.func.__name__,
    )(*args, *after)
    return got[0] if single else got


def tail_part(z_in, d_in, c_in, x1, s_own, z, d, c, sems):
    half = c.shape[1]
    rows = z.shape[0] // 2
    head = d.shape[0] - half
    pieces = [
        (d_in.at[pl.ds(head, half)], d.at[pl.ds(head, half)]),
        (c_in, c),
        (z_in, z),
        (d_in.at[pl.ds(0, head)], d.at[pl.ds(0, head)]),
    ]
    copies = [pltpu.make_async_copy(src, dst, sems.at[i]) for i, (src, dst) in enumerate(pieces)]
    for copy in copies[:3]:
        copy.start()
    copies[0].wait()
    copies[1].wait()
    copies[3].start()
    tail = d[head:]
    x1[:half] = -dot(tail, c[...])
    copies[2].wait()
    s = dot(z[...], tail, 1, 1)
    keep, send = ordered(low_traits(), s[:rows], s[rows:])
    x1[half:] = send
    s_own[...] = keep
    copies[3].wait()


def head_part(z, d, c, x1, s_own, x3, g_own, solved, p):
    half = c.shape[1]
    rows = z.shape[0] // 2
    head = d.shape[0] - half
    first, _, _ = where_am_i()
    p[:head] = dot(d[:head], c[...])
    p[head:] = -x1[:half]
    solved[:, :head] = dot(z[...], d[:head], 1, 1)
    low, high = ordered(low_traits(), s_own[...], x1[half:])
    solved[:rows, head:] = low
    solved[rows:, head:] = high
    g = dot(solved[...], p[...])
    keep, send = ordered(low_traits(), g[:rows], g[rows:])
    x3[:half] = dot(p[...], p[...], 0, 0)
    x3[half:] = send
    g_own[...] = keep


def pair_forward(x1, got1, s_own, x2, x2_n, n_own, s_pair):
    half = x1.shape[1]
    first, _, _ = where_am_i()
    m0, m1 = ordered(first, x1[:half], got1[:half])
    s0, s1 = ordered(first, s_own[...], got1[half:])
    n = dot(m1, m0)
    n_own[...] = n
    x2_n[...] = code(jnp.where(first, n[: half // 2], n[half // 2 :]))
    s = dot(s0, m1, 1, 1) + s1
    s_pair[...] = s
    x2[...] = code(s)


def pair_backward(x1, got1, s_own, x3, got3, g_own, x4_low, x4_high, x4_g, gg_own, gp_own):
    half = x1.shape[1]
    first, first_pair, _ = where_am_i()
    m0, _ = ordered(first, x1[:half], got1[:half])
    s0, _ = ordered(first, s_own[...], got1[half:])
    gg0, gg1 = ordered(first, x3[:half], got3[:half])
    g0, g1 = ordered(first, g_own[...], got3[half:])
    both = dot(jnp.concatenate([gg1, g1 - dot(s0, gg1)], axis=0), m0)
    gg = dot(m0, both[:half], 0, 0) + gg0
    gg_own[...] = gg
    rows = half // 2
    coded = code(jnp.where(first, gg[:rows], gg[rows:]))
    for i, ref in enumerate((x4_low, x4_high)):
        ref[:rows] = coded[i * rows : (i + 1) * rows]
        ref[rows:] = coded[2 * rows :]
    g = both[half:] + g0
    rows = g.shape[0] // 2
    keep, send = ordered(first_pair, g[:rows], g[rows:])
    x4_g[...] = code(send)
    gp_own[...] = keep


def pair_matrices(own, got, got_core):
    first, first_pair, _ = where_am_i()
    other = jnp.concatenate(ordered(first, got_core, got), axis=0)
    return ordered(first_pair, own[...], other)


def pair_vectors(own, got):
    _, first_pair, _ = where_am_i()
    return ordered(first_pair, own, got)


def relay(got, out):
    out[...] = got[: out.shape[0]]


def relay_tiles(got, low, high):
    rows = low.shape[0] - SCALES
    low[:rows] = got[:rows]
    high[:rows] = got[rows : 2 * rows]
    low[rows:] = got[2 * rows :]
    high[rows:] = got[2 * rows :]


def joined(low, high):
    rows = low.shape[0] - SCALES
    return jnp.concatenate([low[:rows], high[...]], axis=0)


def group_forward(n_own, got2, s_pair, out, out_across):
    _, first_pair, group = where_am_i()
    out[...] = jnp.zeros_like(out)
    out_across[...] = jnp.zeros_like(out_across)

    @pl.when(jnp.logical_and(group == 0, jnp.logical_not(first_pair)))
    def _():
        s = dot(decode(got2), n_own[...], 1, 1) + s_pair[...]
        rows = s.shape[0] // 2
        out[...] = code(s[rows:])
        out_across[...] = code(s[:rows])


def quarter_states(got2, s_pair):
    _, first_pair, _ = where_am_i()
    rows = s_pair.shape[0] // 2
    other = decode(got2)
    own_quarter, _ = ordered(first_pair, s_pair[:rows], s_pair[rows:])
    other_quarter, _ = ordered(first_pair, other[:rows], other[rows:])
    return pair_vectors(own_quarter, other_quarter)


def first_arrival(got, got_across, t_in):
    _, first_pair, group = where_am_i()
    t = jnp.where(first_pair, decode(got_across), decode(got))
    t_in[...] = jnp.where(group == 1, t, 0.0)


def first_hop(t_in, n_own, got2, got2_n, core_low, core_high, s_pair, out):
    n0, n1 = pair_matrices(n_own, decode(got2_n), decode(joined(core_low, core_high)))
    s0, s1 = quarter_states(got2, s_pair)
    out[...] = code(dot(dot(t_in[...], n0, 1, 1) + s0, n1, 1, 1) + s1)


def group_map(n_own, got2, got2_n, core_low, core_high, s_pair, s_group, n_group, n_first, n_second, s_first):
    n0, n1 = pair_matrices(n_own, decode(got2_n), decode(joined(core_low, core_high)))
    s0, s1 = quarter_states(got2, s_pair)
    s_first[...] = s0
    s_group[...] = dot(s0, n1, 1, 1) + s1
    n_first[...] = n0
    n_second[...] = n1
    n_group[...] = dot(n1, n0)


def block_map(n_second, x1, got1, d, k):
    half = x1.shape[1]
    first, first_pair, _ = where_am_i()
    rows = lax.broadcasted_iota(jnp.int32, (half, half), 0)
    columns = lax.broadcasted_iota(jnp.int32, (half, half), 1)
    unit = (rows == columns).astype(f32)
    _, m1 = ordered(first, x1[:half], got1[:half])
    above = jnp.where(first_pair, n_second[...], unit)
    above = jnp.where(first, dot(above, m1), above)
    k[...] = dot(above, d[d.shape[0] - half :])


def group_backward(
    n_first, s_first, gg_own, got4_low, got4_high, got4_g, core_low, core_high, gp_own,
    gg_group, g_group, gg_second, g_second,
):
    half = n_first.shape[1]
    n0 = n_first[...]
    gg0, gg1 = pair_matrices(
        gg_own, decode(joined(got4_low, got4_high)), decode(joined(core_low, core_high))
    )
    g0, g1 = pair_vectors(gp_own[...], decode(got4_g))
    gg_second[...] = gg1
    g_second[...] = g1
    both = dot(jnp.concatenate([gg1, g1 - dot(s_first[...], gg1)], axis=0), n0)
    gg_group[...] = dot(n0, both[:half], 0, 0) + gg0
    g_group[...] = both[half:] + g0


def forward_hop(step, got, t_in, n_group, s_group, t_out, out):
    _, _, group = where_am_i()
    t = jnp.where(group == step + 1, decode(got), t_in[...])
    t_out[...] = t
    out[...] = code(dot(t, n_group[...], 1, 1) + s_group[...])


def turn(step, got, t_in, gg_group, g_group, t_out, out):
    _, _, group = where_am_i()
    t = jnp.where(group == step + 1, decode(got), t_in[...])
    t_out[...] = t
    out[...] = jnp.zeros_like(out)

    @pl.when(group == step + 1)
    def _():
        out[...] = code(g_group[...] - dot(t, gg_group[...]))


def backward_hop(step, got, u_in, n_group, local, u_out, out):
    _, _, group = where_am_i()
    u = jnp.where(group == step, decode(got), u_in[...])
    u_out[...] = u
    out[...] = code(dot(u, n_group[...]) + local[...])


def arrive(step, got, u_in, out):
    _, _, group = where_am_i()
    out[...] = code(jnp.where(group == step, decode(got), u_in[...]))


def spread_forward(
    t_in, n_first, s_first, gg_second, g_second, gg_group, g_group, x5, x5_rest, kept, rest_own, local
):
    _, first_pair, _ = where_am_i()
    t_mid = dot(t_in[...], n_first[...], 1, 1) + s_first[...]
    rest = g_second[...] - dot(t_mid, gg_second[...])
    keep, send = ordered(first_pair, t_in[...], t_mid)
    x5[...] = code(send)
    x5_rest[...] = code(rest)
    kept[...] = keep
    rest_own[...] = rest
    local[...] = g_group[...] - dot(t_in[...], gg_group[...])


def pair_states(kept, rest_own, got5, got5_rest, x1, got1, s_own, x3, got3, g_own, x6, own):
    half = x1.shape[1]
    rows = s_own.shape[0]
    first, first_pair, _ = where_am_i()
    t = jnp.concatenate(ordered(first_pair, kept[...], decode(got5)), axis=0)
    rest = jnp.concatenate(ordered(first_pair, rest_own[...], decode(got5_rest)), axis=0)
    m0, m1 = ordered(first, x1[:half], got1[:half])
    s0, _ = ordered(first, s_own[...], got1[half:])
    _, gg1 = ordered(first, x3[:half], got3[:half])
    _, g1 = ordered(first, g_own[...], got3[half:])
    t_mid = dot(t, m0, 1, 1) + s0
    fixed = jnp.where(first_pair, rest, 0.0)
    fixed_mid = dot(fixed, m1) + g1 - dot(t_mid, gg1)
    split = coded_rows(rows, half)
    keep, send = ordered(first, t, t_mid)
    x6[:split] = code(send)
    own[:rows] = keep
    keep, send = ordered(first, fixed_mid, fixed)
    x6[split:] = code(send)
    own[rows:] = keep


def block_parts(solved, p, d, start, maps):
    half = p.shape[1]
    start[...] = dot(solved[...], d[...])
    maps[:half] = dot(p[...], d[...], 0, 0)
    maps[half:] = d[d.shape[0] - half :]


def block_fixed(own, got6, start, maps, fixed_weights):
    rows = own.shape[0] // 2
    split = coded_rows(rows, own.shape[1])
    low = low_traits()
    t = jnp.concatenate(ordered(low, own[:rows], decode(got6[:split])), axis=0)
    above = jnp.concatenate(ordered(low, own[rows:], decode(got6[split:])), axis=0)
    fixed_weights[...] = start[...] - dot(jnp.concatenate([t, above], axis=1), maps[...])


def block_weights(mine, got_u, theirs, their_got, fixed_weights, k, xa, xb):
    half = k.shape[0]
    first, first_pair, _ = where_am_i()
    near = jnp.concatenate(ordered(first_pair, decode(mine), decode(got_u)), axis=0)
    far = jnp.concatenate(ordered(first_pair, decode(theirs), decode(their_got)), axis=0)
    u = jnp.concatenate(ordered(low_traits(), near, far), axis=0)
    weights = (fixed_weights[...] - dot(u, k[...])).astype(bf16)
    a, b = ordered(first, weights[:, :half], weights[:, half:])
    xa[...] = a
    xb[...] = b


def contract(values, coefs):
    return lax.dot_general(values, coefs, (((1,), (1,)), ((), ())), preferred_element_type=f32)


def mask_coefs(coefs_in, anchor_in, masked, coefs, anchor, sems):
    untyped, span = coefs.shape
    half = span // 4
    typed = span - 2 * half
    tile = 128
    place = lax.axis_index(AXIS)
    total = lax.axis_size(AXIS) * typed
    copies = [pltpu.make_async_copy(anchor_in, anchor, sems.at[0])]
    for i in range(untyped // tile):
        rows = pl.ds(i * tile, tile)
        copies.append(pltpu.make_async_copy(coefs_in.at[rows], coefs.at[rows], sems.at[i + 1]))
    for copy in copies:
        copy.start()
    copies[0].wait()
    first_column = place * typed - half
    for i in range(untyped // tile):
        rows = pl.ds(i * tile, tile)
        nearest = jnp.broadcast_to(anchor[:, i * tile : (i + 1) * tile], (tile, tile)).T
        copies[i + 1].wait()
        for j in range(span // tile):
            lanes = pl.ds(j * tile, tile)
            columns = first_column + j * tile + lax.broadcasted_iota(jnp.int32, (tile, tile), 1)
            within = (jnp.abs(columns - nearest) <= half) & (columns >= 0) & (columns < total)
            masked[rows, lanes] = jnp.where(within, coefs[rows, lanes].astype(f32), 0.0).astype(bf16)


def impute_own(xa, xb, masked, out):
    first, _, _ = where_am_i()
    half = xa.shape[1]
    span = masked.shape[1]
    weights = jnp.concatenate(ordered(first, xa[...], xb[...]), axis=1)
    out[...] = contract(weights, masked[:, half : span - half])


def impute_edges(acc, got_a, got_b, masked, out):
    first, _, _ = where_am_i()
    half = got_a.shape[1]
    span = masked.shape[1]
    left, right = ordered(first, got_a[...], got_b[...])
    out[...] = acc[...] + contract(left, masked[:, :half]) + contract(right, masked[:, span - half :])


def swap(block, distance):
    n = lax.axis_size(AXIS)
    return lax.ppermute(block, AXIS, [(i, i ^ distance) for i in range(n)])


def hop(block, step, across=1):
    pairs = []
    for i in range(lax.axis_size(AXIS)):
        g = i // GROUP
        to = i + GROUP if g == step else i - GROUP if g == step + 1 else i
        pairs.append((i, to ^ (1 if to == i else across)))
    return lax.ppermute(block, AXIS, pairs)


def swap_chips(block):
    n, segments = lax.axis_size(AXIS), lax.axis_size(SEGMENTS)
    pairs = []
    for seg in range(segments):
        for i in range(n):
            to, to_seg = i + 1 if i % 2 else i - 1, seg
            if not 0 <= to < n:
                to, to_seg = (i, seg ^ 1) if segments % 2 == 0 else (to % n, seg)
            pairs.append((seg * n + i, to_seg * n + to))
    return lax.ppermute(block, (SEGMENTS, AXIS), pairs)


def per_device(z, diag_inverse, coupling, impute_coef, anchor):
    d = diag_inverse[0]
    c = coupling[0]
    typed = d.shape[0]
    half = c.shape[1]
    traits = z.shape[0]
    untyped, span = impute_coef.shape
    assert span == typed + 2 * half and typed == 2 * half
    assert lax.axis_size(AXIS) >= 3 * GROUP
    groups = lax.axis_size(AXIS) // GROUP
    two, four = traits // 2, traits // 4
    square = (half, half)
    sq, h2, h4 = (square, f32), ((two, half), f32), ((four, half), f32)
    x1_shape, x6_shape = ((half + two, half), f32), ((2 * two, half), f32)
    x6_coded = ((2 * coded_rows(two, half), LANES), i16)
    coded = ((coded_rows(four, half), LANES), i16)
    coded_half = ((coded_rows(half // 2, half), LANES), i16)
    tile = ((half // 2 + SCALES, LANES), i16)

    solved_shape, p_shape = ((traits, typed), f32), ((typed, half), f32)
    x1, s_own, z, d, c = call(
        tail_part, [x1_shape, h2, solved_shape, ((typed, typed), f32), p_shape], z, d, c,
        hbm=True, scratch=[pltpu.SemaphoreType.DMA((4,))],
    )
    got1 = swap(x1, 1)
    x3, g_own, solved, p = call(
        head_part, [x1_shape, h2, solved_shape, p_shape], z, d, c, x1, s_own
    )
    x2, x2_n, n_own, s_pair = call(
        pair_forward, [coded_half, coded_half, sq, h2], x1, got1, s_own, after=(p,)
    )
    got2 = swap(x2, 3)
    got2_n = swap(x2_n, 3)
    got3 = swap(x3, 1)
    masked = call(
        mask_coefs, ((untyped, span), bf16), impute_coef, anchor[None, :], after=(x2,), hbm=True,
        scratch=[
            pltpu.VMEM((untyped, span), bf16),
            pltpu.VMEM((1, untyped), jnp.int32),
            pltpu.SemaphoreType.DMA((untyped // 128 + 1,)),
        ],
    )
    x4_low, x4_high, x4_g, gg_own, gp_own = call(
        pair_backward, [tile, tile, coded, sq, h4], x1, got1, s_own, x3, got3, g_own, after=(x2,)
    )
    out, out_across = call(
        group_forward, [coded, coded], n_own, got2, s_pair, after=(masked, x4_low)
    )
    got, got_across = hop(out, 0), hop(out_across, 0, 2)
    n_low, n_high = call(relay_tiles, [tile, tile], got2_n, after=(out,))
    n_parts = (n_own, got2, got2_n, swap(n_low, 1), swap(n_high, 1), s_pair)
    got4_low, got4_high, got4_g = swap(x4_low, 3), swap(x4_high, 3), swap(x4_g, 3)
    t_in = call(first_arrival, h4, got, got_across)
    out = call(first_hop, coded, t_in, *n_parts)
    s_group, n_group, n_first, n_second, s_first = call(
        group_map, [h4, sq, sq, sq, h4], *n_parts, after=(out,)
    )
    core_low = swap(call(relay, tile, got4_low, after=(out,)), 1)
    core_high = swap(call(relay, tile, got4_high, after=(out,)), 1)
    for step in range(1, groups - 2):
        got = hop(out, step)
        t_in, out = call(
            functools.partial(forward_hop, step), [h4, coded], got, t_in, n_group, s_group
        )
    gg_group, g_group, gg_second, g_second = call(
        group_backward, [sq, h4, sq, h4],
        n_first, s_first, gg_own, got4_low, got4_high, got4_g, core_low, core_high, gp_own,
        after=(out,),
    )
    k = call(block_map, ((half, typed), f32), n_second, x1, got1, d, after=(gg_group,))
    last = groups - 2
    got = hop(out, last)
    t_in, out = call(
        functools.partial(turn, last), [h4, coded], got, t_in, gg_group, g_group, after=(k,)
    )

    u_in = jnp.zeros((four, half), f32)
    for step in reversed(range(groups - 1)):
        got = hop(out, step)
        if step == last:
            x5, x5_rest, kept, rest_own, local = call(
                spread_forward, [coded, coded, h4, h4, h4],
                t_in, n_first, s_first, gg_second, g_second, gg_group, g_group, after=(out,),
            )
            got5, got5_rest = swap(x5, 3), swap(x5_rest, 3)
        if step:
            u_in, out = call(
                functools.partial(backward_hop, step), [h4, coded], got, u_in, n_group, local
            )
        else:
            start, maps = call(
                block_parts, [solved_shape, ((2 * half, typed), f32)], solved, p, d, after=(out,)
            )
            out = call(functools.partial(arrive, step), coded, got, u_in, after=(maps,))
    x6, own = call(
        pair_states, [x6_coded, x6_shape], kept, rest_own, got5, got5_rest, x1, got1, s_own, x3, got3, g_own
    )
    got6 = swap(x6, 1)
    fixed = call(block_fixed, solved_shape, own, got6, start, maps)
    theirs = swap(out, 1)
    got_u = swap(out, 3)
    their_got = swap(got_u, 1)
    edge = (square, bf16)
    xa, xb = call(block_weights, [edge, edge], out, got_u, theirs, their_got, fixed, k)
    got_a = swap_chips(xa)
    got_b = swap(xb, 1)
    acc = call(impute_own, ((traits, untyped), f32), xa, xb, masked)
    return call(
        impute_edges, ((traits, untyped), f32), acc, got_a, got_b, masked, last=True
    )


def solution(mesh):
    in_specs = (
        P(None, (SEGMENTS, AXIS)),
        P((SEGMENTS, AXIS), None, None),
        P((SEGMENTS, AXIS), None, None),
        P((SEGMENTS, AXIS), None),
        P((SEGMENTS, AXIS)),
    )
    return jax.shard_map(
        per_device, mesh=mesh, in_specs=in_specs, out_specs=P(None, (SEGMENTS, AXIS)), check_vma=False
    )
```

```python
import functools

import jax
import jax.numpy as jnp
from jax import lax
from jax.experimental import pallas as pl
from jax.experimental.pallas import tpu as pltpu
from jax.sharding import PartitionSpec as P

AXIS = "genome"
SEGMENTS = "seg"
GROUP = 4
f32 = jnp.float32
bf16 = jnp.bfloat16
i16 = jnp.int16
SCALES = 16
LANES = 128
LIMIT = 32767.0


def parts(x):
    high = x.astype(bf16)
    return high, (x - high.astype(f32)).astype(bf16)


def dot(a, b, ca=1, cb=0):
    ah, al = parts(a)
    bh, bl = parts(b)
    return lax.dot_general(
        jnp.concatenate([al, ah, ah], axis=ca),
        jnp.concatenate([bh, bl, bh], axis=cb),
        (((ca,), (cb,)), ((), ())),
        preferred_element_type=f32,
    )


def code(x):
    top = jnp.maximum(jnp.max(jnp.abs(x), axis=0, keepdims=True), 1e-32)
    power = jnp.ceil(jnp.log2(top) * 4.0)
    root = jnp.exp2(power * -0.125)
    steps = jnp.floor(x * root * (root * LIMIT) + 0.5)
    steps = jnp.clip(steps, -LIMIT, LIMIT)
    tiles = x.shape[1] // LANES
    powers = jnp.broadcast_to(power, (SCALES // tiles, x.shape[1]))
    pieces = [v[:, i * LANES : (i + 1) * LANES] for v in (steps, powers) for i in range(tiles)]
    return jnp.concatenate(pieces, axis=0).astype(jnp.int32).astype(i16)


def decode(coded, tiles=2):
    rows = (coded.shape[0] - SCALES) // tiles
    values = coded[...].astype(jnp.int32).astype(f32)
    columns = []
    for i in range(tiles):
        at = tiles * rows + i * (SCALES // tiles)
        root = jnp.exp2(values[at : at + 1] * 0.125)
        columns.append(values[i * rows : (i + 1) * rows] * (root / LIMIT) * root)
    return jnp.concatenate(columns, axis=1)


def coded_rows(rows, columns):
    return rows * (columns // LANES) + SCALES


def code_rows(x, pieces):
    rows = x.shape[0] // len(pieces)
    for i, ref in enumerate(pieces):
        ref[...] = code(x[i * rows : (i + 1) * rows])


def where_am_i():
    place = lax.axis_index(AXIS)
    return place % 2 == 0, (place // 2) % 2 == 0, place // GROUP


def low_traits():
    place = lax.axis_index(AXIS)
    return (place + place // GROUP) % 2 == 0


def ordered(first, own, other):
    return jnp.where(first, own, other), jnp.where(first, other, own)


def call(kernel, outs, *args, after=(), hbm=False, last=False, scratch=()):
    n_in, n_after = len(args), len(after)

    def body(*refs):
        kernel(*refs[:n_in], *refs[n_in + n_after :])

    single = not isinstance(outs, list)
    shapes = [outs] if single else outs
    vmem = pl.BlockSpec(memory_space=pltpu.VMEM)
    anywhere = pl.BlockSpec(memory_space=pl.ANY)
    if hbm:
        args = [pltpu.with_memory_space_constraint(a, pltpu.HBM) for a in args]
    got = pl.pallas_call(
        body,
        out_shape=[jax.ShapeDtypeStruct(s, t) if last else pltpu.VMEM(s, t) for s, t in shapes],
        in_specs=[anywhere if hbm else vmem] * n_in + [anywhere] * n_after,
        out_specs=[vmem] * len(shapes),
        scratch_shapes=scratch,
        compiler_params=pltpu.CompilerParams(vmem_limit_bytes=8 * 2**20),
        name=kernel.__name__ if hasattr(kernel, "__name__") else kernel.func.__name__,
    )(*args, *after)
    return got[0] if single else got


def tail_part(z_in, d_in, c_in, x1, s_own, z, d, c, sems):
    half = c.shape[1]
    rows = z.shape[0] // 2
    head = d.shape[0] - half
    pieces = [
        (d_in.at[pl.ds(head, half)], d.at[pl.ds(head, half)]),
        (c_in, c),
        (z_in, z),
        (d_in.at[pl.ds(0, head)], d.at[pl.ds(0, head)]),
    ]
    copies = [pltpu.make_async_copy(src, dst, sems.at[i]) for i, (src, dst) in enumerate(pieces)]
    for copy in copies[:3]:
        copy.start()
    copies[0].wait()
    copies[1].wait()
    copies[3].start()
    tail = d[head:]
    x1[:half] = -dot(tail, c[...])
    copies[2].wait()
    s = dot(z[...], tail, 1, 1)
    keep, send = ordered(low_traits(), s[:rows], s[rows:])
    x1[half:] = send
    s_own[...] = keep
    copies[3].wait()


def head_part(z, d, c, x1, s_own, x3, g_own, solved, p):
    half = c.shape[1]
    rows = z.shape[0] // 2
    head = d.shape[0] - half
    first, _, _ = where_am_i()
    p[:head] = dot(d[:head], c[...])
    p[head:] = -x1[:half]
    solved[:, :head] = dot(z[...], d[:head], 1, 1)
    low, high = ordered(low_traits(), s_own[...], x1[half:])
    solved[:rows, head:] = low
    solved[rows:, head:] = high
    g = dot(solved[...], p[...])
    keep, send = ordered(low_traits(), g[:rows], g[rows:])
    x3[:half] = dot(p[...], p[...], 0, 0)
    x3[half:] = send
    g_own[...] = keep


def pair_forward(x1, got1, s_own, x2, n_own, sp_own):
    half = x1.shape[1]
    first, first_pair, _ = where_am_i()
    m0, m1 = ordered(first, x1[:half], got1[:half])
    s0, s1 = ordered(first, s_own[...], got1[half:])
    n = dot(m1, m0)
    n_own[...] = n
    split = coded_rows(half // 2, half)
    x2[:split] = code(jnp.where(first, n[: half // 2], n[half // 2 :]))
    s = dot(s0, m1, 1, 1) + s1
    rows = s.shape[0] // 2
    keep, send = ordered(first_pair, s[:rows], s[rows:])
    x2[split:] = code(send)
    sp_own[...] = keep


def code_back(x3, top, bottom, g):
    half = x3.shape[1]
    code_rows(x3[:half], (top, bottom))
    g[...] = code(x3[half:])


def core_back(x3, got_top, got_bottom):
    first, _, _ = where_am_i()
    got = jnp.concatenate([decode(got_top), decode(got_bottom)], axis=0)
    return ordered(first, x3[: x3.shape[1]], got)


def pair_backward(
    x1, got1, s_own, x3, got_top, got_bottom, got_g, g_own, x4, x4_g, gg_own, gp_own
):
    half = x1.shape[1]
    first, first_pair, _ = where_am_i()
    m0, _ = ordered(first, x1[:half], got1[:half])
    s0, _ = ordered(first, s_own[...], got1[half:])
    gg0, gg1 = core_back(x3, got_top, got_bottom)
    g0, g1 = ordered(first, g_own[...], decode(got_g))
    both = dot(jnp.concatenate([gg1, g1 - dot(s0, gg1)], axis=0), m0)
    gg = dot(m0, both[:half], 0, 0) + gg0
    gg_own[...] = gg
    x4[...] = code(jnp.where(first, gg[: half // 2], gg[half // 2 :]))
    g = both[half:] + g0
    rows = g.shape[0] // 2
    keep, send = ordered(first_pair, g[:rows], g[rows:])
    x4_g[...] = code(send)
    gp_own[...] = keep


def pair_matrices(own, got, got_core):
    first, first_pair, _ = where_am_i()
    other = jnp.concatenate(ordered(first, got, got_core), axis=0)
    return ordered(first_pair, own[...], other)


def pair_vectors(own, got):
    _, first_pair, _ = where_am_i()
    return ordered(first_pair, own[...], got)


def relay(got, out):
    out[...] = got[: out.shape[0]]


def relay_halves(got, low, high):
    rows = low.shape[0] - SCALES
    low[:rows] = got[:rows]
    high[:rows] = got[rows : 2 * rows]
    low[rows:] = got[2 * rows : 2 * rows + SCALES]
    high[rows:] = got[2 * rows : 2 * rows + SCALES]


def group_forward(n_own, got2, got2_core, sp_own, out):
    _, _, group = where_am_i()
    out[...] = jnp.zeros_like(out)

    @pl.when(group == 0)
    def _():
        split = coded_rows(n_own.shape[1] // 2, n_own.shape[1])
        _, n1 = pair_matrices(n_own, decode(got2[:split]), decode(got2_core))
        s0, s1 = pair_vectors(sp_own, decode(got2[split:]))
        out[...] = code(dot(s0, n1, 1, 1) + s1)


def group_map(n_own, got2, got2_core, sp_own, s_group, n_group, n_first, n_second):
    split = coded_rows(n_own.shape[1] // 2, n_own.shape[1])
    n0, n1 = pair_matrices(n_own, decode(got2[:split]), decode(got2_core))
    s0, s1 = pair_vectors(sp_own, decode(got2[split:]))
    s_group[...] = dot(s0, n1, 1, 1) + s1
    n_first[...] = n0
    n_second[...] = n1
    n_group[...] = dot(n1, n0)


def block_map(n_second, x1, got1, d, k):
    half = x1.shape[1]
    first, first_pair, _ = where_am_i()
    rows = lax.broadcasted_iota(jnp.int32, (half, half), 0)
    columns = lax.broadcasted_iota(jnp.int32, (half, half), 1)
    unit = (rows == columns).astype(f32)
    _, m1 = ordered(first, x1[:half], got1[:half])
    above = jnp.where(first_pair, n_second[...], unit)
    above = jnp.where(first, dot(above, m1), above)
    k[...] = dot(above, d[d.shape[0] - half :])


def group_backward(
    n_first, got2, sp_own, gg_own, got4, got4_g, got4_low, got4_high, gp_own,
    gg_group, g_group, gg_second, g_second,
):
    half = n_first.shape[1]
    split = coded_rows(half // 2, half)
    n0 = n_first[...]
    s0, _ = pair_vectors(sp_own, decode(got2[split:]))
    rows = got4_low.shape[0] - SCALES
    got4_core = jnp.concatenate([got4_low[:rows], got4_high[...]], axis=0)
    gg0, gg1 = pair_matrices(gg_own, decode(got4), decode(got4_core))
    g0, g1 = pair_vectors(gp_own, decode(got4_g))
    gg_second[...] = gg1
    g_second[...] = g1
    both = dot(jnp.concatenate([gg1, g1 - dot(s0, gg1)], axis=0), n0)
    gg_group[...] = dot(n0, both[:half], 0, 0) + gg0
    g_group[...] = both[half:] + g0


def forward_hop(step, got, t_in, n_group, s_group, t_out, out):
    _, _, group = where_am_i()
    t = jnp.where(group == step + 1, decode(got), t_in[...])
    t_out[...] = t
    out[...] = code(dot(t, n_group[...], 1, 1) + s_group[...])


def turn(step, got, t_in, gg_group, g_group, t_out, out):
    _, _, group = where_am_i()
    t = jnp.where(group == step + 1, decode(got), t_in[...])
    t_out[...] = t
    out[...] = jnp.zeros_like(out)

    @pl.when(group == step + 1)
    def _():
        out[...] = code(g_group[...] - dot(t, gg_group[...]))


def backward_hop(step, got, u_in, n_group, local, u_out, out):
    _, _, group = where_am_i()
    u = jnp.where(group == step, decode(got), u_in[...])
    u_out[...] = u
    out[...] = code(dot(u, n_group[...]) + local[...])


def arrive(step, got, u_in, out):
    _, _, group = where_am_i()
    out[...] = code(jnp.where(group == step, decode(got), u_in[...]))


def spread_forward(
    t_in, n_first, got2, sp_own, gg_second, g_second, gg_group, g_group, x5, x5_rest, kept, rest_own, local
):
    half = n_first.shape[1]
    _, first_pair, _ = where_am_i()
    s0, _ = pair_vectors(sp_own, decode(got2[coded_rows(half // 2, half) :]))
    t_mid = dot(t_in[...], n_first[...], 1, 1) + s0
    rest = g_second[...] - dot(t_mid, gg_second[...])
    keep, send = ordered(first_pair, t_in[...], t_mid)
    x5[...] = code(send)
    x5_rest[...] = code(rest)
    kept[...] = keep
    rest_own[...] = rest
    local[...] = g_group[...] - dot(t_in[...], gg_group[...])


def pair_states(
    kept, rest_own, got5, got5_rest, x1, got1, s_own, x3, got_top, got_bottom, got_g, g_own, x6, own
):
    half = x1.shape[1]
    rows = s_own.shape[0]
    first, first_pair, _ = where_am_i()
    t = jnp.concatenate(ordered(first_pair, kept[...], decode(got5)), axis=0)
    rest = jnp.concatenate(ordered(first_pair, rest_own[...], decode(got5_rest)), axis=0)
    m0, m1 = ordered(first, x1[:half], got1[:half])
    s0, _ = ordered(first, s_own[...], got1[half:])
    _, gg1 = core_back(x3, got_top, got_bottom)
    _, g1 = ordered(first, g_own[...], decode(got_g))
    t_mid = dot(t, m0, 1, 1) + s0
    fixed = jnp.where(first_pair, rest, 0.0)
    fixed_mid = dot(fixed, m1) + g1 - dot(t_mid, gg1)
    split = coded_rows(rows, half)
    keep, send = ordered(first, t, t_mid)
    x6[:split] = code(send)
    own[:rows] = keep
    keep, send = ordered(first, fixed_mid, fixed)
    x6[split:] = code(send)
    own[rows:] = keep


def block_parts(solved, p, d, start, maps):
    half = p.shape[1]
    start[...] = dot(solved[...], d[...])
    maps[:half] = dot(p[...], d[...], 0, 0)
    maps[half:] = d[d.shape[0] - half :]


def block_fixed(own, got6, start, maps, fixed_weights):
    rows = own.shape[0] // 2
    split = coded_rows(rows, own.shape[1])
    low = low_traits()
    t = jnp.concatenate(ordered(low, own[:rows], decode(got6[:split])), axis=0)
    above = jnp.concatenate(ordered(low, own[rows:], decode(got6[split:])), axis=0)
    fixed_weights[...] = start[...] - dot(jnp.concatenate([t, above], axis=1), maps[...])


def block_weights(mine, got_u, theirs, their_got, fixed_weights, k, xa, xb):
    half = k.shape[0]
    first, first_pair, _ = where_am_i()
    near = jnp.concatenate(ordered(first_pair, decode(mine), decode(got_u)), axis=0)
    far = jnp.concatenate(ordered(first_pair, decode(theirs), decode(their_got)), axis=0)
    u = jnp.concatenate(ordered(low_traits(), near, far), axis=0)
    weights = (fixed_weights[...] - dot(u, k[...])).astype(bf16)
    a, b = ordered(first, weights[:, :half], weights[:, half:])
    xa[...] = a
    xb[...] = b


def contract(values, coefs):
    return lax.dot_general(values, coefs, (((1,), (1,)), ((), ())), preferred_element_type=f32)


def mask_coefs(coefs_in, anchor_in, masked, coefs, anchor, sems):
    untyped, span = coefs.shape
    half = span // 4
    typed = span - 2 * half
    tile = 128
    place = lax.axis_index(AXIS)
    total = lax.axis_size(AXIS) * typed
    copies = [pltpu.make_async_copy(anchor_in, anchor, sems.at[0])]
    for i in range(untyped // tile):
        rows = pl.ds(i * tile, tile)
        copies.append(pltpu.make_async_copy(coefs_in.at[rows], coefs.at[rows], sems.at[i + 1]))
    for copy in copies:
        copy.start()
    copies[0].wait()
    first_column = place * typed - half
    for i in range(untyped // tile):
        rows = pl.ds(i * tile, tile)
        nearest = jnp.broadcast_to(anchor[:, i * tile : (i + 1) * tile], (tile, tile)).T
        copies[i + 1].wait()
        for j in range(span // tile):
            lanes = pl.ds(j * tile, tile)
            columns = first_column + j * tile + lax.broadcasted_iota(jnp.int32, (tile, tile), 1)
            within = (jnp.abs(columns - nearest) <= half) & (columns >= 0) & (columns < total)
            masked[rows, lanes] = jnp.where(within, coefs[rows, lanes].astype(f32), 0.0).astype(bf16)


def impute_own(xa, xb, masked, out):
    first, _, _ = where_am_i()
    half = xa.shape[1]
    span = masked.shape[1]
    weights = jnp.concatenate(ordered(first, xa[...], xb[...]), axis=1)
    out[...] = contract(weights, masked[:, half : span - half])


def impute_edges(acc, got_a, got_b, masked, out):
    first, _, _ = where_am_i()
    half = got_a.shape[1]
    span = masked.shape[1]
    left, right = ordered(first, got_a[...], got_b[...])
    out[...] = acc[...] + contract(left, masked[:, :half]) + contract(right, masked[:, span - half :])


def swap(block, distance):
    n = lax.axis_size(AXIS)
    return lax.ppermute(block, AXIS, [(i, i ^ distance) for i in range(n)])


def hop(block, step):
    pairs = []
    for i in range(lax.axis_size(AXIS)):
        g = i // GROUP
        to = i + GROUP if g == step else i - GROUP if g == step + 1 else i
        pairs.append((i, to ^ 1))
    return lax.ppermute(block, AXIS, pairs)


def swap_chips(block):
    n, segments = lax.axis_size(AXIS), lax.axis_size(SEGMENTS)
    pairs = []
    for seg in range(segments):
        for i in range(n):
            to, to_seg = i + 1 if i % 2 else i - 1, seg
            if not 0 <= to < n:
                to, to_seg = (i, seg ^ 1) if segments % 2 == 0 else (to % n, seg)
            pairs.append((seg * n + i, to_seg * n + to))
    return lax.ppermute(block, (SEGMENTS, AXIS), pairs)


def per_device(z, diag_inverse, coupling, impute_coef, anchor):
    d = diag_inverse[0]
    c = coupling[0]
    typed = d.shape[0]
    half = c.shape[1]
    traits = z.shape[0]
    untyped, span = impute_coef.shape
    assert span == typed + 2 * half and typed == 2 * half
    assert lax.axis_size(AXIS) >= 3 * GROUP
    groups = lax.axis_size(AXIS) // GROUP
    two, four = traits // 2, traits // 4
    square = (half, half)
    sq, h2, h4 = (square, f32), ((two, half), f32), ((four, half), f32)
    x1_shape, x6_shape = ((half + two, half), f32), ((2 * two, half), f32)
    x6_coded = ((2 * coded_rows(two, half), LANES), i16)
    coded = ((coded_rows(four, half), LANES), i16)
    coded_half = ((coded_rows(half // 2, half), LANES), i16)
    mixed = ((coded_rows(half // 2, half) + coded_rows(four, half), LANES), i16)

    solved_shape, p_shape = ((traits, typed), f32), ((typed, half), f32)
    x1, s_own, z, d, c = call(
        tail_part, [x1_shape, h2, solved_shape, ((typed, typed), f32), p_shape], z, d, c,
        hbm=True, scratch=[pltpu.SemaphoreType.DMA((4,))],
    )
    got1 = swap(x1, 1)
    x3, g_own, solved, p = call(
        head_part, [x1_shape, h2, solved_shape, p_shape], z, d, c, x1, s_own
    )
    x2, n_own, sp_own = call(pair_forward, [mixed, sq, h4], x1, got1, s_own, after=(p,))
    got2 = swap(x2, 2)
    got3 = [swap(v, 1) for v in call(code_back, [coded_half] * 3, x3, after=(x2,))]
    masked = call(
        mask_coefs, ((untyped, span), bf16), impute_coef, anchor[None, :], after=(x2,), hbm=True,
        scratch=[
            pltpu.VMEM((untyped, span), bf16),
            pltpu.VMEM((1, untyped), jnp.int32),
            pltpu.SemaphoreType.DMA((untyped // 128 + 1,)),
        ],
    )
    x4, x4_g, gg_own, gp_own = call(
        pair_backward, [coded_half, coded, sq, h4], x1, got1, s_own, x3, *got3, g_own, after=(x2,)
    )
    got2_core = swap(call(relay, coded_half, got2, after=(x4, masked)), 1)
    out = call(group_forward, coded, n_own, got2, got2_core, sp_own)
    s_group, n_group, n_first, n_second = call(
        group_map, [h4, sq, sq, sq], n_own, got2, got2_core, sp_own, after=(out,)
    )
    t_in = jnp.zeros((four, half), f32)
    got4, got4_g = swap(x4, 2), swap(x4_g, 2)
    for step in range(groups - 2):
        got = hop(out, step)
        t_in, out = call(
            functools.partial(forward_hop, step), [h4, coded], got, t_in, n_group, s_group,
        )
        if step == 0:
            pieces = [((half // 2 + SCALES, LANES), i16)] * 2
            low, high = call(relay_halves, pieces, got4, after=(out,))
            got4_low, got4_high = swap(low, 1), swap(high, 1)
    gg_group, g_group, gg_second, g_second = call(
        group_backward, [sq, h4, sq, h4],
        n_first, got2, sp_own, gg_own, got4, got4_g, got4_low, got4_high, gp_own, after=(out,),
    )
    k = call(block_map, ((half, typed), f32), n_second, x1, got1, d, after=(gg_group,))
    last = groups - 2
    got = hop(out, last)
    t_in, out = call(
        functools.partial(turn, last), [h4, coded], got, t_in, gg_group, g_group, after=(k,)
    )

    u_in = jnp.zeros((four, half), f32)
    for step in reversed(range(groups - 1)):
        got = hop(out, step)
        if step == last:
            x5, x5_rest, kept, rest_own, local = call(
                spread_forward, [coded, coded, h4, h4, h4],
                t_in, n_first, got2, sp_own, gg_second, g_second, gg_group, g_group, after=(out,),
            )
            got5, got5_rest = swap(x5, 2), swap(x5_rest, 2)
        if step:
            u_in, out = call(
                functools.partial(backward_hop, step), [h4, coded], got, u_in, n_group, local
            )
        else:
            start, maps = call(
                block_parts, [solved_shape, ((2 * half, typed), f32)], solved, p, d, after=(out,)
            )
            out = call(functools.partial(arrive, step), coded, got, u_in, after=(maps,))
    x6, own = call(
        pair_states, [x6_coded, x6_shape], kept, rest_own, got5, got5_rest, x1, got1, s_own, x3, *got3, g_own
    )
    got6 = swap(x6, 1)
    fixed = call(block_fixed, solved_shape, own, got6, start, maps)
    theirs = swap(out, 1)
    got_u = swap(out, 2)
    their_got = swap(got_u, 1)
    edge = (square, bf16)
    xa, xb = call(block_weights, [edge, edge], out, got_u, theirs, their_got, fixed, k)
    got_a = swap_chips(xa)
    got_b = swap(xb, 1)
    acc = call(impute_own, ((traits, untyped), f32), xa, xb, masked)
    return call(
        impute_edges, ((traits, untyped), f32), acc, got_a, got_b, masked, last=True
    )


def solution(mesh):
    in_specs = (
        P(None, (SEGMENTS, AXIS)),
        P((SEGMENTS, AXIS), None, None),
        P((SEGMENTS, AXIS), None, None),
        P((SEGMENTS, AXIS), None),
        P((SEGMENTS, AXIS)),
    )
    return jax.shard_map(
        per_device, mesh=mesh, in_specs=in_specs, out_specs=P(None, (SEGMENTS, AXIS)), check_vma=False
    )
```

```python
import functools

import jax
import jax.numpy as jnp
from jax import lax
from jax.experimental import pallas as pl
from jax.experimental.pallas import tpu as pltpu
from jax.sharding import PartitionSpec as P

AXIS = "genome"
SEGMENTS = "seg"
GROUP = 4
f32 = jnp.float32
bf16 = jnp.bfloat16
i16 = jnp.int16
SCALES = 16
LANES = 128
LIMIT = 32767.0


def parts(x):
    high = x.astype(bf16)
    return high, (x - high.astype(f32)).astype(bf16)


def dot(a, b, ca=1, cb=0):
    ah, al = parts(a)
    bh, bl = parts(b)
    return lax.dot_general(
        jnp.concatenate([al, ah, ah], axis=ca),
        jnp.concatenate([bh, bl, bh], axis=cb),
        (((ca,), (cb,)), ((), ())),
        preferred_element_type=f32,
    )


def code(x):
    top = jnp.maximum(jnp.max(jnp.abs(x), axis=0, keepdims=True), 1e-32)
    power = jnp.ceil(jnp.log2(top) * 4.0)
    root = jnp.exp2(power * -0.125)
    steps = jnp.floor(x * root * (root * LIMIT) + 0.5)
    steps = jnp.clip(steps, -LIMIT, LIMIT)
    tiles = x.shape[1] // LANES
    powers = jnp.broadcast_to(power, (SCALES // tiles, x.shape[1]))
    pieces = [v[:, i * LANES : (i + 1) * LANES] for v in (steps, powers) for i in range(tiles)]
    return jnp.concatenate(pieces, axis=0).astype(jnp.int32).astype(i16)


def decode(coded, tiles=2):
    rows = (coded.shape[0] - SCALES) // tiles
    values = coded[...].astype(jnp.int32).astype(f32)
    columns = []
    for i in range(tiles):
        at = tiles * rows + i * (SCALES // tiles)
        root = jnp.exp2(values[at : at + 1] * 0.125)
        columns.append(values[i * rows : (i + 1) * rows] * (root / LIMIT) * root)
    return jnp.concatenate(columns, axis=1)


def coded_rows(rows, columns):
    return rows * (columns // LANES) + SCALES


def where_am_i():
    place = lax.axis_index(AXIS)
    return place % 2 == 0, (place // 2) % 2 == 0, place // GROUP


def ready(b):
    bh, bl = parts(b)
    return jnp.concatenate([bh, bl, bh], axis=0)


def dot_ready(a, b):
    ah, al = parts(a)
    return jnp.dot(jnp.concatenate([al, ah, ah], axis=1), b[...], preferred_element_type=f32)


def low_traits():
    place = lax.axis_index(AXIS)
    return (place + place // 2 + place // GROUP) % 2 == 0


def ordered(first, own, other):
    return jnp.where(first, own, other), jnp.where(first, other, own)


def call(kernel, outs, *args, after=(), hbm=False, last=False, scratch=()):
    n_in, n_after = len(args), len(after)

    def body(*refs):
        kernel(*refs[:n_in], *refs[n_in + n_after :])

    single = not isinstance(outs, list)
    shapes = [outs] if single else outs
    vmem = pl.BlockSpec(memory_space=pltpu.VMEM)
    anywhere = pl.BlockSpec(memory_space=pl.ANY)
    if hbm:
        args = [pltpu.with_memory_space_constraint(a, pltpu.HBM) for a in args]
    got = pl.pallas_call(
        body,
        out_shape=[jax.ShapeDtypeStruct(s, t) if last else pltpu.VMEM(s, t) for s, t in shapes],
        in_specs=[anywhere if hbm else vmem] * n_in + [anywhere] * n_after,
        out_specs=[vmem] * len(shapes),
        scratch_shapes=scratch,
        compiler_params=pltpu.CompilerParams(vmem_limit_bytes=8 * 2**20),
        name=kernel.__name__ if hasattr(kernel, "__name__") else kernel.func.__name__,
    )(*args, *after)
    return got[0] if single else got


def tail_part(z_in, d_in, c_in, x1, s_own, z, d, c, sems):
    half = c.shape[1]
    rows = z.shape[0] // 2
    head = d.shape[0] - half
    pieces = [
        (d_in.at[pl.ds(head, half)], d.at[pl.ds(head, half)]),
        (c_in, c),
        (z_in, z),
        (d_in.at[pl.ds(0, head)], d.at[pl.ds(0, head)]),
    ]
    copies = [pltpu.make_async_copy(src, dst, sems.at[i]) for i, (src, dst) in enumerate(pieces)]
    for copy in copies[:3]:
        copy.start()
    copies[0].wait()
    copies[1].wait()
    copies[3].start()
    tail = d[head:]
    x1[:half] = -dot(tail, c[...])
    copies[2].wait()
    s = dot(z[...], tail, 1, 1)
    keep, send = ordered(low_traits(), s[:rows], s[rows:])
    x1[half:] = send
    s_own[...] = keep
    copies[3].wait()


def head_part(z, d, c, x1, s_own, x3, g_own, solved, p):
    half = c.shape[1]
    rows = z.shape[0] // 2
    head = d.shape[0] - half
    first, _, _ = where_am_i()
    p[:head] = dot(d[:head], c[...])
    p[head:] = -x1[:half]
    solved[:, :head] = dot(z[...], d[:head], 1, 1)
    low, high = ordered(low_traits(), s_own[...], x1[half:])
    solved[:rows, head:] = low
    solved[rows:, head:] = high
    g = dot(solved[...], p[...])
    keep, send = ordered(low_traits(), g[:rows], g[rows:])
    x3[:half] = dot(p[...], p[...], 0, 0)
    x3[half:] = send
    g_own[...] = keep


def pair_forward(x1, got1, s_own, x2, n_own, sp_own):
    half = x1.shape[1]
    first, first_pair, _ = where_am_i()
    m0, m1 = ordered(first, x1[:half], got1[:half])
    s0, s1 = ordered(first, s_own[...], got1[half:])
    n = dot(m1, m0)
    n_own[...] = n
    split = coded_rows(half // 2, half)
    x2[:split] = code(jnp.where(first, n[: half // 2], n[half // 2 :]))
    s = dot(s0, m1, 1, 1) + s1
    rows = s.shape[0] // 2
    keep, send = ordered(first_pair, s[:rows], s[rows:])
    x2[split:] = code(send)
    sp_own[...] = keep


def pair_backward(x1, got1, s_own, x3, got3, g_own, x4, gg_own, gp_own):
    half = x1.shape[1]
    first, first_pair, _ = where_am_i()
    m0, _ = ordered(first, x1[:half], got1[:half])
    s0, _ = ordered(first, s_own[...], got1[half:])
    gg0, gg1 = ordered(first, x3[:half], got3[:half])
    g0, g1 = ordered(first, g_own[...], got3[half:])
    both = dot(jnp.concatenate([gg1, g1 - dot(s0, gg1)], axis=0), m0)
    gg = dot(m0, both[:half], 0, 0) + gg0
    gg_own[...] = gg
    split = coded_rows(half, half)
    x4[:split] = code(gg)
    g = both[half:] + g0
    rows = g.shape[0] // 2
    keep, send = ordered(first_pair, g[:rows], g[rows:])
    x4[split:] = code(send)
    gp_own[...] = keep


def pair_matrices(own, got, got_core):
    first, first_pair, _ = where_am_i()
    other = jnp.concatenate(ordered(first, got_core, got), axis=0)
    return ordered(first_pair, own[...], other)


def pair_vectors(own, got):
    _, first_pair, _ = where_am_i()
    return ordered(first_pair, own[...], got)


def relay(got, out):
    out[...] = got[: out.shape[0]]


def group_forward(n_own, got2, got2_core, sp_own, out):
    _, _, group = where_am_i()
    out[...] = jnp.zeros_like(out)

    @pl.when(group == 0)
    def _():
        split = coded_rows(n_own.shape[1] // 2, n_own.shape[1])
        _, n1 = pair_matrices(n_own, decode(got2[:split]), decode(got2_core))
        s0, s1 = pair_vectors(sp_own, decode(got2[split:]))
        out[...] = code(dot(s0, n1, 1, 1) + s1)


def group_map(n_own, got2, got2_core, sp_own, s_group, up, down, n_first, n_second):
    split = coded_rows(n_own.shape[1] // 2, n_own.shape[1])
    n0, n1 = pair_matrices(n_own, decode(got2[:split]), decode(got2_core))
    s0, s1 = pair_vectors(sp_own, decode(got2[split:]))
    s_group[...] = dot(s0, n1, 1, 1) + s1
    n_first[...] = n0
    n_second[...] = n1
    n_group = dot(n1, n0)
    up[...] = ready(n_group.T)
    down[...] = ready(n_group)


def block_map(n_second, x1, got1, d, k):
    half = x1.shape[1]
    first, first_pair, _ = where_am_i()
    rows = lax.broadcasted_iota(jnp.int32, (half, half), 0)
    columns = lax.broadcasted_iota(jnp.int32, (half, half), 1)
    unit = (rows == columns).astype(f32)
    _, m1 = ordered(first, x1[:half], got1[:half])
    above = jnp.where(first_pair, n_second[...], unit)
    above = jnp.where(first, dot(above, m1), above)
    k[...] = dot(above, d[d.shape[0] - half :])


def group_backward(
    n_first, got2, sp_own, gg_own, got4, gp_own, gg_group, g_group, gg_second, g_second
):
    half = n_first.shape[1]
    split = coded_rows(half, half)
    _, first_pair, _ = where_am_i()
    n0 = n_first[...]
    s0, _ = pair_vectors(sp_own, decode(got2[coded_rows(half // 2, half) :]))
    gg0, gg1 = ordered(first_pair, gg_own[...], decode(got4[:split]))
    g0, g1 = pair_vectors(gp_own, decode(got4[split:]))
    gg_second[...] = gg1
    g_second[...] = g1
    both = dot(jnp.concatenate([gg1, g1 - dot(s0, gg1)], axis=0), n0)
    gg_group[...] = dot(n0, both[:half], 0, 0) + gg0
    g_group[...] = both[half:] + g0


def forward_hop(step, got, t_in, up, s_group, t_out, out):
    _, _, group = where_am_i()
    t = jnp.where(group == step + 1, decode(got), t_in[...])
    t_out[...] = t
    out[...] = code(dot_ready(t, up) + s_group[...])


def turn(step, got, t_in, gg_group, g_group, t_out, out):
    _, _, group = where_am_i()
    t = jnp.where(group == step + 1, decode(got), t_in[...])
    t_out[...] = t
    out[...] = jnp.zeros_like(out)

    @pl.when(group == step + 1)
    def _():
        out[...] = code(g_group[...] - dot(t, gg_group[...]))


def backward_hop(step, got, u_in, down, local, u_out, out):
    _, _, group = where_am_i()
    u = jnp.where(group == step, decode(got), u_in[...])
    u_out[...] = u
    out[...] = code(dot_ready(u, down) + local[...])


def arrive(step, got, u_in, out):
    _, _, group = where_am_i()
    out[...] = code(jnp.where(group == step, decode(got), u_in[...]))


def spread_forward(
    t_in, n_first, got2, sp_own, gg_second, g_second, gg_group, g_group, x5, x5_rest, kept, rest_own, local
):
    half = n_first.shape[1]
    _, first_pair, _ = where_am_i()
    s0, _ = pair_vectors(sp_own, decode(got2[coded_rows(half // 2, half) :]))
    t_mid = dot(t_in[...], n_first[...], 1, 1) + s0
    rest = g_second[...] - dot(t_mid, gg_second[...])
    keep, send = ordered(first_pair, t_in[...], t_mid)
    x5[...] = code(send)
    x5_rest[...] = code(rest)
    kept[...] = keep
    rest_own[...] = rest
    local[...] = g_group[...] - dot(t_in[...], gg_group[...])


def pair_states(kept, rest_own, got5, got5_rest, x1, got1, s_own, x3, got3, g_own, x6, own):
    half = x1.shape[1]
    rows = s_own.shape[0]
    first, first_pair, _ = where_am_i()
    t = jnp.concatenate(ordered(first_pair, kept[...], decode(got5)), axis=0)
    rest = jnp.concatenate(ordered(first_pair, rest_own[...], decode(got5_rest)), axis=0)
    m0, m1 = ordered(first, x1[:half], got1[:half])
    s0, _ = ordered(first, s_own[...], got1[half:])
    _, gg1 = ordered(first, x3[:half], got3[:half])
    _, g1 = ordered(first, g_own[...], got3[half:])
    t_mid = dot(t, m0, 1, 1) + s0
    fixed = jnp.where(first_pair, rest, 0.0)
    fixed_mid = dot(fixed, m1) + g1 - dot(t_mid, gg1)
    split = coded_rows(rows, half)
    keep, send = ordered(first, t, t_mid)
    x6[:split] = code(send)
    own[:rows] = keep
    keep, send = ordered(first, fixed_mid, fixed)
    x6[split:] = code(send)
    own[rows:] = keep


def block_parts(solved, p, d, start, maps):
    half = p.shape[1]
    start[...] = dot(solved[...], d[...])
    maps[:half] = dot(p[...], d[...], 0, 0)
    maps[half:] = d[d.shape[0] - half :]


def block_fixed(own, got6, start, maps, fixed_weights):
    rows = own.shape[0] // 2
    split = coded_rows(rows, own.shape[1])
    low = low_traits()
    t = jnp.concatenate(ordered(low, own[:rows], decode(got6[:split])), axis=0)
    above = jnp.concatenate(ordered(low, own[rows:], decode(got6[split:])), axis=0)
    fixed_weights[...] = start[...] - dot(jnp.concatenate([t, above], axis=1), maps[...])


def block_weights(mine, got_u, theirs, their_got, fixed_weights, k, xa, xb):
    half = k.shape[0]
    first, first_pair, _ = where_am_i()
    near = jnp.concatenate(ordered(first_pair, decode(mine), decode(got_u)), axis=0)
    far = jnp.concatenate(ordered(first_pair, decode(theirs), decode(their_got)), axis=0)
    u = jnp.concatenate(ordered(low_traits(), near, far), axis=0)
    weights = (fixed_weights[...] - dot(u, k[...])).astype(bf16)
    a, b = ordered(first, weights[:, :half], weights[:, half:])
    xa[...] = a
    xb[...] = b


def contract(values, coefs):
    return lax.dot_general(values, coefs, (((1,), (1,)), ((), ())), preferred_element_type=f32)


def mask_coefs(coefs_in, anchor_in, masked, coefs, anchor, sems):
    untyped, span = coefs.shape
    half = span // 4
    typed = span - 2 * half
    tile = 128
    place = lax.axis_index(AXIS)
    total = lax.axis_size(AXIS) * typed
    copies = [pltpu.make_async_copy(anchor_in, anchor, sems.at[0])]
    for i in range(untyped // tile):
        rows = pl.ds(i * tile, tile)
        copies.append(pltpu.make_async_copy(coefs_in.at[rows], coefs.at[rows], sems.at[i + 1]))
    for copy in copies:
        copy.start()
    copies[0].wait()
    first_column = place * typed - half
    for i in range(untyped // tile):
        rows = pl.ds(i * tile, tile)
        nearest = jnp.broadcast_to(anchor[:, i * tile : (i + 1) * tile], (tile, tile)).T
        copies[i + 1].wait()
        for j in range(span // tile):
            lanes = pl.ds(j * tile, tile)
            columns = first_column + j * tile + lax.broadcasted_iota(jnp.int32, (tile, tile), 1)
            within = (jnp.abs(columns - nearest) <= half) & (columns >= 0) & (columns < total)
            masked[rows, lanes] = jnp.where(within, coefs[rows, lanes].astype(f32), 0.0).astype(bf16)


def impute_own(xa, xb, masked, out):
    first, _, _ = where_am_i()
    half = xa.shape[1]
    span = masked.shape[1]
    weights = jnp.concatenate(ordered(first, xa[...], xb[...]), axis=1)
    out[...] = contract(weights, masked[:, half : span - half])


def impute_edges(acc, got_a, got_b, masked, out):
    first, _, _ = where_am_i()
    half = got_a.shape[1]
    span = masked.shape[1]
    left, right = ordered(first, got_a[...], got_b[...])
    out[...] = acc[...] + contract(left, masked[:, :half]) + contract(right, masked[:, span - half :])


def swap(block, distance):
    n = lax.axis_size(AXIS)
    return lax.ppermute(block, AXIS, [(i, i ^ distance) for i in range(n)])


def hop(block, step):
    pairs = []
    for i in range(lax.axis_size(AXIS)):
        g = i // GROUP
        to = i + GROUP if g == step else i - GROUP if g == step + 1 else i
        pairs.append((i, to ^ 1))
    return lax.ppermute(block, AXIS, pairs)


def swap_chips(block):
    n, segments = lax.axis_size(AXIS), lax.axis_size(SEGMENTS)
    pairs = []
    for seg in range(segments):
        for i in range(n):
            to, to_seg = i + 1 if i % 2 else i - 1, seg
            if not 0 <= to < n:
                to, to_seg = (i, seg ^ 1) if segments % 2 == 0 else (to % n, seg)
            pairs.append((seg * n + i, to_seg * n + to))
    return lax.ppermute(block, (SEGMENTS, AXIS), pairs)


def per_device(z, diag_inverse, coupling, impute_coef, anchor):
    d = diag_inverse[0]
    c = coupling[0]
    typed = d.shape[0]
    half = c.shape[1]
    traits = z.shape[0]
    untyped, span = impute_coef.shape
    assert span == typed + 2 * half and typed == 2 * half
    assert lax.axis_size(AXIS) >= 3 * GROUP
    groups = lax.axis_size(AXIS) // GROUP
    two, four = traits // 2, traits // 4
    square = (half, half)
    sq, h2, h4 = (square, f32), ((two, half), f32), ((four, half), f32)
    x1_shape, x6_shape = ((half + two, half), f32), ((2 * two, half), f32)
    x6_coded = ((2 * coded_rows(two, half), LANES), i16)
    coded = ((coded_rows(four, half), LANES), i16)
    coded_half = ((coded_rows(half // 2, half), LANES), i16)
    whole = ((coded_rows(half, half) + coded_rows(four, half), LANES), i16)
    mixed = ((coded_rows(half // 2, half) + coded_rows(four, half), LANES), i16)

    solved_shape, p_shape = ((traits, typed), f32), ((typed, half), f32)
    x1, s_own, z, d, c = call(
        tail_part, [x1_shape, h2, solved_shape, ((typed, typed), f32), p_shape], z, d, c,
        hbm=True, scratch=[pltpu.SemaphoreType.DMA((4,))],
    )
    got1 = swap(x1, 1)
    x3, g_own, solved, p = call(
        head_part, [x1_shape, h2, solved_shape, p_shape], z, d, c, x1, s_own
    )
    x2, n_own, sp_own = call(pair_forward, [mixed, sq, h4], x1, got1, s_own, after=(p,))
    got2 = swap(x2, 3)
    got3 = swap(x3, 1)
    masked = call(
        mask_coefs, ((untyped, span), bf16), impute_coef, anchor[None, :], after=(x2,), hbm=True,
        scratch=[
            pltpu.VMEM((untyped, span), bf16),
            pltpu.VMEM((1, untyped), jnp.int32),
            pltpu.SemaphoreType.DMA((untyped // 128 + 1,)),
        ],
    )
    x4, gg_own, gp_own = call(
        pair_backward, [whole, sq, h4], x1, got1, s_own, x3, got3, g_own, after=(x2,)
    )
    got2_core = swap(call(relay, coded_half, got2, after=(x4, masked)), 1)
    out = call(group_forward, coded, n_own, got2, got2_core, sp_own)
    parts3 = ((3 * half, half), bf16)
    s_group, up, down, n_first, n_second = call(
        group_map, [h4, parts3, parts3, sq, sq], n_own, got2, got2_core, sp_own, after=(out,)
    )
    k = call(block_map, ((half, typed), f32), n_second, x1, got1, d)
    t_in = jnp.zeros((four, half), f32)
    got4 = swap(x4, 3)
    for step in range(groups - 2):
        got = hop(out, step)
        t_in, out = call(
            functools.partial(forward_hop, step), [h4, coded], got, t_in, up, s_group,
            after=(k,) if step == 0 else (),
        )
    gg_group, g_group, gg_second, g_second = call(
        group_backward, [sq, h4, sq, h4],
        n_first, got2, sp_own, gg_own, got4, gp_own, after=(out,),
    )
    last = groups - 2
    got = hop(out, last)
    t_in, out = call(
        functools.partial(turn, last), [h4, coded], got, t_in, gg_group, g_group
    )

    u_in = jnp.zeros((four, half), f32)
    for step in reversed(range(groups - 1)):
        got = hop(out, step)
        if step == last:
            x5, x5_rest, kept, rest_own, local = call(
                spread_forward, [coded, coded, h4, h4, h4],
                t_in, n_first, got2, sp_own, gg_second, g_second, gg_group, g_group, after=(out,),
            )
            got5, got5_rest = swap(x5, 3), swap(x5_rest, 3)
        if step:
            u_in, out = call(
                functools.partial(backward_hop, step), [h4, coded], got, u_in, down, local
            )
        else:
            start, maps = call(
                block_parts, [solved_shape, ((2 * half, typed), f32)], solved, p, d, after=(out,)
            )
            out = call(functools.partial(arrive, step), coded, got, u_in, after=(maps,))
    x6, own = call(
        pair_states, [x6_coded, x6_shape], kept, rest_own, got5, got5_rest, x1, got1, s_own, x3, got3, g_own
    )
    got6 = swap(x6, 1)
    fixed = call(block_fixed, solved_shape, own, got6, start, maps)
    theirs = swap(out, 1)
    got_u = swap(out, 3)
    their_got = swap(out, 2)
    edge = (square, bf16)
    xa, xb = call(block_weights, [edge, edge], out, got_u, theirs, their_got, fixed, k)
    got_a = swap_chips(xa)
    got_b = swap(xb, 1)
    acc = call(impute_own, ((traits, untyped), f32), xa, xb, masked)
    return call(
        impute_edges, ((traits, untyped), f32), acc, got_a, got_b, masked, last=True
    )


def solution(mesh):
    in_specs = (
        P(None, (SEGMENTS, AXIS)),
        P((SEGMENTS, AXIS), None, None),
        P((SEGMENTS, AXIS), None, None),
        P((SEGMENTS, AXIS), None),
        P((SEGMENTS, AXIS)),
    )
    return jax.shard_map(
        per_device, mesh=mesh, in_specs=in_specs, out_specs=P(None, (SEGMENTS, AXIS)), check_vma=False
    )
```

```python
import functools

import jax
import jax.numpy as jnp
from jax import lax
from jax.experimental import pallas as pl
from jax.experimental.pallas import tpu as pltpu
from jax.sharding import PartitionSpec as P

AXIS = "genome"
SEGMENTS = "seg"
GROUP = 4
f32 = jnp.float32
bf16 = jnp.bfloat16
i16 = jnp.int16
SCALES = 16
LANES = 128
LIMIT = 32767.0


def parts(x):
    high = x.astype(bf16)
    return high, (x - high.astype(f32)).astype(bf16)


def dot(a, b, ca=1, cb=0):
    ah, al = parts(a)
    bh, bl = parts(b)
    return lax.dot_general(
        jnp.concatenate([al, ah, ah], axis=ca),
        jnp.concatenate([bh, bl, bh], axis=cb),
        (((ca,), (cb,)), ((), ())),
        preferred_element_type=f32,
    )


def code(x):
    top = jnp.maximum(jnp.max(jnp.abs(x), axis=0, keepdims=True), 1e-32)
    power = jnp.ceil(jnp.log2(top) * 4.0)
    root = jnp.exp2(power * -0.125)
    steps = jnp.floor(x * root * (root * LIMIT) + 0.5)
    steps = jnp.clip(steps, -LIMIT, LIMIT)
    tiles = x.shape[1] // LANES
    powers = jnp.broadcast_to(power, (SCALES // tiles, x.shape[1]))
    pieces = [v[:, i * LANES : (i + 1) * LANES] for v in (steps, powers) for i in range(tiles)]
    return jnp.concatenate(pieces, axis=0).astype(jnp.int32).astype(i16)


def decode(coded, tiles=2):
    rows = (coded.shape[0] - SCALES) // tiles
    values = coded[...].astype(jnp.int32).astype(f32)
    columns = []
    for i in range(tiles):
        at = tiles * rows + i * (SCALES // tiles)
        root = jnp.exp2(values[at : at + 1] * 0.125)
        columns.append(values[i * rows : (i + 1) * rows] * (root / LIMIT) * root)
    return jnp.concatenate(columns, axis=1)


def coded_rows(rows, columns):
    return rows * (columns // LANES) + SCALES


def where_am_i():
    place = lax.axis_index(AXIS)
    return place % 2 == 0, (place // 2) % 2 == 0, place // GROUP


def ready(b):
    bh, bl = parts(b)
    return jnp.concatenate([bh, bl, bh], axis=0)


def dot_ready(a, b):
    ah, al = parts(a)
    return jnp.dot(jnp.concatenate([al, ah, ah], axis=1), b[...], preferred_element_type=f32)


def low_traits():
    place = lax.axis_index(AXIS)
    return (place + place // 2 + place // GROUP) % 2 == 0


def ordered(first, own, other):
    return jnp.where(first, own, other), jnp.where(first, other, own)


def call(kernel, outs, *args, after=(), hbm=False, last=False, scratch=()):
    n_in, n_after = len(args), len(after)

    def body(*refs):
        kernel(*refs[:n_in], *refs[n_in + n_after :])

    single = not isinstance(outs, list)
    shapes = [outs] if single else outs
    vmem = pl.BlockSpec(memory_space=pltpu.VMEM)
    anywhere = pl.BlockSpec(memory_space=pl.ANY)
    if hbm:
        args = [pltpu.with_memory_space_constraint(a, pltpu.HBM) for a in args]
    got = pl.pallas_call(
        body,
        out_shape=[jax.ShapeDtypeStruct(s, t) if last else pltpu.VMEM(s, t) for s, t in shapes],
        in_specs=[anywhere if hbm else vmem] * n_in + [anywhere] * n_after,
        out_specs=[vmem] * len(shapes),
        scratch_shapes=scratch,
        compiler_params=pltpu.CompilerParams(vmem_limit_bytes=8 * 2**20),
        name=kernel.__name__ if hasattr(kernel, "__name__") else kernel.func.__name__,
    )(*args, *after)
    return got[0] if single else got


def tail_part(z_in, d_in, c_in, x1, s_own, z, d, c, sems):
    typed, half = c.shape
    rows = z.shape[0] // 2
    head = typed - half
    step = typed // 2
    copies = []
    for i in range(2):
        here = pl.ds(i * step, step)
        tail = (pl.ds(head, half), here)
        copies.append(pltpu.make_async_copy(d_in.at[tail], d.at[tail], sems.at[3 * i]))
        copies.append(pltpu.make_async_copy(c_in.at[here], c.at[here], sems.at[3 * i + 1]))
        copies.append(pltpu.make_async_copy(z_in.at[:, here], z.at[:, here], sems.at[3 * i + 2]))
    rest = pl.ds(0, head)
    copies.append(pltpu.make_async_copy(d_in.at[rest], d.at[rest], sems.at[6]))
    for copy in copies:
        copy.start()
    m = s = 0.0
    for i in range(2):
        here = pl.ds(i * step, step)
        for copy in copies[3 * i : 3 * i + 3]:
            copy.wait()
        tail = d[head:, here]
        m = m - dot(tail, c[here])
        s = s + dot(z[:, here], tail, 1, 1)
    x1[:half] = m
    keep, send = ordered(low_traits(), s[:rows], s[rows:])
    x1[half:] = send
    s_own[...] = keep
    copies[6].wait()


def head_part(z, d, c, x1, s_own, x3, g_own, solved, p):
    half = c.shape[1]
    rows = z.shape[0] // 2
    head = d.shape[0] - half
    first, _, _ = where_am_i()
    p[:head] = dot(d[:head], c[...])
    p[head:] = -x1[:half]
    solved[:, :head] = dot(z[...], d[:head], 1, 1)
    low, high = ordered(low_traits(), s_own[...], x1[half:])
    solved[:rows, head:] = low
    solved[rows:, head:] = high
    g = dot(solved[...], p[...])
    keep, send = ordered(low_traits(), g[:rows], g[rows:])
    x3[:half] = dot(p[...], p[...], 0, 0)
    x3[half:] = send
    g_own[...] = keep


def pair_forward(x1, got1, s_own, x2, n_own, sp_own):
    half = x1.shape[1]
    first, first_pair, _ = where_am_i()
    m0, m1 = ordered(first, x1[:half], got1[:half])
    s0, s1 = ordered(first, s_own[...], got1[half:])
    n = dot(m1, m0)
    n_own[...] = n
    split = coded_rows(half // 2, half)
    x2[:split] = code(jnp.where(first, n[: half // 2], n[half // 2 :]))
    s = dot(s0, m1, 1, 1) + s1
    rows = s.shape[0] // 2
    keep, send = ordered(first_pair, s[:rows], s[rows:])
    x2[split:] = code(send)
    sp_own[...] = keep


def pair_backward(x1, got1, s_own, x3, got3, g_own, x4, gg_own, gp_own):
    half = x1.shape[1]
    first, first_pair, _ = where_am_i()
    m0, _ = ordered(first, x1[:half], got1[:half])
    s0, _ = ordered(first, s_own[...], got1[half:])
    gg0, gg1 = ordered(first, x3[:half], got3[:half])
    g0, g1 = ordered(first, g_own[...], got3[half:])
    both = dot(jnp.concatenate([gg1, g1 - dot(s0, gg1)], axis=0), m0)
    gg = dot(m0, both[:half], 0, 0) + gg0
    gg_own[...] = gg
    split = coded_rows(half // 2, half)
    x4[:split] = code(jnp.where(first, gg[: half // 2], gg[half // 2 :]))
    g = both[half:] + g0
    rows = g.shape[0] // 2
    keep, send = ordered(first_pair, g[:rows], g[rows:])
    x4[split:] = code(send)
    gp_own[...] = keep


def pair_matrices(own, got, got_core):
    first, first_pair, _ = where_am_i()
    other = jnp.concatenate(ordered(first, got_core, got), axis=0)
    return ordered(first_pair, own[...], other)


def pair_vectors(own, got):
    _, first_pair, _ = where_am_i()
    return ordered(first_pair, own[...], got)


def relay(got, out):
    out[...] = got[: out.shape[0]]


def relay_halves(got, low, high):
    rows = low.shape[0] - SCALES
    low[:rows] = got[:rows]
    high[:rows] = got[rows : 2 * rows]
    low[rows:] = got[2 * rows : 2 * rows + SCALES]
    high[rows:] = got[2 * rows : 2 * rows + SCALES]


def group_forward(n_own, got2, got2_core, sp_own, out):
    _, _, group = where_am_i()
    out[...] = jnp.zeros_like(out)

    @pl.when(group == 0)
    def _():
        split = coded_rows(n_own.shape[1] // 2, n_own.shape[1])
        _, n1 = pair_matrices(n_own, decode(got2[:split]), decode(got2_core))
        s0, s1 = pair_vectors(sp_own, decode(got2[split:]))
        out[...] = code(dot(s0, n1, 1, 1) + s1)


def group_map(n_own, got2, got2_core, sp_own, s_group, up, down, n_first, n_second):
    split = coded_rows(n_own.shape[1] // 2, n_own.shape[1])
    n0, n1 = pair_matrices(n_own, decode(got2[:split]), decode(got2_core))
    s0, s1 = pair_vectors(sp_own, decode(got2[split:]))
    s_group[...] = dot(s0, n1, 1, 1) + s1
    n_first[...] = n0
    n_second[...] = n1
    n_group = dot(n1, n0)
    up[...] = ready(n_group.T)
    down[...] = ready(n_group)


def block_map(n_second, x1, got1, d, k):
    half = x1.shape[1]
    first, first_pair, _ = where_am_i()
    rows = lax.broadcasted_iota(jnp.int32, (half, half), 0)
    columns = lax.broadcasted_iota(jnp.int32, (half, half), 1)
    unit = (rows == columns).astype(f32)
    _, m1 = ordered(first, x1[:half], got1[:half])
    above = jnp.where(first_pair, n_second[...], unit)
    above = jnp.where(first, dot(above, m1), above)
    k[...] = dot(above, d[d.shape[0] - half :])


def group_backward(
    n_first, got2, sp_own, gg_own, got4, got4_low, got4_high, gp_own,
    gg_group, g_group, gg_second, g_second,
):
    half = n_first.shape[1]
    split = coded_rows(half // 2, half)
    n0 = n_first[...]
    s0, _ = pair_vectors(sp_own, decode(got2[split:]))
    rows = got4_low.shape[0] - SCALES
    got4_core = jnp.concatenate([got4_low[:rows], got4_high[...]], axis=0)
    gg0, gg1 = pair_matrices(gg_own, decode(got4[:split]), decode(got4_core))
    g0, g1 = pair_vectors(gp_own, decode(got4[split:]))
    gg_second[...] = gg1
    g_second[...] = g1
    both = dot(jnp.concatenate([gg1, g1 - dot(s0, gg1)], axis=0), n0)
    gg_group[...] = dot(n0, both[:half], 0, 0) + gg0
    g_group[...] = both[half:] + g0


def forward_hop(step, got, t_in, up, s_group, t_out, out):
    _, _, group = where_am_i()
    t = jnp.where(group == step + 1, decode(got), t_in[...])
    t_out[...] = t
    out[...] = code(dot_ready(t, up) + s_group[...])


def turn(step, got, t_in, gg_group, g_group, t_out, out):
    _, _, group = where_am_i()
    t = jnp.where(group == step + 1, decode(got), t_in[...])
    t_out[...] = t
    out[...] = jnp.zeros_like(out)

    @pl.when(group == step + 1)
    def _():
        out[...] = code(g_group[...] - dot(t, gg_group[...]))


def backward_hop(step, got, u_in, down, local, u_out, out):
    _, _, group = where_am_i()
    u = jnp.where(group == step, decode(got), u_in[...])
    u_out[...] = u
    out[...] = code(dot_ready(u, down) + local[...])


def arrive(step, got, u_in, out):
    _, _, group = where_am_i()
    out[...] = code(jnp.where(group == step, decode(got), u_in[...]))


def spread_forward(
    t_in, n_first, got2, sp_own, gg_second, g_second, gg_group, g_group, x5, x5_rest, kept, rest_own, local
):
    half = n_first.shape[1]
    _, first_pair, _ = where_am_i()
    s0, _ = pair_vectors(sp_own, decode(got2[coded_rows(half // 2, half) :]))
    t_mid = dot(t_in[...], n_first[...], 1, 1) + s0
    rest = g_second[...] - dot(t_mid, gg_second[...])
    keep, send = ordered(first_pair, t_in[...], t_mid)
    x5[...] = code(send)
    x5_rest[...] = code(rest)
    kept[...] = keep
    rest_own[...] = rest
    local[...] = g_group[...] - dot(t_in[...], gg_group[...])


def pair_states(kept, rest_own, got5, got5_rest, x1, got1, s_own, x3, got3, g_own, x6, own):
    half = x1.shape[1]
    rows = s_own.shape[0]
    first, first_pair, _ = where_am_i()
    t = jnp.concatenate(ordered(first_pair, kept[...], decode(got5)), axis=0)
    rest = jnp.concatenate(ordered(first_pair, rest_own[...], decode(got5_rest)), axis=0)
    m0, m1 = ordered(first, x1[:half], got1[:half])
    s0, _ = ordered(first, s_own[...], got1[half:])
    _, gg1 = ordered(first, x3[:half], got3[:half])
    _, g1 = ordered(first, g_own[...], got3[half:])
    t_mid = dot(t, m0, 1, 1) + s0
    fixed = jnp.where(first_pair, rest, 0.0)
    fixed_mid = dot(fixed, m1) + g1 - dot(t_mid, gg1)
    split = coded_rows(rows, half)
    keep, send = ordered(first, t, t_mid)
    x6[:split] = code(send)
    own[:rows] = keep
    keep, send = ordered(first, fixed_mid, fixed)
    x6[split:] = code(send)
    own[rows:] = keep


def block_parts(solved, p, d, start, maps):
    half = p.shape[1]
    start[...] = dot(solved[...], d[...])
    maps[:half] = dot(p[...], d[...], 0, 0)
    maps[half:] = d[d.shape[0] - half :]


def block_fixed(own, got6, start, maps, fixed_weights):
    rows = own.shape[0] // 2
    split = coded_rows(rows, own.shape[1])
    low = low_traits()
    t = jnp.concatenate(ordered(low, own[:rows], decode(got6[:split])), axis=0)
    above = jnp.concatenate(ordered(low, own[rows:], decode(got6[split:])), axis=0)
    fixed_weights[...] = start[...] - dot(jnp.concatenate([t, above], axis=1), maps[...])


def block_weights(mine, got_u, theirs, their_got, fixed_weights, k, xa, xb):
    half = k.shape[0]
    first, first_pair, _ = where_am_i()
    near = jnp.concatenate(ordered(first_pair, decode(mine), decode(got_u)), axis=0)
    far = jnp.concatenate(ordered(first_pair, decode(theirs), decode(their_got)), axis=0)
    u = jnp.concatenate(ordered(low_traits(), near, far), axis=0)
    weights = (fixed_weights[...] - dot(u, k[...])).astype(bf16)
    a, b = ordered(first, weights[:, :half], weights[:, half:])
    xa[...] = a
    xb[...] = b


def contract(values, coefs):
    return lax.dot_general(values, coefs, (((1,), (1,)), ((), ())), preferred_element_type=f32)


def mask_coefs(coefs_in, anchor_in, masked, coefs, anchor, sems):
    untyped, span = coefs.shape
    half = span // 4
    typed = span - 2 * half
    tile = 128
    place = lax.axis_index(AXIS)
    total = lax.axis_size(AXIS) * typed
    copies = [pltpu.make_async_copy(anchor_in, anchor, sems.at[0])]
    for i in range(untyped // tile):
        rows = pl.ds(i * tile, tile)
        copies.append(pltpu.make_async_copy(coefs_in.at[rows], coefs.at[rows], sems.at[i + 1]))
    for copy in copies:
        copy.start()
    copies[0].wait()
    first_column = place * typed - half
    for i in range(untyped // tile):
        rows = pl.ds(i * tile, tile)
        nearest = jnp.broadcast_to(anchor[:, i * tile : (i + 1) * tile], (tile, tile)).T
        copies[i + 1].wait()
        for j in range(span // tile):
            lanes = pl.ds(j * tile, tile)
            columns = first_column + j * tile + lax.broadcasted_iota(jnp.int32, (tile, tile), 1)
            within = (jnp.abs(columns - nearest) <= half) & (columns >= 0) & (columns < total)
            masked[rows, lanes] = jnp.where(within, coefs[rows, lanes].astype(f32), 0.0).astype(bf16)


def impute_own(xa, xb, masked, out):
    first, _, _ = where_am_i()
    half = xa.shape[1]
    span = masked.shape[1]
    weights = jnp.concatenate(ordered(first, xa[...], xb[...]), axis=1)
    out[...] = contract(weights, masked[:, half : span - half])


def impute_edges(acc, got_a, got_b, masked, out):
    first, _, _ = where_am_i()
    half = got_a.shape[1]
    span = masked.shape[1]
    left, right = ordered(first, got_a[...], got_b[...])
    out[...] = acc[...] + contract(left, masked[:, :half]) + contract(right, masked[:, span - half :])


def swap(block, distance):
    n = lax.axis_size(AXIS)
    return lax.ppermute(block, AXIS, [(i, i ^ distance) for i in range(n)])


def hop(block, step):
    pairs = []
    for i in range(lax.axis_size(AXIS)):
        g = i // GROUP
        to = i + GROUP if g == step else i - GROUP if g == step + 1 else i
        pairs.append((i, to ^ 1))
    return lax.ppermute(block, AXIS, pairs)


def swap_chips(block):
    n, segments = lax.axis_size(AXIS), lax.axis_size(SEGMENTS)
    pairs = []
    for seg in range(segments):
        for i in range(n):
            to, to_seg = i + 1 if i % 2 else i - 1, seg
            if not 0 <= to < n:
                to, to_seg = (i, seg ^ 1) if segments % 2 == 0 else (to % n, seg)
            pairs.append((seg * n + i, to_seg * n + to))
    return lax.ppermute(block, (SEGMENTS, AXIS), pairs)


def per_device(z, diag_inverse, coupling, impute_coef, anchor):
    d = diag_inverse[0]
    c = coupling[0]
    typed = d.shape[0]
    half = c.shape[1]
    traits = z.shape[0]
    untyped, span = impute_coef.shape
    assert span == typed + 2 * half and typed == 2 * half
    assert lax.axis_size(AXIS) >= 3 * GROUP
    groups = lax.axis_size(AXIS) // GROUP
    two, four = traits // 2, traits // 4
    square = (half, half)
    sq, h2, h4 = (square, f32), ((two, half), f32), ((four, half), f32)
    x1_shape, x6_shape = ((half + two, half), f32), ((2 * two, half), f32)
    x6_coded = ((2 * coded_rows(two, half), LANES), i16)
    coded = ((coded_rows(four, half), LANES), i16)
    coded_half = ((coded_rows(half // 2, half), LANES), i16)
    mixed = ((coded_rows(half // 2, half) + coded_rows(four, half), LANES), i16)

    solved_shape, p_shape = ((traits, typed), f32), ((typed, half), f32)
    x1, s_own, z, d, c = call(
        tail_part, [x1_shape, h2, solved_shape, ((typed, typed), f32), p_shape], z, d, c,
        hbm=True, scratch=[pltpu.SemaphoreType.DMA((7,))],
    )
    got1 = swap(x1, 1)
    x3, g_own, solved, p = call(
        head_part, [x1_shape, h2, solved_shape, p_shape], z, d, c, x1, s_own
    )
    x2, n_own, sp_own = call(pair_forward, [mixed, sq, h4], x1, got1, s_own, after=(p,))
    got2 = swap(x2, 3)
    got3 = swap(x3, 1)
    masked = call(
        mask_coefs, ((untyped, span), bf16), impute_coef, anchor[None, :], after=(x2,), hbm=True,
        scratch=[
            pltpu.VMEM((untyped, span), bf16),
            pltpu.VMEM((1, untyped), jnp.int32),
            pltpu.SemaphoreType.DMA((untyped // 128 + 1,)),
        ],
    )
    x4, gg_own, gp_own = call(
        pair_backward, [mixed, sq, h4], x1, got1, s_own, x3, got3, g_own, after=(x2,)
    )
    got2_core = swap(call(relay, coded_half, got2, after=(x4, masked)), 1)
    out = call(group_forward, coded, n_own, got2, got2_core, sp_own)
    parts3 = ((3 * half, half), bf16)
    s_group, up, down, n_first, n_second = call(
        group_map, [h4, parts3, parts3, sq, sq], n_own, got2, got2_core, sp_own, after=(out,)
    )
    k = call(block_map, ((half, typed), f32), n_second, x1, got1, d)
    t_in = jnp.zeros((four, half), f32)
    got4 = swap(x4, 3)
    for step in range(groups - 2):
        got = hop(out, step)
        t_in, out = call(
            functools.partial(forward_hop, step), [h4, coded], got, t_in, up, s_group,
            after=(k,) if step == 0 else (),
        )
        if step == 0:
            pieces = [((half // 2 + SCALES, LANES), i16)] * 2
            low, high = call(relay_halves, pieces, got4, after=(out,))
            got4_low, got4_high = swap(low, 1), swap(high, 1)
    gg_group, g_group, gg_second, g_second = call(
        group_backward, [sq, h4, sq, h4],
        n_first, got2, sp_own, gg_own, got4, got4_low, got4_high, gp_own, after=(out,),
    )
    last = groups - 2
    got = hop(out, last)
    t_in, out = call(
        functools.partial(turn, last), [h4, coded], got, t_in, gg_group, g_group
    )

    u_in = jnp.zeros((four, half), f32)
    for step in reversed(range(groups - 1)):
        got = hop(out, step)
        if step == last:
            x5, x5_rest, kept, rest_own, local = call(
                spread_forward, [coded, coded, h4, h4, h4],
                t_in, n_first, got2, sp_own, gg_second, g_second, gg_group, g_group, after=(out,),
            )
            got5, got5_rest = swap(x5, 3), swap(x5_rest, 3)
        if step:
            u_in, out = call(
                functools.partial(backward_hop, step), [h4, coded], got, u_in, down, local
            )
        else:
            start, maps = call(
                block_parts, [solved_shape, ((2 * half, typed), f32)], solved, p, d, after=(out,)
            )
            out = call(functools.partial(arrive, step), coded, got, u_in, after=(maps,))
    x6, own = call(
        pair_states, [x6_coded, x6_shape], kept, rest_own, got5, got5_rest, x1, got1, s_own, x3, got3, g_own
    )
    got6 = swap(x6, 1)
    fixed = call(block_fixed, solved_shape, own, got6, start, maps)
    theirs = swap(out, 1)
    got_u = swap(out, 3)
    their_got = swap(got_u, 1)
    edge = (square, bf16)
    xa, xb = call(block_weights, [edge, edge], out, got_u, theirs, their_got, fixed, k)
    got_a = swap_chips(xa)
    got_b = swap(xb, 1)
    acc = call(impute_own, ((traits, untyped), f32), xa, xb, masked)
    return call(
        impute_edges, ((traits, untyped), f32), acc, got_a, got_b, masked, last=True
    )


def solution(mesh):
    in_specs = (
        P(None, (SEGMENTS, AXIS)),
        P((SEGMENTS, AXIS), None, None),
        P((SEGMENTS, AXIS), None, None),
        P((SEGMENTS, AXIS), None),
        P((SEGMENTS, AXIS)),
    )
    return jax.shard_map(
        per_device, mesh=mesh, in_specs=in_specs, out_specs=P(None, (SEGMENTS, AXIS)), check_vma=False
    )
```

```python
import functools

import jax
import jax.numpy as jnp
from jax import lax
from jax.experimental import pallas as pl
from jax.experimental.pallas import tpu as pltpu
from jax.sharding import PartitionSpec as P

AXIS = "genome"
SEGMENTS = "seg"
GROUP = 4
f32 = jnp.float32
bf16 = jnp.bfloat16
i16 = jnp.int16
SCALES = 16
LANES = 128
LIMIT = 32767.0


def parts(x):
    high = x.astype(bf16)
    return high, (x - high.astype(f32)).astype(bf16)


def dot(a, b, ca=1, cb=0):
    ah, al = parts(a)
    bh, bl = parts(b)
    return lax.dot_general(
        jnp.concatenate([al, ah, ah], axis=ca),
        jnp.concatenate([bh, bl, bh], axis=cb),
        (((ca,), (cb,)), ((), ())),
        preferred_element_type=f32,
    )


def code(x):
    top = jnp.maximum(jnp.max(jnp.abs(x), axis=0, keepdims=True), 1e-32)
    power = jnp.ceil(jnp.log2(top) * 4.0)
    root = jnp.exp2(power * -0.125)
    steps = jnp.floor(x * root * (root * LIMIT) + 0.5)
    steps = jnp.clip(steps, -LIMIT, LIMIT)
    tiles = x.shape[1] // LANES
    powers = jnp.broadcast_to(power, (SCALES // tiles, x.shape[1]))
    pieces = [v[:, i * LANES : (i + 1) * LANES] for v in (steps, powers) for i in range(tiles)]
    return jnp.concatenate(pieces, axis=0).astype(jnp.int32).astype(i16)


def decode(coded, tiles=2):
    rows = (coded.shape[0] - SCALES) // tiles
    values = coded[...].astype(jnp.int32).astype(f32)
    columns = []
    for i in range(tiles):
        at = tiles * rows + i * (SCALES // tiles)
        root = jnp.exp2(values[at : at + 1] * 0.125)
        columns.append(values[i * rows : (i + 1) * rows] * (root / LIMIT) * root)
    return jnp.concatenate(columns, axis=1)


def coded_rows(rows, columns):
    return rows * (columns // LANES) + SCALES


def where_am_i():
    place = lax.axis_index(AXIS)
    return place % 2 == 0, (place // 2) % 2 == 0, place // GROUP


def ready(b):
    bh, bl = parts(b)
    return jnp.concatenate([bh, bl, bh], axis=0)


def dot_ready(a, b):
    ah, al = parts(a)
    return jnp.dot(jnp.concatenate([al, ah, ah], axis=1), b[...], preferred_element_type=f32)


def low_traits():
    place = lax.axis_index(AXIS)
    return (place + place // 2 + place // GROUP) % 2 == 0


def ordered(first, own, other):
    return jnp.where(first, own, other), jnp.where(first, other, own)


def call(kernel, outs, *args, after=(), hbm=False, last=False, scratch=()):
    n_in, n_after = len(args), len(after)

    def body(*refs):
        kernel(*refs[:n_in], *refs[n_in + n_after :])

    single = not isinstance(outs, list)
    shapes = [outs] if single else outs
    vmem = pl.BlockSpec(memory_space=pltpu.VMEM)
    anywhere = pl.BlockSpec(memory_space=pl.ANY)
    if hbm:
        args = [pltpu.with_memory_space_constraint(a, pltpu.HBM) for a in args]
    got = pl.pallas_call(
        body,
        out_shape=[jax.ShapeDtypeStruct(s, t) if last else pltpu.VMEM(s, t) for s, t in shapes],
        in_specs=[anywhere if hbm else vmem] * n_in + [anywhere] * n_after,
        out_specs=[vmem] * len(shapes),
        scratch_shapes=scratch,
        compiler_params=pltpu.CompilerParams(vmem_limit_bytes=8 * 2**20),
        name=kernel.__name__ if hasattr(kernel, "__name__") else kernel.func.__name__,
    )(*args, *after)
    return got[0] if single else got


def tail_part(z_in, d_in, c_in, x1, s_own, z, d, c, sems):
    typed, half = c.shape
    rows = z.shape[0] // 2
    head = typed - half
    step = typed // 2
    copies = []
    for i in range(2):
        here = pl.ds(i * step, step)
        tail = (pl.ds(head, half), here)
        copies.append(pltpu.make_async_copy(d_in.at[tail], d.at[tail], sems.at[3 * i]))
        copies.append(pltpu.make_async_copy(c_in.at[here], c.at[here], sems.at[3 * i + 1]))
        copies.append(pltpu.make_async_copy(z_in.at[:, here], z.at[:, here], sems.at[3 * i + 2]))
    rest = pl.ds(0, head)
    copies.append(pltpu.make_async_copy(d_in.at[rest], d.at[rest], sems.at[6]))
    for copy in copies:
        copy.start()
    m = s = 0.0
    for i in range(2):
        here = pl.ds(i * step, step)
        for copy in copies[3 * i : 3 * i + 3]:
            copy.wait()
        tail = d[head:, here]
        m = m - dot(tail, c[here])
        s = s + dot(z[:, here], tail, 1, 1)
    x1[:half] = m
    keep, send = ordered(low_traits(), s[:rows], s[rows:])
    x1[half:] = send
    s_own[...] = keep
    copies[6].wait()


def head_part(z, d, c, x1, s_own, x3, g_own, solved, p):
    half = c.shape[1]
    rows = z.shape[0] // 2
    head = d.shape[0] - half
    first, _, _ = where_am_i()
    p[:head] = dot(d[:head], c[...])
    p[head:] = -x1[:half]
    solved[:, :head] = dot(z[...], d[:head], 1, 1)
    low, high = ordered(low_traits(), s_own[...], x1[half:])
    solved[:rows, head:] = low
    solved[rows:, head:] = high
    g = dot(solved[...], p[...])
    keep, send = ordered(low_traits(), g[:rows], g[rows:])
    x3[:half] = dot(p[...], p[...], 0, 0)
    x3[half:] = send
    g_own[...] = keep


def pair_forward(x1, got1, s_own, x2, n_own, sp_own):
    half = x1.shape[1]
    first, first_pair, _ = where_am_i()
    m0, m1 = ordered(first, x1[:half], got1[:half])
    s0, s1 = ordered(first, s_own[...], got1[half:])
    n = dot(m1, m0)
    n_own[...] = n
    split = coded_rows(half // 2, half)
    x2[:split] = code(jnp.where(first, n[: half // 2], n[half // 2 :]))
    s = dot(s0, m1, 1, 1) + s1
    rows = s.shape[0] // 2
    keep, send = ordered(first_pair, s[:rows], s[rows:])
    x2[split:] = code(send)
    sp_own[...] = keep


def pair_backward(x1, got1, s_own, x3, got3, g_own, x4, gg_own, gp_own):
    half = x1.shape[1]
    first, first_pair, _ = where_am_i()
    m0, _ = ordered(first, x1[:half], got1[:half])
    s0, _ = ordered(first, s_own[...], got1[half:])
    gg0, gg1 = ordered(first, x3[:half], got3[:half])
    g0, g1 = ordered(first, g_own[...], got3[half:])
    both = dot(jnp.concatenate([gg1, g1 - dot(s0, gg1)], axis=0), m0)
    gg = dot(m0, both[:half], 0, 0) + gg0
    gg_own[...] = gg
    split = coded_rows(half // 2, half)
    x4[:split] = code(jnp.where(first, gg[: half // 2], gg[half // 2 :]))
    g = both[half:] + g0
    rows = g.shape[0] // 2
    keep, send = ordered(first_pair, g[:rows], g[rows:])
    x4[split:] = code(send)
    gp_own[...] = keep


def pair_matrices(own, got, got_core):
    first, first_pair, _ = where_am_i()
    other = jnp.concatenate(ordered(first, got_core, got), axis=0)
    return ordered(first_pair, own[...], other)


def pair_vectors(own, got):
    _, first_pair, _ = where_am_i()
    return ordered(first_pair, own[...], got)


def relay(got, out):
    out[...] = got[: out.shape[0]]


def relay_halves(got, low, high):
    rows = low.shape[0] - SCALES
    low[:rows] = got[:rows]
    high[:rows] = got[rows : 2 * rows]
    low[rows:] = got[2 * rows : 2 * rows + SCALES]
    high[rows:] = got[2 * rows : 2 * rows + SCALES]


def group_forward(n_own, got2, got2_core, sp_own, out):
    _, _, group = where_am_i()
    out[...] = jnp.zeros_like(out)

    @pl.when(group == 0)
    def _():
        split = coded_rows(n_own.shape[1] // 2, n_own.shape[1])
        _, n1 = pair_matrices(n_own, decode(got2[:split]), decode(got2_core))
        s0, s1 = pair_vectors(sp_own, decode(got2[split:]))
        out[...] = code(dot(s0, n1, 1, 1) + s1)


def group_map(n_own, got2, got2_core, sp_own, s_group, up, down, n_first, n_second):
    split = coded_rows(n_own.shape[1] // 2, n_own.shape[1])
    n0, n1 = pair_matrices(n_own, decode(got2[:split]), decode(got2_core))
    s0, s1 = pair_vectors(sp_own, decode(got2[split:]))
    s_group[...] = dot(s0, n1, 1, 1) + s1
    n_first[...] = n0
    n_second[...] = n1
    n_group = dot(n1, n0)
    up[...] = ready(n_group.T)
    down[...] = ready(n_group)


def block_map(n_second, x1, got1, d, k):
    half = x1.shape[1]
    first, first_pair, _ = where_am_i()
    rows = lax.broadcasted_iota(jnp.int32, (half, half), 0)
    columns = lax.broadcasted_iota(jnp.int32, (half, half), 1)
    unit = (rows == columns).astype(f32)
    _, m1 = ordered(first, x1[:half], got1[:half])
    above = jnp.where(first_pair, n_second[...], unit)
    above = jnp.where(first, dot(above, m1), above)
    k[...] = dot(above, d[d.shape[0] - half :])


def group_backward(
    n_first, got2, sp_own, gg_own, got4, got4_low, got4_high, gp_own,
    gg_group, g_group, gg_second, g_second,
):
    half = n_first.shape[1]
    split = coded_rows(half // 2, half)
    n0 = n_first[...]
    s0, _ = pair_vectors(sp_own, decode(got2[split:]))
    rows = got4_low.shape[0] - SCALES
    got4_core = jnp.concatenate([got4_low[:rows], got4_high[...]], axis=0)
    gg0, gg1 = pair_matrices(gg_own, decode(got4[:split]), decode(got4_core))
    g0, g1 = pair_vectors(gp_own, decode(got4[split:]))
    gg_second[...] = gg1
    g_second[...] = g1
    both = dot(jnp.concatenate([gg1, g1 - dot(s0, gg1)], axis=0), n0)
    gg_group[...] = dot(n0, both[:half], 0, 0) + gg0
    g_group[...] = both[half:] + g0


def forward_hop(step, got, t_in, up, s_group, t_out, out):
    _, _, group = where_am_i()
    t = jnp.where(group == step + 1, decode(got), t_in[...])
    t_out[...] = t
    out[...] = code(dot_ready(t, up) + s_group[...])


def turn(step, got, t_in, gg_group, g_group, t_out, out):
    _, _, group = where_am_i()
    t = jnp.where(group == step + 1, decode(got), t_in[...])
    t_out[...] = t
    out[...] = jnp.zeros_like(out)

    @pl.when(group == step + 1)
    def _():
        out[...] = code(g_group[...] - dot(t, gg_group[...]))


def backward_hop(step, got, u_in, down, local, u_out, out):
    _, _, group = where_am_i()
    u = jnp.where(group == step, decode(got), u_in[...])
    u_out[...] = u
    out[...] = code(dot_ready(u, down) + local[...])


def arrive(step, got, u_in, out):
    _, _, group = where_am_i()
    out[...] = code(jnp.where(group == step, decode(got), u_in[...]))


def spread_forward(
    t_in, n_first, got2, sp_own, gg_second, g_second, gg_group, g_group, x5, x5_rest, kept, rest_own, local
):
    half = n_first.shape[1]
    _, first_pair, _ = where_am_i()
    s0, _ = pair_vectors(sp_own, decode(got2[coded_rows(half // 2, half) :]))
    t_mid = dot(t_in[...], n_first[...], 1, 1) + s0
    rest = g_second[...] - dot(t_mid, gg_second[...])
    keep, send = ordered(first_pair, t_in[...], t_mid)
    x5[...] = code(send)
    x5_rest[...] = code(rest)
    kept[...] = keep
    rest_own[...] = rest
    local[...] = g_group[...] - dot(t_in[...], gg_group[...])


def pair_states(kept, rest_own, got5, got5_rest, x1, got1, s_own, x3, got3, g_own, x6, own):
    half = x1.shape[1]
    rows = s_own.shape[0]
    first, first_pair, _ = where_am_i()
    t = jnp.concatenate(ordered(first_pair, kept[...], decode(got5)), axis=0)
    rest = jnp.concatenate(ordered(first_pair, rest_own[...], decode(got5_rest)), axis=0)
    m0, m1 = ordered(first, x1[:half], got1[:half])
    s0, _ = ordered(first, s_own[...], got1[half:])
    _, gg1 = ordered(first, x3[:half], got3[:half])
    _, g1 = ordered(first, g_own[...], got3[half:])
    t_mid = dot(t, m0, 1, 1) + s0
    fixed = jnp.where(first_pair, rest, 0.0)
    fixed_mid = dot(fixed, m1) + g1 - dot(t_mid, gg1)
    split = coded_rows(rows, half)
    keep, send = ordered(first, t, t_mid)
    x6[:split] = code(send)
    own[:rows] = keep
    keep, send = ordered(first, fixed_mid, fixed)
    x6[split:] = code(send)
    own[rows:] = keep


def block_parts(solved, p, d, start, maps):
    half = p.shape[1]
    start[...] = dot(solved[...], d[...])
    maps[:half] = dot(p[...], d[...], 0, 0)
    maps[half:] = d[d.shape[0] - half :]


def block_fixed(own, got6, start, maps, fixed_weights):
    rows = own.shape[0] // 2
    split = coded_rows(rows, own.shape[1])
    low = low_traits()
    t = jnp.concatenate(ordered(low, own[:rows], decode(got6[:split])), axis=0)
    above = jnp.concatenate(ordered(low, own[rows:], decode(got6[split:])), axis=0)
    fixed_weights[...] = start[...] - dot(jnp.concatenate([t, above], axis=1), maps[...])


def near_weights(mine, got_u, fixed_weights, k, xa, xb, weights):
    half = k.shape[0]
    first, first_pair, _ = where_am_i()
    u = jnp.concatenate(ordered(first_pair, decode(mine), decode(got_u)), axis=0)
    rows = u.shape[0]
    fixed, _ = ordered(low_traits(), fixed_weights[:rows], fixed_weights[rows:])
    w = (fixed - dot(u, k[...])).astype(bf16)
    weights[...] = w
    xa[...], xb[...] = ordered(first, w[:, :half], w[:, half:])


def far_weights(theirs, their_got, fixed_weights, k, near, xa, xb, weights):
    half = k.shape[0]
    first, first_pair, _ = where_am_i()
    low = low_traits()
    u = jnp.concatenate(ordered(first_pair, decode(theirs), decode(their_got)), axis=0)
    rows = u.shape[0]
    _, fixed = ordered(low, fixed_weights[:rows], fixed_weights[rows:])
    w = (fixed - dot(u, k[...])).astype(bf16)
    xa[...], xb[...] = ordered(first, w[:, :half], w[:, half:])
    weights[...] = jnp.concatenate(ordered(low, near[...], w), axis=0)


def contract(values, coefs):
    return lax.dot_general(values, coefs, (((1,), (1,)), ((), ())), preferred_element_type=f32)


def mask_coefs(coefs_in, anchor_in, masked, coefs, anchor, sems):
    untyped, span = coefs.shape
    half = span // 4
    typed = span - 2 * half
    tile = 128
    place = lax.axis_index(AXIS)
    total = lax.axis_size(AXIS) * typed
    copies = [pltpu.make_async_copy(anchor_in, anchor, sems.at[0])]
    for i in range(untyped // tile):
        rows = pl.ds(i * tile, tile)
        copies.append(pltpu.make_async_copy(coefs_in.at[rows], coefs.at[rows], sems.at[i + 1]))
    for copy in copies:
        copy.start()
    copies[0].wait()
    first_column = place * typed - half
    for i in range(untyped // tile):
        rows = pl.ds(i * tile, tile)
        nearest = jnp.broadcast_to(anchor[:, i * tile : (i + 1) * tile], (tile, tile)).T
        copies[i + 1].wait()
        for j in range(span // tile):
            lanes = pl.ds(j * tile, tile)
            columns = first_column + j * tile + lax.broadcasted_iota(jnp.int32, (tile, tile), 1)
            within = (jnp.abs(columns - nearest) <= half) & (columns >= 0) & (columns < total)
            masked[rows, lanes] = jnp.where(within, coefs[rows, lanes].astype(f32), 0.0).astype(bf16)


def impute_own(weights, masked, out):
    span = masked.shape[1]
    half = (span - weights.shape[1]) // 2
    out[...] = contract(weights[...], masked[:, half : span - half])


def near_half():
    first, first_pair, _ = where_am_i()
    within_group = jnp.logical_xor(first, first_pair)
    return jnp.logical_not(jnp.logical_xor(low_traits(), within_group))


def edge_coefs(masked, half):
    first, _, _ = where_am_i()
    span = masked.shape[1]
    return ordered(first, masked[:, :half], masked[:, span - half :])


def impute_near(acc, got_near, b_near, b_far, masked, out):
    half = got_near.shape[1]
    rows = got_near.shape[0]
    coefs_a, coefs_b = edge_coefs(masked, half)
    got_b = jnp.concatenate(ordered(low_traits(), b_far[...], b_near[...]), axis=0)
    part = contract(got_near[...], coefs_a)
    low, high = ordered(near_half(), part, jnp.zeros_like(part))
    out[...] = acc[...] + contract(got_b, coefs_b) + jnp.concatenate([low, high], axis=0)


def impute_far(acc, got_far, masked, out):
    half = got_far.shape[1]
    coefs_a, _ = edge_coefs(masked, half)
    part = contract(got_far[...], coefs_a)
    high, low = ordered(near_half(), part, jnp.zeros_like(part))
    out[...] = acc[...] + jnp.concatenate([low, high], axis=0)


def swap(block, distance):
    n = lax.axis_size(AXIS)
    return lax.ppermute(block, AXIS, [(i, i ^ distance) for i in range(n)])


def hop(block, step):
    pairs = []
    for i in range(lax.axis_size(AXIS)):
        g = i // GROUP
        to = i + GROUP if g == step else i - GROUP if g == step + 1 else i
        pairs.append((i, to ^ 1))
    return lax.ppermute(block, AXIS, pairs)


def swap_chips(block):
    n, segments = lax.axis_size(AXIS), lax.axis_size(SEGMENTS)
    pairs = []
    for seg in range(segments):
        for i in range(n):
            to, to_seg = i + 1 if i % 2 else i - 1, seg
            if not 0 <= to < n:
                to, to_seg = (i, seg ^ 1) if segments % 2 == 0 else (to % n, seg)
            pairs.append((seg * n + i, to_seg * n + to))
    return lax.ppermute(block, (SEGMENTS, AXIS), pairs)


def per_device(z, diag_inverse, coupling, impute_coef, anchor):
    d = diag_inverse[0]
    c = coupling[0]
    typed = d.shape[0]
    half = c.shape[1]
    traits = z.shape[0]
    untyped, span = impute_coef.shape
    assert span == typed + 2 * half and typed == 2 * half
    assert lax.axis_size(AXIS) >= 3 * GROUP
    groups = lax.axis_size(AXIS) // GROUP
    two, four = traits // 2, traits // 4
    square = (half, half)
    sq, h2, h4 = (square, f32), ((two, half), f32), ((four, half), f32)
    x1_shape, x6_shape = ((half + two, half), f32), ((2 * two, half), f32)
    x6_coded = ((2 * coded_rows(two, half), LANES), i16)
    coded = ((coded_rows(four, half), LANES), i16)
    coded_half = ((coded_rows(half // 2, half), LANES), i16)
    mixed = ((coded_rows(half // 2, half) + coded_rows(four, half), LANES), i16)

    solved_shape, p_shape = ((traits, typed), f32), ((typed, half), f32)
    x1, s_own, z, d, c = call(
        tail_part, [x1_shape, h2, solved_shape, ((typed, typed), f32), p_shape], z, d, c,
        hbm=True, scratch=[pltpu.SemaphoreType.DMA((7,))],
    )
    got1 = swap(x1, 1)
    x3, g_own, solved, p = call(
        head_part, [x1_shape, h2, solved_shape, p_shape], z, d, c, x1, s_own
    )
    x2, n_own, sp_own = call(pair_forward, [mixed, sq, h4], x1, got1, s_own, after=(p,))
    got2 = swap(x2, 3)
    got3 = swap(x3, 1)
    masked = call(
        mask_coefs, ((untyped, span), bf16), impute_coef, anchor[None, :], after=(x2,), hbm=True,
        scratch=[
            pltpu.VMEM((untyped, span), bf16),
            pltpu.VMEM((1, untyped), jnp.int32),
            pltpu.SemaphoreType.DMA((untyped // 128 + 1,)),
        ],
    )
    x4, gg_own, gp_own = call(
        pair_backward, [mixed, sq, h4], x1, got1, s_own, x3, got3, g_own, after=(x2,)
    )
    got2_core = swap(call(relay, coded_half, got2, after=(x4, masked)), 1)
    out = call(group_forward, coded, n_own, got2, got2_core, sp_own)
    parts3 = ((3 * half, half), bf16)
    s_group, up, down, n_first, n_second = call(
        group_map, [h4, parts3, parts3, sq, sq], n_own, got2, got2_core, sp_own, after=(out,)
    )
    k = call(block_map, ((half, typed), f32), n_second, x1, got1, d)
    t_in = jnp.zeros((four, half), f32)
    got4 = swap(x4, 3)
    for step in range(groups - 2):
        got = hop(out, step)
        t_in, out = call(
            functools.partial(forward_hop, step), [h4, coded], got, t_in, up, s_group,
            after=(k,) if step == 0 else (),
        )
        if step == 0:
            pieces = [((half // 2 + SCALES, LANES), i16)] * 2
            low, high = call(relay_halves, pieces, got4, after=(out,))
            got4_low, got4_high = swap(low, 1), swap(high, 1)
    gg_group, g_group, gg_second, g_second = call(
        group_backward, [sq, h4, sq, h4],
        n_first, got2, sp_own, gg_own, got4, got4_low, got4_high, gp_own, after=(out,),
    )
    last = groups - 2
    got = hop(out, last)
    t_in, out = call(
        functools.partial(turn, last), [h4, coded], got, t_in, gg_group, g_group
    )

    u_in = jnp.zeros((four, half), f32)
    for step in reversed(range(groups - 1)):
        got = hop(out, step)
        if step == last:
            x5, x5_rest, kept, rest_own, local = call(
                spread_forward, [coded, coded, h4, h4, h4],
                t_in, n_first, got2, sp_own, gg_second, g_second, gg_group, g_group, after=(out,),
            )
            got5, got5_rest = swap(x5, 3), swap(x5_rest, 3)
        if step:
            u_in, out = call(
                functools.partial(backward_hop, step), [h4, coded], got, u_in, down, local
            )
        else:
            start, maps = call(
                block_parts, [solved_shape, ((2 * half, typed), f32)], solved, p, d, after=(out,)
            )
            out = call(functools.partial(arrive, step), coded, got, u_in, after=(maps,))
    x6, own = call(
        pair_states, [x6_coded, x6_shape], kept, rest_own, got5, got5_rest, x1, got1, s_own, x3, got3, g_own
    )
    got6 = swap(x6, 1)
    fixed = call(block_fixed, solved_shape, own, got6, start, maps)
    theirs = swap(out, 1)
    got_u = swap(out, 3)
    their_got = swap(got_u, 1)
    edge_half = ((two, half), bf16)
    xa, xb, near = call(
        near_weights, [edge_half, edge_half, ((two, typed), bf16)], out, got_u, fixed, k
    )
    got_near, b_near = swap_chips(xa), swap(xb, 1)
    xa, xb, weights = call(
        far_weights, [edge_half, edge_half, ((traits, typed), bf16)], theirs, their_got, fixed, k, near
    )
    got_far, b_far = swap_chips(xa), swap(xb, 1)
    result = ((traits, untyped), f32)
    acc = call(impute_own, result, weights, masked)
    acc = call(impute_near, result, acc, got_near, b_near, b_far, masked)
    return call(impute_far, result, acc, got_far, masked, last=True)


def solution(mesh):
    in_specs = (
        P(None, (SEGMENTS, AXIS)),
        P((SEGMENTS, AXIS), None, None),
        P((SEGMENTS, AXIS), None, None),
        P((SEGMENTS, AXIS), None),
        P((SEGMENTS, AXIS)),
    )
    return jax.shard_map(
        per_device, mesh=mesh, in_specs=in_specs, out_specs=P(None, (SEGMENTS, AXIS)), check_vma=False
    )
```

```python
import functools

import jax
import jax.numpy as jnp
from jax import lax
from jax.experimental import pallas as pl
from jax.experimental.pallas import tpu as pltpu
from jax.sharding import PartitionSpec as P

AXIS = "genome"
SEGMENTS = "seg"
GROUP = 4
f32 = jnp.float32
bf16 = jnp.bfloat16
i16 = jnp.int16
SCALES = 16
LANES = 128
LIMIT = 32767.0


def parts(x):
    high = x.astype(bf16)
    return high, (x - high.astype(f32)).astype(bf16)


def dot(a, b, ca=1, cb=0):
    ah, al = parts(a)
    bh, bl = parts(b)
    return lax.dot_general(
        jnp.concatenate([al, ah, ah], axis=ca),
        jnp.concatenate([bh, bl, bh], axis=cb),
        (((ca,), (cb,)), ((), ())),
        preferred_element_type=f32,
    )


def code(x):
    top = jnp.maximum(jnp.max(jnp.abs(x), axis=0, keepdims=True), 1e-32)
    power = jnp.ceil(jnp.log2(top) * 4.0)
    root = jnp.exp2(power * -0.125)
    steps = jnp.floor(x * root * (root * LIMIT) + 0.5)
    steps = jnp.clip(steps, -LIMIT, LIMIT)
    tiles = x.shape[1] // LANES
    powers = jnp.broadcast_to(power, (SCALES // tiles, x.shape[1]))
    pieces = [v[:, i * LANES : (i + 1) * LANES] for v in (steps, powers) for i in range(tiles)]
    return jnp.concatenate(pieces, axis=0).astype(jnp.int32).astype(i16)


def decode(coded, tiles=2):
    rows = (coded.shape[0] - SCALES) // tiles
    values = coded[...].astype(jnp.int32).astype(f32)
    columns = []
    for i in range(tiles):
        at = tiles * rows + i * (SCALES // tiles)
        root = jnp.exp2(values[at : at + 1] * 0.125)
        columns.append(values[i * rows : (i + 1) * rows] * (root / LIMIT) * root)
    return jnp.concatenate(columns, axis=1)


def coded_rows(rows, columns):
    return rows * (columns // LANES) + SCALES


def where_am_i():
    place = lax.axis_index(AXIS)
    return place % 2 == 0, (place // 2) % 2 == 0, place // GROUP


def ready(b):
    bh, bl = parts(b)
    return jnp.concatenate([bh, bl, bh], axis=0)


def dot_ready(a, b):
    ah, al = parts(a)
    return jnp.dot(jnp.concatenate([al, ah, ah], axis=1), b[...], preferred_element_type=f32)


def low_traits():
    place = lax.axis_index(AXIS)
    return (place + place // 2) % 2 == 0


def ordered(first, own, other):
    return jnp.where(first, own, other), jnp.where(first, other, own)


def call(kernel, outs, *args, after=(), hbm=False, last=False, scratch=()):
    n_in, n_after = len(args), len(after)

    def body(*refs):
        kernel(*refs[:n_in], *refs[n_in + n_after :])

    single = not isinstance(outs, list)
    shapes = [outs] if single else outs
    vmem = pl.BlockSpec(memory_space=pltpu.VMEM)
    anywhere = pl.BlockSpec(memory_space=pl.ANY)
    if hbm:
        args = [pltpu.with_memory_space_constraint(a, pltpu.HBM) for a in args]
    got = pl.pallas_call(
        body,
        out_shape=[jax.ShapeDtypeStruct(s, t) if last else pltpu.VMEM(s, t) for s, t in shapes],
        in_specs=[anywhere if hbm else vmem] * n_in + [anywhere] * n_after,
        out_specs=[vmem] * len(shapes),
        scratch_shapes=scratch,
        compiler_params=pltpu.CompilerParams(vmem_limit_bytes=8 * 2**20),
        name=kernel.__name__ if hasattr(kernel, "__name__") else kernel.func.__name__,
    )(*args, *after)
    return got[0] if single else got


def tail_part(z_in, d_in, c_in, x1, s_own, z, d, c, sems):
    typed, half = c.shape
    rows = z.shape[0] // 2
    head = typed - half
    step = typed // 2
    copies = []
    for i in range(2):
        here = pl.ds(i * step, step)
        tail = (pl.ds(head, half), here)
        copies.append(pltpu.make_async_copy(d_in.at[tail], d.at[tail], sems.at[3 * i]))
        copies.append(pltpu.make_async_copy(c_in.at[here], c.at[here], sems.at[3 * i + 1]))
        copies.append(pltpu.make_async_copy(z_in.at[:, here], z.at[:, here], sems.at[3 * i + 2]))
    rest = pl.ds(0, head)
    copies.append(pltpu.make_async_copy(d_in.at[rest], d.at[rest], sems.at[6]))
    for copy in copies:
        copy.start()
    m = s = 0.0
    for i in range(2):
        here = pl.ds(i * step, step)
        for copy in copies[3 * i : 3 * i + 3]:
            copy.wait()
        tail = d[head:, here]
        m = m - dot(tail, c[here])
        s = s + dot(z[:, here], tail, 1, 1)
    x1[:half] = m
    keep, send = ordered(low_traits(), s[:rows], s[rows:])
    x1[half:] = send
    s_own[...] = keep
    copies[6].wait()


def head_part(z, d, c, x1, s_own, x3, g_own, solved, p):
    half = c.shape[1]
    rows = z.shape[0] // 2
    head = d.shape[0] - half
    first, _, _ = where_am_i()
    p[:head] = dot(d[:head], c[...])
    p[head:] = -x1[:half]
    solved[:, :head] = dot(z[...], d[:head], 1, 1)
    low, high = ordered(low_traits(), s_own[...], x1[half:])
    solved[:rows, head:] = low
    solved[rows:, head:] = high
    g = dot(solved[...], p[...])
    keep, send = ordered(low_traits(), g[:rows], g[rows:])
    x3[:half] = dot(p[...], p[...], 0, 0)
    x3[half:] = send
    g_own[...] = keep


def pair_forward(x1, got1, s_own, x2, n_own, sp_own):
    half = x1.shape[1]
    first, first_pair, _ = where_am_i()
    m0, m1 = ordered(first, x1[:half], got1[:half])
    s0, s1 = ordered(first, s_own[...], got1[half:])
    n = dot(m1, m0)
    n_own[...] = n
    split = coded_rows(half // 2, half)
    x2[:split] = code(jnp.where(first, n[: half // 2], n[half // 2 :]))
    s = dot(s0, m1, 1, 1) + s1
    rows = s.shape[0] // 2
    keep, send = ordered(first_pair, s[:rows], s[rows:])
    x2[split:] = code(send)
    sp_own[...] = keep


def pair_backward(x1, got1, s_own, x3, got3, g_own, x4, gg_own, gp_own):
    half = x1.shape[1]
    first, first_pair, _ = where_am_i()
    m0, _ = ordered(first, x1[:half], got1[:half])
    s0, _ = ordered(first, s_own[...], got1[half:])
    gg0, gg1 = ordered(first, x3[:half], got3[:half])
    g0, g1 = ordered(first, g_own[...], got3[half:])
    both = dot(jnp.concatenate([gg1, g1 - dot(s0, gg1)], axis=0), m0)
    gg = dot(m0, both[:half], 0, 0) + gg0
    gg_own[...] = gg
    split = coded_rows(half // 2, half)
    x4[:split] = code(jnp.where(first, gg[: half // 2], gg[half // 2 :]))
    g = both[half:] + g0
    rows = g.shape[0] // 2
    keep, send = ordered(first_pair, g[:rows], g[rows:])
    x4[split:] = code(send)
    gp_own[...] = keep


def pair_matrices(own, got, got_core):
    first, first_pair, _ = where_am_i()
    other = jnp.concatenate(ordered(first, got_core, got), axis=0)
    return ordered(first_pair, own[...], other)


def pair_vectors(own, got):
    _, first_pair, _ = where_am_i()
    return ordered(first_pair, own[...], got)


def relay(got, out):
    out[...] = got[: out.shape[0]]


def relay_halves(got, low, high):
    rows = low.shape[0] - SCALES
    low[:rows] = got[:rows]
    high[:rows] = got[rows : 2 * rows]
    low[rows:] = got[2 * rows : 2 * rows + SCALES]
    high[rows:] = got[2 * rows : 2 * rows + SCALES]


def group_forward(n_own, got2, got2_core, sp_own, out):
    _, _, group = where_am_i()
    out[...] = jnp.zeros_like(out)

    @pl.when(group == 0)
    def _():
        split = coded_rows(n_own.shape[1] // 2, n_own.shape[1])
        _, n1 = pair_matrices(n_own, decode(got2[:split]), decode(got2_core))
        s0, s1 = pair_vectors(sp_own, decode(got2[split:]))
        out[...] = code(dot(s0, n1, 1, 1) + s1)


def group_map(n_own, got2, got2_core, sp_own, s_group, up, down, n_first, n_second):
    split = coded_rows(n_own.shape[1] // 2, n_own.shape[1])
    n0, n1 = pair_matrices(n_own, decode(got2[:split]), decode(got2_core))
    s0, s1 = pair_vectors(sp_own, decode(got2[split:]))
    s_group[...] = dot(s0, n1, 1, 1) + s1
    n_first[...] = n0
    n_second[...] = n1
    n_group = dot(n1, n0)
    up[...] = ready(n_group.T)
    down[...] = ready(n_group)


def block_map(n_second, x1, got1, d, k):
    half = x1.shape[1]
    first, first_pair, _ = where_am_i()
    rows = lax.broadcasted_iota(jnp.int32, (half, half), 0)
    columns = lax.broadcasted_iota(jnp.int32, (half, half), 1)
    unit = (rows == columns).astype(f32)
    _, m1 = ordered(first, x1[:half], got1[:half])
    above = jnp.where(first_pair, n_second[...], unit)
    above = jnp.where(first, dot(above, m1), above)
    k[...] = ready(dot(above, d[d.shape[0] - half :]))


def group_backward(
    n_first, got2, sp_own, gg_own, got4, got4_low, got4_high, gp_own,
    gg_group, g_group, gg_second, g_second,
):
    half = n_first.shape[1]
    split = coded_rows(half // 2, half)
    n0 = n_first[...]
    s0, _ = pair_vectors(sp_own, decode(got2[split:]))
    rows = got4_low.shape[0] - SCALES
    got4_core = jnp.concatenate([got4_low[:rows], got4_high[...]], axis=0)
    gg0, gg1 = pair_matrices(gg_own, decode(got4[:split]), decode(got4_core))
    g0, g1 = pair_vectors(gp_own, decode(got4[split:]))
    gg_second[...] = gg1
    g_second[...] = g1
    both = dot(jnp.concatenate([gg1, g1 - dot(s0, gg1)], axis=0), n0)
    gg = dot(n0, both[:half], 0, 0) + gg0
    gg_group[...] = ready(gg)
    g_group[...] = both[half:] + g0


def forward_hop(step, got, t_in, up, s_group, t_out, out):
    _, _, group = where_am_i()
    t = jnp.where(group == step + 1, decode(got), t_in[...])
    t_out[...] = t
    out[...] = code(dot_ready(t, up) + s_group[...])


def turn(step, got, t_in, gg_group, g_group, t_out, out):
    _, _, group = where_am_i()
    t = jnp.where(group == step + 1, decode(got), t_in[...])
    t_out[...] = t
    out[...] = jnp.zeros_like(out)

    @pl.when(group == step + 1)
    def _():
        out[...] = code(g_group[...] - dot_ready(t, gg_group))


def backward_hop(step, got, u_in, down, local, u_out, out):
    _, _, group = where_am_i()
    u = jnp.where(group == step, decode(got), u_in[...])
    u_out[...] = u
    out[...] = code(dot_ready(u, down) + local[...])


def arrive(step, got, u_in, out):
    _, _, group = where_am_i()
    out[...] = code(jnp.where(group == step, decode(got), u_in[...]))


def spread_forward(
    t_in, n_first, got2, sp_own, gg_second, g_second, gg_group, g_group, x5, x5_rest, kept, rest_own, local
):
    half = n_first.shape[1]
    _, first_pair, _ = where_am_i()
    s0, _ = pair_vectors(sp_own, decode(got2[coded_rows(half // 2, half) :]))
    t_mid = dot(t_in[...], n_first[...], 1, 1) + s0
    rest = g_second[...] - dot(t_mid, gg_second[...])
    keep, send = ordered(first_pair, t_in[...], t_mid)
    x5[...] = code(send)
    x5_rest[...] = code(rest)
    kept[...] = keep
    rest_own[...] = rest
    local[...] = g_group[...] - dot_ready(t_in[...], gg_group)


def pair_states(kept, rest_own, got5, got5_rest, x1, got1, s_own, x3, got3, g_own, x6, own):
    half = x1.shape[1]
    rows = s_own.shape[0]
    first, first_pair, _ = where_am_i()
    t = jnp.concatenate(ordered(first_pair, kept[...], decode(got5)), axis=0)
    rest = jnp.concatenate(ordered(first_pair, rest_own[...], decode(got5_rest)), axis=0)
    m0, m1 = ordered(first, x1[:half], got1[:half])
    s0, _ = ordered(first, s_own[...], got1[half:])
    _, gg1 = ordered(first, x3[:half], got3[:half])
    _, g1 = ordered(first, g_own[...], got3[half:])
    t_mid = dot(t, m0, 1, 1) + s0
    fixed = jnp.where(first_pair, rest, 0.0)
    fixed_mid = dot(fixed, m1) + g1 - dot(t_mid, gg1)
    split = coded_rows(rows, half)
    keep, send = ordered(first, t, t_mid)
    x6[:split] = code(send)
    own[:rows] = keep
    keep, send = ordered(first, fixed_mid, fixed)
    x6[split:] = code(send)
    own[rows:] = keep


def block_parts(solved, p, d, start, maps):
    half = p.shape[1]
    start[...] = dot(solved[...], d[...])
    maps[:half] = dot(p[...], d[...], 0, 0)
    maps[half:] = d[d.shape[0] - half :]


def block_fixed(own, got6, start, maps, fixed_weights):
    rows = own.shape[0] // 2
    split = coded_rows(rows, own.shape[1])
    low = low_traits()
    t = jnp.concatenate(ordered(low, own[:rows], decode(got6[:split])), axis=0)
    above = jnp.concatenate(ordered(low, own[rows:], decode(got6[split:])), axis=0)
    fixed_weights[...] = start[...] - dot(jnp.concatenate([t, above], axis=1), maps[...])


def block_weights(mine, got_u, theirs, their_got, fixed_weights, k, xa, xb):
    half = xa.shape[1]
    first, first_pair, _ = where_am_i()
    near = jnp.concatenate(ordered(first_pair, decode(mine), decode(got_u)), axis=0)
    far = jnp.concatenate(ordered(first_pair, decode(theirs), decode(their_got)), axis=0)
    u = jnp.concatenate(ordered(low_traits(), near, far), axis=0)
    weights = (fixed_weights[...] - dot_ready(u, k)).astype(bf16)
    a, b = ordered(first, weights[:, :half], weights[:, half:])
    xa[...] = a
    xb[...] = b


def contract(values, coefs):
    return lax.dot_general(values, coefs, (((1,), (1,)), ((), ())), preferred_element_type=f32)


def mask_coefs(coefs_in, anchor_in, masked, coefs, anchor, sems):
    untyped, span = coefs.shape
    half = span // 4
    typed = span - 2 * half
    tile = 128
    place = lax.axis_index(AXIS)
    total = lax.axis_size(AXIS) * typed
    copies = [pltpu.make_async_copy(anchor_in, anchor, sems.at[0])]
    for i in range(untyped // tile):
        rows = pl.ds(i * tile, tile)
        copies.append(pltpu.make_async_copy(coefs_in.at[rows], coefs.at[rows], sems.at[i + 1]))
    for copy in copies:
        copy.start()
    copies[0].wait()
    first_column = place * typed - half
    for i in range(untyped // tile):
        rows = pl.ds(i * tile, tile)
        nearest = jnp.broadcast_to(anchor[:, i * tile : (i + 1) * tile], (tile, tile)).T
        copies[i + 1].wait()
        for j in range(span // tile):
            lanes = pl.ds(j * tile, tile)
            columns = first_column + j * tile + lax.broadcasted_iota(jnp.int32, (tile, tile), 1)
            within = (jnp.abs(columns - nearest) <= half) & (columns >= 0) & (columns < total)
            masked[rows, lanes] = jnp.where(within, coefs[rows, lanes].astype(f32), 0.0).astype(bf16)


def impute_own(xa, xb, masked, out):
    first, _, _ = where_am_i()
    half = xa.shape[1]
    span = masked.shape[1]
    weights = jnp.concatenate(ordered(first, xa[...], xb[...]), axis=1)
    out[...] = contract(weights, masked[:, half : span - half])


def impute_edges(acc, got_a, got_b, masked, out):
    first, _, _ = where_am_i()
    half = got_a.shape[1]
    span = masked.shape[1]
    left, right = ordered(first, got_a[...], got_b[...])
    out[...] = acc[...] + contract(left, masked[:, :half]) + contract(right, masked[:, span - half :])


def swap(block, distance):
    n = lax.axis_size(AXIS)
    return lax.ppermute(block, AXIS, [(i, i ^ distance) for i in range(n)])


def hop(block, step):
    pairs = []
    for i in range(lax.axis_size(AXIS)):
        g = i // GROUP
        pairs.append((i, i + GROUP if g == step else i - GROUP if g == step + 1 else i ^ 1))
    return lax.ppermute(block, AXIS, pairs)


def swap_chips(block):
    n, segments = lax.axis_size(AXIS), lax.axis_size(SEGMENTS)
    pairs = []
    for seg in range(segments):
        for i in range(n):
            to, to_seg = i + 1 if i % 2 else i - 1, seg
            if not 0 <= to < n:
                to, to_seg = (i, seg ^ 1) if segments % 2 == 0 else (to % n, seg)
            pairs.append((seg * n + i, to_seg * n + to))
    return lax.ppermute(block, (SEGMENTS, AXIS), pairs)


def per_device(z, diag_inverse, coupling, impute_coef, anchor):
    d = diag_inverse[0]
    c = coupling[0]
    typed = d.shape[0]
    half = c.shape[1]
    traits = z.shape[0]
    untyped, span = impute_coef.shape
    assert span == typed + 2 * half and typed == 2 * half
    assert lax.axis_size(AXIS) >= 3 * GROUP
    groups = lax.axis_size(AXIS) // GROUP
    two, four = traits // 2, traits // 4
    square = (half, half)
    sq, h2, h4 = (square, f32), ((two, half), f32), ((four, half), f32)
    x1_shape, x6_shape = ((half + two, half), f32), ((2 * two, half), f32)
    x6_coded = ((2 * coded_rows(two, half), LANES), i16)
    coded = ((coded_rows(four, half), LANES), i16)
    coded_half = ((coded_rows(half // 2, half), LANES), i16)
    mixed = ((coded_rows(half // 2, half) + coded_rows(four, half), LANES), i16)

    solved_shape, p_shape = ((traits, typed), f32), ((typed, half), f32)
    x1, s_own, z, d, c = call(
        tail_part, [x1_shape, h2, solved_shape, ((typed, typed), f32), p_shape], z, d, c,
        hbm=True, scratch=[pltpu.SemaphoreType.DMA((7,))],
    )
    got1 = swap(x1, 1)
    x3, g_own, solved, p = call(
        head_part, [x1_shape, h2, solved_shape, p_shape], z, d, c, x1, s_own
    )
    x2, n_own, sp_own = call(pair_forward, [mixed, sq, h4], x1, got1, s_own, after=(p,))
    got2 = swap(x2, 3)
    got3 = swap(x3, 1)
    masked = call(
        mask_coefs, ((untyped, span), bf16), impute_coef, anchor[None, :], after=(x2,), hbm=True,
        scratch=[
            pltpu.VMEM((untyped, span), bf16),
            pltpu.VMEM((1, untyped), jnp.int32),
            pltpu.SemaphoreType.DMA((untyped // 128 + 1,)),
        ],
    )
    x4, gg_own, gp_own = call(
        pair_backward, [mixed, sq, h4], x1, got1, s_own, x3, got3, g_own, after=(x2,)
    )
    got2_core = swap(call(relay, coded_half, got2, after=(x4, masked)), 1)
    out = call(group_forward, coded, n_own, got2, got2_core, sp_own)
    parts3 = ((3 * half, half), bf16)
    s_group, up, down, n_first, n_second = call(
        group_map, [h4, parts3, parts3, sq, sq], n_own, got2, got2_core, sp_own, after=(out,)
    )
    k = call(block_map, ((3 * half, typed), bf16), n_second, x1, got1, d)
    t_in = jnp.zeros((four, half), f32)
    got4 = swap(x4, 3)
    for step in range(groups - 2):
        got = hop(out, step)
        t_in, out = call(
            functools.partial(forward_hop, step), [h4, coded], got, t_in, up, s_group,
            after=(k,) if step == 0 else (),
        )
        if step == 0:
            pieces = [((half // 2 + SCALES, LANES), i16)] * 2
            low, high = call(relay_halves, pieces, got4, after=(out,))
            got4_low, got4_high = swap(low, 1), swap(high, 1)
    gg_group, g_group, gg_second, g_second = call(
        group_backward, [parts3, h4, sq, h4],
        n_first, got2, sp_own, gg_own, got4, got4_low, got4_high, gp_own, after=(out,),
    )
    last = groups - 2
    got = hop(out, last)
    t_in, out = call(
        functools.partial(turn, last), [h4, coded], got, t_in, gg_group, g_group
    )

    u_in = jnp.zeros((four, half), f32)
    for step in reversed(range(groups - 1)):
        got = hop(out, step)
        if step == last:
            x5, x5_rest, kept, rest_own, local = call(
                spread_forward, [coded, coded, h4, h4, h4],
                t_in, n_first, got2, sp_own, gg_second, g_second, gg_group, g_group, after=(out,),
            )
            got5, got5_rest = swap(x5, 3), swap(x5_rest, 3)
        if step:
            u_in, out = call(
                functools.partial(backward_hop, step), [h4, coded], got, u_in, down, local
            )
        else:
            start, maps = call(
                block_parts, [solved_shape, ((2 * half, typed), f32)], solved, p, d, after=(out,)
            )
            out = call(functools.partial(arrive, step), coded, got, u_in, after=(maps,))
    x6, own = call(
        pair_states, [x6_coded, x6_shape], kept, rest_own, got5, got5_rest, x1, got1, s_own, x3, got3, g_own
    )
    got6 = swap(x6, 1)
    fixed = call(block_fixed, solved_shape, own, got6, start, maps)
    theirs = swap(out, 1)
    got_u = swap(out, 3)
    their_got = swap(got_u, 1)
    edge = (square, bf16)
    xa, xb = call(block_weights, [edge, edge], out, got_u, theirs, their_got, fixed, k)
    got_a = swap_chips(xa)
    got_b = swap(xb, 1)
    acc = call(impute_own, ((traits, untyped), f32), xa, xb, masked)
    return call(
        impute_edges, ((traits, untyped), f32), acc, got_a, got_b, masked, last=True
    )


def solution(mesh):
    in_specs = (
        P(None, (SEGMENTS, AXIS)),
        P((SEGMENTS, AXIS), None, None),
        P((SEGMENTS, AXIS), None, None),
        P((SEGMENTS, AXIS), None),
        P((SEGMENTS, AXIS)),
    )
    return jax.shard_map(
        per_device, mesh=mesh, in_specs=in_specs, out_specs=P(None, (SEGMENTS, AXIS)), check_vma=False
    )
```

```python
import functools

import jax
import jax.numpy as jnp
from jax import lax
from jax.experimental import pallas as pl
from jax.experimental.pallas import tpu as pltpu
from jax.sharding import PartitionSpec as P

AXIS = "genome"
SEGMENTS = "seg"
GROUP = 4
f32 = jnp.float32
bf16 = jnp.bfloat16
i16 = jnp.int16
SCALES = 16
LANES = 128
LIMIT = 32767.0


def parts(x):
    high = x.astype(bf16)
    return high, (x - high.astype(f32)).astype(bf16)


def dot(a, b, ca=1, cb=0):
    ah, al = parts(a)
    bh, bl = parts(b)
    return lax.dot_general(
        jnp.concatenate([al, ah, ah], axis=ca),
        jnp.concatenate([bh, bl, bh], axis=cb),
        (((ca,), (cb,)), ((), ())),
        preferred_element_type=f32,
    )


def code(x):
    top = jnp.maximum(jnp.max(jnp.abs(x), axis=0, keepdims=True), 1e-32)
    power = jnp.ceil(jnp.log2(top) * 4.0)
    root = jnp.exp2(power * -0.125)
    steps = jnp.floor(x * root * (root * LIMIT) + 0.5)
    steps = jnp.clip(steps, -LIMIT, LIMIT)
    tiles = x.shape[1] // LANES
    powers = jnp.broadcast_to(power, (SCALES // tiles, x.shape[1]))
    pieces = [v[:, i * LANES : (i + 1) * LANES] for v in (steps, powers) for i in range(tiles)]
    return jnp.concatenate(pieces, axis=0).astype(jnp.int32).astype(i16)


def decode(coded, tiles=2):
    rows = (coded.shape[0] - SCALES) // tiles
    values = coded[...].astype(jnp.int32).astype(f32)
    columns = []
    for i in range(tiles):
        at = tiles * rows + i * (SCALES // tiles)
        root = jnp.exp2(values[at : at + 1] * 0.125)
        columns.append(values[i * rows : (i + 1) * rows] * (root / LIMIT) * root)
    return jnp.concatenate(columns, axis=1)


def coded_rows(rows, columns):
    return rows * (columns // LANES) + SCALES


def where_am_i():
    place = lax.axis_index(AXIS)
    return place % 2 == 0, (place // 2) % 2 == 0, place // GROUP


def ready(b):
    bh, bl = parts(b)
    return jnp.concatenate([bh, bl, bh], axis=0)


def dot_ready(a, b):
    ah, al = parts(a)
    return jnp.dot(jnp.concatenate([al, ah, ah], axis=1), b[...], preferred_element_type=f32)


def ordered(first, own, other):
    return jnp.where(first, own, other), jnp.where(first, other, own)


def call(kernel, outs, *args, after=(), hbm=False, last=False, scratch=()):
    n_in, n_after = len(args), len(after)

    def body(*refs):
        kernel(*refs[:n_in], *refs[n_in + n_after :])

    single = not isinstance(outs, list)
    shapes = [outs] if single else outs
    vmem = pl.BlockSpec(memory_space=pltpu.VMEM)
    anywhere = pl.BlockSpec(memory_space=pl.ANY)
    if hbm:
        args = [pltpu.with_memory_space_constraint(a, pltpu.HBM) for a in args]
    got = pl.pallas_call(
        body,
        out_shape=[jax.ShapeDtypeStruct(s, t) if last else pltpu.VMEM(s, t) for s, t in shapes],
        in_specs=[anywhere if hbm else vmem] * n_in + [anywhere] * n_after,
        out_specs=[vmem] * len(shapes),
        scratch_shapes=scratch,
        compiler_params=pltpu.CompilerParams(vmem_limit_bytes=8 * 2**20),
        name=kernel.__name__ if hasattr(kernel, "__name__") else kernel.func.__name__,
    )(*args, *after)
    return got[0] if single else got


def tail_part(z_in, d_in, c_in, x1, z, d, c, sems):
    typed, half = c.shape
    head = typed - half
    step = typed // 2
    copies = []
    for i in range(2):
        here = pl.ds(i * step, step)
        tail = (pl.ds(head, half), here)
        copies.append(pltpu.make_async_copy(d_in.at[tail], d.at[tail], sems.at[3 * i]))
        copies.append(pltpu.make_async_copy(c_in.at[here], c.at[here], sems.at[3 * i + 1]))
        copies.append(pltpu.make_async_copy(z_in.at[:, here], z.at[:, here], sems.at[3 * i + 2]))
    rest = pl.ds(0, head)
    copies.append(pltpu.make_async_copy(d_in.at[rest], d.at[rest], sems.at[6]))
    for copy in copies:
        copy.start()
    m = s = 0.0
    for i in range(2):
        here = pl.ds(i * step, step)
        for copy in copies[3 * i : 3 * i + 3]:
            copy.wait()
        tail = d[head:, here]
        m = m - dot(tail, c[here])
        s = s + dot(z[:, here], tail, 1, 1)
    x1[:half] = m
    x1[half:] = s
    copies[6].wait()


def head_part(z, d, c, x1, x3, solved, p):
    half = c.shape[1]
    head = d.shape[0] - half
    p[:head] = dot(d[:head], c[...])
    p[head:] = -x1[:half]
    solved[:, :head] = dot(z[...], d[:head], 1, 1)
    solved[:, head:] = x1[half:]
    x3[:half] = dot(p[...], p[...], 0, 0)
    x3[half:] = dot(solved[...], p[...])


def pair_forward(x1, got1, x2, n_own, s_keep):
    half = x1.shape[1]
    _, first_pair, _ = where_am_i()
    m1 = x1[:half]
    n = dot(m1, got1[:half])
    s = dot(got1[half:], m1, 1, 1) + x1[half:]
    rows = s.shape[0] // 2
    keep, send = ordered(first_pair, s[:rows], s[rows:])
    split = coded_rows(half, half)
    x2[:split] = code(n)
    x2[split:] = code(send)
    n_own[...] = n
    s_keep[...] = keep


def pair_backward(x1, got1, x3, got3, x4, gg_own, g_keep):
    half = x1.shape[1]
    _, first_pair, _ = where_am_i()
    m0 = got1[:half]
    gg1 = x3[:half]
    both = dot(jnp.concatenate([gg1, x3[half:] - dot(got1[half:], gg1)], axis=0), m0)
    gg = dot(m0, both[:half], 0, 0) + got3[:half]
    g = both[half:] + got3[half:]
    rows = g.shape[0] // 2
    keep, send = ordered(first_pair, g[:rows], g[rows:])
    split = coded_rows(half, half)
    x4[:split] = code(gg)
    x4[split:] = code(send)
    gg_own[...] = gg
    g_keep[...] = keep


def both_pairs(own, own_rows, got):
    _, first_pair, _ = where_am_i()
    split = coded_rows(own.shape[1], own.shape[1])
    m0, m1 = ordered(first_pair, own[...], decode(got[:split]))
    v0, v1 = ordered(first_pair, own_rows[...], decode(got[split:]))
    return m0, v0, m1, v1


def group_forward(n_own, got2, s_keep, out):
    _, _, group = where_am_i()
    out[...] = jnp.zeros_like(out)

    @pl.when(group == 0)
    def _():
        _, s0, n1, s1 = both_pairs(n_own, s_keep, got2)
        out[...] = code(dot(s0, n1, 1, 1) + s1)


def group_map(n_own, got2, s_keep, x1, s_group, up, down, n_first, s_first, above, x7):
    half = n_own.shape[1]
    _, first_pair, _ = where_am_i()
    n0, s0, n1, s1 = both_pairs(n_own, s_keep, got2)
    s_group[...] = dot(s0, n1, 1, 1) + s1
    n_first[...] = n0
    s_first[...] = s0
    n_group = dot(n1, n0)
    up[...] = ready(n_group.T)
    down[...] = ready(n_group)
    rows = lax.broadcasted_iota(jnp.int32, (half, half), 0)
    columns = lax.broadcasted_iota(jnp.int32, (half, half), 1)
    pair_above = jnp.where(first_pair, n1, (rows == columns).astype(f32))
    above[...] = pair_above
    x7[...] = code(dot(pair_above, x1[:half]))


def block_map(above, got7, d, k):
    half = above.shape[1]
    first, _, _ = where_am_i()
    here = jnp.where(first, decode(got7), above[...])
    k[...] = ready(dot(here, d[d.shape[0] - half :]))


def group_backward(n_first, s_first, gg_own, got4, g_keep, gg_group, g_group, gg_second, g_second):
    half = n_first.shape[1]
    n0 = n_first[...]
    gg0, g0, gg1, g1 = both_pairs(gg_own, g_keep, got4)
    gg_second[...] = gg1
    g_second[...] = g1
    both = dot(jnp.concatenate([gg1, g1 - dot(s_first[...], gg1)], axis=0), n0)
    gg_group[...] = ready(dot(n0, both[:half], 0, 0) + gg0)
    g_group[...] = both[half:] + g0


def forward_hop(step, got, t_in, up, s_group, t_out, out):
    _, _, group = where_am_i()
    t = jnp.where(group == step + 1, decode(got), t_in[...])
    t_out[...] = t
    out[...] = code(dot_ready(t, up) + s_group[...])


def turn(step, got, t_in, gg_group, g_group, t_out, out):
    _, _, group = where_am_i()
    t = jnp.where(group == step + 1, decode(got), t_in[...])
    t_out[...] = t
    out[...] = jnp.zeros_like(out)

    @pl.when(group == step + 1)
    def _():
        out[...] = code(g_group[...] - dot_ready(t, gg_group))


def backward_hop(step, got, u_in, down, local, u_out, out):
    _, _, group = where_am_i()
    u = jnp.where(group == step, decode(got), u_in[...])
    u_out[...] = u
    out[...] = code(dot_ready(u, down) + local[...])


def arrive(step, got, u_in, out):
    _, _, group = where_am_i()
    out[...] = code(jnp.where(group == step, decode(got), u_in[...]))


def spread_forward(
    t_in, n_first, s_first, gg_second, g_second, gg_group, g_group, x5, x5_rest, kept, rest_own, local
):
    _, first_pair, _ = where_am_i()
    t_mid = dot(t_in[...], n_first[...], 1, 1) + s_first[...]
    rest = g_second[...] - dot(t_mid, gg_second[...])
    keep, send = ordered(first_pair, t_in[...], t_mid)
    x5[...] = code(send)
    x5_rest[...] = code(rest)
    kept[...] = keep
    rest_own[...] = rest
    local[...] = g_group[...] - dot_ready(t_in[...], gg_group)


def pair_states(kept, rest_own, got5, got5_rest, x1, got1, x3, x6, own):
    half = x1.shape[1]
    _, first_pair, _ = where_am_i()
    t = jnp.concatenate(ordered(first_pair, kept[...], decode(got5)), axis=0)
    rest = jnp.concatenate(ordered(first_pair, rest_own[...], decode(got5_rest)), axis=0)
    t_mid = dot(t, got1[:half], 1, 1) + got1[half:]
    fixed = jnp.where(first_pair, rest, 0.0)
    fixed_mid = dot(fixed, x1[:half]) + x3[half:] - dot(t_mid, x3[:half])
    split = coded_rows(t.shape[0], half)
    x6[:split] = code(t)
    x6[split:] = code(fixed_mid)
    own[: t.shape[0]] = t_mid
    own[t.shape[0] :] = fixed


def block_parts(solved, p, d, start, maps):
    half = p.shape[1]
    start[...] = dot(solved[...], d[...])
    maps[:half] = dot(p[...], d[...], 0, 0)
    maps[half:] = d[d.shape[0] - half :]


def block_fixed(own, got6, start, maps, fixed_weights):
    rows = own.shape[0] // 2
    split = coded_rows(rows, own.shape[1])
    first, _, _ = where_am_i()
    t = jnp.where(first, decode(got6[:split]), own[:rows])
    above = jnp.where(first, decode(got6[split:]), own[rows:])
    fixed_weights[...] = start[...] - dot(jnp.concatenate([t, above], axis=1), maps[...])


def gather(mine, got_u, both):
    rows = mine.shape[0]
    both[:rows] = mine[...]
    both[rows:] = got_u[...]


def block_weights(both, got_both, fixed_weights, k, xa, xb):
    half = xa.shape[1]
    first, first_pair, _ = where_am_i()
    rows = both.shape[0] // 2
    coded = jnp.where(first, got_both[...].astype(jnp.int32), both[...].astype(jnp.int32))
    u = jnp.concatenate(ordered(first_pair, decode(coded[:rows]), decode(coded[rows:])), axis=0)
    weights = (fixed_weights[...] - dot_ready(u, k)).astype(bf16)
    a, b = ordered(first, weights[:, :half], weights[:, half:])
    xa[...] = a
    xb[...] = b


def contract(values, coefs):
    return lax.dot_general(values, coefs, (((1,), (1,)), ((), ())), preferred_element_type=f32)


def mask_coefs(coefs_in, anchor_in, masked, coefs, anchor, sems):
    untyped, span = coefs.shape
    half = span // 4
    typed = span - 2 * half
    tile = 128
    place = lax.axis_index(AXIS)
    total = lax.axis_size(AXIS) * typed
    copies = [pltpu.make_async_copy(anchor_in, anchor, sems.at[0])]
    for i in range(untyped // tile):
        rows = pl.ds(i * tile, tile)
        copies.append(pltpu.make_async_copy(coefs_in.at[rows], coefs.at[rows], sems.at[i + 1]))
    for copy in copies:
        copy.start()
    copies[0].wait()
    first_column = place * typed - half
    for i in range(untyped // tile):
        rows = pl.ds(i * tile, tile)
        nearest = jnp.broadcast_to(anchor[:, i * tile : (i + 1) * tile], (tile, tile)).T
        copies[i + 1].wait()
        for j in range(span // tile):
            lanes = pl.ds(j * tile, tile)
            columns = first_column + j * tile + lax.broadcasted_iota(jnp.int32, (tile, tile), 1)
            within = (jnp.abs(columns - nearest) <= half) & (columns >= 0) & (columns < total)
            masked[rows, lanes] = jnp.where(within, coefs[rows, lanes].astype(f32), 0.0).astype(bf16)


def impute_own(xa, xb, masked, out):
    first, _, _ = where_am_i()
    half = xa.shape[1]
    span = masked.shape[1]
    weights = jnp.concatenate(ordered(first, xa[...], xb[...]), axis=1)
    out[...] = contract(weights, masked[:, half : span - half])


def impute_edges(acc, got_a, got_b, masked, out):
    first, _, _ = where_am_i()
    half = got_a.shape[1]
    span = masked.shape[1]
    left, right = ordered(first, got_a[...], got_b[...])
    out[...] = acc[...] + contract(left, masked[:, :half]) + contract(right, masked[:, span - half :])


def permute(block, partner):
    n, segments = lax.axis_size(AXIS), lax.axis_size(SEGMENTS)
    pairs = []
    for seg in range(segments):
        for i in range(n):
            to, to_seg = partner(i), seg
            if to is None:
                to, to_seg = (i, seg ^ 1) if segments % 2 == 0 else (i ^ 2, seg)
            pairs.append((seg * n + i, to_seg * n + to))
    return lax.ppermute(block, (SEGMENTS, AXIS), pairs)


def swap_cores(block):
    return permute(block, lambda i: i ^ 1)


def swap_pairs(block):
    return permute(block, lambda i: i ^ 2 if i % 2 else None)


def hop(block, step):
    def partner(i):
        g = i // GROUP
        if g not in (step, step + 1):
            return i ^ 1
        if i % 2 == 0:
            return None
        return i + GROUP if g == step else i - GROUP

    return permute(block, partner)


def swap_chips(block):
    n, segments = lax.axis_size(AXIS), lax.axis_size(SEGMENTS)
    pairs = []
    for seg in range(segments):
        for i in range(n):
            to, to_seg = i + 1 if i % 2 else i - 1, seg
            if not 0 <= to < n:
                to, to_seg = (i, seg ^ 1) if segments % 2 == 0 else (to % n, seg)
            pairs.append((seg * n + i, to_seg * n + to))
    return lax.ppermute(block, (SEGMENTS, AXIS), pairs)


def per_device(z, diag_inverse, coupling, impute_coef, anchor):
    d = diag_inverse[0]
    c = coupling[0]
    typed = d.shape[0]
    half = c.shape[1]
    traits = z.shape[0]
    untyped, span = impute_coef.shape
    assert span == typed + 2 * half and typed == 2 * half
    assert lax.axis_size(AXIS) >= 3 * GROUP
    groups = lax.axis_size(AXIS) // GROUP
    two = traits // 2
    square = (half, half)
    sq, h2 = (square, f32), ((two, half), f32)
    stacked = ((half + traits, half), f32)
    both_states = ((2 * traits, half), f32)
    coded = ((coded_rows(two, half), LANES), i16)
    coded_both = ((2 * coded_rows(two, half), LANES), i16)
    coded_square = ((coded_rows(half, half), LANES), i16)
    coded_states = ((2 * coded_rows(traits, half), LANES), i16)
    mixed = ((coded_rows(half, half) + coded_rows(two, half), LANES), i16)
    parts3 = ((3 * half, half), bf16)
    solved_shape, p_shape = ((traits, typed), f32), ((typed, half), f32)

    x1, z, d, c = call(
        tail_part, [stacked, solved_shape, ((typed, typed), f32), p_shape], z, d, c,
        hbm=True, scratch=[pltpu.SemaphoreType.DMA((7,))],
    )
    got1 = swap_cores(x1)
    x3, solved, p = call(head_part, [stacked, solved_shape, p_shape], z, d, c, x1)
    x2, n_own, s_keep = call(pair_forward, [mixed, sq, h2], x1, got1, after=(p,))
    got2 = swap_pairs(x2)
    got3 = swap_cores(x3)
    masked = call(
        mask_coefs, ((untyped, span), bf16), impute_coef, anchor[None, :], after=(x2,), hbm=True,
        scratch=[
            pltpu.VMEM((untyped, span), bf16),
            pltpu.VMEM((1, untyped), jnp.int32),
            pltpu.SemaphoreType.DMA((untyped // 128 + 1,)),
        ],
    )
    x4, gg_own, g_keep = call(
        pair_backward, [mixed, sq, h2], x1, got1, x3, got3, after=(x2,)
    )
    out = call(group_forward, coded, n_own, got2, s_keep, after=(x4, masked))
    s_group, up, down, n_first, s_first, above, x7 = call(
        group_map, [h2, parts3, parts3, sq, h2, sq, coded_square], n_own, got2, s_keep, x1, after=(out,)
    )
    got7 = swap_cores(x7)
    got4 = swap_pairs(x4)

    t_in = jnp.zeros((two, half), f32)
    for step in range(groups - 2):
        got = hop(out, step)
        t_in, out = call(
            functools.partial(forward_hop, step), [h2, coded], got, t_in, up, s_group,
            after=(maps,) if step == 1 else (),
        )
        if step == 0:
            start, maps = call(
                block_parts, [solved_shape, ((2 * half, typed), f32)], solved, p, d, after=(out,)
            )
    gg_group, g_group, gg_second, g_second = call(
        group_backward, [parts3, h2, sq, h2], n_first, s_first, gg_own, got4, g_keep, after=(out,)
    )
    last = groups - 2
    got = hop(out, last)
    t_in, out = call(
        functools.partial(turn, last), [h2, coded], got, t_in, gg_group, g_group
    )

    k = call(block_map, ((3 * half, typed), bf16), above, got7, d, after=(out,))

    u_in = jnp.zeros((two, half), f32)
    for step in reversed(range(groups - 1)):
        got = hop(out, step)
        if step == last:
            x5, x5_rest, kept, rest_own, local = call(
                spread_forward, [coded, coded, h2, h2, h2],
                t_in, n_first, s_first, gg_second, g_second, gg_group, g_group, after=(out, k),
            )
            got5, got5_rest = swap_pairs(x5), swap_pairs(x5_rest)
        if step:
            u_in, out = call(
                functools.partial(backward_hop, step), [h2, coded], got, u_in, down, local
            )
        else:
            out = call(functools.partial(arrive, step), coded, got, u_in)
    x6, own = call(
        pair_states, [coded_states, both_states], kept, rest_own, got5, got5_rest, x1, got1, x3
    )
    got6 = swap_cores(x6)
    fixed = call(block_fixed, solved_shape, own, got6, start, maps)
    both = call(gather, coded_both, out, swap_pairs(out))
    got_both = swap_cores(both)
    edge = (square, bf16)
    xa, xb = call(block_weights, [edge, edge], both, got_both, fixed, k)
    got_a = swap_chips(xa)
    got_b = swap_cores(xb)
    acc = call(impute_own, ((traits, untyped), f32), xa, xb, masked)
    return call(
        impute_edges, ((traits, untyped), f32), acc, got_a, got_b, masked, last=True
    )


def solution(mesh):
    in_specs = (
        P(None, (SEGMENTS, AXIS)),
        P((SEGMENTS, AXIS), None, None),
        P((SEGMENTS, AXIS), None, None),
        P((SEGMENTS, AXIS), None),
        P((SEGMENTS, AXIS)),
    )
    return jax.shard_map(
        per_device, mesh=mesh, in_specs=in_specs, out_specs=P(None, (SEGMENTS, AXIS)), check_vma=False
    )
```

```python
import functools

import jax
import jax.numpy as jnp
from jax import lax
from jax.experimental import pallas as pl
from jax.experimental.pallas import tpu as pltpu
from jax.sharding import PartitionSpec as P

AXIS = "genome"
SEGMENTS = "seg"
GROUP = 4
f32 = jnp.float32
bf16 = jnp.bfloat16
i16 = jnp.int16
SCALES = 16
LANES = 128
LIMIT = 32767.0


def parts(x):
    high = x.astype(bf16)
    return high, (x - high.astype(f32)).astype(bf16)


def dot(a, b, ca=1, cb=0):
    ah, al = parts(a)
    bh, bl = parts(b)
    return lax.dot_general(
        jnp.concatenate([al, ah, ah], axis=ca),
        jnp.concatenate([bh, bl, bh], axis=cb),
        (((ca,), (cb,)), ((), ())),
        preferred_element_type=f32,
    )


def code(x):
    top = jnp.maximum(jnp.max(jnp.abs(x), axis=0, keepdims=True), 1e-32)
    power = jnp.ceil(jnp.log2(top) * 4.0)
    root = jnp.exp2(power * -0.125)
    steps = jnp.floor(x * root * (root * LIMIT) + 0.5)
    steps = jnp.clip(steps, -LIMIT, LIMIT)
    tiles = x.shape[1] // LANES
    powers = jnp.broadcast_to(power, (SCALES // tiles, x.shape[1]))
    pieces = [v[:, i * LANES : (i + 1) * LANES] for v in (steps, powers) for i in range(tiles)]
    return jnp.concatenate(pieces, axis=0).astype(jnp.int32).astype(i16)


def decode(coded, tiles=2):
    rows = (coded.shape[0] - SCALES) // tiles
    values = coded[...].astype(jnp.int32).astype(f32)
    columns = []
    for i in range(tiles):
        at = tiles * rows + i * (SCALES // tiles)
        root = jnp.exp2(values[at : at + 1] * 0.125)
        columns.append(values[i * rows : (i + 1) * rows] * (root / LIMIT) * root)
    return jnp.concatenate(columns, axis=1)


def coded_rows(rows, columns):
    return rows * (columns // LANES) + SCALES


def where_am_i():
    place = lax.axis_index(AXIS)
    return place % 2 == 0, (place // 2) % 2 == 0, place // GROUP


def ready(b):
    bh, bl = parts(b)
    return jnp.concatenate([bh, bl, bh], axis=0)


def dot_ready(a, b):
    ah, al = parts(a)
    return jnp.dot(jnp.concatenate([al, ah, ah], axis=1), b[...], preferred_element_type=f32)


def low_traits():
    place = lax.axis_index(AXIS)
    return (place + place // 2 + place // GROUP) % 2 == 0


def ordered(first, own, other):
    return jnp.where(first, own, other), jnp.where(first, other, own)


def call(kernel, outs, *args, after=(), hbm=False, last=False, scratch=()):
    n_in, n_after = len(args), len(after)

    def body(*refs):
        kernel(*refs[:n_in], *refs[n_in + n_after :])

    single = not isinstance(outs, list)
    shapes = [outs] if single else outs
    vmem = pl.BlockSpec(memory_space=pltpu.VMEM)
    anywhere = pl.BlockSpec(memory_space=pl.ANY)
    if hbm:
        args = [pltpu.with_memory_space_constraint(a, pltpu.HBM) for a in args]
    got = pl.pallas_call(
        body,
        out_shape=[jax.ShapeDtypeStruct(s, t) if last else pltpu.VMEM(s, t) for s, t in shapes],
        in_specs=[anywhere if hbm else vmem] * n_in + [anywhere] * n_after,
        out_specs=[vmem] * len(shapes),
        scratch_shapes=scratch,
        compiler_params=pltpu.CompilerParams(vmem_limit_bytes=8 * 2**20),
        name=kernel.__name__ if hasattr(kernel, "__name__") else kernel.func.__name__,
    )(*args, *after)
    return got[0] if single else got


def tail_part(z_in, d_in, c_in, x1, s_own, z, d, c, sems):
    typed, half = c.shape
    rows = z.shape[0] // 2
    head = typed - half
    step = typed // 2
    copies = []
    for i in range(2):
        here = pl.ds(i * step, step)
        tail = (pl.ds(head, half), here)
        copies.append(pltpu.make_async_copy(d_in.at[tail], d.at[tail], sems.at[3 * i]))
        copies.append(pltpu.make_async_copy(c_in.at[here], c.at[here], sems.at[3 * i + 1]))
        copies.append(pltpu.make_async_copy(z_in.at[:, here], z.at[:, here], sems.at[3 * i + 2]))
    rest = pl.ds(0, head)
    copies.append(pltpu.make_async_copy(d_in.at[rest], d.at[rest], sems.at[6]))
    for copy in copies:
        copy.start()
    m = s = 0.0
    for i in range(2):
        here = pl.ds(i * step, step)
        for copy in copies[3 * i : 3 * i + 3]:
            copy.wait()
        tail = d[head:, here]
        m = m - dot(tail, c[here])
        s = s + dot(z[:, here], tail, 1, 1)
    x1[:half] = m
    keep, send = ordered(low_traits(), s[:rows], s[rows:])
    x1[half:] = send
    s_own[...] = keep
    copies[6].wait()


def head_part(z, d, c, x1, s_own, x3, g_own, solved, p):
    half = c.shape[1]
    rows = z.shape[0] // 2
    head = d.shape[0] - half
    first, _, _ = where_am_i()
    p[:head] = dot(d[:head], c[...])
    p[head:] = -x1[:half]
    solved[:, :head] = dot(z[...], d[:head], 1, 1)
    low, high = ordered(low_traits(), s_own[...], x1[half:])
    solved[:rows, head:] = low
    solved[rows:, head:] = high
    g = dot(solved[...], p[...])
    keep, send = ordered(low_traits(), g[:rows], g[rows:])
    x3[:half] = dot(p[...], p[...], 0, 0)
    x3[half:] = send
    g_own[...] = keep


def pair_forward(x1, got1, s_own, x2, n_own, sp_own):
    half = x1.shape[1]
    first, first_pair, _ = where_am_i()
    m0, m1 = ordered(first, x1[:half], got1[:half])
    s0, s1 = ordered(first, s_own[...], got1[half:])
    n = dot(m1, m0)
    n_own[...] = n
    split = coded_rows(half, half)
    x2[:split] = code(n)
    s = dot(s0, m1, 1, 1) + s1
    rows = s.shape[0] // 2
    keep, send = ordered(first_pair, s[:rows], s[rows:])
    x2[split:] = code(send)
    sp_own[...] = keep


def pair_backward(x1, got1, s_own, x3, got3, g_own, x4, gg_own, gp_own):
    half = x1.shape[1]
    first, first_pair, _ = where_am_i()
    m0, _ = ordered(first, x1[:half], got1[:half])
    s0, _ = ordered(first, s_own[...], got1[half:])
    gg0, gg1 = ordered(first, x3[:half], got3[:half])
    g0, g1 = ordered(first, g_own[...], got3[half:])
    both = dot(jnp.concatenate([gg1, g1 - dot(s0, gg1)], axis=0), m0)
    gg = dot(m0, both[:half], 0, 0) + gg0
    gg_own[...] = gg
    split = coded_rows(half // 2, half)
    x4[:split] = code(jnp.where(first, gg[: half // 2], gg[half // 2 :]))
    g = both[half:] + g0
    rows = g.shape[0] // 2
    keep, send = ordered(first_pair, g[:rows], g[rows:])
    x4[split:] = code(send)
    gp_own[...] = keep


def pair_matrices(own, got, got_core):
    first, first_pair, _ = where_am_i()
    other = jnp.concatenate(ordered(first, got_core, got), axis=0)
    return ordered(first_pair, own[...], other)


def pair_vectors(own, got):
    _, first_pair, _ = where_am_i()
    return ordered(first_pair, own[...], got)


def relay(got, out):
    out[...] = got[: out.shape[0]]


def relay_halves(got, low, high):
    rows = low.shape[0] - SCALES
    low[:rows] = got[:rows]
    high[:rows] = got[rows : 2 * rows]
    low[rows:] = got[2 * rows : 2 * rows + SCALES]
    high[rows:] = got[2 * rows : 2 * rows + SCALES]


def both_pairs(own, own_rows, got):
    _, first_pair, _ = where_am_i()
    split = coded_rows(own.shape[1], own.shape[1])
    m0, m1 = ordered(first_pair, own[...], decode(got[:split]))
    v0, v1 = ordered(first_pair, own_rows[...], decode(got[split:]))
    return m0, v0, m1, v1


def group_forward(n_own, got2, sp_own, out):
    _, _, group = where_am_i()
    out[...] = jnp.zeros_like(out)

    @pl.when(group == 0)
    def _():
        _, s0, n1, s1 = both_pairs(n_own, sp_own, got2)
        out[...] = code(dot(s0, n1, 1, 1) + s1)


def group_map(n_own, got2, sp_own, s_group, up, down, n_first, n_second, s_first):
    n0, s0, n1, s1 = both_pairs(n_own, sp_own, got2)
    s_group[...] = dot(s0, n1, 1, 1) + s1
    s_first[...] = s0
    n_first[...] = n0
    n_second[...] = n1
    n_group = dot(n1, n0)
    up[...] = ready(n_group.T)
    down[...] = ready(n_group)


def block_map(n_second, x1, got1, d, k):
    half = x1.shape[1]
    first, first_pair, _ = where_am_i()
    rows = lax.broadcasted_iota(jnp.int32, (half, half), 0)
    columns = lax.broadcasted_iota(jnp.int32, (half, half), 1)
    unit = (rows == columns).astype(f32)
    _, m1 = ordered(first, x1[:half], got1[:half])
    above = jnp.where(first_pair, n_second[...], unit)
    above = jnp.where(first, dot(above, m1), above)
    k[...] = dot(above, d[d.shape[0] - half :])


def group_backward(
    n_first, s_first, gg_own, got4, got4_low, got4_high, gp_own,
    gg_group, g_group, gg_second, g_second,
):
    half = n_first.shape[1]
    split = coded_rows(half // 2, half)
    n0 = n_first[...]
    rows = got4_low.shape[0] - SCALES
    got4_core = jnp.concatenate([got4_low[:rows], got4_high[...]], axis=0)
    gg0, gg1 = pair_matrices(gg_own, decode(got4[:split]), decode(got4_core))
    g0, g1 = pair_vectors(gp_own, decode(got4[split:]))
    gg_second[...] = gg1
    g_second[...] = g1
    both = dot(jnp.concatenate([gg1, g1 - dot(s_first[...], gg1)], axis=0), n0)
    gg_group[...] = dot(n0, both[:half], 0, 0) + gg0
    g_group[...] = both[half:] + g0


def forward_hop(step, got, t_in, up, s_group, t_out, out):
    _, _, group = where_am_i()
    t = jnp.where(group == step + 1, decode(got), t_in[...])
    t_out[...] = t
    out[...] = code(dot_ready(t, up) + s_group[...])


def turn(step, got, t_in, gg_group, g_group, t_out, out):
    _, _, group = where_am_i()
    t = jnp.where(group == step + 1, decode(got), t_in[...])
    t_out[...] = t
    out[...] = jnp.zeros_like(out)

    @pl.when(group == step + 1)
    def _():
        out[...] = code(g_group[...] - dot(t, gg_group[...]))


def backward_hop(step, got, u_in, down, local, u_out, out):
    _, _, group = where_am_i()
    u = jnp.where(group == step, decode(got), u_in[...])
    u_out[...] = u
    out[...] = code(dot_ready(u, down) + local[...])


def arrive(step, got, u_in, out):
    _, _, group = where_am_i()
    out[...] = code(jnp.where(group == step, decode(got), u_in[...]))


def spread_forward(
    t_in, n_first, s_first, gg_second, g_second, gg_group, g_group, x5, x5_rest, kept, rest_own, local
):
    half = n_first.shape[1]
    _, first_pair, _ = where_am_i()
    t_mid = dot(t_in[...], n_first[...], 1, 1) + s_first[...]
    rest = g_second[...] - dot(t_mid, gg_second[...])
    keep, send = ordered(first_pair, t_in[...], t_mid)
    x5[...] = code(send)
    x5_rest[...] = code(rest)
    kept[...] = keep
    rest_own[...] = rest
    local[...] = g_group[...] - dot(t_in[...], gg_group[...])


def pair_states(kept, rest_own, got5, got5_rest, x1, got1, s_own, x3, got3, g_own, x6, own):
    half = x1.shape[1]
    rows = s_own.shape[0]
    first, first_pair, _ = where_am_i()
    t = jnp.concatenate(ordered(first_pair, kept[...], decode(got5)), axis=0)
    rest = jnp.concatenate(ordered(first_pair, rest_own[...], decode(got5_rest)), axis=0)
    m0, m1 = ordered(first, x1[:half], got1[:half])
    s0, _ = ordered(first, s_own[...], got1[half:])
    _, gg1 = ordered(first, x3[:half], got3[:half])
    _, g1 = ordered(first, g_own[...], got3[half:])
    t_mid = dot(t, m0, 1, 1) + s0
    fixed = jnp.where(first_pair, rest, 0.0)
    fixed_mid = dot(fixed, m1) + g1 - dot(t_mid, gg1)
    split = coded_rows(rows, half)
    keep, send = ordered(first, t, t_mid)
    x6[:split] = code(send)
    own[:rows] = keep
    keep, send = ordered(first, fixed_mid, fixed)
    x6[split:] = code(send)
    own[rows:] = keep


def block_parts(solved, p, d, start, maps):
    half = p.shape[1]
    start[...] = dot(solved[...], d[...])
    maps[:half] = dot(p[...], d[...], 0, 0)
    maps[half:] = d[d.shape[0] - half :]


def block_fixed(own, got6, start, maps, fixed_weights):
    rows = own.shape[0] // 2
    split = coded_rows(rows, own.shape[1])
    low = low_traits()
    t = jnp.concatenate(ordered(low, own[:rows], decode(got6[:split])), axis=0)
    above = jnp.concatenate(ordered(low, own[rows:], decode(got6[split:])), axis=0)
    fixed_weights[...] = start[...] - dot(jnp.concatenate([t, above], axis=1), maps[...])


def block_weights(mine, got_u, theirs, their_got, fixed_weights, k, xa, xb):
    half = k.shape[0]
    first, first_pair, _ = where_am_i()
    near = jnp.concatenate(ordered(first_pair, decode(mine), decode(got_u)), axis=0)
    far = jnp.concatenate(ordered(first_pair, decode(theirs), decode(their_got)), axis=0)
    u = jnp.concatenate(ordered(low_traits(), near, far), axis=0)
    weights = (fixed_weights[...] - dot(u, k[...])).astype(bf16)
    a, b = ordered(first, weights[:, :half], weights[:, half:])
    xa[...] = a
    xb[...] = b


def contract(values, coefs):
    return lax.dot_general(values, coefs, (((1,), (1,)), ((), ())), preferred_element_type=f32)


def mask_coefs(coefs_in, anchor_in, masked, coefs, anchor, sems):
    untyped, span = coefs.shape
    half = span // 4
    typed = span - 2 * half
    tile = 128
    place = lax.axis_index(AXIS)
    total = lax.axis_size(AXIS) * typed
    copies = [pltpu.make_async_copy(anchor_in, anchor, sems.at[0])]
    for i in range(untyped // tile):
        rows = pl.ds(i * tile, tile)
        copies.append(pltpu.make_async_copy(coefs_in.at[rows], coefs.at[rows], sems.at[i + 1]))
    for copy in copies:
        copy.start()
    copies[0].wait()
    first_column = place * typed - half
    for i in range(untyped // tile):
        rows = pl.ds(i * tile, tile)
        nearest = jnp.broadcast_to(anchor[:, i * tile : (i + 1) * tile], (tile, tile)).T
        copies[i + 1].wait()
        for j in range(span // tile):
            lanes = pl.ds(j * tile, tile)
            columns = first_column + j * tile + lax.broadcasted_iota(jnp.int32, (tile, tile), 1)
            within = (jnp.abs(columns - nearest) <= half) & (columns >= 0) & (columns < total)
            masked[rows, lanes] = jnp.where(within, coefs[rows, lanes].astype(f32), 0.0).astype(bf16)


def impute_own(xa, xb, masked, out):
    first, _, _ = where_am_i()
    half = xa.shape[1]
    span = masked.shape[1]
    weights = jnp.concatenate(ordered(first, xa[...], xb[...]), axis=1)
    out[...] = contract(weights, masked[:, half : span - half])


def impute_edges(acc, got_a, got_b, masked, out):
    first, _, _ = where_am_i()
    half = got_a.shape[1]
    span = masked.shape[1]
    left, right = ordered(first, got_a[...], got_b[...])
    out[...] = acc[...] + contract(left, masked[:, :half]) + contract(right, masked[:, span - half :])


def swap(block, distance):
    n = lax.axis_size(AXIS)
    return lax.ppermute(block, AXIS, [(i, i ^ distance) for i in range(n)])


def hop(block, step):
    pairs = []
    for i in range(lax.axis_size(AXIS)):
        g = i // GROUP
        to = i + GROUP if g == step else i - GROUP if g == step + 1 else i
        pairs.append((i, to ^ 1))
    return lax.ppermute(block, AXIS, pairs)


def swap_chips(block):
    n, segments = lax.axis_size(AXIS), lax.axis_size(SEGMENTS)
    pairs = []
    for seg in range(segments):
        for i in range(n):
            to, to_seg = i + 1 if i % 2 else i - 1, seg
            if not 0 <= to < n:
                to, to_seg = (i, seg ^ 1) if segments % 2 == 0 else (to % n, seg)
            pairs.append((seg * n + i, to_seg * n + to))
    return lax.ppermute(block, (SEGMENTS, AXIS), pairs)


def per_device(z, diag_inverse, coupling, impute_coef, anchor):
    d = diag_inverse[0]
    c = coupling[0]
    typed = d.shape[0]
    half = c.shape[1]
    traits = z.shape[0]
    untyped, span = impute_coef.shape
    assert span == typed + 2 * half and typed == 2 * half
    assert lax.axis_size(AXIS) >= 3 * GROUP
    groups = lax.axis_size(AXIS) // GROUP
    two, four = traits // 2, traits // 4
    square = (half, half)
    sq, h2, h4 = (square, f32), ((two, half), f32), ((four, half), f32)
    x1_shape, x6_shape = ((half + two, half), f32), ((2 * two, half), f32)
    x6_coded = ((2 * coded_rows(two, half), LANES), i16)
    coded = ((coded_rows(four, half), LANES), i16)
    coded_half = ((coded_rows(half // 2, half), LANES), i16)
    whole = ((coded_rows(half, half) + coded_rows(four, half), LANES), i16)
    mixed = ((coded_rows(half // 2, half) + coded_rows(four, half), LANES), i16)

    solved_shape, p_shape = ((traits, typed), f32), ((typed, half), f32)
    x1, s_own, z, d, c = call(
        tail_part, [x1_shape, h2, solved_shape, ((typed, typed), f32), p_shape], z, d, c,
        hbm=True, scratch=[pltpu.SemaphoreType.DMA((7,))],
    )
    got1 = swap(x1, 1)
    x3, g_own, solved, p = call(
        head_part, [x1_shape, h2, solved_shape, p_shape], z, d, c, x1, s_own
    )
    x2, n_own, sp_own = call(pair_forward, [whole, sq, h4], x1, got1, s_own, after=(p,))
    got2 = swap(x2, 3)
    got3 = swap(x3, 1)
    masked = call(
        mask_coefs, ((untyped, span), bf16), impute_coef, anchor[None, :], after=(x2,), hbm=True,
        scratch=[
            pltpu.VMEM((untyped, span), bf16),
            pltpu.VMEM((1, untyped), jnp.int32),
            pltpu.SemaphoreType.DMA((untyped // 128 + 1,)),
        ],
    )
    x4, gg_own, gp_own = call(
        pair_backward, [mixed, sq, h4], x1, got1, s_own, x3, got3, g_own, after=(x2,)
    )
    out = call(group_forward, coded, n_own, got2, sp_own, after=(x4, masked))
    parts3 = ((3 * half, half), bf16)
    s_group, up, down, n_first, n_second, s_first = call(
        group_map, [h4, parts3, parts3, sq, sq, h4], n_own, got2, sp_own, after=(out,)
    )
    t_in = jnp.zeros((four, half), f32)
    got4 = swap(x4, 3)
    for step in range(groups - 2):
        got = hop(out, step)
        t_in, out = call(
            functools.partial(forward_hop, step), [h4, coded], got, t_in, up, s_group,
        )
        if step == 0:
            pieces = [((half // 2 + SCALES, LANES), i16)] * 2
            low, high = call(relay_halves, pieces, got4, after=(out,))
            got4_low, got4_high = swap(low, 1), swap(high, 1)
    gg_group, g_group, gg_second, g_second = call(
        group_backward, [sq, h4, sq, h4],
        n_first, s_first, gg_own, got4, got4_low, got4_high, gp_own, after=(out,),
    )
    k = call(block_map, ((half, typed), f32), n_second, x1, got1, d, after=(gg_group,))
    last = groups - 2
    got = hop(out, last)
    t_in, out = call(
        functools.partial(turn, last), [h4, coded], got, t_in, gg_group, g_group, after=(k,)
    )

    u_in = jnp.zeros((four, half), f32)
    for step in reversed(range(groups - 1)):
        got = hop(out, step)
        if step == last:
            x5, x5_rest, kept, rest_own, local = call(
                spread_forward, [coded, coded, h4, h4, h4],
                t_in, n_first, s_first, gg_second, g_second, gg_group, g_group, after=(out,),
            )
            got5, got5_rest = swap(x5, 3), swap(x5_rest, 3)
        if step:
            u_in, out = call(
                functools.partial(backward_hop, step), [h4, coded], got, u_in, down, local
            )
        else:
            start, maps = call(
                block_parts, [solved_shape, ((2 * half, typed), f32)], solved, p, d, after=(out,)
            )
            out = call(functools.partial(arrive, step), coded, got, u_in, after=(maps,))
    x6, own = call(
        pair_states, [x6_coded, x6_shape], kept, rest_own, got5, got5_rest, x1, got1, s_own, x3, got3, g_own
    )
    got6 = swap(x6, 1)
    fixed = call(block_fixed, solved_shape, own, got6, start, maps)
    theirs = swap(out, 1)
    got_u = swap(out, 3)
    their_got = swap(got_u, 1)
    edge = (square, bf16)
    xa, xb = call(block_weights, [edge, edge], out, got_u, theirs, their_got, fixed, k)
    got_a = swap_chips(xa)
    got_b = swap(xb, 1)
    acc = call(impute_own, ((traits, untyped), f32), xa, xb, masked)
    return call(
        impute_edges, ((traits, untyped), f32), acc, got_a, got_b, masked, last=True
    )


def solution(mesh):
    in_specs = (
        P(None, (SEGMENTS, AXIS)),
        P((SEGMENTS, AXIS), None, None),
        P((SEGMENTS, AXIS), None, None),
        P((SEGMENTS, AXIS), None),
        P((SEGMENTS, AXIS)),
    )
    return jax.shard_map(
        per_device, mesh=mesh, in_specs=in_specs, out_specs=P(None, (SEGMENTS, AXIS)), check_vma=False
    )
```

```python
import functools

import jax
import jax.numpy as jnp
from jax import lax
from jax.experimental import pallas as pl
from jax.experimental.pallas import tpu as pltpu
from jax.sharding import PartitionSpec as P

AXIS = "genome"
SEGMENTS = "seg"
GROUP = 4
f32 = jnp.float32
bf16 = jnp.bfloat16
i16 = jnp.int16
SCALES = 16
LANES = 128
LIMIT = 32767.0


def parts(x):
    high = x.astype(bf16)
    return high, (x - high.astype(f32)).astype(bf16)


def dot(a, b, ca=1, cb=0):
    ah, al = parts(a)
    bh, bl = parts(b)
    return lax.dot_general(
        jnp.concatenate([al, ah, ah], axis=ca),
        jnp.concatenate([bh, bl, bh], axis=cb),
        (((ca,), (cb,)), ((), ())),
        preferred_element_type=f32,
    )


def code(x):
    top = jnp.maximum(jnp.max(jnp.abs(x), axis=0, keepdims=True), 1e-32)
    power = jnp.ceil(jnp.log2(top) * 4.0)
    root = jnp.exp2(power * -0.125)
    steps = jnp.floor(x * root * (root * LIMIT) + 0.5)
    steps = jnp.clip(steps, -LIMIT, LIMIT)
    tiles = x.shape[1] // LANES
    powers = jnp.broadcast_to(power, (SCALES // tiles, x.shape[1]))
    pieces = [v[:, i * LANES : (i + 1) * LANES] for v in (steps, powers) for i in range(tiles)]
    return jnp.concatenate(pieces, axis=0).astype(jnp.int32).astype(i16)


def decode(coded, tiles=2):
    rows = (coded.shape[0] - SCALES) // tiles
    values = coded[...].astype(jnp.int32).astype(f32)
    columns = []
    for i in range(tiles):
        at = tiles * rows + i * (SCALES // tiles)
        root = jnp.exp2(values[at : at + 1] * 0.125)
        columns.append(values[i * rows : (i + 1) * rows] * (root / LIMIT) * root)
    return jnp.concatenate(columns, axis=1)


def coded_rows(rows, columns):
    return rows * (columns // LANES) + SCALES


def where_am_i():
    place = lax.axis_index(AXIS)
    return place % 2 == 0, (place // 2) % 2 == 0, place // GROUP


def ready(b):
    bh, bl = parts(b)
    return jnp.concatenate([bh, bl, bh], axis=0)


def dot_ready(a, b):
    ah, al = parts(a)
    return jnp.dot(jnp.concatenate([al, ah, ah], axis=1), b[...], preferred_element_type=f32)


def low_traits():
    place = lax.axis_index(AXIS)
    return (place + place // 2 + place // GROUP) % 2 == 0


def ordered(first, own, other):
    return jnp.where(first, own, other), jnp.where(first, other, own)


def call(kernel, outs, *args, after=(), hbm=False, last=False, scratch=()):
    n_in, n_after = len(args), len(after)

    def body(*refs):
        kernel(*refs[:n_in], *refs[n_in + n_after :])

    single = not isinstance(outs, list)
    shapes = [outs] if single else outs
    vmem = pl.BlockSpec(memory_space=pltpu.VMEM)
    anywhere = pl.BlockSpec(memory_space=pl.ANY)
    if hbm:
        args = [pltpu.with_memory_space_constraint(a, pltpu.HBM) for a in args]
    got = pl.pallas_call(
        body,
        out_shape=[jax.ShapeDtypeStruct(s, t) if last else pltpu.VMEM(s, t) for s, t in shapes],
        in_specs=[anywhere if hbm else vmem] * n_in + [anywhere] * n_after,
        out_specs=[vmem] * len(shapes),
        scratch_shapes=scratch,
        compiler_params=pltpu.CompilerParams(vmem_limit_bytes=8 * 2**20),
        name=kernel.__name__ if hasattr(kernel, "__name__") else kernel.func.__name__,
    )(*args, *after)
    return got[0] if single else got


def tail_part(z_in, d_in, c_in, x1, s_own, z, d, c, sems):
    typed, half = c.shape
    rows = z.shape[0] // 2
    head = typed - half
    step = typed // 2
    copies = []
    for i in range(2):
        here = pl.ds(i * step, step)
        tail = (pl.ds(head, half), here)
        copies.append(pltpu.make_async_copy(d_in.at[tail], d.at[tail], sems.at[3 * i]))
        copies.append(pltpu.make_async_copy(c_in.at[here], c.at[here], sems.at[3 * i + 1]))
        copies.append(pltpu.make_async_copy(z_in.at[:, here], z.at[:, here], sems.at[3 * i + 2]))
    rest = pl.ds(0, head)
    copies.append(pltpu.make_async_copy(d_in.at[rest], d.at[rest], sems.at[6]))
    for copy in copies:
        copy.start()
    m = s = 0.0
    for i in range(2):
        here = pl.ds(i * step, step)
        for copy in copies[3 * i : 3 * i + 3]:
            copy.wait()
        tail = d[head:, here]
        m = m - dot(tail, c[here])
        s = s + dot(z[:, here], tail, 1, 1)
    x1[:half] = m
    keep, send = ordered(low_traits(), s[:rows], s[rows:])
    x1[half:] = send
    s_own[...] = keep
    copies[6].wait()


def head_part(z, d, c, x1, s_own, x3, g_own, solved, p):
    half = c.shape[1]
    rows = z.shape[0] // 2
    head = d.shape[0] - half
    first, _, _ = where_am_i()
    p[:head] = dot(d[:head], c[...])
    p[head:] = -x1[:half]
    solved[:, :head] = dot(z[...], d[:head], 1, 1)
    low, high = ordered(low_traits(), s_own[...], x1[half:])
    solved[:rows, head:] = low
    solved[rows:, head:] = high
    g = dot(solved[...], p[...])
    keep, send = ordered(low_traits(), g[:rows], g[rows:])
    x3[:half] = dot(p[...], p[...], 0, 0)
    x3[half:] = send
    g_own[...] = keep


def pair_forward(x1, got1, s_own, x2, n_own, sp_own):
    half = x1.shape[1]
    first, first_pair, _ = where_am_i()
    m0, m1 = ordered(first, x1[:half], got1[:half])
    s0, s1 = ordered(first, s_own[...], got1[half:])
    n = dot(m1, m0)
    n_own[...] = n
    split = coded_rows(half, half)
    x2[:split] = code(n)
    s = dot(s0, m1, 1, 1) + s1
    rows = s.shape[0] // 2
    keep, send = ordered(first_pair, s[:rows], s[rows:])
    x2[split:] = code(send)
    sp_own[...] = keep


def pair_backward(x1, got1, s_own, x3, got3, g_own, x4, x4_g, gg_own, gp_own):
    half = x1.shape[1]
    first, first_pair, _ = where_am_i()
    m0, _ = ordered(first, x1[:half], got1[:half])
    s0, _ = ordered(first, s_own[...], got1[half:])
    gg0, gg1 = ordered(first, x3[:half], got3[:half])
    g0, g1 = ordered(first, g_own[...], got3[half:])
    both = dot(jnp.concatenate([gg1, g1 - dot(s0, gg1)], axis=0), m0)
    gg = dot(m0, both[:half], 0, 0) + gg0
    gg_own[...] = gg
    x4[...] = code(jnp.where(first, gg[: half // 2], gg[half // 2 :]))
    g = both[half:] + g0
    rows = g.shape[0] // 2
    keep, send = ordered(first_pair, g[:rows], g[rows:])
    x4_g[...] = code(send)
    gp_own[...] = keep


def pair_matrices(own, got, got_core):
    first, first_pair, _ = where_am_i()
    other = jnp.concatenate(ordered(first, got_core, got), axis=0)
    return ordered(first_pair, own[...], other)


def pair_vectors(own, got):
    _, first_pair, _ = where_am_i()
    return ordered(first_pair, own[...], got)


def relay(got, out):
    out[...] = got[: out.shape[0]]


def relay_halves(got, low, high):
    rows = low.shape[0] - SCALES
    low[:rows] = got[:rows]
    high[:rows] = got[rows : 2 * rows]
    low[rows:] = got[2 * rows : 2 * rows + SCALES]
    high[rows:] = got[2 * rows : 2 * rows + SCALES]


def both_pairs(own, own_rows, got):
    _, first_pair, _ = where_am_i()
    split = coded_rows(own.shape[1], own.shape[1])
    m0, m1 = ordered(first_pair, own[...], decode(got[:split]))
    v0, v1 = ordered(first_pair, own_rows[...], decode(got[split:]))
    return m0, v0, m1, v1


def group_forward(n_own, got2, sp_own, out):
    _, _, group = where_am_i()
    out[...] = jnp.zeros_like(out)

    @pl.when(group == 0)
    def _():
        _, s0, n1, s1 = both_pairs(n_own, sp_own, got2)
        out[...] = code(dot(s0, n1, 1, 1) + s1)


def group_map(n_own, got2, sp_own, s_group, up, down, n_first, n_second, s_first):
    n0, s0, n1, s1 = both_pairs(n_own, sp_own, got2)
    s_group[...] = dot(s0, n1, 1, 1) + s1
    s_first[...] = s0
    n_first[...] = n0
    n_second[...] = n1
    n_group = dot(n1, n0)
    up[...] = ready(n_group.T)
    down[...] = ready(n_group)


def block_map(n_second, x1, got1, d, k):
    half = x1.shape[1]
    first, first_pair, _ = where_am_i()
    rows = lax.broadcasted_iota(jnp.int32, (half, half), 0)
    columns = lax.broadcasted_iota(jnp.int32, (half, half), 1)
    unit = (rows == columns).astype(f32)
    _, m1 = ordered(first, x1[:half], got1[:half])
    above = jnp.where(first_pair, n_second[...], unit)
    above = jnp.where(first, dot(above, m1), above)
    k[...] = dot(above, d[d.shape[0] - half :])


def group_backward(
    n_first, s_first, gg_own, got4, got4_g, got4_low, got4_high, gp_own,
    gg_group, g_group, gg_second, g_second,
):
    half = n_first.shape[1]
    split = coded_rows(half // 2, half)
    n0 = n_first[...]
    rows = got4_low.shape[0] - SCALES
    got4_core = jnp.concatenate([got4_low[:rows], got4_high[...]], axis=0)
    gg0, gg1 = pair_matrices(gg_own, decode(got4), decode(got4_core))
    g0, g1 = pair_vectors(gp_own, decode(got4_g))
    gg_second[...] = gg1
    g_second[...] = g1
    both = dot(jnp.concatenate([gg1, g1 - dot(s_first[...], gg1)], axis=0), n0)
    gg_group[...] = dot(n0, both[:half], 0, 0) + gg0
    g_group[...] = both[half:] + g0


def forward_hop(step, got, t_in, up, s_group, t_out, out):
    _, _, group = where_am_i()
    t = jnp.where(group == step + 1, decode(got), t_in[...])
    t_out[...] = t
    out[...] = code(dot_ready(t, up) + s_group[...])


def turn(step, got, t_in, gg_group, g_group, t_out, out):
    _, _, group = where_am_i()
    t = jnp.where(group == step + 1, decode(got), t_in[...])
    t_out[...] = t
    out[...] = jnp.zeros_like(out)

    @pl.when(group == step + 1)
    def _():
        out[...] = code(g_group[...] - dot(t, gg_group[...]))


def backward_hop(step, got, u_in, down, local, u_out, out):
    _, _, group = where_am_i()
    u = jnp.where(group == step, decode(got), u_in[...])
    u_out[...] = u
    out[...] = code(dot_ready(u, down) + local[...])


def arrive(step, got, u_in, out):
    _, _, group = where_am_i()
    out[...] = code(jnp.where(group == step, decode(got), u_in[...]))


def spread_forward(
    t_in, n_first, s_first, gg_second, g_second, gg_group, g_group, x5, x5_rest, kept, rest_own, local
):
    half = n_first.shape[1]
    _, first_pair, _ = where_am_i()
    t_mid = dot(t_in[...], n_first[...], 1, 1) + s_first[...]
    rest = g_second[...] - dot(t_mid, gg_second[...])
    keep, send = ordered(first_pair, t_in[...], t_mid)
    x5[...] = code(send)
    x5_rest[...] = code(rest)
    kept[...] = keep
    rest_own[...] = rest
    local[...] = g_group[...] - dot(t_in[...], gg_group[...])


def pair_states(kept, rest_own, got5, got5_rest, x1, got1, s_own, x3, got3, g_own, x6, own):
    half = x1.shape[1]
    rows = s_own.shape[0]
    first, first_pair, _ = where_am_i()
    t = jnp.concatenate(ordered(first_pair, kept[...], decode(got5)), axis=0)
    rest = jnp.concatenate(ordered(first_pair, rest_own[...], decode(got5_rest)), axis=0)
    m0, m1 = ordered(first, x1[:half], got1[:half])
    s0, _ = ordered(first, s_own[...], got1[half:])
    _, gg1 = ordered(first, x3[:half], got3[:half])
    _, g1 = ordered(first, g_own[...], got3[half:])
    t_mid = dot(t, m0, 1, 1) + s0
    fixed = jnp.where(first_pair, rest, 0.0)
    fixed_mid = dot(fixed, m1) + g1 - dot(t_mid, gg1)
    split = coded_rows(rows, half)
    keep, send = ordered(first, t, t_mid)
    x6[:split] = code(send)
    own[:rows] = keep
    keep, send = ordered(first, fixed_mid, fixed)
    x6[split:] = code(send)
    own[rows:] = keep


def block_parts(solved, p, d, start, maps):
    half = p.shape[1]
    start[...] = dot(solved[...], d[...])
    maps[:half] = dot(p[...], d[...], 0, 0)
    maps[half:] = d[d.shape[0] - half :]


def block_fixed(own, got6, start, maps, fixed_weights):
    rows = own.shape[0] // 2
    split = coded_rows(rows, own.shape[1])
    low = low_traits()
    t = jnp.concatenate(ordered(low, own[:rows], decode(got6[:split])), axis=0)
    above = jnp.concatenate(ordered(low, own[rows:], decode(got6[split:])), axis=0)
    fixed_weights[...] = start[...] - dot(jnp.concatenate([t, above], axis=1), maps[...])


def block_weights(mine, got_u, theirs, their_got, fixed_weights, k, xa, xb):
    half = k.shape[0]
    first, first_pair, _ = where_am_i()
    near = jnp.concatenate(ordered(first_pair, decode(mine), decode(got_u)), axis=0)
    far = jnp.concatenate(ordered(first_pair, decode(theirs), decode(their_got)), axis=0)
    u = jnp.concatenate(ordered(low_traits(), near, far), axis=0)
    weights = (fixed_weights[...] - dot(u, k[...])).astype(bf16)
    a, b = ordered(first, weights[:, :half], weights[:, half:])
    xa[...] = a
    xb[...] = b


def contract(values, coefs):
    return lax.dot_general(values, coefs, (((1,), (1,)), ((), ())), preferred_element_type=f32)


def mask_coefs(coefs_in, anchor_in, masked, coefs, anchor, sems):
    untyped, span = coefs.shape
    half = span // 4
    typed = span - 2 * half
    tile = 128
    place = lax.axis_index(AXIS)
    total = lax.axis_size(AXIS) * typed
    copies = [pltpu.make_async_copy(anchor_in, anchor, sems.at[0])]
    for i in range(untyped // tile):
        rows = pl.ds(i * tile, tile)
        copies.append(pltpu.make_async_copy(coefs_in.at[rows], coefs.at[rows], sems.at[i + 1]))
    for copy in copies:
        copy.start()
    copies[0].wait()
    first_column = place * typed - half
    for i in range(untyped // tile):
        rows = pl.ds(i * tile, tile)
        nearest = jnp.broadcast_to(anchor[:, i * tile : (i + 1) * tile], (tile, tile)).T
        copies[i + 1].wait()
        for j in range(span // tile):
            lanes = pl.ds(j * tile, tile)
            columns = first_column + j * tile + lax.broadcasted_iota(jnp.int32, (tile, tile), 1)
            within = (jnp.abs(columns - nearest) <= half) & (columns >= 0) & (columns < total)
            masked[rows, lanes] = jnp.where(within, coefs[rows, lanes].astype(f32), 0.0).astype(bf16)


def impute_own(xa, xb, masked, out):
    first, _, _ = where_am_i()
    half = xa.shape[1]
    span = masked.shape[1]
    weights = jnp.concatenate(ordered(first, xa[...], xb[...]), axis=1)
    out[...] = contract(weights, masked[:, half : span - half])


def impute_edges(acc, got_a, got_b, masked, out):
    first, _, _ = where_am_i()
    half = got_a.shape[1]
    span = masked.shape[1]
    left, right = ordered(first, got_a[...], got_b[...])
    out[...] = acc[...] + contract(left, masked[:, :half]) + contract(right, masked[:, span - half :])


def swap(block, distance):
    n = lax.axis_size(AXIS)
    return lax.ppermute(block, AXIS, [(i, i ^ distance) for i in range(n)])


def hop(block, step):
    pairs = []
    for i in range(lax.axis_size(AXIS)):
        g = i // GROUP
        to = i + GROUP if g == step else i - GROUP if g == step + 1 else i
        pairs.append((i, to ^ 1))
    return lax.ppermute(block, AXIS, pairs)


def swap_chips(block):
    n, segments = lax.axis_size(AXIS), lax.axis_size(SEGMENTS)
    pairs = []
    for seg in range(segments):
        for i in range(n):
            to, to_seg = i + 1 if i % 2 else i - 1, seg
            if not 0 <= to < n:
                to, to_seg = (i, seg ^ 1) if segments % 2 == 0 else (to % n, seg)
            pairs.append((seg * n + i, to_seg * n + to))
    return lax.ppermute(block, (SEGMENTS, AXIS), pairs)


def per_device(z, diag_inverse, coupling, impute_coef, anchor):
    d = diag_inverse[0]
    c = coupling[0]
    typed = d.shape[0]
    half = c.shape[1]
    traits = z.shape[0]
    untyped, span = impute_coef.shape
    assert span == typed + 2 * half and typed == 2 * half
    assert lax.axis_size(AXIS) >= 3 * GROUP
    groups = lax.axis_size(AXIS) // GROUP
    two, four = traits // 2, traits // 4
    square = (half, half)
    sq, h2, h4 = (square, f32), ((two, half), f32), ((four, half), f32)
    x1_shape, x6_shape = ((half + two, half), f32), ((2 * two, half), f32)
    x6_coded = ((2 * coded_rows(two, half), LANES), i16)
    coded = ((coded_rows(four, half), LANES), i16)
    coded_half = ((coded_rows(half // 2, half), LANES), i16)
    whole = ((coded_rows(half, half) + coded_rows(four, half), LANES), i16)

    solved_shape, p_shape = ((traits, typed), f32), ((typed, half), f32)
    x1, s_own, z, d, c = call(
        tail_part, [x1_shape, h2, solved_shape, ((typed, typed), f32), p_shape], z, d, c,
        hbm=True, scratch=[pltpu.SemaphoreType.DMA((7,))],
    )
    got1 = swap(x1, 1)
    x3, g_own, solved, p = call(
        head_part, [x1_shape, h2, solved_shape, p_shape], z, d, c, x1, s_own
    )
    x2, n_own, sp_own = call(pair_forward, [whole, sq, h4], x1, got1, s_own, after=(p,))
    got2 = swap(x2, 3)
    got3 = swap(x3, 1)
    masked = call(
        mask_coefs, ((untyped, span), bf16), impute_coef, anchor[None, :], after=(x2,), hbm=True,
        scratch=[
            pltpu.VMEM((untyped, span), bf16),
            pltpu.VMEM((1, untyped), jnp.int32),
            pltpu.SemaphoreType.DMA((untyped // 128 + 1,)),
        ],
    )
    x4, x4_g, gg_own, gp_own = call(
        pair_backward, [coded_half, coded, sq, h4], x1, got1, s_own, x3, got3, g_own, after=(x2,)
    )
    out = call(group_forward, coded, n_own, got2, sp_own, after=(x4, masked))
    parts3 = ((3 * half, half), bf16)
    s_group, up, down, n_first, n_second, s_first = call(
        group_map, [h4, parts3, parts3, sq, sq, h4], n_own, got2, sp_own, after=(out,)
    )
    t_in = jnp.zeros((four, half), f32)
    got4, got4_g = swap(x4, 3), swap(x4_g, 3)
    for step in range(groups - 2):
        got = hop(out, step)
        t_in, out = call(
            functools.partial(forward_hop, step), [h4, coded], got, t_in, up, s_group,
        )
        if step == 0:
            pieces = [((half // 2 + SCALES, LANES), i16)] * 2
            low, high = call(relay_halves, pieces, got4, after=(out, got4_g))
            got4_low, got4_high = swap(low, 1), swap(high, 1)
    gg_group, g_group, gg_second, g_second = call(
        group_backward, [sq, h4, sq, h4],
        n_first, s_first, gg_own, got4, got4_g, got4_low, got4_high, gp_own, after=(out,),
    )
    k = call(block_map, ((half, typed), f32), n_second, x1, got1, d, after=(gg_group,))
    last = groups - 2
    got = hop(out, last)
    t_in, out = call(
        functools.partial(turn, last), [h4, coded], got, t_in, gg_group, g_group, after=(k,)
    )

    u_in = jnp.zeros((four, half), f32)
    for step in reversed(range(groups - 1)):
        got = hop(out, step)
        if step == last:
            x5, x5_rest, kept, rest_own, local = call(
                spread_forward, [coded, coded, h4, h4, h4],
                t_in, n_first, s_first, gg_second, g_second, gg_group, g_group, after=(out,),
            )
            got5, got5_rest = swap(x5, 3), swap(x5_rest, 3)
        if step:
            u_in, out = call(
                functools.partial(backward_hop, step), [h4, coded], got, u_in, down, local
            )
        else:
            start, maps = call(
                block_parts, [solved_shape, ((2 * half, typed), f32)], solved, p, d, after=(out,)
            )
            out = call(functools.partial(arrive, step), coded, got, u_in, after=(maps,))
    x6, own = call(
        pair_states, [x6_coded, x6_shape], kept, rest_own, got5, got5_rest, x1, got1, s_own, x3, got3, g_own
    )
    got6 = swap(x6, 1)
    fixed = call(block_fixed, solved_shape, own, got6, start, maps)
    theirs = swap(out, 1)
    got_u = swap(out, 3)
    their_got = swap(got_u, 1)
    edge = (square, bf16)
    xa, xb = call(block_weights, [edge, edge], out, got_u, theirs, their_got, fixed, k)
    got_a = swap_chips(xa)
    got_b = swap(xb, 1)
    acc = call(impute_own, ((traits, untyped), f32), xa, xb, masked)
    return call(
        impute_edges, ((traits, untyped), f32), acc, got_a, got_b, masked, last=True
    )


def solution(mesh):
    in_specs = (
        P(None, (SEGMENTS, AXIS)),
        P((SEGMENTS, AXIS), None, None),
        P((SEGMENTS, AXIS), None, None),
        P((SEGMENTS, AXIS), None),
        P((SEGMENTS, AXIS)),
    )
    return jax.shard_map(
        per_device, mesh=mesh, in_specs=in_specs, out_specs=P(None, (SEGMENTS, AXIS)), check_vma=False
    )
```

```python
import functools

import jax
import jax.numpy as jnp
from jax import lax
from jax.experimental import pallas as pl
from jax.experimental.pallas import tpu as pltpu
from jax.sharding import PartitionSpec as P

AXIS = "genome"
SEGMENTS = "seg"
GROUP = 4
f32 = jnp.float32
bf16 = jnp.bfloat16
i16 = jnp.int16
SCALES = 16
LANES = 128
LIMIT = 32767.0


def parts(x):
    high = x.astype(bf16)
    return high, (x - high.astype(f32)).astype(bf16)


def dot(a, b, ca=1, cb=0):
    ah, al = parts(a)
    bh, bl = parts(b)
    return lax.dot_general(
        jnp.concatenate([al, ah, ah], axis=ca),
        jnp.concatenate([bh, bl, bh], axis=cb),
        (((ca,), (cb,)), ((), ())),
        preferred_element_type=f32,
    )


def code(x):
    top = jnp.maximum(jnp.max(jnp.abs(x), axis=0, keepdims=True), 1e-32)
    power = jnp.ceil(jnp.log2(top) * 4.0)
    root = jnp.exp2(power * -0.125)
    steps = jnp.floor(x * root * (root * LIMIT) + 0.5)
    steps = jnp.clip(steps, -LIMIT, LIMIT)
    tiles = x.shape[1] // LANES
    powers = jnp.broadcast_to(power, (SCALES // tiles, x.shape[1]))
    pieces = [v[:, i * LANES : (i + 1) * LANES] for v in (steps, powers) for i in range(tiles)]
    return jnp.concatenate(pieces, axis=0).astype(jnp.int32).astype(i16)


def decode(coded, tiles=2):
    rows = (coded.shape[0] - SCALES) // tiles
    values = coded[...].astype(jnp.int32).astype(f32)
    columns = []
    for i in range(tiles):
        at = tiles * rows + i * (SCALES // tiles)
        root = jnp.exp2(values[at : at + 1] * 0.125)
        columns.append(values[i * rows : (i + 1) * rows] * (root / LIMIT) * root)
    return jnp.concatenate(columns, axis=1)


def coded_rows(rows, columns):
    return rows * (columns // LANES) + SCALES


def where_am_i():
    place = lax.axis_index(AXIS)
    return place % 2 == 0, (place // 2) % 2 == 0, place // GROUP


def ready(b):
    bh, bl = parts(b)
    return jnp.concatenate([bh, bl, bh], axis=0)


def dot_ready(a, b):
    ah, al = parts(a)
    return jnp.dot(jnp.concatenate([al, ah, ah], axis=1), b[...], preferred_element_type=f32)


def low_traits():
    place = lax.axis_index(AXIS)
    return (place + place // 2 + place // GROUP) % 2 == 0


def ordered(first, own, other):
    return jnp.where(first, own, other), jnp.where(first, other, own)


def call(kernel, outs, *args, after=(), hbm=False, last=False, scratch=()):
    n_in, n_after = len(args), len(after)

    def body(*refs):
        kernel(*refs[:n_in], *refs[n_in + n_after :])

    single = not isinstance(outs, list)
    shapes = [outs] if single else outs
    vmem = pl.BlockSpec(memory_space=pltpu.VMEM)
    anywhere = pl.BlockSpec(memory_space=pl.ANY)
    if hbm:
        args = [pltpu.with_memory_space_constraint(a, pltpu.HBM) for a in args]
    got = pl.pallas_call(
        body,
        out_shape=[jax.ShapeDtypeStruct(s, t) if last else pltpu.VMEM(s, t) for s, t in shapes],
        in_specs=[anywhere if hbm else vmem] * n_in + [anywhere] * n_after,
        out_specs=[vmem] * len(shapes),
        scratch_shapes=scratch,
        compiler_params=pltpu.CompilerParams(vmem_limit_bytes=8 * 2**20),
        name=kernel.__name__ if hasattr(kernel, "__name__") else kernel.func.__name__,
    )(*args, *after)
    return got[0] if single else got


def tail_part(z_in, d_in, c_in, x1, s_own, z, d, c, sems):
    typed, half = c.shape
    rows = z.shape[0] // 2
    head = typed - half
    step = typed // 2
    copies = []
    for i in range(2):
        here = pl.ds(i * step, step)
        tail = (pl.ds(head, half), here)
        copies.append(pltpu.make_async_copy(d_in.at[tail], d.at[tail], sems.at[3 * i]))
        copies.append(pltpu.make_async_copy(c_in.at[here], c.at[here], sems.at[3 * i + 1]))
        copies.append(pltpu.make_async_copy(z_in.at[:, here], z.at[:, here], sems.at[3 * i + 2]))
    rest = pl.ds(0, head)
    copies.append(pltpu.make_async_copy(d_in.at[rest], d.at[rest], sems.at[6]))
    for copy in copies:
        copy.start()
    m = s = 0.0
    for i in range(2):
        here = pl.ds(i * step, step)
        for copy in copies[3 * i : 3 * i + 3]:
            copy.wait()
        tail = d[head:, here]
        m = m - dot(tail, c[here])
        s = s + dot(z[:, here], tail, 1, 1)
    x1[:half] = m
    keep, send = ordered(low_traits(), s[:rows], s[rows:])
    x1[half:] = send
    s_own[...] = keep
    copies[6].wait()


def head_part(z, d, c, x1, s_own, x3, g_own, solved, p):
    half = c.shape[1]
    rows = z.shape[0] // 2
    head = d.shape[0] - half
    first, _, _ = where_am_i()
    p[:head] = dot(d[:head], c[...])
    p[head:] = -x1[:half]
    solved[:, :head] = dot(z[...], d[:head], 1, 1)
    low, high = ordered(low_traits(), s_own[...], x1[half:])
    solved[:rows, head:] = low
    solved[rows:, head:] = high
    g = dot(solved[...], p[...])
    keep, send = ordered(low_traits(), g[:rows], g[rows:])
    x3[:half] = dot(p[...], p[...], 0, 0)
    x3[half:] = send
    g_own[...] = keep


def pair_forward(x1, got1, s_own, x2, n_own, sp_own):
    half = x1.shape[1]
    first, first_pair, _ = where_am_i()
    m0, m1 = ordered(first, x1[:half], got1[:half])
    s0, s1 = ordered(first, s_own[...], got1[half:])
    n = dot(m1, m0)
    n_own[...] = n
    split = coded_rows(half // 2, half)
    x2[:split] = code(jnp.where(first, n[: half // 2], n[half // 2 :]))
    s = dot(s0, m1, 1, 1) + s1
    rows = s.shape[0] // 2
    keep, send = ordered(first_pair, s[:rows], s[rows:])
    x2[split:] = code(send)
    sp_own[...] = keep


def pair_backward(x1, got1, s_own, x3, got3, g_own, x4, gg_own, gp_own):
    half = x1.shape[1]
    first, first_pair, _ = where_am_i()
    m0, _ = ordered(first, x1[:half], got1[:half])
    s0, _ = ordered(first, s_own[...], got1[half:])
    gg0, gg1 = ordered(first, x3[:half], got3[:half])
    g0, g1 = ordered(first, g_own[...], got3[half:])
    both = dot(jnp.concatenate([gg1, g1 - dot(s0, gg1)], axis=0), m0)
    gg = dot(m0, both[:half], 0, 0) + gg0
    gg_own[...] = gg
    split = coded_rows(half // 2, half)
    x4[:split] = code(jnp.where(first, gg[: half // 2], gg[half // 2 :]))
    g = both[half:] + g0
    rows = g.shape[0] // 2
    keep, send = ordered(first_pair, g[:rows], g[rows:])
    x4[split:] = code(send)
    gp_own[...] = keep


def pair_matrices(own, got, got_core):
    first, first_pair, _ = where_am_i()
    other = jnp.concatenate(ordered(first, got_core, got), axis=0)
    return ordered(first_pair, own[...], other)


def pair_vectors(own, got):
    _, first_pair, _ = where_am_i()
    return ordered(first_pair, own[...], got)


def relay(got, out):
    out[...] = got[: out.shape[0]]


def relay_halves(got, low, high):
    rows = low.shape[0] - SCALES
    low[:rows] = got[:rows]
    high[:rows] = got[rows : 2 * rows]
    low[rows:] = got[2 * rows : 2 * rows + SCALES]
    high[rows:] = got[2 * rows : 2 * rows + SCALES]


def group_forward(n_own, got2, got2_core, sp_own, out):
    _, _, group = where_am_i()
    out[...] = jnp.zeros_like(out)

    @pl.when(group == 0)
    def _():
        split = coded_rows(n_own.shape[1] // 2, n_own.shape[1])
        _, n1 = pair_matrices(n_own, decode(got2[:split]), decode(got2_core))
        s0, s1 = pair_vectors(sp_own, decode(got2[split:]))
        out[...] = code(dot(s0, n1, 1, 1) + s1)


def group_map(n_own, got2, got2_core, sp_own, s_group, up, down, n_first, n_second):
    split = coded_rows(n_own.shape[1] // 2, n_own.shape[1])
    n0, n1 = pair_matrices(n_own, decode(got2[:split]), decode(got2_core))
    s0, s1 = pair_vectors(sp_own, decode(got2[split:]))
    s_group[...] = dot(s0, n1, 1, 1) + s1
    n_first[...] = n0
    n_second[...] = n1
    n_group = dot(n1, n0)
    up[...] = ready(n_group.T)
    down[...] = ready(n_group)


def block_map(n_second, x1, got1, d, k):
    half = x1.shape[1]
    first, first_pair, _ = where_am_i()
    rows = lax.broadcasted_iota(jnp.int32, (half, half), 0)
    columns = lax.broadcasted_iota(jnp.int32, (half, half), 1)
    unit = (rows == columns).astype(f32)
    _, m1 = ordered(first, x1[:half], got1[:half])
    above = jnp.where(first_pair, n_second[...], unit)
    above = jnp.where(first, dot(above, m1), above)
    k[...] = dot(above, d[d.shape[0] - half :])


def group_backward(
    n_first, got2, sp_own, gg_own, got4, got4_low, got4_high, gp_own,
    gg_group, g_group, gg_second, g_second,
):
    half = n_first.shape[1]
    split = coded_rows(half // 2, half)
    n0 = n_first[...]
    s0, _ = pair_vectors(sp_own, decode(got2[split:]))
    rows = got4_low.shape[0] - SCALES
    got4_core = jnp.concatenate([got4_low[:rows], got4_high[...]], axis=0)
    gg0, gg1 = pair_matrices(gg_own, decode(got4[:split]), decode(got4_core))
    g0, g1 = pair_vectors(gp_own, decode(got4[split:]))
    gg_second[...] = gg1
    g_second[...] = g1
    both = dot(jnp.concatenate([gg1, g1 - dot(s0, gg1)], axis=0), n0)
    gg_group[...] = dot(n0, both[:half], 0, 0) + gg0
    g_group[...] = both[half:] + g0


def forward_hop(step, got, t_in, up, s_group, t_out, out):
    _, _, group = where_am_i()
    t = jnp.where(group == step + 1, decode(got), t_in[...])
    t_out[...] = t
    out[...] = code(dot_ready(t, up) + s_group[...])


def turn(step, got, t_in, gg_group, g_group, t_out, out):
    _, _, group = where_am_i()
    t = jnp.where(group == step + 1, decode(got), t_in[...])
    t_out[...] = t
    out[...] = jnp.zeros_like(out)

    @pl.when(group == step + 1)
    def _():
        out[...] = code(g_group[...] - dot(t, gg_group[...]))


def backward_hop(step, got, u_in, down, local, u_out, out):
    _, _, group = where_am_i()
    u = jnp.where(group == step, decode(got), u_in[...])
    u_out[...] = u
    out[...] = code(dot_ready(u, down) + local[...])


def arrive(step, got, u_in, out):
    _, _, group = where_am_i()
    out[...] = code(jnp.where(group == step, decode(got), u_in[...]))


def spread_forward(
    t_in, n_first, got2, sp_own, gg_second, g_second, gg_group, g_group, x5, x5_rest, kept, rest_own, local
):
    half = n_first.shape[1]
    _, first_pair, _ = where_am_i()
    s0, _ = pair_vectors(sp_own, decode(got2[coded_rows(half // 2, half) :]))
    t_mid = dot(t_in[...], n_first[...], 1, 1) + s0
    rest = g_second[...] - dot(t_mid, gg_second[...])
    keep, send = ordered(first_pair, t_in[...], t_mid)
    x5[...] = code(send)
    x5_rest[...] = code(rest)
    kept[...] = keep
    rest_own[...] = rest
    local[...] = g_group[...] - dot(t_in[...], gg_group[...])


def pair_states(kept, rest_own, got5, got5_rest, x1, got1, s_own, x3, got3, g_own, x6, own):
    half = x1.shape[1]
    rows = s_own.shape[0]
    first, first_pair, _ = where_am_i()
    t = jnp.concatenate(ordered(first_pair, kept[...], decode(got5)), axis=0)
    rest = jnp.concatenate(ordered(first_pair, rest_own[...], decode(got5_rest)), axis=0)
    m0, m1 = ordered(first, x1[:half], got1[:half])
    s0, _ = ordered(first, s_own[...], got1[half:])
    _, gg1 = ordered(first, x3[:half], got3[:half])
    _, g1 = ordered(first, g_own[...], got3[half:])
    t_mid = dot(t, m0, 1, 1) + s0
    fixed = jnp.where(first_pair, rest, 0.0)
    fixed_mid = dot(fixed, m1) + g1 - dot(t_mid, gg1)
    split = coded_rows(rows, half)
    keep, send = ordered(first, t, t_mid)
    x6[:split] = code(send)
    own[:rows] = keep
    keep, send = ordered(first, fixed_mid, fixed)
    x6[split:] = code(send)
    own[rows:] = keep


def block_parts(solved, p, d, start, maps):
    half = p.shape[1]
    start[...] = dot(solved[...], d[...])
    maps[:half] = dot(p[...], d[...], 0, 0)
    maps[half:] = d[d.shape[0] - half :]


def block_fixed(own, got6, start, maps, fixed_weights):
    rows = own.shape[0] // 2
    split = coded_rows(rows, own.shape[1])
    low = low_traits()
    t = jnp.concatenate(ordered(low, own[:rows], decode(got6[:split])), axis=0)
    above = jnp.concatenate(ordered(low, own[rows:], decode(got6[split:])), axis=0)
    fixed_weights[...] = start[...] - dot(jnp.concatenate([t, above], axis=1), maps[...])


def block_weights(quarters, fixed_weights, k, xa, xb):
    half = k.shape[0]
    first, _, group = where_am_i()
    q = [decode(quarters[i]) for i in range(GROUP)]
    even = group % 2 == 0
    a, b = ordered(even, q[0], q[1])
    c, d = ordered(even, q[3], q[2])
    u = jnp.concatenate([a, c, b, d], axis=0)
    weights = (fixed_weights[...] - dot(u, k[...])).astype(bf16)
    a, b = ordered(first, weights[:, :half], weights[:, half:])
    xa[...] = a
    xb[...] = b


def contract(values, coefs):
    return lax.dot_general(values, coefs, (((1,), (1,)), ((), ())), preferred_element_type=f32)


def mask_coefs(coefs_in, anchor_in, masked, coefs, anchor, sems):
    untyped, span = coefs.shape
    half = span // 4
    typed = span - 2 * half
    tile = 128
    place = lax.axis_index(AXIS)
    total = lax.axis_size(AXIS) * typed
    copies = [pltpu.make_async_copy(anchor_in, anchor, sems.at[0])]
    for i in range(untyped // tile):
        rows = pl.ds(i * tile, tile)
        copies.append(pltpu.make_async_copy(coefs_in.at[rows], coefs.at[rows], sems.at[i + 1]))
    for copy in copies:
        copy.start()
    copies[0].wait()
    first_column = place * typed - half
    for i in range(untyped // tile):
        rows = pl.ds(i * tile, tile)
        nearest = jnp.broadcast_to(anchor[:, i * tile : (i + 1) * tile], (tile, tile)).T
        copies[i + 1].wait()
        for j in range(span // tile):
            lanes = pl.ds(j * tile, tile)
            columns = first_column + j * tile + lax.broadcasted_iota(jnp.int32, (tile, tile), 1)
            within = (jnp.abs(columns - nearest) <= half) & (columns >= 0) & (columns < total)
            masked[rows, lanes] = jnp.where(within, coefs[rows, lanes].astype(f32), 0.0).astype(bf16)


def impute_own(xa, xb, masked, out):
    first, _, _ = where_am_i()
    half = xa.shape[1]
    span = masked.shape[1]
    weights = jnp.concatenate(ordered(first, xa[...], xb[...]), axis=1)
    out[...] = contract(weights, masked[:, half : span - half])


def impute_edges(acc, got_a, got_b, masked, out):
    first, _, _ = where_am_i()
    half = got_a.shape[1]
    span = masked.shape[1]
    left, right = ordered(first, got_a[...], got_b[...])
    out[...] = acc[...] + contract(left, masked[:, :half]) + contract(right, masked[:, span - half :])


def swap(block, distance):
    n = lax.axis_size(AXIS)
    return lax.ppermute(block, AXIS, [(i, i ^ distance) for i in range(n)])


def hop(block, step):
    pairs = []
    for i in range(lax.axis_size(AXIS)):
        g = i // GROUP
        to = i + GROUP if g == step else i - GROUP if g == step + 1 else i
        pairs.append((i, to ^ 1))
    return lax.ppermute(block, AXIS, pairs)


def swap_chips(block):
    n, segments = lax.axis_size(AXIS), lax.axis_size(SEGMENTS)
    pairs = []
    for seg in range(segments):
        for i in range(n):
            to, to_seg = i + 1 if i % 2 else i - 1, seg
            if not 0 <= to < n:
                to, to_seg = (i, seg ^ 1) if segments % 2 == 0 else (to % n, seg)
            pairs.append((seg * n + i, to_seg * n + to))
    return lax.ppermute(block, (SEGMENTS, AXIS), pairs)


def per_device(z, diag_inverse, coupling, impute_coef, anchor):
    d = diag_inverse[0]
    c = coupling[0]
    typed = d.shape[0]
    half = c.shape[1]
    traits = z.shape[0]
    untyped, span = impute_coef.shape
    assert span == typed + 2 * half and typed == 2 * half
    assert lax.axis_size(AXIS) >= 3 * GROUP
    groups = lax.axis_size(AXIS) // GROUP
    two, four = traits // 2, traits // 4
    square = (half, half)
    sq, h2, h4 = (square, f32), ((two, half), f32), ((four, half), f32)
    x1_shape, x6_shape = ((half + two, half), f32), ((2 * two, half), f32)
    x6_coded = ((2 * coded_rows(two, half), LANES), i16)
    coded = ((coded_rows(four, half), LANES), i16)
    coded_half = ((coded_rows(half // 2, half), LANES), i16)
    mixed = ((coded_rows(half // 2, half) + coded_rows(four, half), LANES), i16)

    solved_shape, p_shape = ((traits, typed), f32), ((typed, half), f32)
    x1, s_own, z, d, c = call(
        tail_part, [x1_shape, h2, solved_shape, ((typed, typed), f32), p_shape], z, d, c,
        hbm=True, scratch=[pltpu.SemaphoreType.DMA((7,))],
    )
    got1 = swap(x1, 1)
    x3, g_own, solved, p = call(
        head_part, [x1_shape, h2, solved_shape, p_shape], z, d, c, x1, s_own
    )
    x2, n_own, sp_own = call(pair_forward, [mixed, sq, h4], x1, got1, s_own, after=(p,))
    got2 = swap(x2, 3)
    got3 = swap(x3, 1)
    masked = call(
        mask_coefs, ((untyped, span), bf16), impute_coef, anchor[None, :], after=(x2,), hbm=True,
        scratch=[
            pltpu.VMEM((untyped, span), bf16),
            pltpu.VMEM((1, untyped), jnp.int32),
            pltpu.SemaphoreType.DMA((untyped // 128 + 1,)),
        ],
    )
    x4, gg_own, gp_own = call(
        pair_backward, [mixed, sq, h4], x1, got1, s_own, x3, got3, g_own, after=(x2,)
    )
    got2_core = swap(call(relay, coded_half, got2, after=(x4, masked)), 1)
    out = call(group_forward, coded, n_own, got2, got2_core, sp_own)
    parts3 = ((3 * half, half), bf16)
    s_group, up, down, n_first, n_second = call(
        group_map, [h4, parts3, parts3, sq, sq], n_own, got2, got2_core, sp_own, after=(out,)
    )
    k = call(block_map, ((half, typed), f32), n_second, x1, got1, d)
    t_in = jnp.zeros((four, half), f32)
    got4 = swap(x4, 3)
    for step in range(groups - 2):
        got = hop(out, step)
        t_in, out = call(
            functools.partial(forward_hop, step), [h4, coded], got, t_in, up, s_group,
            after=(k,) if step == 0 else (),
        )
        if step == 0:
            pieces = [((half // 2 + SCALES, LANES), i16)] * 2
            low, high = call(relay_halves, pieces, got4, after=(out,))
            got4_low, got4_high = swap(low, 1), swap(high, 1)
    gg_group, g_group, gg_second, g_second = call(
        group_backward, [sq, h4, sq, h4],
        n_first, got2, sp_own, gg_own, got4, got4_low, got4_high, gp_own, after=(out,),
    )
    last = groups - 2
    got = hop(out, last)
    t_in, out = call(
        functools.partial(turn, last), [h4, coded], got, t_in, gg_group, g_group
    )

    u_in = jnp.zeros((four, half), f32)
    for step in reversed(range(groups - 1)):
        got = hop(out, step)
        if step == last:
            x5, x5_rest, kept, rest_own, local = call(
                spread_forward, [coded, coded, h4, h4, h4],
                t_in, n_first, got2, sp_own, gg_second, g_second, gg_group, g_group, after=(out,),
            )
            got5, got5_rest = swap(x5, 3), swap(x5_rest, 3)
        if step:
            u_in, out = call(
                functools.partial(backward_hop, step), [h4, coded], got, u_in, down, local
            )
        else:
            start, maps = call(
                block_parts, [solved_shape, ((2 * half, typed), f32)], solved, p, d, after=(out,)
            )
            out = call(functools.partial(arrive, step), coded, got, u_in, after=(maps,))
    x6, own = call(
        pair_states, [x6_coded, x6_shape], kept, rest_own, got5, got5_rest, x1, got1, s_own, x3, got3, g_own
    )
    got6 = swap(x6, 1)
    fixed = call(block_fixed, solved_shape, own, got6, start, maps)
    members = [[q * GROUP + i for i in range(GROUP)] for q in range(groups)]
    quarters = lax.all_to_all(
        jnp.broadcast_to(out[None], (GROUP, *out.shape)), AXIS, 0, 0, axis_index_groups=members
    )
    edge = (square, bf16)
    xa, xb = call(block_weights, [edge, edge], quarters, fixed, k)
    got_a = swap_chips(xa)
    got_b = swap(xb, 1)
    acc = call(impute_own, ((traits, untyped), f32), xa, xb, masked)
    return call(
        impute_edges, ((traits, untyped), f32), acc, got_a, got_b, masked, last=True
    )


def solution(mesh):
    in_specs = (
        P(None, (SEGMENTS, AXIS)),
        P((SEGMENTS, AXIS), None, None),
        P((SEGMENTS, AXIS), None, None),
        P((SEGMENTS, AXIS), None),
        P((SEGMENTS, AXIS)),
    )
    return jax.shard_map(
        per_device, mesh=mesh, in_specs=in_specs, out_specs=P(None, (SEGMENTS, AXIS)), check_vma=False
    )
```

```python
import functools

import jax
import jax.numpy as jnp
from jax import lax
from jax.experimental import pallas as pl
from jax.experimental.pallas import tpu as pltpu
from jax.sharding import PartitionSpec as P

AXIS = "genome"
SEGMENTS = "seg"
GROUP = 4
f32 = jnp.float32
bf16 = jnp.bfloat16
i16 = jnp.int16
SCALES = 16
LANES = 128
LIMIT = 32767.0


def parts(x):
    high = x.astype(bf16)
    return high, (x - high.astype(f32)).astype(bf16)


def dot(a, b, ca=1, cb=0):
    ah, al = parts(a)
    bh, bl = parts(b)
    return lax.dot_general(
        jnp.concatenate([al, ah, ah], axis=ca),
        jnp.concatenate([bh, bl, bh], axis=cb),
        (((ca,), (cb,)), ((), ())),
        preferred_element_type=f32,
    )


def code(x):
    top = jnp.maximum(jnp.max(jnp.abs(x), axis=0, keepdims=True), 1e-32)
    power = jnp.ceil(jnp.log2(top) * 4.0)
    root = jnp.exp2(power * -0.125)
    steps = jnp.floor(x * root * (root * LIMIT) + 0.5)
    steps = jnp.clip(steps, -LIMIT, LIMIT)
    tiles = x.shape[1] // LANES
    powers = jnp.broadcast_to(power, (SCALES // tiles, x.shape[1]))
    pieces = [v[:, i * LANES : (i + 1) * LANES] for v in (steps, powers) for i in range(tiles)]
    return jnp.concatenate(pieces, axis=0).astype(jnp.int32).astype(i16)


def decode(coded, tiles=2):
    rows = (coded.shape[0] - SCALES) // tiles
    values = coded[...].astype(jnp.int32).astype(f32)
    columns = []
    for i in range(tiles):
        at = tiles * rows + i * (SCALES // tiles)
        root = jnp.exp2(values[at : at + 1] * 0.125)
        columns.append(values[i * rows : (i + 1) * rows] * (root / LIMIT) * root)
    return jnp.concatenate(columns, axis=1)


def coded_rows(rows, columns):
    return rows * (columns // LANES) + SCALES


def where_am_i():
    place = lax.axis_index(AXIS)
    return place % 2 == 0, (place // 2) % 2 == 0, place // GROUP


def ready(b):
    bh, bl = parts(b)
    return jnp.concatenate([bh, bl, bh], axis=0)


def dot_ready(a, b):
    ah, al = parts(a)
    return jnp.dot(jnp.concatenate([al, ah, ah], axis=1), b[...], preferred_element_type=f32)


def low_traits():
    place = lax.axis_index(AXIS)
    return (place + place // 2 + place // GROUP) % 2 == 0


def ordered(first, own, other):
    return jnp.where(first, own, other), jnp.where(first, other, own)


def call(kernel, outs, *args, after=(), hbm=False, last=False, scratch=()):
    n_in, n_after = len(args), len(after)

    def body(*refs):
        kernel(*refs[:n_in], *refs[n_in + n_after :])

    single = not isinstance(outs, list)
    shapes = [outs] if single else outs
    vmem = pl.BlockSpec(memory_space=pltpu.VMEM)
    anywhere = pl.BlockSpec(memory_space=pl.ANY)
    if hbm:
        args = [pltpu.with_memory_space_constraint(a, pltpu.HBM) for a in args]
    got = pl.pallas_call(
        body,
        out_shape=[jax.ShapeDtypeStruct(s, t) if last else pltpu.VMEM(s, t) for s, t in shapes],
        in_specs=[anywhere if hbm else vmem] * n_in + [anywhere] * n_after,
        out_specs=[vmem] * len(shapes),
        scratch_shapes=scratch,
        compiler_params=pltpu.CompilerParams(vmem_limit_bytes=8 * 2**20),
        name=kernel.__name__ if hasattr(kernel, "__name__") else kernel.func.__name__,
    )(*args, *after)
    return got[0] if single else got


def tail_part(z_in, d_in, c_in, x1, s_own, z, d, c, sems):
    typed, half = c.shape
    rows = z.shape[0] // 2
    head = typed - half
    step = typed // 2
    copies = []
    for i in range(2):
        here = pl.ds(i * step, step)
        tail = (pl.ds(head, half), here)
        copies.append(pltpu.make_async_copy(d_in.at[tail], d.at[tail], sems.at[3 * i]))
        copies.append(pltpu.make_async_copy(c_in.at[here], c.at[here], sems.at[3 * i + 1]))
        copies.append(pltpu.make_async_copy(z_in.at[:, here], z.at[:, here], sems.at[3 * i + 2]))
    rest = pl.ds(0, head)
    copies.append(pltpu.make_async_copy(d_in.at[rest], d.at[rest], sems.at[6]))
    for copy in copies:
        copy.start()
    m = s = 0.0
    for i in range(2):
        here = pl.ds(i * step, step)
        for copy in copies[3 * i : 3 * i + 3]:
            copy.wait()
        tail = d[head:, here]
        m = m - dot(tail, c[here])
        s = s + dot(z[:, here], tail, 1, 1)
    x1[:half] = m
    keep, send = ordered(low_traits(), s[:rows], s[rows:])
    x1[half:] = send
    s_own[...] = keep
    copies[6].wait()


def head_part(z, d, c, x1, s_own, x3, g_own, solved, p):
    half = c.shape[1]
    rows = z.shape[0] // 2
    head = d.shape[0] - half
    first, _, _ = where_am_i()
    p[:head] = dot(d[:head], c[...])
    p[head:] = -x1[:half]
    solved[:, :head] = dot(z[...], d[:head], 1, 1)
    low, high = ordered(low_traits(), s_own[...], x1[half:])
    solved[:rows, head:] = low
    solved[rows:, head:] = high
    g = dot(solved[...], p[...])
    keep, send = ordered(low_traits(), g[:rows], g[rows:])
    x3[:half] = dot(p[...], p[...], 0, 0)
    x3[half:] = send
    g_own[...] = keep


def pair_forward(x1, got1, s_own, x2, n_own, sp_own):
    half = x1.shape[1]
    first, first_pair, _ = where_am_i()
    m0, m1 = ordered(first, x1[:half], got1[:half])
    s0, s1 = ordered(first, s_own[...], got1[half:])
    n = dot(m1, m0)
    n_own[...] = n
    split = coded_rows(half, half)
    x2[:split] = code(n)
    s = dot(s0, m1, 1, 1) + s1
    rows = s.shape[0] // 2
    keep, send = ordered(first_pair, s[:rows], s[rows:])
    x2[split:] = code(send)
    sp_own[...] = keep


def pair_backward(x1, got1, s_own, x3, got3, g_own, x4, gg_own, gp_own):
    half = x1.shape[1]
    first, first_pair, _ = where_am_i()
    m0, _ = ordered(first, x1[:half], got1[:half])
    s0, _ = ordered(first, s_own[...], got1[half:])
    gg0, gg1 = ordered(first, x3[:half], got3[:half])
    g0, g1 = ordered(first, g_own[...], got3[half:])
    both = dot(jnp.concatenate([gg1, g1 - dot(s0, gg1)], axis=0), m0)
    gg = dot(m0, both[:half], 0, 0) + gg0
    gg_own[...] = gg
    split = coded_rows(half // 2, half)
    x4[:split] = code(jnp.where(first, gg[: half // 2], gg[half // 2 :]))
    g = both[half:] + g0
    rows = g.shape[0] // 2
    keep, send = ordered(first_pair, g[:rows], g[rows:])
    x4[split:] = code(send)
    gp_own[...] = keep


def pair_matrices(own, got, got_core):
    first, first_pair, _ = where_am_i()
    other = jnp.concatenate(ordered(first, got_core, got), axis=0)
    return ordered(first_pair, own[...], other)


def pair_vectors(own, got):
    _, first_pair, _ = where_am_i()
    return ordered(first_pair, own[...], got)


def relay(got, out):
    out[...] = got[: out.shape[0]]


def relay_halves(got, low, high):
    rows = low.shape[0] - SCALES
    low[:rows] = got[:rows]
    high[:rows] = got[rows : 2 * rows]
    low[rows:] = got[2 * rows : 2 * rows + SCALES]
    high[rows:] = got[2 * rows : 2 * rows + SCALES]


def both_pairs(own, own_rows, got):
    _, first_pair, _ = where_am_i()
    split = coded_rows(own.shape[1], own.shape[1])
    m0, m1 = ordered(first_pair, own[...], decode(got[:split]))
    v0, v1 = ordered(first_pair, own_rows[...], decode(got[split:]))
    return m0, v0, m1, v1


def group_forward(n_own, got2, sp_own, out):
    _, _, group = where_am_i()
    out[...] = jnp.zeros_like(out)

    @pl.when(group == 0)
    def _():
        _, s0, n1, s1 = both_pairs(n_own, sp_own, got2)
        out[...] = code(dot(s0, n1, 1, 1) + s1)


def group_map(n_own, got2, sp_own, s_group, up, down, n_first, n_second, s_first):
    n0, s0, n1, s1 = both_pairs(n_own, sp_own, got2)
    s_group[...] = dot(s0, n1, 1, 1) + s1
    s_first[...] = s0
    n_first[...] = n0
    n_second[...] = n1
    n_group = dot(n1, n0)
    up[...] = ready(n_group.T)
    down[...] = ready(n_group)


def block_map(n_second, x1, got1, d, k):
    half = x1.shape[1]
    first, first_pair, _ = where_am_i()
    rows = lax.broadcasted_iota(jnp.int32, (half, half), 0)
    columns = lax.broadcasted_iota(jnp.int32, (half, half), 1)
    unit = (rows == columns).astype(f32)
    _, m1 = ordered(first, x1[:half], got1[:half])
    above = jnp.where(first_pair, n_second[...], unit)
    above = jnp.where(first, dot(above, m1), above)
    k[...] = ready(dot(above, d[d.shape[0] - half :]))


def group_backward(
    n_first, s_first, gg_own, got4, got4_low, got4_high, gp_own,
    gg_group, g_group, gg_second, g_second,
):
    half = n_first.shape[1]
    split = coded_rows(half // 2, half)
    n0 = n_first[...]
    rows = got4_low.shape[0] - SCALES
    got4_core = jnp.concatenate([got4_low[:rows], got4_high[...]], axis=0)
    gg0, gg1 = pair_matrices(gg_own, decode(got4[:split]), decode(got4_core))
    g0, g1 = pair_vectors(gp_own, decode(got4[split:]))
    gg_second[...] = gg1
    g_second[...] = g1
    both = dot(jnp.concatenate([gg1, g1 - dot(s_first[...], gg1)], axis=0), n0)
    gg_group[...] = ready(dot(n0, both[:half], 0, 0) + gg0)
    g_group[...] = both[half:] + g0


def forward_hop(step, got, t_in, up, s_group, t_out, out):
    _, _, group = where_am_i()
    t = jnp.where(group == step + 1, decode(got), t_in[...])
    t_out[...] = t
    out[...] = code(dot_ready(t, up) + s_group[...])


def turn(step, got, t_in, gg_group, g_group, t_out, out):
    _, _, group = where_am_i()
    t = jnp.where(group == step + 1, decode(got), t_in[...])
    t_out[...] = t
    out[...] = jnp.zeros_like(out)

    @pl.when(group == step + 1)
    def _():
        out[...] = code(g_group[...] - dot_ready(t, gg_group))


def backward_hop(step, got, u_in, down, local, u_out, out):
    _, _, group = where_am_i()
    u = jnp.where(group == step, decode(got), u_in[...])
    u_out[...] = u
    out[...] = code(dot_ready(u, down) + local[...])


def arrive(step, got, u_in, out):
    _, _, group = where_am_i()
    out[...] = code(jnp.where(group == step, decode(got), u_in[...]))


def spread_forward(
    t_in, n_first, s_first, gg_second, g_second, gg_group, g_group, x5, x5_rest, kept, rest_own, local
):
    half = n_first.shape[1]
    _, first_pair, _ = where_am_i()
    t_mid = dot(t_in[...], n_first[...], 1, 1) + s_first[...]
    rest = g_second[...] - dot(t_mid, gg_second[...])
    keep, send = ordered(first_pair, t_in[...], t_mid)
    x5[...] = code(send)
    x5_rest[...] = code(rest)
    kept[...] = keep
    rest_own[...] = rest
    local[...] = g_group[...] - dot_ready(t_in[...], gg_group)


def pair_states(kept, rest_own, got5, got5_rest, x1, got1, s_own, x3, got3, g_own, x6, own):
    half = x1.shape[1]
    rows = s_own.shape[0]
    first, first_pair, _ = where_am_i()
    t = jnp.concatenate(ordered(first_pair, kept[...], decode(got5)), axis=0)
    rest = jnp.concatenate(ordered(first_pair, rest_own[...], decode(got5_rest)), axis=0)
    m0, m1 = ordered(first, x1[:half], got1[:half])
    s0, _ = ordered(first, s_own[...], got1[half:])
    _, gg1 = ordered(first, x3[:half], got3[:half])
    _, g1 = ordered(first, g_own[...], got3[half:])
    t_mid = dot(t, m0, 1, 1) + s0
    fixed = jnp.where(first_pair, rest, 0.0)
    fixed_mid = dot(fixed, m1) + g1 - dot(t_mid, gg1)
    split = coded_rows(rows, half)
    keep, send = ordered(first, t, t_mid)
    x6[:split] = code(send)
    own[:rows] = keep
    keep, send = ordered(first, fixed_mid, fixed)
    x6[split:] = code(send)
    own[rows:] = keep


def block_parts(solved, p, d, start, maps):
    half = p.shape[1]
    start[...] = dot(solved[...], d[...])
    maps[:half] = dot(p[...], d[...], 0, 0)
    maps[half:] = d[d.shape[0] - half :]


def block_fixed(own, got6, start, maps, fixed_weights):
    rows = own.shape[0] // 2
    split = coded_rows(rows, own.shape[1])
    low = low_traits()
    t = jnp.concatenate(ordered(low, own[:rows], decode(got6[:split])), axis=0)
    above = jnp.concatenate(ordered(low, own[rows:], decode(got6[split:])), axis=0)
    fixed_weights[...] = start[...] - dot(jnp.concatenate([t, above], axis=1), maps[...])


def block_weights(mine, got_u, theirs, their_got, fixed_weights, k, xa, xb):
    half = xa.shape[1]
    first, first_pair, _ = where_am_i()
    near = jnp.concatenate(ordered(first_pair, decode(mine), decode(got_u)), axis=0)
    far = jnp.concatenate(ordered(first_pair, decode(theirs), decode(their_got)), axis=0)
    u = jnp.concatenate(ordered(low_traits(), near, far), axis=0)
    weights = (fixed_weights[...] - dot_ready(u, k)).astype(bf16)
    a, b = ordered(first, weights[:, :half], weights[:, half:])
    xa[...] = a
    xb[...] = b


def contract(values, coefs):
    return lax.dot_general(values, coefs, (((1,), (1,)), ((), ())), preferred_element_type=f32)


def mask_coefs(coefs_in, anchor_in, masked, coefs, anchor, sems):
    untyped, span = coefs.shape
    half = span // 4
    typed = span - 2 * half
    tile = 128
    place = lax.axis_index(AXIS)
    total = lax.axis_size(AXIS) * typed
    copies = [pltpu.make_async_copy(anchor_in, anchor, sems.at[0])]
    for i in range(untyped // tile):
        rows = pl.ds(i * tile, tile)
        copies.append(pltpu.make_async_copy(coefs_in.at[rows], coefs.at[rows], sems.at[i + 1]))
    for copy in copies:
        copy.start()
    copies[0].wait()
    first_column = place * typed - half
    for i in range(untyped // tile):
        rows = pl.ds(i * tile, tile)
        nearest = jnp.broadcast_to(anchor[:, i * tile : (i + 1) * tile], (tile, tile)).T
        copies[i + 1].wait()
        for j in range(span // tile):
            lanes = pl.ds(j * tile, tile)
            columns = first_column + j * tile + lax.broadcasted_iota(jnp.int32, (tile, tile), 1)
            within = (jnp.abs(columns - nearest) <= half) & (columns >= 0) & (columns < total)
            masked[rows, lanes] = jnp.where(within, coefs[rows, lanes].astype(f32), 0.0).astype(bf16)


def impute_own(xa, xb, masked, out):
    first, _, _ = where_am_i()
    half = xa.shape[1]
    span = masked.shape[1]
    weights = jnp.concatenate(ordered(first, xa[...], xb[...]), axis=1)
    out[...] = contract(weights, masked[:, half : span - half])


def impute_edges(acc, got_a, got_b, masked, out):
    first, _, _ = where_am_i()
    half = got_a.shape[1]
    span = masked.shape[1]
    left, right = ordered(first, got_a[...], got_b[...])
    out[...] = acc[...] + contract(left, masked[:, :half]) + contract(right, masked[:, span - half :])


def swap(block, distance):
    n = lax.axis_size(AXIS)
    return lax.ppermute(block, AXIS, [(i, i ^ distance) for i in range(n)])


def hop(block, step):
    pairs = []
    for i in range(lax.axis_size(AXIS)):
        g = i // GROUP
        to = i + GROUP if g == step else i - GROUP if g == step + 1 else i
        pairs.append((i, to ^ 1))
    return lax.ppermute(block, AXIS, pairs)


def swap_chips(block):
    n, segments = lax.axis_size(AXIS), lax.axis_size(SEGMENTS)
    pairs = []
    for seg in range(segments):
        for i in range(n):
            to, to_seg = i + 1 if i % 2 else i - 1, seg
            if not 0 <= to < n:
                to, to_seg = (i, seg ^ 1) if segments % 2 == 0 else (to % n, seg)
            pairs.append((seg * n + i, to_seg * n + to))
    return lax.ppermute(block, (SEGMENTS, AXIS), pairs)


def per_device(z, diag_inverse, coupling, impute_coef, anchor):
    d = diag_inverse[0]
    c = coupling[0]
    typed = d.shape[0]
    half = c.shape[1]
    traits = z.shape[0]
    untyped, span = impute_coef.shape
    assert span == typed + 2 * half and typed == 2 * half
    assert lax.axis_size(AXIS) >= 3 * GROUP
    groups = lax.axis_size(AXIS) // GROUP
    two, four = traits // 2, traits // 4
    square = (half, half)
    sq, h2, h4 = (square, f32), ((two, half), f32), ((four, half), f32)
    x1_shape, x6_shape = ((half + two, half), f32), ((2 * two, half), f32)
    x6_coded = ((2 * coded_rows(two, half), LANES), i16)
    coded = ((coded_rows(four, half), LANES), i16)
    coded_half = ((coded_rows(half // 2, half), LANES), i16)
    whole = ((coded_rows(half, half) + coded_rows(four, half), LANES), i16)
    mixed = ((coded_rows(half // 2, half) + coded_rows(four, half), LANES), i16)

    solved_shape, p_shape = ((traits, typed), f32), ((typed, half), f32)
    x1, s_own, z, d, c = call(
        tail_part, [x1_shape, h2, solved_shape, ((typed, typed), f32), p_shape], z, d, c,
        hbm=True, scratch=[pltpu.SemaphoreType.DMA((7,))],
    )
    got1 = swap(x1, 1)
    x3, g_own, solved, p = call(
        head_part, [x1_shape, h2, solved_shape, p_shape], z, d, c, x1, s_own
    )
    x2, n_own, sp_own = call(pair_forward, [whole, sq, h4], x1, got1, s_own, after=(p,))
    got2 = swap(x2, 3)
    got3 = swap(x3, 1)
    masked = call(
        mask_coefs, ((untyped, span), bf16), impute_coef, anchor[None, :], after=(x2,), hbm=True,
        scratch=[
            pltpu.VMEM((untyped, span), bf16),
            pltpu.VMEM((1, untyped), jnp.int32),
            pltpu.SemaphoreType.DMA((untyped // 128 + 1,)),
        ],
    )
    x4, gg_own, gp_own = call(
        pair_backward, [mixed, sq, h4], x1, got1, s_own, x3, got3, g_own, after=(masked,)
    )
    out = call(group_forward, coded, n_own, got2, sp_own, after=(x4, masked))
    parts3 = ((3 * half, half), bf16)
    s_group, up, down, n_first, n_second, s_first = call(
        group_map, [h4, parts3, parts3, sq, sq, h4], n_own, got2, sp_own, after=(out,)
    )
    k = call(block_map, ((3 * half, typed), bf16), n_second, x1, got1, d)
    t_in = jnp.zeros((four, half), f32)
    got4 = swap(x4, 3)
    for step in range(groups - 2):
        got = hop(out, step)
        t_in, out = call(
            functools.partial(forward_hop, step), [h4, coded], got, t_in, up, s_group,
            after=(k,) if step == 0 else (),
        )
        if step == 0:
            pieces = [((half // 2 + SCALES, LANES), i16)] * 2
            low, high = call(relay_halves, pieces, got4, after=(out,))
            got4_low, got4_high = swap(low, 1), swap(high, 1)
    gg_group, g_group, gg_second, g_second = call(
        group_backward, [parts3, h4, sq, h4],
        n_first, s_first, gg_own, got4, got4_low, got4_high, gp_own, after=(out,),
    )
    last = groups - 2
    got = hop(out, last)
    t_in, out = call(
        functools.partial(turn, last), [h4, coded], got, t_in, gg_group, g_group
    )

    u_in = jnp.zeros((four, half), f32)
    for step in reversed(range(groups - 1)):
        got = hop(out, step)
        if step == last:
            x5, x5_rest, kept, rest_own, local = call(
                spread_forward, [coded, coded, h4, h4, h4],
                t_in, n_first, s_first, gg_second, g_second, gg_group, g_group, after=(out,),
            )
            got5, got5_rest = swap(x5, 3), swap(x5_rest, 3)
        if step:
            u_in, out = call(
                functools.partial(backward_hop, step), [h4, coded], got, u_in, down, local
            )
        else:
            start, maps = call(
                block_parts, [solved_shape, ((2 * half, typed), f32)], solved, p, d, after=(out,)
            )
            out = call(functools.partial(arrive, step), coded, got, u_in, after=(maps,))
    x6, own = call(
        pair_states, [x6_coded, x6_shape], kept, rest_own, got5, got5_rest, x1, got1, s_own, x3, got3, g_own
    )
    got6 = swap(x6, 1)
    fixed = call(block_fixed, solved_shape, own, got6, start, maps)
    theirs = swap(out, 1)
    got_u = swap(out, 3)
    their_got = swap(got_u, 1)
    edge = (square, bf16)
    xa, xb = call(block_weights, [edge, edge], out, got_u, theirs, their_got, fixed, k)
    got_a = swap_chips(xa)
    got_b = swap(xb, 1)
    acc = call(impute_own, ((traits, untyped), f32), xa, xb, masked)
    return call(
        impute_edges, ((traits, untyped), f32), acc, got_a, got_b, masked, last=True
    )


def solution(mesh):
    in_specs = (
        P(None, (SEGMENTS, AXIS)),
        P((SEGMENTS, AXIS), None, None),
        P((SEGMENTS, AXIS), None, None),
        P((SEGMENTS, AXIS), None),
        P((SEGMENTS, AXIS)),
    )
    return jax.shard_map(
        per_device, mesh=mesh, in_specs=in_specs, out_specs=P(None, (SEGMENTS, AXIS)), check_vma=False
    )
```

```python
import functools

import jax
import jax.numpy as jnp
from jax import lax
from jax.experimental import pallas as pl
from jax.experimental.pallas import tpu as pltpu
from jax.sharding import PartitionSpec as P

AXIS = "genome"
SEGMENTS = "seg"
GROUP = 4
f32 = jnp.float32
bf16 = jnp.bfloat16
i16 = jnp.int16
SCALES = 16
LANES = 128
LIMIT = 32767.0


def parts(x):
    high = x.astype(bf16)
    return high, (x - high.astype(f32)).astype(bf16)


def dot(a, b, ca=1, cb=0):
    ah, al = parts(a)
    bh, bl = parts(b)
    return lax.dot_general(
        jnp.concatenate([al, ah, ah], axis=ca),
        jnp.concatenate([bh, bl, bh], axis=cb),
        (((ca,), (cb,)), ((), ())),
        preferred_element_type=f32,
    )


def code(x):
    top = jnp.maximum(jnp.max(jnp.abs(x), axis=0, keepdims=True), 1e-32)
    power = jnp.ceil(jnp.log2(top) * 4.0)
    root = jnp.exp2(power * -0.125)
    steps = jnp.floor(x * root * (root * LIMIT) + 0.5)
    steps = jnp.clip(steps, -LIMIT, LIMIT)
    tiles = x.shape[1] // LANES
    powers = jnp.broadcast_to(power, (SCALES // tiles, x.shape[1]))
    pieces = [v[:, i * LANES : (i + 1) * LANES] for v in (steps, powers) for i in range(tiles)]
    return jnp.concatenate(pieces, axis=0).astype(jnp.int32).astype(i16)


def decode(coded, tiles=2):
    rows = (coded.shape[0] - SCALES) // tiles
    values = coded[...].astype(jnp.int32).astype(f32)
    columns = []
    for i in range(tiles):
        at = tiles * rows + i * (SCALES // tiles)
        root = jnp.exp2(values[at : at + 1] * 0.125)
        columns.append(values[i * rows : (i + 1) * rows] * (root / LIMIT) * root)
    return jnp.concatenate(columns, axis=1)


def coded_rows(rows, columns):
    return rows * (columns // LANES) + SCALES


def where_am_i():
    place = lax.axis_index(AXIS)
    return place % 2 == 0, (place // 2) % 2 == 0, place // GROUP


def ready(b):
    bh, bl = parts(b)
    return jnp.concatenate([bh, bl, bh], axis=0)


def dot_ready(a, b):
    ah, al = parts(a)
    return jnp.dot(jnp.concatenate([al, ah, ah], axis=1), b[...], preferred_element_type=f32)


def low_traits():
    place = lax.axis_index(AXIS)
    return (place + place // 2 + place // GROUP) % 2 == 0


def ordered(first, own, other):
    return jnp.where(first, own, other), jnp.where(first, other, own)


def call(kernel, outs, *args, after=(), hbm=False, last=False, scratch=()):
    n_in, n_after = len(args), len(after)

    def body(*refs):
        kernel(*refs[:n_in], *refs[n_in + n_after :])

    single = not isinstance(outs, list)
    shapes = [outs] if single else outs
    vmem = pl.BlockSpec(memory_space=pltpu.VMEM)
    anywhere = pl.BlockSpec(memory_space=pl.ANY)
    if hbm:
        args = [pltpu.with_memory_space_constraint(a, pltpu.HBM) for a in args]
    got = pl.pallas_call(
        body,
        out_shape=[jax.ShapeDtypeStruct(s, t) if last else pltpu.VMEM(s, t) for s, t in shapes],
        in_specs=[anywhere if hbm else vmem] * n_in + [anywhere] * n_after,
        out_specs=[vmem] * len(shapes),
        scratch_shapes=scratch,
        compiler_params=pltpu.CompilerParams(vmem_limit_bytes=8 * 2**20),
        name=kernel.__name__ if hasattr(kernel, "__name__") else kernel.func.__name__,
    )(*args, *after)
    return got[0] if single else got


def tail_part(z_in, d_in, c_in, x1, s_own, z, d, c, sems):
    typed, half = c.shape
    rows = z.shape[0] // 2
    head = typed - half
    step = typed // 2
    copies = []
    for i in range(2):
        here = pl.ds(i * step, step)
        tail = (pl.ds(head, half), here)
        copies.append(pltpu.make_async_copy(d_in.at[tail], d.at[tail], sems.at[3 * i]))
        copies.append(pltpu.make_async_copy(c_in.at[here], c.at[here], sems.at[3 * i + 1]))
        copies.append(pltpu.make_async_copy(z_in.at[:, here], z.at[:, here], sems.at[3 * i + 2]))
    rest = pl.ds(0, head)
    copies.append(pltpu.make_async_copy(d_in.at[rest], d.at[rest], sems.at[6]))
    for copy in copies:
        copy.start()
    m = s = 0.0
    for i in range(2):
        here = pl.ds(i * step, step)
        for copy in copies[3 * i : 3 * i + 3]:
            copy.wait()
        tail = d[head:, here]
        m = m - dot(tail, c[here])
        s = s + dot(z[:, here], tail, 1, 1)
    x1[:half] = m
    keep, send = ordered(low_traits(), s[:rows], s[rows:])
    x1[half:] = send
    s_own[...] = keep
    copies[6].wait()


def head_part(z, d, c, x1, s_own, x3, g_own, solved, p):
    half = c.shape[1]
    rows = z.shape[0] // 2
    head = d.shape[0] - half
    first, _, _ = where_am_i()
    p[:head] = dot(d[:head], c[...])
    p[head:] = -x1[:half]
    solved[:, :head] = dot(z[...], d[:head], 1, 1)
    low, high = ordered(low_traits(), s_own[...], x1[half:])
    solved[:rows, head:] = low
    solved[rows:, head:] = high
    g = dot(solved[...], p[...])
    keep, send = ordered(low_traits(), g[:rows], g[rows:])
    x3[:half] = dot(p[...], p[...], 0, 0)
    x3[half:] = send
    g_own[...] = keep


def pair_forward(x1, got1, s_own, x2, n_own, sp_own):
    half = x1.shape[1]
    first, first_pair, _ = where_am_i()
    m0, m1 = ordered(first, x1[:half], got1[:half])
    s0, s1 = ordered(first, s_own[...], got1[half:])
    n = dot(m1, m0)
    n_own[...] = n
    split = coded_rows(half // 2, half)
    x2[:split] = code(jnp.where(first, n[: half // 2], n[half // 2 :]))
    s = dot(s0, m1, 1, 1) + s1
    rows = s.shape[0] // 2
    keep, send = ordered(first_pair, s[:rows], s[rows:])
    x2[split:] = code(send)
    sp_own[...] = keep


def packed(m):
    half, quarter = m.shape[0] // 2, m.shape[0] // 4
    corner = m[half:, half:]
    low = jnp.concatenate([corner[:quarter], corner[quarter:]], axis=1)
    return jnp.concatenate([m[:half], low], axis=0)


def unpacked(rows):
    half = rows.shape[1] // 2
    corner = jnp.concatenate([rows[half:, :half], rows[half:, half:]], axis=0)
    low = jnp.concatenate([rows[:half, half:].T, corner], axis=1)
    return jnp.concatenate([rows[:half], low], axis=0)


def pair_backward(x1, got1, s_own, x3, got3, g_own, x4, x4_low, gg_own, gp_own):
    half = x1.shape[1]
    first, first_pair, _ = where_am_i()
    m0, _ = ordered(first, x1[:half], got1[:half])
    s0, _ = ordered(first, s_own[...], got1[half:])
    gg0, gg1 = ordered(first, x3[:half], got3[:half])
    g0, g1 = ordered(first, g_own[...], got3[half:])
    both = dot(jnp.concatenate([gg1, g1 - dot(s0, gg1)], axis=0), m0)
    gg = dot(m0, both[:half], 0, 0) + gg0
    gg_own[...] = gg
    rows = packed(gg)
    split = coded_rows(half // 4, half)
    x4[...] = code(rows[: half // 2])
    x4_low[:split] = code(rows[half // 2 :])
    g = both[half:] + g0
    rows = g.shape[0] // 2
    keep, send = ordered(first_pair, g[:rows], g[rows:])
    x4_low[split:] = code(send)
    gp_own[...] = keep


def pair_matrices(own, got, got_core):
    first, first_pair, _ = where_am_i()
    other = jnp.concatenate(ordered(first, got_core, got), axis=0)
    return ordered(first_pair, own[...], other)


def pair_vectors(own, got):
    _, first_pair, _ = where_am_i()
    return ordered(first_pair, own[...], got)


def relay(got, out):
    out[...] = got[: out.shape[0]]


def group_forward(n_own, got2, got2_core, sp_own, out):
    _, _, group = where_am_i()
    out[...] = jnp.zeros_like(out)

    @pl.when(group == 0)
    def _():
        split = coded_rows(n_own.shape[1] // 2, n_own.shape[1])
        _, n1 = pair_matrices(n_own, decode(got2[:split]), decode(got2_core))
        s0, s1 = pair_vectors(sp_own, decode(got2[split:]))
        out[...] = code(dot(s0, n1, 1, 1) + s1)


def group_map(n_own, got2, got2_core, sp_own, s_group, up, down, n_first, n_second):
    split = coded_rows(n_own.shape[1] // 2, n_own.shape[1])
    n0, n1 = pair_matrices(n_own, decode(got2[:split]), decode(got2_core))
    s0, s1 = pair_vectors(sp_own, decode(got2[split:]))
    s_group[...] = dot(s0, n1, 1, 1) + s1
    n_first[...] = n0
    n_second[...] = n1
    n_group = dot(n1, n0)
    up[...] = ready(n_group.T)
    down[...] = ready(n_group)


def block_map(n_second, x1, got1, d, k):
    half = x1.shape[1]
    first, first_pair, _ = where_am_i()
    rows = lax.broadcasted_iota(jnp.int32, (half, half), 0)
    columns = lax.broadcasted_iota(jnp.int32, (half, half), 1)
    unit = (rows == columns).astype(f32)
    _, m1 = ordered(first, x1[:half], got1[:half])
    above = jnp.where(first_pair, n_second[...], unit)
    above = jnp.where(first, dot(above, m1), above)
    k[...] = dot(above, d[d.shape[0] - half :])


def group_backward(
    n_first, got2, sp_own, gg_own, got4, got4_low, gp_own, gg_group, g_group, gg_second, g_second
):
    half = n_first.shape[1]
    split = coded_rows(half // 4, half)
    _, first_pair, _ = where_am_i()
    n0 = n_first[...]
    s0, _ = pair_vectors(sp_own, decode(got2[coded_rows(half // 2, half) :]))
    other = jnp.concatenate([decode(got4), decode(got4_low[:split])], axis=0)
    gg0, gg1 = ordered(first_pair, gg_own[...], unpacked(other))
    g0, g1 = pair_vectors(gp_own, decode(got4_low[split:]))
    gg_second[...] = gg1
    g_second[...] = g1
    both = dot(jnp.concatenate([gg1, g1 - dot(s0, gg1)], axis=0), n0)
    gg_group[...] = dot(n0, both[:half], 0, 0) + gg0
    g_group[...] = both[half:] + g0


def forward_hop(step, got, t_in, up, s_group, t_out, out):
    _, _, group = where_am_i()
    t = jnp.where(group == step + 1, decode(got), t_in[...])
    t_out[...] = t
    out[...] = code(dot_ready(t, up) + s_group[...])


def turn(step, got, t_in, gg_group, g_group, t_out, out):
    _, _, group = where_am_i()
    t = jnp.where(group == step + 1, decode(got), t_in[...])
    t_out[...] = t
    out[...] = jnp.zeros_like(out)

    @pl.when(group == step + 1)
    def _():
        out[...] = code(g_group[...] - dot(t, gg_group[...]))


def backward_hop(step, got, u_in, down, local, u_out, out):
    _, _, group = where_am_i()
    u = jnp.where(group == step, decode(got), u_in[...])
    u_out[...] = u
    out[...] = code(dot_ready(u, down) + local[...])


def arrive(step, got, u_in, out):
    _, _, group = where_am_i()
    out[...] = code(jnp.where(group == step, decode(got), u_in[...]))


def spread_forward(
    t_in, n_first, got2, sp_own, gg_second, g_second, gg_group, g_group, x5, x5_rest, kept, rest_own, local
):
    half = n_first.shape[1]
    _, first_pair, _ = where_am_i()
    s0, _ = pair_vectors(sp_own, decode(got2[coded_rows(half // 2, half) :]))
    t_mid = dot(t_in[...], n_first[...], 1, 1) + s0
    rest = g_second[...] - dot(t_mid, gg_second[...])
    keep, send = ordered(first_pair, t_in[...], t_mid)
    x5[...] = code(send)
    x5_rest[...] = code(rest)
    kept[...] = keep
    rest_own[...] = rest
    local[...] = g_group[...] - dot(t_in[...], gg_group[...])


def pair_states(kept, rest_own, got5, got5_rest, x1, got1, s_own, x3, got3, g_own, x6, own):
    half = x1.shape[1]
    rows = s_own.shape[0]
    first, first_pair, _ = where_am_i()
    t = jnp.concatenate(ordered(first_pair, kept[...], decode(got5)), axis=0)
    rest = jnp.concatenate(ordered(first_pair, rest_own[...], decode(got5_rest)), axis=0)
    m0, m1 = ordered(first, x1[:half], got1[:half])
    s0, _ = ordered(first, s_own[...], got1[half:])
    _, gg1 = ordered(first, x3[:half], got3[:half])
    _, g1 = ordered(first, g_own[...], got3[half:])
    t_mid = dot(t, m0, 1, 1) + s0
    fixed = jnp.where(first_pair, rest, 0.0)
    fixed_mid = dot(fixed, m1) + g1 - dot(t_mid, gg1)
    split = coded_rows(rows, half)
    keep, send = ordered(first, t, t_mid)
    x6[:split] = code(send)
    own[:rows] = keep
    keep, send = ordered(first, fixed_mid, fixed)
    x6[split:] = code(send)
    own[rows:] = keep


def block_parts(solved, p, d, start, maps):
    half = p.shape[1]
    start[...] = dot(solved[...], d[...])
    maps[:half] = dot(p[...], d[...], 0, 0)
    maps[half:] = d[d.shape[0] - half :]


def block_fixed(own, got6, start, maps, fixed_weights):
    rows = own.shape[0] // 2
    split = coded_rows(rows, own.shape[1])
    low = low_traits()
    t = jnp.concatenate(ordered(low, own[:rows], decode(got6[:split])), axis=0)
    above = jnp.concatenate(ordered(low, own[rows:], decode(got6[split:])), axis=0)
    fixed_weights[...] = start[...] - dot(jnp.concatenate([t, above], axis=1), maps[...])


def block_weights(mine, got_u, theirs, their_got, fixed_weights, k, xa, xb):
    half = k.shape[0]
    first, first_pair, _ = where_am_i()
    near = jnp.concatenate(ordered(first_pair, decode(mine), decode(got_u)), axis=0)
    far = jnp.concatenate(ordered(first_pair, decode(theirs), decode(their_got)), axis=0)
    u = jnp.concatenate(ordered(low_traits(), near, far), axis=0)
    weights = (fixed_weights[...] - dot(u, k[...])).astype(bf16)
    a, b = ordered(first, weights[:, :half], weights[:, half:])
    xa[...] = a
    xb[...] = b


def contract(values, coefs):
    return lax.dot_general(values, coefs, (((1,), (1,)), ((), ())), preferred_element_type=f32)


def mask_coefs(coefs_in, anchor_in, masked, coefs, anchor, sems):
    untyped, span = coefs.shape
    half = span // 4
    typed = span - 2 * half
    tile = 128
    place = lax.axis_index(AXIS)
    total = lax.axis_size(AXIS) * typed
    copies = [pltpu.make_async_copy(anchor_in, anchor, sems.at[0])]
    for i in range(untyped // tile):
        rows = pl.ds(i * tile, tile)
        copies.append(pltpu.make_async_copy(coefs_in.at[rows], coefs.at[rows], sems.at[i + 1]))
    for copy in copies:
        copy.start()
    copies[0].wait()
    first_column = place * typed - half
    for i in range(untyped // tile):
        rows = pl.ds(i * tile, tile)
        nearest = jnp.broadcast_to(anchor[:, i * tile : (i + 1) * tile], (tile, tile)).T
        copies[i + 1].wait()
        for j in range(span // tile):
            lanes = pl.ds(j * tile, tile)
            columns = first_column + j * tile + lax.broadcasted_iota(jnp.int32, (tile, tile), 1)
            within = (jnp.abs(columns - nearest) <= half) & (columns >= 0) & (columns < total)
            masked[rows, lanes] = jnp.where(within, coefs[rows, lanes].astype(f32), 0.0).astype(bf16)


def impute_own(xa, xb, masked, out):
    first, _, _ = where_am_i()
    half = xa.shape[1]
    span = masked.shape[1]
    weights = jnp.concatenate(ordered(first, xa[...], xb[...]), axis=1)
    out[...] = contract(weights, masked[:, half : span - half])


def impute_edges(acc, got_a, got_b, masked, out):
    first, _, _ = where_am_i()
    half = got_a.shape[1]
    span = masked.shape[1]
    left, right = ordered(first, got_a[...], got_b[...])
    out[...] = acc[...] + contract(left, masked[:, :half]) + contract(right, masked[:, span - half :])


def swap(block, distance):
    n = lax.axis_size(AXIS)
    return lax.ppermute(block, AXIS, [(i, i ^ distance) for i in range(n)])


def hop(block, step):
    pairs = []
    for i in range(lax.axis_size(AXIS)):
        g = i // GROUP
        to = i + GROUP if g == step else i - GROUP if g == step + 1 else i
        pairs.append((i, to ^ 1))
    return lax.ppermute(block, AXIS, pairs)


def swap_chips(block):
    n, segments = lax.axis_size(AXIS), lax.axis_size(SEGMENTS)
    pairs = []
    for seg in range(segments):
        for i in range(n):
            to, to_seg = i + 1 if i % 2 else i - 1, seg
            if not 0 <= to < n:
                to, to_seg = (i, seg ^ 1) if segments % 2 == 0 else (to % n, seg)
            pairs.append((seg * n + i, to_seg * n + to))
    return lax.ppermute(block, (SEGMENTS, AXIS), pairs)


def per_device(z, diag_inverse, coupling, impute_coef, anchor):
    d = diag_inverse[0]
    c = coupling[0]
    typed = d.shape[0]
    half = c.shape[1]
    traits = z.shape[0]
    untyped, span = impute_coef.shape
    assert span == typed + 2 * half and typed == 2 * half
    assert lax.axis_size(AXIS) >= 3 * GROUP
    groups = lax.axis_size(AXIS) // GROUP
    two, four = traits // 2, traits // 4
    square = (half, half)
    sq, h2, h4 = (square, f32), ((two, half), f32), ((four, half), f32)
    x1_shape, x6_shape = ((half + two, half), f32), ((2 * two, half), f32)
    x6_coded = ((2 * coded_rows(two, half), LANES), i16)
    coded = ((coded_rows(four, half), LANES), i16)
    coded_half = ((coded_rows(half // 2, half), LANES), i16)
    two_coded = ((2 * coded_rows(four, half), LANES), i16)
    mixed = ((coded_rows(half // 2, half) + coded_rows(four, half), LANES), i16)

    solved_shape, p_shape = ((traits, typed), f32), ((typed, half), f32)
    x1, s_own, z, d, c = call(
        tail_part, [x1_shape, h2, solved_shape, ((typed, typed), f32), p_shape], z, d, c,
        hbm=True, scratch=[pltpu.SemaphoreType.DMA((7,))],
    )
    got1 = swap(x1, 1)
    x3, g_own, solved, p = call(
        head_part, [x1_shape, h2, solved_shape, p_shape], z, d, c, x1, s_own
    )
    x2, n_own, sp_own = call(pair_forward, [mixed, sq, h4], x1, got1, s_own, after=(p,))
    got2 = swap(x2, 3)
    got3 = swap(x3, 1)
    masked = call(
        mask_coefs, ((untyped, span), bf16), impute_coef, anchor[None, :], after=(x2,), hbm=True,
        scratch=[
            pltpu.VMEM((untyped, span), bf16),
            pltpu.VMEM((1, untyped), jnp.int32),
            pltpu.SemaphoreType.DMA((untyped // 128 + 1,)),
        ],
    )
    x4, x4_low, gg_own, gp_own = call(
        pair_backward, [coded_half, two_coded, sq, h4], x1, got1, s_own, x3, got3, g_own, after=(x2,)
    )
    got2_core = swap(call(relay, coded_half, got2, after=(x4, masked)), 1)
    out = call(group_forward, coded, n_own, got2, got2_core, sp_own)
    parts3 = ((3 * half, half), bf16)
    s_group, up, down, n_first, n_second = call(
        group_map, [h4, parts3, parts3, sq, sq], n_own, got2, got2_core, sp_own, after=(out,)
    )
    t_in = jnp.zeros((four, half), f32)
    got4, got4_low = swap(x4, 3), swap(x4_low, 3)
    for step in range(groups - 2):
        got = hop(out, step)
        t_in, out = call(
            functools.partial(forward_hop, step), [h4, coded], got, t_in, up, s_group,
            after=(k,) if step == 1 else (),
        )
        if step == 0:
            k = call(block_map, ((half, typed), f32), n_second, x1, got1, d, after=(out,))
    gg_group, g_group, gg_second, g_second = call(
        group_backward, [sq, h4, sq, h4],
        n_first, got2, sp_own, gg_own, got4, got4_low, gp_own, after=(out,),
    )
    last = groups - 2
    got = hop(out, last)
    t_in, out = call(
        functools.partial(turn, last), [h4, coded], got, t_in, gg_group, g_group
    )

    u_in = jnp.zeros((four, half), f32)
    for step in reversed(range(groups - 1)):
        got = hop(out, step)
        if step == last:
            x5, x5_rest, kept, rest_own, local = call(
                spread_forward, [coded, coded, h4, h4, h4],
                t_in, n_first, got2, sp_own, gg_second, g_second, gg_group, g_group, after=(out,),
            )
            got5, got5_rest = swap(x5, 3), swap(x5_rest, 3)
        if step:
            u_in, out = call(
                functools.partial(backward_hop, step), [h4, coded], got, u_in, down, local
            )
        else:
            start, maps = call(
                block_parts, [solved_shape, ((2 * half, typed), f32)], solved, p, d, after=(out,)
            )
            out = call(functools.partial(arrive, step), coded, got, u_in, after=(maps,))
    x6, own = call(
        pair_states, [x6_coded, x6_shape], kept, rest_own, got5, got5_rest, x1, got1, s_own, x3, got3, g_own
    )
    got6 = swap(x6, 1)
    fixed = call(block_fixed, solved_shape, own, got6, start, maps)
    theirs = swap(out, 1)
    got_u = swap(out, 3)
    their_got = swap(got_u, 1)
    edge = (square, bf16)
    xa, xb = call(block_weights, [edge, edge], out, got_u, theirs, their_got, fixed, k)
    got_a = swap_chips(xa)
    got_b = swap(xb, 1)
    acc = call(impute_own, ((traits, untyped), f32), xa, xb, masked)
    return call(
        impute_edges, ((traits, untyped), f32), acc, got_a, got_b, masked, last=True
    )


def solution(mesh):
    in_specs = (
        P(None, (SEGMENTS, AXIS)),
        P((SEGMENTS, AXIS), None, None),
        P((SEGMENTS, AXIS), None, None),
        P((SEGMENTS, AXIS), None),
        P((SEGMENTS, AXIS)),
    )
    return jax.shard_map(
        per_device, mesh=mesh, in_specs=in_specs, out_specs=P(None, (SEGMENTS, AXIS)), check_vma=False
    )
```

```python
import functools

import jax
import jax.numpy as jnp
from jax import lax
from jax.experimental import pallas as pl
from jax.experimental.pallas import tpu as pltpu
from jax.sharding import PartitionSpec as P

AXIS = "genome"
SEGMENTS = "seg"
GROUP = 4
f32 = jnp.float32
bf16 = jnp.bfloat16
i16 = jnp.int16
SCALES = 16
LANES = 128
LIMIT = 32767.0


def parts(x):
    high = x.astype(bf16)
    return high, (x - high.astype(f32)).astype(bf16)


def dot(a, b, ca=1, cb=0):
    ah, al = parts(a)
    bh, bl = parts(b)
    return lax.dot_general(
        jnp.concatenate([al, ah, ah], axis=ca),
        jnp.concatenate([bh, bl, bh], axis=cb),
        (((ca,), (cb,)), ((), ())),
        preferred_element_type=f32,
    )


def code(x):
    top = jnp.maximum(jnp.max(jnp.abs(x), axis=0, keepdims=True), 1e-32)
    power = jnp.ceil(jnp.log2(top) * 4.0)
    root = jnp.exp2(power * -0.125)
    steps = jnp.floor(x * root * (root * LIMIT) + 0.5)
    steps = jnp.clip(steps, -LIMIT, LIMIT)
    tiles = x.shape[1] // LANES
    powers = jnp.broadcast_to(power, (SCALES // tiles, x.shape[1]))
    pieces = [v[:, i * LANES : (i + 1) * LANES] for v in (steps, powers) for i in range(tiles)]
    return jnp.concatenate(pieces, axis=0).astype(jnp.int32).astype(i16)


def decode(coded, tiles=2):
    rows = (coded.shape[0] - SCALES) // tiles
    values = coded[...].astype(jnp.int32).astype(f32)
    columns = []
    for i in range(tiles):
        at = tiles * rows + i * (SCALES // tiles)
        root = jnp.exp2(values[at : at + 1] * 0.125)
        columns.append(values[i * rows : (i + 1) * rows] * (root / LIMIT) * root)
    return jnp.concatenate(columns, axis=1)


def coded_rows(rows, columns):
    return rows * (columns // LANES) + SCALES


def where_am_i():
    place = lax.axis_index(AXIS)
    return place % 2 == 0, (place // 2) % 2 == 0, place // GROUP


def ready(b):
    bh, bl = parts(b)
    return jnp.concatenate([bh, bl, bh], axis=0)


def dot_ready(a, b):
    ah, al = parts(a)
    return jnp.dot(jnp.concatenate([al, ah, ah], axis=1), b[...], preferred_element_type=f32)


def low_traits():
    place = lax.axis_index(AXIS)
    return (place + place // 2 + place // GROUP) % 2 == 0


def ordered(first, own, other):
    return jnp.where(first, own, other), jnp.where(first, other, own)


def call(kernel, outs, *args, after=(), hbm=False, last=False, scratch=()):
    n_in, n_after = len(args), len(after)

    def body(*refs):
        kernel(*refs[:n_in], *refs[n_in + n_after :])

    single = not isinstance(outs, list)
    shapes = [outs] if single else outs
    vmem = pl.BlockSpec(memory_space=pltpu.VMEM)
    anywhere = pl.BlockSpec(memory_space=pl.ANY)
    if hbm:
        args = [pltpu.with_memory_space_constraint(a, pltpu.HBM) for a in args]
    got = pl.pallas_call(
        body,
        out_shape=[jax.ShapeDtypeStruct(s, t) if last else pltpu.VMEM(s, t) for s, t in shapes],
        in_specs=[anywhere if hbm else vmem] * n_in + [anywhere] * n_after,
        out_specs=[vmem] * len(shapes),
        scratch_shapes=scratch,
        compiler_params=pltpu.CompilerParams(vmem_limit_bytes=8 * 2**20),
        name=kernel.__name__ if hasattr(kernel, "__name__") else kernel.func.__name__,
    )(*args, *after)
    return got[0] if single else got


def tail_part(z_in, d_in, c_in, x1, s_own, z, d, c, sems):
    typed, half = c.shape
    rows = z.shape[0] // 2
    head = typed - half
    step = typed // 2
    copies = []
    for i in range(2):
        here = pl.ds(i * step, step)
        tail = (pl.ds(head, half), here)
        copies.append(pltpu.make_async_copy(d_in.at[tail], d.at[tail], sems.at[3 * i]))
        copies.append(pltpu.make_async_copy(c_in.at[here], c.at[here], sems.at[3 * i + 1]))
        copies.append(pltpu.make_async_copy(z_in.at[:, here], z.at[:, here], sems.at[3 * i + 2]))
    rest = pl.ds(0, head)
    copies.append(pltpu.make_async_copy(d_in.at[rest], d.at[rest], sems.at[6]))
    for copy in copies:
        copy.start()
    m = s = 0.0
    for i in range(2):
        here = pl.ds(i * step, step)
        for copy in copies[3 * i : 3 * i + 3]:
            copy.wait()
        tail = d[head:, here]
        m = m - dot(tail, c[here])
        s = s + dot(z[:, here], tail, 1, 1)
    x1[:half] = m
    keep, send = ordered(low_traits(), s[:rows], s[rows:])
    x1[half:] = send
    s_own[...] = keep
    copies[6].wait()


def head_part(z, d, c, x1, s_own, x3, g_own, solved, p):
    half = c.shape[1]
    rows = z.shape[0] // 2
    head = d.shape[0] - half
    first, _, _ = where_am_i()
    p[:head] = dot(d[:head], c[...])
    p[head:] = -x1[:half]
    solved[:, :head] = dot(z[...], d[:head], 1, 1)
    low, high = ordered(low_traits(), s_own[...], x1[half:])
    solved[:rows, head:] = low
    solved[rows:, head:] = high
    g = dot(solved[...], p[...])
    keep, send = ordered(low_traits(), g[:rows], g[rows:])
    x3[:half] = dot(p[...], p[...], 0, 0)
    x3[half:] = send
    g_own[...] = keep


def pair_forward(x1, got1, s_own, x2, n_own, sp_own):
    half = x1.shape[1]
    first, first_pair, _ = where_am_i()
    m0, m1 = ordered(first, x1[:half], got1[:half])
    s0, s1 = ordered(first, s_own[...], got1[half:])
    n = dot(m1, m0)
    n_own[...] = n
    split = coded_rows(half // 2, half)
    x2[:split] = code(jnp.where(first, n[: half // 2], n[half // 2 :]))
    s = dot(s0, m1, 1, 1) + s1
    rows = s.shape[0] // 2
    keep, send = ordered(first_pair, s[:rows], s[rows:])
    x2[split:] = code(send)
    sp_own[...] = keep


def packed(m):
    half, quarter = m.shape[0] // 2, m.shape[0] // 4
    corner = m[half:, half:]
    low = jnp.concatenate([corner[:quarter], corner[quarter:]], axis=1)
    return jnp.concatenate([m[:half], low], axis=0)


def unpacked(rows):
    half = rows.shape[1] // 2
    corner = jnp.concatenate([rows[half:, :half], rows[half:, half:]], axis=0)
    low = jnp.concatenate([rows[:half, half:].T, corner], axis=1)
    return jnp.concatenate([rows[:half], low], axis=0)


def pair_backward(x1, got1, s_own, x3, got3, g_own, x4, gg_own, gp_own):
    half = x1.shape[1]
    first, first_pair, _ = where_am_i()
    m0, _ = ordered(first, x1[:half], got1[:half])
    s0, _ = ordered(first, s_own[...], got1[half:])
    gg0, gg1 = ordered(first, x3[:half], got3[:half])
    g0, g1 = ordered(first, g_own[...], got3[half:])
    both = dot(jnp.concatenate([gg1, g1 - dot(s0, gg1)], axis=0), m0)
    gg = dot(m0, both[:half], 0, 0) + gg0
    gg_own[...] = gg
    split = coded_rows(3 * half // 4, half)
    x4[:split] = code(packed(gg))
    g = both[half:] + g0
    rows = g.shape[0] // 2
    keep, send = ordered(first_pair, g[:rows], g[rows:])
    x4[split:] = code(send)
    gp_own[...] = keep


def pair_matrices(own, got, got_core):
    first, first_pair, _ = where_am_i()
    other = jnp.concatenate(ordered(first, got_core, got), axis=0)
    return ordered(first_pair, own[...], other)


def pair_vectors(own, got):
    _, first_pair, _ = where_am_i()
    return ordered(first_pair, own[...], got)


def relay(got, out):
    out[...] = got[: out.shape[0]]


def group_forward(n_own, got2, got2_core, sp_own, out):
    _, _, group = where_am_i()
    out[...] = jnp.zeros_like(out)

    @pl.when(group == 0)
    def _():
        split = coded_rows(n_own.shape[1] // 2, n_own.shape[1])
        _, n1 = pair_matrices(n_own, decode(got2[:split]), decode(got2_core))
        s0, s1 = pair_vectors(sp_own, decode(got2[split:]))
        out[...] = code(dot(s0, n1, 1, 1) + s1)


def group_map(n_own, got2, got2_core, sp_own, s_group, up, down, n_first, n_second):
    split = coded_rows(n_own.shape[1] // 2, n_own.shape[1])
    n0, n1 = pair_matrices(n_own, decode(got2[:split]), decode(got2_core))
    s0, s1 = pair_vectors(sp_own, decode(got2[split:]))
    s_group[...] = dot(s0, n1, 1, 1) + s1
    n_first[...] = n0
    n_second[...] = n1
    n_group = dot(n1, n0)
    up[...] = ready(n_group.T)
    down[...] = ready(n_group)


def block_map(n_second, x1, got1, d, k):
    half = x1.shape[1]
    first, first_pair, _ = where_am_i()
    rows = lax.broadcasted_iota(jnp.int32, (half, half), 0)
    columns = lax.broadcasted_iota(jnp.int32, (half, half), 1)
    unit = (rows == columns).astype(f32)
    _, m1 = ordered(first, x1[:half], got1[:half])
    above = jnp.where(first_pair, n_second[...], unit)
    above = jnp.where(first, dot(above, m1), above)
    k[...] = dot(above, d[d.shape[0] - half :])


def group_backward(
    n_first, got2, sp_own, gg_own, got4, gp_own, gg_group, g_group, gg_second, g_second
):
    half = n_first.shape[1]
    split = coded_rows(3 * half // 4, half)
    _, first_pair, _ = where_am_i()
    n0 = n_first[...]
    s0, _ = pair_vectors(sp_own, decode(got2[coded_rows(half // 2, half) :]))
    gg0, gg1 = ordered(first_pair, gg_own[...], unpacked(decode(got4[:split])))
    g0, g1 = pair_vectors(gp_own, decode(got4[split:]))
    gg_second[...] = gg1
    g_second[...] = g1
    both = dot(jnp.concatenate([gg1, g1 - dot(s0, gg1)], axis=0), n0)
    gg_group[...] = dot(n0, both[:half], 0, 0) + gg0
    g_group[...] = both[half:] + g0


def forward_hop(step, got, t_in, up, s_group, t_out, out):
    _, _, group = where_am_i()
    t = jnp.where(group == step + 1, decode(got), t_in[...])
    t_out[...] = t
    out[...] = code(dot_ready(t, up) + s_group[...])


def turn(step, got, t_in, gg_group, g_group, t_out, out):
    _, _, group = where_am_i()
    t = jnp.where(group == step + 1, decode(got), t_in[...])
    t_out[...] = t
    out[...] = jnp.zeros_like(out)

    @pl.when(group == step + 1)
    def _():
        out[...] = code(g_group[...] - dot(t, gg_group[...]))


def backward_hop(step, got, u_in, down, local, u_out, out):
    _, _, group = where_am_i()
    u = jnp.where(group == step, decode(got), u_in[...])
    u_out[...] = u
    out[...] = code(dot_ready(u, down) + local[...])


def arrive(step, got, u_in, out):
    _, _, group = where_am_i()
    out[...] = code(jnp.where(group == step, decode(got), u_in[...]))


def spread_forward(
    t_in, n_first, got2, sp_own, gg_second, g_second, gg_group, g_group, x5, x5_rest, kept, rest_own, local
):
    half = n_first.shape[1]
    _, first_pair, _ = where_am_i()
    s0, _ = pair_vectors(sp_own, decode(got2[coded_rows(half // 2, half) :]))
    t_mid = dot(t_in[...], n_first[...], 1, 1) + s0
    rest = g_second[...] - dot(t_mid, gg_second[...])
    keep, send = ordered(first_pair, t_in[...], t_mid)
    x5[...] = code(send)
    x5_rest[...] = code(rest)
    kept[...] = keep
    rest_own[...] = rest
    local[...] = g_group[...] - dot(t_in[...], gg_group[...])


def pair_states(kept, rest_own, got5, got5_rest, x1, got1, s_own, x3, got3, g_own, x6, own):
    half = x1.shape[1]
    rows = s_own.shape[0]
    first, first_pair, _ = where_am_i()
    t = jnp.concatenate(ordered(first_pair, kept[...], decode(got5)), axis=0)
    rest = jnp.concatenate(ordered(first_pair, rest_own[...], decode(got5_rest)), axis=0)
    m0, m1 = ordered(first, x1[:half], got1[:half])
    s0, _ = ordered(first, s_own[...], got1[half:])
    _, gg1 = ordered(first, x3[:half], got3[:half])
    _, g1 = ordered(first, g_own[...], got3[half:])
    t_mid = dot(t, m0, 1, 1) + s0
    fixed = jnp.where(first_pair, rest, 0.0)
    fixed_mid = dot(fixed, m1) + g1 - dot(t_mid, gg1)
    split = coded_rows(rows, half)
    keep, send = ordered(first, t, t_mid)
    x6[:split] = code(send)
    own[:rows] = keep
    keep, send = ordered(first, fixed_mid, fixed)
    x6[split:] = code(send)
    own[rows:] = keep


def block_parts(solved, p, d, start, maps):
    half = p.shape[1]
    start[...] = dot(solved[...], d[...])
    maps[:half] = dot(p[...], d[...], 0, 0)
    maps[half:] = d[d.shape[0] - half :]


def block_fixed(own, got6, start, maps, fixed_weights):
    rows = own.shape[0] // 2
    split = coded_rows(rows, own.shape[1])
    low = low_traits()
    t = jnp.concatenate(ordered(low, own[:rows], decode(got6[:split])), axis=0)
    above = jnp.concatenate(ordered(low, own[rows:], decode(got6[split:])), axis=0)
    fixed_weights[...] = start[...] - dot(jnp.concatenate([t, above], axis=1), maps[...])


def block_weights(mine, got_u, theirs, their_got, fixed_weights, k, xa, xb):
    half = k.shape[0]
    first, first_pair, _ = where_am_i()
    near = jnp.concatenate(ordered(first_pair, decode(mine), decode(got_u)), axis=0)
    far = jnp.concatenate(ordered(first_pair, decode(theirs), decode(their_got)), axis=0)
    u = jnp.concatenate(ordered(low_traits(), near, far), axis=0)
    weights = (fixed_weights[...] - dot(u, k[...])).astype(bf16)
    a, b = ordered(first, weights[:, :half], weights[:, half:])
    xa[...] = a
    xb[...] = b


def contract(values, coefs):
    return lax.dot_general(values, coefs, (((1,), (1,)), ((), ())), preferred_element_type=f32)


def mask_coefs(coefs_in, anchor_in, masked, coefs, anchor, sems):
    untyped, span = coefs.shape
    half = span // 4
    typed = span - 2 * half
    tile = 128
    place = lax.axis_index(AXIS)
    total = lax.axis_size(AXIS) * typed
    copies = [pltpu.make_async_copy(anchor_in, anchor, sems.at[0])]
    for i in range(untyped // tile):
        rows = pl.ds(i * tile, tile)
        copies.append(pltpu.make_async_copy(coefs_in.at[rows], coefs.at[rows], sems.at[i + 1]))
    for copy in copies:
        copy.start()
    copies[0].wait()
    first_column = place * typed - half
    for i in range(untyped // tile):
        rows = pl.ds(i * tile, tile)
        nearest = jnp.broadcast_to(anchor[:, i * tile : (i + 1) * tile], (tile, tile)).T
        copies[i + 1].wait()
        for j in range(span // tile):
            lanes = pl.ds(j * tile, tile)
            columns = first_column + j * tile + lax.broadcasted_iota(jnp.int32, (tile, tile), 1)
            within = (jnp.abs(columns - nearest) <= half) & (columns >= 0) & (columns < total)
            masked[rows, lanes] = jnp.where(within, coefs[rows, lanes].astype(f32), 0.0).astype(bf16)


def impute_own(xa, xb, masked, out):
    first, _, _ = where_am_i()
    half = xa.shape[1]
    span = masked.shape[1]
    weights = jnp.concatenate(ordered(first, xa[...], xb[...]), axis=1)
    out[...] = contract(weights, masked[:, half : span - half])


def impute_edges(acc, got_a, got_b, masked, out):
    first, _, _ = where_am_i()
    half = got_a.shape[1]
    span = masked.shape[1]
    left, right = ordered(first, got_a[...], got_b[...])
    out[...] = acc[...] + contract(left, masked[:, :half]) + contract(right, masked[:, span - half :])


def swap(block, distance):
    n = lax.axis_size(AXIS)
    return lax.ppermute(block, AXIS, [(i, i ^ distance) for i in range(n)])


def hop(block, step):
    pairs = []
    for i in range(lax.axis_size(AXIS)):
        g = i // GROUP
        to = i + GROUP if g == step else i - GROUP if g == step + 1 else i
        pairs.append((i, to ^ 1))
    return lax.ppermute(block, AXIS, pairs)


def swap_chips(block):
    n, segments = lax.axis_size(AXIS), lax.axis_size(SEGMENTS)
    pairs = []
    for seg in range(segments):
        for i in range(n):
            to, to_seg = i + 1 if i % 2 else i - 1, seg
            if not 0 <= to < n:
                to, to_seg = (i, seg ^ 1) if segments % 2 == 0 else (to % n, seg)
            pairs.append((seg * n + i, to_seg * n + to))
    return lax.ppermute(block, (SEGMENTS, AXIS), pairs)


def per_device(z, diag_inverse, coupling, impute_coef, anchor):
    d = diag_inverse[0]
    c = coupling[0]
    typed = d.shape[0]
    half = c.shape[1]
    traits = z.shape[0]
    untyped, span = impute_coef.shape
    assert span == typed + 2 * half and typed == 2 * half
    assert lax.axis_size(AXIS) >= 3 * GROUP
    groups = lax.axis_size(AXIS) // GROUP
    two, four = traits // 2, traits // 4
    square = (half, half)
    sq, h2, h4 = (square, f32), ((two, half), f32), ((four, half), f32)
    x1_shape, x6_shape = ((half + two, half), f32), ((2 * two, half), f32)
    x6_coded = ((2 * coded_rows(two, half), LANES), i16)
    coded = ((coded_rows(four, half), LANES), i16)
    coded_half = ((coded_rows(half // 2, half), LANES), i16)
    symmetric = ((coded_rows(3 * half // 4, half) + coded_rows(four, half), LANES), i16)
    mixed = ((coded_rows(half // 2, half) + coded_rows(four, half), LANES), i16)

    solved_shape, p_shape = ((traits, typed), f32), ((typed, half), f32)
    x1, s_own, z, d, c = call(
        tail_part, [x1_shape, h2, solved_shape, ((typed, typed), f32), p_shape], z, d, c,
        hbm=True, scratch=[pltpu.SemaphoreType.DMA((7,))],
    )
    got1 = swap(x1, 1)
    x3, g_own, solved, p = call(
        head_part, [x1_shape, h2, solved_shape, p_shape], z, d, c, x1, s_own
    )
    x2, n_own, sp_own = call(pair_forward, [mixed, sq, h4], x1, got1, s_own, after=(p,))
    got2 = swap(x2, 3)
    got3 = swap(x3, 1)
    masked = call(
        mask_coefs, ((untyped, span), bf16), impute_coef, anchor[None, :], after=(x2,), hbm=True,
        scratch=[
            pltpu.VMEM((untyped, span), bf16),
            pltpu.VMEM((1, untyped), jnp.int32),
            pltpu.SemaphoreType.DMA((untyped // 128 + 1,)),
        ],
    )
    x4, gg_own, gp_own = call(
        pair_backward, [symmetric, sq, h4], x1, got1, s_own, x3, got3, g_own, after=(x2,)
    )
    got2_core = swap(call(relay, coded_half, got2, after=(x4, masked)), 1)
    out = call(group_forward, coded, n_own, got2, got2_core, sp_own)
    parts3 = ((3 * half, half), bf16)
    s_group, up, down, n_first, n_second = call(
        group_map, [h4, parts3, parts3, sq, sq], n_own, got2, got2_core, sp_own, after=(out,)
    )
    t_in = jnp.zeros((four, half), f32)
    got4 = swap(x4, 3)
    for step in range(groups - 2):
        got = hop(out, step)
        t_in, out = call(
            functools.partial(forward_hop, step), [h4, coded], got, t_in, up, s_group,
            after=(k,) if step == 1 else (),
        )
        if step == 0:
            k = call(block_map, ((half, typed), f32), n_second, x1, got1, d, after=(out,))
    gg_group, g_group, gg_second, g_second = call(
        group_backward, [sq, h4, sq, h4],
        n_first, got2, sp_own, gg_own, got4, gp_own, after=(out,),
    )
    last = groups - 2
    got = hop(out, last)
    t_in, out = call(
        functools.partial(turn, last), [h4, coded], got, t_in, gg_group, g_group
    )

    u_in = jnp.zeros((four, half), f32)
    for step in reversed(range(groups - 1)):
        got = hop(out, step)
        if step == last:
            x5, x5_rest, kept, rest_own, local = call(
                spread_forward, [coded, coded, h4, h4, h4],
                t_in, n_first, got2, sp_own, gg_second, g_second, gg_group, g_group, after=(out,),
            )
            got5, got5_rest = swap(x5, 3), swap(x5_rest, 3)
        if step:
            u_in, out = call(
                functools.partial(backward_hop, step), [h4, coded], got, u_in, down, local
            )
        else:
            start, maps = call(
                block_parts, [solved_shape, ((2 * half, typed), f32)], solved, p, d, after=(out,)
            )
            out = call(functools.partial(arrive, step), coded, got, u_in, after=(maps,))
    x6, own = call(
        pair_states, [x6_coded, x6_shape], kept, rest_own, got5, got5_rest, x1, got1, s_own, x3, got3, g_own
    )
    got6 = swap(x6, 1)
    fixed = call(block_fixed, solved_shape, own, got6, start, maps)
    theirs = swap(out, 1)
    got_u = swap(out, 3)
    their_got = swap(got_u, 1)
    edge = (square, bf16)
    xa, xb = call(block_weights, [edge, edge], out, got_u, theirs, their_got, fixed, k)
    got_a = swap_chips(xa)
    got_b = swap(xb, 1)
    acc = call(impute_own, ((traits, untyped), f32), xa, xb, masked)
    return call(
        impute_edges, ((traits, untyped), f32), acc, got_a, got_b, masked, last=True
    )


def solution(mesh):
    in_specs = (
        P(None, (SEGMENTS, AXIS)),
        P((SEGMENTS, AXIS), None, None),
        P((SEGMENTS, AXIS), None, None),
        P((SEGMENTS, AXIS), None),
        P((SEGMENTS, AXIS)),
    )
    return jax.shard_map(
        per_device, mesh=mesh, in_specs=in_specs, out_specs=P(None, (SEGMENTS, AXIS)), check_vma=False
    )
```

```python
import functools

import jax
import jax.numpy as jnp
from jax import lax
from jax.experimental import pallas as pl
from jax.experimental.pallas import tpu as pltpu
from jax.sharding import PartitionSpec as P

AXIS = "genome"
SEGMENTS = "seg"
GROUP = 4
f32 = jnp.float32
bf16 = jnp.bfloat16
i16 = jnp.int16
SCALES = 16
LANES = 128
LIMIT = 32767.0


def parts(x):
    high = x.astype(bf16)
    return high, (x - high.astype(f32)).astype(bf16)


def dot(a, b, ca=1, cb=0):
    ah, al = parts(a)
    bh, bl = parts(b)
    return lax.dot_general(
        jnp.concatenate([al, ah, ah], axis=ca),
        jnp.concatenate([bh, bl, bh], axis=cb),
        (((ca,), (cb,)), ((), ())),
        preferred_element_type=f32,
    )


def code(x):
    top = jnp.maximum(jnp.max(jnp.abs(x), axis=0, keepdims=True), 1e-32)
    power = jnp.ceil(jnp.log2(top) * 4.0)
    root = jnp.exp2(power * -0.125)
    steps = jnp.floor(x * root * (root * LIMIT) + 0.5)
    steps = jnp.clip(steps, -LIMIT, LIMIT)
    tiles = x.shape[1] // LANES
    powers = jnp.broadcast_to(power, (SCALES // tiles, x.shape[1]))
    pieces = [v[:, i * LANES : (i + 1) * LANES] for v in (steps, powers) for i in range(tiles)]
    return jnp.concatenate(pieces, axis=0).astype(jnp.int32).astype(i16)


def decode(coded, tiles=2):
    rows = (coded.shape[0] - SCALES) // tiles
    values = coded[...].astype(jnp.int32).astype(f32)
    columns = []
    for i in range(tiles):
        at = tiles * rows + i * (SCALES // tiles)
        root = jnp.exp2(values[at : at + 1] * 0.125)
        columns.append(values[i * rows : (i + 1) * rows] * (root / LIMIT) * root)
    return jnp.concatenate(columns, axis=1)


def coded_rows(rows, columns):
    return rows * (columns // LANES) + SCALES


def where_am_i():
    place = lax.axis_index(AXIS)
    return place % 2 == 0, (place // 2) % 2 == 0, place // GROUP


def ready(b):
    bh, bl = parts(b)
    return jnp.concatenate([bh, bl, bh], axis=0)


def dot_ready(a, b):
    ah, al = parts(a)
    return jnp.dot(jnp.concatenate([al, ah, ah], axis=1), b[...], preferred_element_type=f32)


def low_traits():
    place = lax.axis_index(AXIS)
    return (place + place // 2 + place // GROUP) % 2 == 0


def ordered(first, own, other):
    return jnp.where(first, own, other), jnp.where(first, other, own)


def call(kernel, outs, *args, after=(), hbm=False, last=False, scratch=()):
    n_in, n_after = len(args), len(after)

    def body(*refs):
        kernel(*refs[:n_in], *refs[n_in + n_after :])

    single = not isinstance(outs, list)
    shapes = [outs] if single else outs
    vmem = pl.BlockSpec(memory_space=pltpu.VMEM)
    anywhere = pl.BlockSpec(memory_space=pl.ANY)
    if hbm:
        args = [pltpu.with_memory_space_constraint(a, pltpu.HBM) for a in args]
    got = pl.pallas_call(
        body,
        out_shape=[jax.ShapeDtypeStruct(s, t) if last else pltpu.VMEM(s, t) for s, t in shapes],
        in_specs=[anywhere if hbm else vmem] * n_in + [anywhere] * n_after,
        out_specs=[vmem] * len(shapes),
        scratch_shapes=scratch,
        compiler_params=pltpu.CompilerParams(vmem_limit_bytes=8 * 2**20),
        name=kernel.__name__ if hasattr(kernel, "__name__") else kernel.func.__name__,
    )(*args, *after)
    return got[0] if single else got


def tail_part(z_in, d_in, c_in, x1, s_own, z, d, c, sems):
    typed, half = c.shape
    rows = z.shape[0] // 2
    head = typed - half
    step = typed // 2
    copies = []
    for i in range(2):
        here = pl.ds(i * step, step)
        tail = (pl.ds(head, half), here)
        copies.append(pltpu.make_async_copy(d_in.at[tail], d.at[tail], sems.at[3 * i]))
        copies.append(pltpu.make_async_copy(c_in.at[here], c.at[here], sems.at[3 * i + 1]))
        copies.append(pltpu.make_async_copy(z_in.at[:, here], z.at[:, here], sems.at[3 * i + 2]))
    rest = pl.ds(0, head)
    copies.append(pltpu.make_async_copy(d_in.at[rest], d.at[rest], sems.at[6]))
    for copy in copies:
        copy.start()
    m = s = 0.0
    for i in range(2):
        here = pl.ds(i * step, step)
        for copy in copies[3 * i : 3 * i + 3]:
            copy.wait()
        tail = d[head:, here]
        m = m - dot(tail, c[here])
        s = s + dot(z[:, here], tail, 1, 1)
    x1[:half] = m
    keep, send = ordered(low_traits(), s[:rows], s[rows:])
    x1[half:] = send
    s_own[...] = keep
    copies[6].wait()


def head_part(z, d, c, x1, s_own, x3, g_own, solved, p):
    half = c.shape[1]
    rows = z.shape[0] // 2
    head = d.shape[0] - half
    first, _, _ = where_am_i()
    p[:head] = dot(d[:head], c[...])
    p[head:] = -x1[:half]
    solved[:, :head] = dot(z[...], d[:head], 1, 1)
    low, high = ordered(low_traits(), s_own[...], x1[half:])
    solved[:rows, head:] = low
    solved[rows:, head:] = high
    g = dot(solved[...], p[...])
    keep, send = ordered(low_traits(), g[:rows], g[rows:])
    x3[:half] = dot(p[...], p[...], 0, 0)
    x3[half:] = send
    g_own[...] = keep


def pair_forward(x1, got1, s_own, x2, n_own, sp_own):
    half = x1.shape[1]
    first, first_pair, _ = where_am_i()
    m0, m1 = ordered(first, x1[:half], got1[:half])
    s0, s1 = ordered(first, s_own[...], got1[half:])
    n = dot(m1, m0)
    n_own[...] = n
    split = coded_rows(half // 2, half)
    x2[:split] = code(jnp.where(first, n[: half // 2], n[half // 2 :]))
    s = dot(s0, m1, 1, 1) + s1
    rows = s.shape[0] // 2
    keep, send = ordered(first_pair, s[:rows], s[rows:])
    x2[split:] = code(send)
    sp_own[...] = keep


def pair_backward(x1, got1, s_own, x3, got3, g_own, x4, gg_own, gp_own):
    half = x1.shape[1]
    first, first_pair, _ = where_am_i()
    m0, _ = ordered(first, x1[:half], got1[:half])
    s0, _ = ordered(first, s_own[...], got1[half:])
    gg0, gg1 = ordered(first, x3[:half], got3[:half])
    g0, g1 = ordered(first, g_own[...], got3[half:])
    both = dot(jnp.concatenate([gg1, g1 - dot(s0, gg1)], axis=0), m0)
    gg = dot(m0, both[:half], 0, 0) + gg0
    gg_own[...] = gg
    split = coded_rows(half // 2, half)
    x4[:split] = code(jnp.where(first, gg[: half // 2], gg[half // 2 :]))
    g = both[half:] + g0
    rows = g.shape[0] // 2
    keep, send = ordered(first_pair, g[:rows], g[rows:])
    x4[split:] = code(send)
    gp_own[...] = keep


def pair_matrices(own, got, got_core):
    first, first_pair, _ = where_am_i()
    other = jnp.concatenate(ordered(first, got_core, got), axis=0)
    return ordered(first_pair, own[...], other)


def pair_vectors(own, got):
    _, first_pair, _ = where_am_i()
    return ordered(first_pair, own[...], got)


def relay(got, out):
    out[...] = got[: out.shape[0]]


def relay_halves(got, low, high):
    rows = low.shape[0] - SCALES
    low[:rows] = got[:rows]
    high[:rows] = got[rows : 2 * rows]
    low[rows:] = got[2 * rows : 2 * rows + SCALES]
    high[rows:] = got[2 * rows : 2 * rows + SCALES]


def group_forward(n_own, got2, got2_core, sp_own, out):
    _, _, group = where_am_i()
    out[...] = jnp.zeros_like(out)

    @pl.when(group == 0)
    def _():
        split = coded_rows(n_own.shape[1] // 2, n_own.shape[1])
        _, n1 = pair_matrices(n_own, decode(got2[:split]), decode(got2_core))
        s0, s1 = pair_vectors(sp_own, decode(got2[split:]))
        out[...] = code(dot(s0, n1, 1, 1) + s1)


def group_map(n_own, got2, got2_core, sp_own, s_group, up, down, n_first, n_second):
    split = coded_rows(n_own.shape[1] // 2, n_own.shape[1])
    n0, n1 = pair_matrices(n_own, decode(got2[:split]), decode(got2_core))
    s0, s1 = pair_vectors(sp_own, decode(got2[split:]))
    s_group[...] = dot(s0, n1, 1, 1) + s1
    n_first[...] = n0
    n_second[...] = n1
    n_group = dot(n1, n0)
    up[...] = ready(n_group.T)
    down[...] = ready(n_group)


def block_map(n_second, x1, got1, d, k):
    half = x1.shape[1]
    first, first_pair, _ = where_am_i()
    rows = lax.broadcasted_iota(jnp.int32, (half, half), 0)
    columns = lax.broadcasted_iota(jnp.int32, (half, half), 1)
    unit = (rows == columns).astype(f32)
    _, m1 = ordered(first, x1[:half], got1[:half])
    above = jnp.where(first_pair, n_second[...], unit)
    above = jnp.where(first, dot(above, m1), above)
    k[...] = dot(above, d[d.shape[0] - half :])


def group_backward(
    n_first, got2, sp_own, gg_own, got4, got4_low, got4_high, gp_own,
    gg_group, g_group, gg_second, g_second,
):
    half = n_first.shape[1]
    split = coded_rows(half // 2, half)
    n0 = n_first[...]
    s0, _ = pair_vectors(sp_own, decode(got2[split:]))
    rows = got4_low.shape[0] - SCALES
    got4_core = jnp.concatenate([got4_low[:rows], got4_high[...]], axis=0)
    gg0, gg1 = pair_matrices(gg_own, decode(got4[:split]), decode(got4_core))
    g0, g1 = pair_vectors(gp_own, decode(got4[split:]))
    gg_second[...] = gg1
    g_second[...] = g1
    both = dot(jnp.concatenate([gg1, g1 - dot(s0, gg1)], axis=0), n0)
    gg_group[...] = dot(n0, both[:half], 0, 0) + gg0
    g_group[...] = both[half:] + g0


def forward_hop(step, got, t_in, up, s_group, t_out, out):
    _, _, group = where_am_i()
    t = jnp.where(group == step + 1, decode(got), t_in[...])
    t_out[...] = t
    out[...] = code(dot_ready(t, up) + s_group[...])


def turn(step, got, t_in, gg_group, g_group, t_out, out):
    _, _, group = where_am_i()
    t = jnp.where(group == step + 1, decode(got), t_in[...])
    t_out[...] = t
    out[...] = jnp.zeros_like(out)

    @pl.when(group == step + 1)
    def _():
        out[...] = code(g_group[...] - dot(t, gg_group[...]))


def backward_hop(step, got, u_in, down, local, u_out, out):
    _, _, group = where_am_i()
    u = jnp.where(group == step, decode(got), u_in[...])
    u_out[...] = u
    out[...] = code(dot_ready(u, down) + local[...])


def arrive(step, got, u_in, out):
    _, _, group = where_am_i()
    out[...] = code(jnp.where(group == step, decode(got), u_in[...]))


def spread_forward(
    t_in, n_first, got2, sp_own, gg_second, g_second, gg_group, g_group, x5, x5_rest, kept, rest_own, local
):
    half = n_first.shape[1]
    _, first_pair, _ = where_am_i()
    s0, _ = pair_vectors(sp_own, decode(got2[coded_rows(half // 2, half) :]))
    t_mid = dot(t_in[...], n_first[...], 1, 1) + s0
    rest = g_second[...] - dot(t_mid, gg_second[...])
    keep, send = ordered(first_pair, t_in[...], t_mid)
    x5[...] = code(send)
    x5_rest[...] = code(rest)
    kept[...] = keep
    rest_own[...] = rest
    local[...] = g_group[...] - dot(t_in[...], gg_group[...])


def pair_states(kept, rest_own, got5, got5_rest, x1, got1, s_own, x3, got3, g_own, x6, own):
    half = x1.shape[1]
    rows = s_own.shape[0]
    first, first_pair, _ = where_am_i()
    t = jnp.concatenate(ordered(first_pair, kept[...], decode(got5)), axis=0)
    rest = jnp.concatenate(ordered(first_pair, rest_own[...], decode(got5_rest)), axis=0)
    m0, m1 = ordered(first, x1[:half], got1[:half])
    s0, _ = ordered(first, s_own[...], got1[half:])
    _, gg1 = ordered(first, x3[:half], got3[:half])
    _, g1 = ordered(first, g_own[...], got3[half:])
    t_mid = dot(t, m0, 1, 1) + s0
    fixed = jnp.where(first_pair, rest, 0.0)
    fixed_mid = dot(fixed, m1) + g1 - dot(t_mid, gg1)
    split = coded_rows(rows, half)
    keep, send = ordered(first, t, t_mid)
    x6[:split] = code(send)
    own[:rows] = keep
    keep, send = ordered(first, fixed_mid, fixed)
    x6[split:] = code(send)
    own[rows:] = keep


def block_parts(solved, p, d, start, maps):
    half = p.shape[1]
    start[...] = dot(solved[...], d[...])
    maps[:half] = dot(p[...], d[...], 0, 0)
    maps[half:] = d[d.shape[0] - half :]


def block_fixed(own, got6, start, maps, fixed_weights):
    rows = own.shape[0] // 2
    split = coded_rows(rows, own.shape[1])
    low = low_traits()
    t = jnp.concatenate(ordered(low, own[:rows], decode(got6[:split])), axis=0)
    above = jnp.concatenate(ordered(low, own[rows:], decode(got6[split:])), axis=0)
    fixed_weights[...] = start[...] - dot(jnp.concatenate([t, above], axis=1), maps[...])


def block_weights(mine, got_u, theirs, their_got, fixed_weights, k, xa, xb):
    half = k.shape[0]
    first, first_pair, _ = where_am_i()
    near = jnp.concatenate(ordered(first_pair, decode(mine), decode(got_u)), axis=0)
    far = jnp.concatenate(ordered(first_pair, decode(theirs), decode(their_got)), axis=0)
    u = jnp.concatenate(ordered(low_traits(), near, far), axis=0)
    weights = (fixed_weights[...] - dot(u, k[...])).astype(bf16)
    a, b = ordered(first, weights[:, :half], weights[:, half:])
    xa[...] = a
    xb[...] = b


def contract(values, coefs):
    return lax.dot_general(values, coefs, (((1,), (1,)), ((), ())), preferred_element_type=f32)


def mask_coefs(coefs_in, anchor_in, masked, coefs, anchor, sems):
    untyped, span = coefs.shape
    half = span // 4
    typed = span - 2 * half
    tile = 128
    place = lax.axis_index(AXIS)
    total = lax.axis_size(AXIS) * typed
    copies = [pltpu.make_async_copy(anchor_in, anchor, sems.at[0])]
    for i in range(untyped // tile):
        rows = pl.ds(i * tile, tile)
        copies.append(pltpu.make_async_copy(coefs_in.at[rows], coefs.at[rows], sems.at[i + 1]))
    for copy in copies:
        copy.start()
    copies[0].wait()
    first_column = place * typed - half
    for i in range(untyped // tile):
        rows = pl.ds(i * tile, tile)
        nearest = jnp.broadcast_to(anchor[:, i * tile : (i + 1) * tile], (tile, tile)).T
        copies[i + 1].wait()
        for j in range(span // tile):
            lanes = pl.ds(j * tile, tile)
            columns = first_column + j * tile + lax.broadcasted_iota(jnp.int32, (tile, tile), 1)
            within = (jnp.abs(columns - nearest) <= half) & (columns >= 0) & (columns < total)
            masked[rows, lanes] = jnp.where(within, coefs[rows, lanes].astype(f32), 0.0).astype(bf16)


def impute_own(xa, xb, masked, out):
    first, _, _ = where_am_i()
    half = xa.shape[1]
    span = masked.shape[1]
    weights = jnp.concatenate(ordered(first, xa[...], xb[...]), axis=1)
    out[...] = contract(weights, masked[:, half : span - half])


def impute_edges(acc, got_a, got_b, masked, out):
    first, _, _ = where_am_i()
    half = got_a.shape[1]
    span = masked.shape[1]
    left, right = ordered(first, got_a[...], got_b[...])
    out[...] = acc[...] + contract(left, masked[:, :half]) + contract(right, masked[:, span - half :])


def swap(block, distance):
    n = lax.axis_size(AXIS)
    return lax.ppermute(block, AXIS, [(i, i ^ distance) for i in range(n)])


def hop(block, step):
    pairs = []
    for i in range(lax.axis_size(AXIS)):
        g = i // GROUP
        to = i + GROUP if g == step else i - GROUP if g == step + 1 else i
        pairs.append((i, to ^ 1))
    return lax.ppermute(block, AXIS, pairs)


def hop_one_way(block, step):
    lower = [step * GROUP + i for i in range(GROUP)]
    return lax.ppermute(block, AXIS, [(i, (i + GROUP) ^ 1) for i in lower])


def swap_chips(block):
    n, segments = lax.axis_size(AXIS), lax.axis_size(SEGMENTS)
    pairs = []
    for seg in range(segments):
        for i in range(n):
            to, to_seg = i + 1 if i % 2 else i - 1, seg
            if not 0 <= to < n:
                to, to_seg = (i, seg ^ 1) if segments % 2 == 0 else (to % n, seg)
            pairs.append((seg * n + i, to_seg * n + to))
    return lax.ppermute(block, (SEGMENTS, AXIS), pairs)


def per_device(z, diag_inverse, coupling, impute_coef, anchor):
    d = diag_inverse[0]
    c = coupling[0]
    typed = d.shape[0]
    half = c.shape[1]
    traits = z.shape[0]
    untyped, span = impute_coef.shape
    assert span == typed + 2 * half and typed == 2 * half
    assert lax.axis_size(AXIS) >= 3 * GROUP
    groups = lax.axis_size(AXIS) // GROUP
    two, four = traits // 2, traits // 4
    square = (half, half)
    sq, h2, h4 = (square, f32), ((two, half), f32), ((four, half), f32)
    x1_shape, x6_shape = ((half + two, half), f32), ((2 * two, half), f32)
    x6_coded = ((2 * coded_rows(two, half), LANES), i16)
    coded = ((coded_rows(four, half), LANES), i16)
    coded_half = ((coded_rows(half // 2, half), LANES), i16)
    mixed = ((coded_rows(half // 2, half) + coded_rows(four, half), LANES), i16)

    solved_shape, p_shape = ((traits, typed), f32), ((typed, half), f32)
    x1, s_own, z, d, c = call(
        tail_part, [x1_shape, h2, solved_shape, ((typed, typed), f32), p_shape], z, d, c,
        hbm=True, scratch=[pltpu.SemaphoreType.DMA((7,))],
    )
    got1 = swap(x1, 1)
    x3, g_own, solved, p = call(
        head_part, [x1_shape, h2, solved_shape, p_shape], z, d, c, x1, s_own
    )
    x2, n_own, sp_own = call(pair_forward, [mixed, sq, h4], x1, got1, s_own, after=(p,))
    got2 = swap(x2, 3)
    got3 = swap(x3, 1)
    masked = call(
        mask_coefs, ((untyped, span), bf16), impute_coef, anchor[None, :], after=(x2,), hbm=True,
        scratch=[
            pltpu.VMEM((untyped, span), bf16),
            pltpu.VMEM((1, untyped), jnp.int32),
            pltpu.SemaphoreType.DMA((untyped // 128 + 1,)),
        ],
    )
    x4, gg_own, gp_own = call(
        pair_backward, [mixed, sq, h4], x1, got1, s_own, x3, got3, g_own, after=(x2,)
    )
    got2_core = swap(call(relay, coded_half, got2, after=(x4, masked)), 1)
    out = call(group_forward, coded, n_own, got2, got2_core, sp_own)
    parts3 = ((3 * half, half), bf16)
    s_group, up, down, n_first, n_second = call(
        group_map, [h4, parts3, parts3, sq, sq], n_own, got2, got2_core, sp_own, after=(out,)
    )
    k = call(block_map, ((half, typed), f32), n_second, x1, got1, d)
    t_in = jnp.zeros((four, half), f32)
    got4 = swap(x4, 3)
    for step in range(groups - 2):
        got = hop(out, step)
        t_in, out = call(
            functools.partial(forward_hop, step), [h4, coded], got, t_in, up, s_group,
            after=(k,) if step == 0 else (),
        )
        if step == 0:
            pieces = [((half // 2 + SCALES, LANES), i16)] * 2
            low, high = call(relay_halves, pieces, got4, after=(out,))
            got4_low, got4_high = swap(low, 1), swap(high, 1)
    gg_group, g_group, gg_second, g_second = call(
        group_backward, [sq, h4, sq, h4],
        n_first, got2, sp_own, gg_own, got4, got4_low, got4_high, gp_own, after=(out,),
    )
    last = groups - 2
    got = hop_one_way(out, last)
    t_in, out = call(
        functools.partial(turn, last), [h4, coded], got, t_in, gg_group, g_group
    )

    u_in = jnp.zeros((four, half), f32)
    for step in reversed(range(groups - 1)):
        got = hop(out, step)
        if step == last:
            x5, x5_rest, kept, rest_own, local = call(
                spread_forward, [coded, coded, h4, h4, h4],
                t_in, n_first, got2, sp_own, gg_second, g_second, gg_group, g_group, after=(out,),
            )
            got5, got5_rest = swap(x5, 3), swap(x5_rest, 3)
        if step:
            u_in, out = call(
                functools.partial(backward_hop, step), [h4, coded], got, u_in, down, local
            )
        else:
            start, maps = call(
                block_parts, [solved_shape, ((2 * half, typed), f32)], solved, p, d, after=(out,)
            )
            out = call(functools.partial(arrive, step), coded, got, u_in, after=(maps,))
    x6, own = call(
        pair_states, [x6_coded, x6_shape], kept, rest_own, got5, got5_rest, x1, got1, s_own, x3, got3, g_own
    )
    got6 = swap(x6, 1)
    fixed = call(block_fixed, solved_shape, own, got6, start, maps)
    theirs = swap(out, 1)
    got_u = swap(out, 3)
    their_got = swap(got_u, 1)
    edge = (square, bf16)
    xa, xb = call(block_weights, [edge, edge], out, got_u, theirs, their_got, fixed, k)
    got_a = swap_chips(xa)
    got_b = swap(xb, 1)
    acc = call(impute_own, ((traits, untyped), f32), xa, xb, masked)
    return call(
        impute_edges, ((traits, untyped), f32), acc, got_a, got_b, masked, last=True
    )


def solution(mesh):
    in_specs = (
        P(None, (SEGMENTS, AXIS)),
        P((SEGMENTS, AXIS), None, None),
        P((SEGMENTS, AXIS), None, None),
        P((SEGMENTS, AXIS), None),
        P((SEGMENTS, AXIS)),
    )
    return jax.shard_map(
        per_device, mesh=mesh, in_specs=in_specs, out_specs=P(None, (SEGMENTS, AXIS)), check_vma=False
    )
```

```python
import functools

import jax
import jax.numpy as jnp
from jax import lax
from jax.experimental import pallas as pl
from jax.experimental.pallas import tpu as pltpu
from jax.sharding import PartitionSpec as P

AXIS = "genome"
SEGMENTS = "seg"
GROUP = 4
f32 = jnp.float32
bf16 = jnp.bfloat16
i16 = jnp.int16
SCALES = 16
LANES = 128
LIMIT = 32767.0


def parts(x):
    high = x.astype(bf16)
    return high, (x - high.astype(f32)).astype(bf16)


def dot(a, b, ca=1, cb=0):
    ah, al = parts(a)
    bh, bl = parts(b)
    return lax.dot_general(
        jnp.concatenate([al, ah, ah], axis=ca),
        jnp.concatenate([bh, bl, bh], axis=cb),
        (((ca,), (cb,)), ((), ())),
        preferred_element_type=f32,
    )


def code(x):
    top = jnp.maximum(jnp.max(jnp.abs(x), axis=0, keepdims=True), 1e-32)
    power = jnp.ceil(jnp.log2(top) * 4.0)
    root = jnp.exp2(power * -0.125)
    steps = jnp.floor(x * root * (root * LIMIT) + 0.5)
    steps = jnp.clip(steps, -LIMIT, LIMIT)
    tiles = x.shape[1] // LANES
    powers = jnp.broadcast_to(power, (SCALES // tiles, x.shape[1]))
    pieces = [v[:, i * LANES : (i + 1) * LANES] for v in (steps, powers) for i in range(tiles)]
    return jnp.concatenate(pieces, axis=0).astype(jnp.int32).astype(i16)


def decode(coded, tiles=2):
    rows = (coded.shape[0] - SCALES) // tiles
    values = coded[...].astype(jnp.int32).astype(f32)
    columns = []
    for i in range(tiles):
        at = tiles * rows + i * (SCALES // tiles)
        root = jnp.exp2(values[at : at + 1] * 0.125)
        columns.append(values[i * rows : (i + 1) * rows] * (root / LIMIT) * root)
    return jnp.concatenate(columns, axis=1)


def coded_rows(rows, columns):
    return rows * (columns // LANES) + SCALES


def where_am_i():
    place = lax.axis_index(AXIS)
    return place % 2 == 0, (place // 2) % 2 == 0, place // GROUP


def ready(b):
    bh, bl = parts(b)
    return jnp.concatenate([bh, bl, bh], axis=0)


def dot_ready(a, b):
    ah, al = parts(a)
    return jnp.dot(jnp.concatenate([al, ah, ah], axis=1), b[...], preferred_element_type=f32)


def low_traits():
    place = lax.axis_index(AXIS)
    return (place + place // 2 + place // GROUP) % 2 == 0


def ordered(first, own, other):
    return jnp.where(first, own, other), jnp.where(first, other, own)


def call(kernel, outs, *args, after=(), hbm=False, last=False, scratch=()):
    n_in, n_after = len(args), len(after)

    def body(*refs):
        kernel(*refs[:n_in], *refs[n_in + n_after :])

    single = not isinstance(outs, list)
    shapes = [outs] if single else outs
    vmem = pl.BlockSpec(memory_space=pltpu.VMEM)
    anywhere = pl.BlockSpec(memory_space=pl.ANY)
    if hbm:
        args = [pltpu.with_memory_space_constraint(a, pltpu.HBM) for a in args]
    got = pl.pallas_call(
        body,
        out_shape=[jax.ShapeDtypeStruct(s, t) if last else pltpu.VMEM(s, t) for s, t in shapes],
        in_specs=[anywhere if hbm else vmem] * n_in + [anywhere] * n_after,
        out_specs=[vmem] * len(shapes),
        scratch_shapes=scratch,
        compiler_params=pltpu.CompilerParams(vmem_limit_bytes=8 * 2**20),
        name=kernel.__name__ if hasattr(kernel, "__name__") else kernel.func.__name__,
    )(*args, *after)
    return got[0] if single else got


def tail_part(z_in, d_in, c_in, x1, s_own, z, d, c, sems):
    typed, half = c.shape
    rows = z.shape[0] // 2
    head = typed - half
    step = typed // 2
    copies = []
    for i in range(2):
        here = pl.ds(i * step, step)
        tail = (pl.ds(head, half), here)
        copies.append(pltpu.make_async_copy(d_in.at[tail], d.at[tail], sems.at[3 * i]))
        copies.append(pltpu.make_async_copy(c_in.at[here], c.at[here], sems.at[3 * i + 1]))
        copies.append(pltpu.make_async_copy(z_in.at[:, here], z.at[:, here], sems.at[3 * i + 2]))
    rest = pl.ds(0, head)
    copies.append(pltpu.make_async_copy(d_in.at[rest], d.at[rest], sems.at[6]))
    for copy in copies:
        copy.start()
    m = s = 0.0
    for i in range(2):
        here = pl.ds(i * step, step)
        for copy in copies[3 * i : 3 * i + 3]:
            copy.wait()
        tail = d[head:, here]
        m = m - dot(tail, c[here])
        s = s + dot(z[:, here], tail, 1, 1)
    x1[:half] = m
    keep, send = ordered(low_traits(), s[:rows], s[rows:])
    x1[half:] = send
    s_own[...] = keep
    copies[6].wait()


def head_part(z, d, c, x1, s_own, x3, g_own, solved, p):
    half = c.shape[1]
    rows = z.shape[0] // 2
    head = d.shape[0] - half
    first, _, _ = where_am_i()
    p[:head] = dot(d[:head], c[...])
    p[head:] = -x1[:half]
    solved[:, :head] = dot(z[...], d[:head], 1, 1)
    low, high = ordered(low_traits(), s_own[...], x1[half:])
    solved[:rows, head:] = low
    solved[rows:, head:] = high
    g = dot(solved[...], p[...])
    keep, send = ordered(low_traits(), g[:rows], g[rows:])
    x3[:half] = dot(p[...], p[...], 0, 0)
    x3[half:] = send
    g_own[...] = keep


def pair_forward(x1, got1, s_own, x2, n_own, sp_own):
    half = x1.shape[1]
    first, first_pair, _ = where_am_i()
    m0, m1 = ordered(first, x1[:half], got1[:half])
    s0, s1 = ordered(first, s_own[...], got1[half:])
    n = dot(m1, m0)
    n_own[...] = n
    split = coded_rows(half // 2, half)
    x2[:split] = code(jnp.where(first, n[: half // 2], n[half // 2 :]))
    s = dot(s0, m1, 1, 1) + s1
    rows = s.shape[0] // 2
    keep, send = ordered(first_pair, s[:rows], s[rows:])
    x2[split:] = code(send)
    sp_own[...] = keep


def pair_backward(x1, got1, s_own, x3, got3, g_own, x4, gg_own, gp_own):
    half = x1.shape[1]
    first, first_pair, _ = where_am_i()
    m0, _ = ordered(first, x1[:half], got1[:half])
    s0, _ = ordered(first, s_own[...], got1[half:])
    gg0, gg1 = ordered(first, x3[:half], got3[:half])
    g0, g1 = ordered(first, g_own[...], got3[half:])
    both = dot(jnp.concatenate([gg1, g1 - dot(s0, gg1)], axis=0), m0)
    gg = dot(m0, both[:half], 0, 0) + gg0
    gg_own[...] = gg
    split = coded_rows(half // 2, half)
    x4[:split] = code(jnp.where(first, gg[: half // 2], gg[half // 2 :]))
    g = both[half:] + g0
    rows = g.shape[0] // 2
    keep, send = ordered(first_pair, g[:rows], g[rows:])
    x4[split:] = code(send)
    gp_own[...] = keep


def pair_matrices(own, got, got_core):
    first, first_pair, _ = where_am_i()
    other = jnp.concatenate(ordered(first, got_core, got), axis=0)
    return ordered(first_pair, own[...], other)


def pair_vectors(own, got):
    _, first_pair, _ = where_am_i()
    return ordered(first_pair, own[...], got)


def relay(got, out):
    out[...] = got[: out.shape[0]]


def relay_halves(got, low, high):
    rows = low.shape[0] - SCALES
    low[:rows] = got[:rows]
    high[:rows] = got[rows : 2 * rows]
    low[rows:] = got[2 * rows : 2 * rows + SCALES]
    high[rows:] = got[2 * rows : 2 * rows + SCALES]


def group_forward(n_own, got2, got2_core, sp_own, out):
    _, _, group = where_am_i()
    out[...] = jnp.zeros_like(out)

    @pl.when(group == 0)
    def _():
        split = coded_rows(n_own.shape[1] // 2, n_own.shape[1])
        _, n1 = pair_matrices(n_own, decode(got2[:split]), decode(got2_core))
        s0, s1 = pair_vectors(sp_own, decode(got2[split:]))
        out[...] = code(dot(s0, n1, 1, 1) + s1)


def group_map(n_own, got2, got2_core, sp_own, s_group, up, down, n_first, n_second):
    split = coded_rows(n_own.shape[1] // 2, n_own.shape[1])
    n0, n1 = pair_matrices(n_own, decode(got2[:split]), decode(got2_core))
    s0, s1 = pair_vectors(sp_own, decode(got2[split:]))
    s_group[...] = dot(s0, n1, 1, 1) + s1
    n_first[...] = n0
    n_second[...] = n1
    n_group = dot(n1, n0)
    up[...] = ready(n_group.T)
    down[...] = ready(n_group)


def block_map(n_second, x1, got1, d, k):
    half = x1.shape[1]
    first, first_pair, _ = where_am_i()
    rows = lax.broadcasted_iota(jnp.int32, (half, half), 0)
    columns = lax.broadcasted_iota(jnp.int32, (half, half), 1)
    unit = (rows == columns).astype(f32)
    _, m1 = ordered(first, x1[:half], got1[:half])
    above = jnp.where(first_pair, n_second[...], unit)
    above = jnp.where(first, dot(above, m1), above)
    k[...] = ready(dot(above, d[d.shape[0] - half :]))


def group_backward(
    n_first, got2, sp_own, gg_own, got4, got4_low, got4_high, gp_own,
    gg_group, g_group, gg_second, g_second,
):
    half = n_first.shape[1]
    split = coded_rows(half // 2, half)
    n0 = n_first[...]
    s0, _ = pair_vectors(sp_own, decode(got2[split:]))
    rows = got4_low.shape[0] - SCALES
    got4_core = jnp.concatenate([got4_low[:rows], got4_high[...]], axis=0)
    gg0, gg1 = pair_matrices(gg_own, decode(got4[:split]), decode(got4_core))
    g0, g1 = pair_vectors(gp_own, decode(got4[split:]))
    gg_second[...] = gg1
    g_second[...] = g1
    both = dot(jnp.concatenate([gg1, g1 - dot(s0, gg1)], axis=0), n0)
    gg_group[...] = ready(dot(n0, both[:half], 0, 0) + gg0)
    g_group[...] = both[half:] + g0


def forward_hop(step, got, t_in, up, s_group, t_out, out):
    _, _, group = where_am_i()
    t = jnp.where(group == step + 1, decode(got), t_in[...])
    t_out[...] = t
    out[...] = code(dot_ready(t, up) + s_group[...])


def turn(step, got, t_in, gg_group, g_group, t_out, out):
    _, _, group = where_am_i()
    t = jnp.where(group == step + 1, decode(got), t_in[...])
    t_out[...] = t
    out[...] = jnp.zeros_like(out)

    @pl.when(group == step + 1)
    def _():
        out[...] = code(g_group[...] - dot_ready(t, gg_group))


def backward_hop(step, got, u_in, down, local, u_out, out):
    _, _, group = where_am_i()
    u = jnp.where(group == step, decode(got), u_in[...])
    u_out[...] = u
    out[...] = code(dot_ready(u, down) + local[...])


def arrive(step, got, u_in, out):
    _, _, group = where_am_i()
    out[...] = code(jnp.where(group == step, decode(got), u_in[...]))


def spread_forward(
    t_in, n_first, got2, sp_own, gg_second, g_second, gg_group, g_group, x5, x5_rest, kept, rest_own, local
):
    half = n_first.shape[1]
    _, first_pair, _ = where_am_i()
    s0, _ = pair_vectors(sp_own, decode(got2[coded_rows(half // 2, half) :]))
    t_mid = dot(t_in[...], n_first[...], 1, 1) + s0
    rest = g_second[...] - dot(t_mid, gg_second[...])
    keep, send = ordered(first_pair, t_in[...], t_mid)
    x5[...] = code(send)
    x5_rest[...] = code(rest)
    kept[...] = keep
    rest_own[...] = rest
    local[...] = g_group[...] - dot_ready(t_in[...], gg_group)


def pair_states(kept, rest_own, got5, got5_rest, x1, got1, s_own, x3, got3, g_own, x6, own):
    half = x1.shape[1]
    rows = s_own.shape[0]
    first, first_pair, _ = where_am_i()
    t = jnp.concatenate(ordered(first_pair, kept[...], decode(got5)), axis=0)
    rest = jnp.concatenate(ordered(first_pair, rest_own[...], decode(got5_rest)), axis=0)
    m0, m1 = ordered(first, x1[:half], got1[:half])
    s0, _ = ordered(first, s_own[...], got1[half:])
    _, gg1 = ordered(first, x3[:half], got3[:half])
    _, g1 = ordered(first, g_own[...], got3[half:])
    t_mid = dot(t, m0, 1, 1) + s0
    fixed = jnp.where(first_pair, rest, 0.0)
    fixed_mid = dot(fixed, m1) + g1 - dot(t_mid, gg1)
    split = coded_rows(rows, half)
    keep, send = ordered(first, t, t_mid)
    x6[:split] = code(send)
    own[:rows] = keep
    keep, send = ordered(first, fixed_mid, fixed)
    x6[split:] = code(send)
    own[rows:] = keep


def block_parts(solved, p, d, start, maps):
    half = p.shape[1]
    start[...] = dot(solved[...], d[...])
    maps[:half] = dot(p[...], d[...], 0, 0)
    maps[half:] = d[d.shape[0] - half :]


def block_fixed(own, got6, start, maps, fixed_weights):
    rows = own.shape[0] // 2
    split = coded_rows(rows, own.shape[1])
    low = low_traits()
    t = jnp.concatenate(ordered(low, own[:rows], decode(got6[:split])), axis=0)
    above = jnp.concatenate(ordered(low, own[rows:], decode(got6[split:])), axis=0)
    fixed_weights[...] = start[...] - dot(jnp.concatenate([t, above], axis=1), maps[...])


def gather(mine, got_u, both):
    rows = mine.shape[0]
    both[:rows] = mine[...]
    both[rows:] = got_u[...]


def block_weights(both, got_both, fixed_weights, k, xa, xb):
    half = xa.shape[1]
    rows = both.shape[0] // 2
    first, first_pair, _ = where_am_i()
    near = jnp.concatenate(ordered(first_pair, decode(both[:rows]), decode(both[rows:])), axis=0)
    far = jnp.concatenate(
        ordered(first_pair, decode(got_both[:rows]), decode(got_both[rows:])), axis=0
    )
    u = jnp.concatenate(ordered(low_traits(), near, far), axis=0)
    weights = (fixed_weights[...] - dot_ready(u, k)).astype(bf16)
    a, b = ordered(first, weights[:, :half], weights[:, half:])
    xa[...] = a
    xb[...] = b


def contract(values, coefs):
    return lax.dot_general(values, coefs, (((1,), (1,)), ((), ())), preferred_element_type=f32)


def mask_coefs(coefs_in, anchor_in, masked, coefs, anchor, sems):
    untyped, span = coefs.shape
    half = span // 4
    typed = span - 2 * half
    tile = 128
    place = lax.axis_index(AXIS)
    total = lax.axis_size(AXIS) * typed
    copies = [pltpu.make_async_copy(anchor_in, anchor, sems.at[0])]
    for i in range(untyped // tile):
        rows = pl.ds(i * tile, tile)
        copies.append(pltpu.make_async_copy(coefs_in.at[rows], coefs.at[rows], sems.at[i + 1]))
    for copy in copies:
        copy.start()
    copies[0].wait()
    first_column = place * typed - half
    for i in range(untyped // tile):
        rows = pl.ds(i * tile, tile)
        nearest = jnp.broadcast_to(anchor[:, i * tile : (i + 1) * tile], (tile, tile)).T
        copies[i + 1].wait()
        for j in range(span // tile):
            lanes = pl.ds(j * tile, tile)
            columns = first_column + j * tile + lax.broadcasted_iota(jnp.int32, (tile, tile), 1)
            within = (jnp.abs(columns - nearest) <= half) & (columns >= 0) & (columns < total)
            masked[rows, lanes] = jnp.where(within, coefs[rows, lanes].astype(f32), 0.0).astype(bf16)


def impute_own(xa, xb, masked, out):
    first, _, _ = where_am_i()
    half = xa.shape[1]
    span = masked.shape[1]
    weights = jnp.concatenate(ordered(first, xa[...], xb[...]), axis=1)
    out[...] = contract(weights, masked[:, half : span - half])


def impute_edges(acc, got_a, got_b, masked, out):
    first, _, _ = where_am_i()
    half = got_a.shape[1]
    span = masked.shape[1]
    left, right = ordered(first, got_a[...], got_b[...])
    out[...] = acc[...] + contract(left, masked[:, :half]) + contract(right, masked[:, span - half :])


def swap(block, distance):
    n = lax.axis_size(AXIS)
    return lax.ppermute(block, AXIS, [(i, i ^ distance) for i in range(n)])


def hop(block, step):
    pairs = []
    for i in range(lax.axis_size(AXIS)):
        g = i // GROUP
        to = i + GROUP if g == step else i - GROUP if g == step + 1 else i
        pairs.append((i, to ^ 1))
    return lax.ppermute(block, AXIS, pairs)


def swap_chips(block):
    n, segments = lax.axis_size(AXIS), lax.axis_size(SEGMENTS)
    pairs = []
    for seg in range(segments):
        for i in range(n):
            to, to_seg = i + 1 if i % 2 else i - 1, seg
            if not 0 <= to < n:
                to, to_seg = (i, seg ^ 1) if segments % 2 == 0 else (to % n, seg)
            pairs.append((seg * n + i, to_seg * n + to))
    return lax.ppermute(block, (SEGMENTS, AXIS), pairs)


def per_device(z, diag_inverse, coupling, impute_coef, anchor):
    d = diag_inverse[0]
    c = coupling[0]
    typed = d.shape[0]
    half = c.shape[1]
    traits = z.shape[0]
    untyped, span = impute_coef.shape
    assert span == typed + 2 * half and typed == 2 * half
    assert lax.axis_size(AXIS) >= 3 * GROUP
    groups = lax.axis_size(AXIS) // GROUP
    two, four = traits // 2, traits // 4
    square = (half, half)
    sq, h2, h4 = (square, f32), ((two, half), f32), ((four, half), f32)
    x1_shape, x6_shape = ((half + two, half), f32), ((2 * two, half), f32)
    x6_coded = ((2 * coded_rows(two, half), LANES), i16)
    coded = ((coded_rows(four, half), LANES), i16)
    coded_half = ((coded_rows(half // 2, half), LANES), i16)
    mixed = ((coded_rows(half // 2, half) + coded_rows(four, half), LANES), i16)

    solved_shape, p_shape = ((traits, typed), f32), ((typed, half), f32)
    x1, s_own, z, d, c = call(
        tail_part, [x1_shape, h2, solved_shape, ((typed, typed), f32), p_shape], z, d, c,
        hbm=True, scratch=[pltpu.SemaphoreType.DMA((7,))],
    )
    got1 = swap(x1, 1)
    x3, g_own, solved, p = call(
        head_part, [x1_shape, h2, solved_shape, p_shape], z, d, c, x1, s_own
    )
    x2, n_own, sp_own = call(pair_forward, [mixed, sq, h4], x1, got1, s_own, after=(p,))
    got2 = swap(x2, 3)
    got3 = swap(x3, 1)
    masked = call(
        mask_coefs, ((untyped, span), bf16), impute_coef, anchor[None, :], after=(x2,), hbm=True,
        scratch=[
            pltpu.VMEM((untyped, span), bf16),
            pltpu.VMEM((1, untyped), jnp.int32),
            pltpu.SemaphoreType.DMA((untyped // 128 + 1,)),
        ],
    )
    x4, gg_own, gp_own = call(
        pair_backward, [mixed, sq, h4], x1, got1, s_own, x3, got3, g_own, after=(x2,)
    )
    got2_core = swap(call(relay, coded_half, got2, after=(x4, masked)), 1)
    out = call(group_forward, coded, n_own, got2, got2_core, sp_own)
    parts3 = ((3 * half, half), bf16)
    s_group, up, down, n_first, n_second = call(
        group_map, [h4, parts3, parts3, sq, sq], n_own, got2, got2_core, sp_own, after=(out,)
    )
    k = call(block_map, ((3 * half, typed), bf16), n_second, x1, got1, d)
    start, maps = call(
        block_parts, [solved_shape, ((2 * half, typed), f32)], solved, p, d, after=(k,)
    )
    t_in = jnp.zeros((four, half), f32)
    got4 = swap(x4, 3)
    for step in range(groups - 2):
        got = hop(out, step)
        t_in, out = call(
            functools.partial(forward_hop, step), [h4, coded], got, t_in, up, s_group,
            after=(maps,) if step == 0 else (),
        )
        if step == 0:
            pieces = [((half // 2 + SCALES, LANES), i16)] * 2
            low, high = call(relay_halves, pieces, got4, after=(out,))
            got4_low, got4_high = swap(low, 1), swap(high, 1)
    gg_group, g_group, gg_second, g_second = call(
        group_backward, [parts3, h4, sq, h4],
        n_first, got2, sp_own, gg_own, got4, got4_low, got4_high, gp_own, after=(out,),
    )
    last = groups - 2
    got = hop(out, last)
    t_in, out = call(
        functools.partial(turn, last), [h4, coded], got, t_in, gg_group, g_group
    )

    u_in = jnp.zeros((four, half), f32)
    for step in reversed(range(groups - 1)):
        got = hop(out, step)
        if step == last:
            x5, x5_rest, kept, rest_own, local = call(
                spread_forward, [coded, coded, h4, h4, h4],
                t_in, n_first, got2, sp_own, gg_second, g_second, gg_group, g_group, after=(out,),
            )
            got5, got5_rest = swap(x5, 3), swap(x5_rest, 3)
        if step:
            u_in, out = call(
                functools.partial(backward_hop, step), [h4, coded], got, u_in, down, local
            )
        else:
            out = call(functools.partial(arrive, step), coded, got, u_in)
    x6, own = call(
        pair_states, [x6_coded, x6_shape], kept, rest_own, got5, got5_rest, x1, got1, s_own, x3, got3, g_own
    )
    got6 = swap(x6, 1)
    fixed = call(block_fixed, solved_shape, own, got6, start, maps)
    both = call(gather, ((2 * coded[0][0], LANES), i16), out, swap(out, 3))
    got_both = swap(both, 1)
    edge = (square, bf16)
    xa, xb = call(block_weights, [edge, edge], both, got_both, fixed, k)
    got_a = swap_chips(xa)
    got_b = swap(xb, 1)
    acc = call(impute_own, ((traits, untyped), f32), xa, xb, masked)
    return call(
        impute_edges, ((traits, untyped), f32), acc, got_a, got_b, masked, last=True
    )


def solution(mesh):
    in_specs = (
        P(None, (SEGMENTS, AXIS)),
        P((SEGMENTS, AXIS), None, None),
        P((SEGMENTS, AXIS), None, None),
        P((SEGMENTS, AXIS), None),
        P((SEGMENTS, AXIS)),
    )
    return jax.shard_map(
        per_device, mesh=mesh, in_specs=in_specs, out_specs=P(None, (SEGMENTS, AXIS)), check_vma=False
    )
```

```python
import functools

import jax
import jax.numpy as jnp
from jax import lax
from jax.experimental import pallas as pl
from jax.experimental.pallas import tpu as pltpu
from jax.sharding import PartitionSpec as P

AXIS = "genome"
SEGMENTS = "seg"
GROUP = 4
f32 = jnp.float32
bf16 = jnp.bfloat16
i16 = jnp.int16
SCALES = 16
LANES = 128
LIMIT = 32767.0


def parts(x):
    high = x.astype(bf16)
    return high, (x - high.astype(f32)).astype(bf16)


def dot(a, b, ca=1, cb=0):
    ah, al = parts(a)
    bh, bl = parts(b)
    return lax.dot_general(
        jnp.concatenate([al, ah, ah], axis=ca),
        jnp.concatenate([bh, bl, bh], axis=cb),
        (((ca,), (cb,)), ((), ())),
        preferred_element_type=f32,
    )


def code(x):
    top = jnp.maximum(jnp.max(jnp.abs(x), axis=0, keepdims=True), 1e-32)
    power = jnp.ceil(jnp.log2(top) * 4.0)
    root = jnp.exp2(power * -0.125)
    steps = jnp.floor(x * root * (root * LIMIT) + 0.5)
    steps = jnp.clip(steps, -LIMIT, LIMIT)
    tiles = x.shape[1] // LANES
    powers = jnp.broadcast_to(power, (SCALES // tiles, x.shape[1]))
    pieces = [v[:, i * LANES : (i + 1) * LANES] for v in (steps, powers) for i in range(tiles)]
    return jnp.concatenate(pieces, axis=0).astype(jnp.int32).astype(i16)


def decode(coded, tiles=2):
    rows = (coded.shape[0] - SCALES) // tiles
    values = coded[...].astype(jnp.int32).astype(f32)
    columns = []
    for i in range(tiles):
        at = tiles * rows + i * (SCALES // tiles)
        root = jnp.exp2(values[at : at + 1] * 0.125)
        columns.append(values[i * rows : (i + 1) * rows] * (root / LIMIT) * root)
    return jnp.concatenate(columns, axis=1)


def coded_rows(rows, columns):
    return rows * (columns // LANES) + SCALES


def where_am_i():
    place = lax.axis_index(AXIS)
    return place % 2 == 0, (place // 2) % 2 == 0, place // GROUP


def ready(b):
    bh, bl = parts(b)
    return jnp.concatenate([bh, bl, bh], axis=0)


def dot_ready(a, b):
    ah, al = parts(a)
    return jnp.dot(jnp.concatenate([al, ah, ah], axis=1), b[...], preferred_element_type=f32)


def low_traits():
    place = lax.axis_index(AXIS)
    return (place + place // 2 + place // GROUP) % 2 == 0


def ordered(first, own, other):
    return jnp.where(first, own, other), jnp.where(first, other, own)


def call(kernel, outs, *args, after=(), hbm=False, last=False, scratch=()):
    n_in, n_after = len(args), len(after)

    def body(*refs):
        kernel(*refs[:n_in], *refs[n_in + n_after :])

    single = not isinstance(outs, list)
    shapes = [outs] if single else outs
    vmem = pl.BlockSpec(memory_space=pltpu.VMEM)
    anywhere = pl.BlockSpec(memory_space=pl.ANY)
    if hbm:
        args = [pltpu.with_memory_space_constraint(a, pltpu.HBM) for a in args]
    got = pl.pallas_call(
        body,
        out_shape=[jax.ShapeDtypeStruct(s, t) if last else pltpu.VMEM(s, t) for s, t in shapes],
        in_specs=[anywhere if hbm else vmem] * n_in + [anywhere] * n_after,
        out_specs=[vmem] * len(shapes),
        scratch_shapes=scratch,
        compiler_params=pltpu.CompilerParams(vmem_limit_bytes=8 * 2**20),
        name=kernel.__name__ if hasattr(kernel, "__name__") else kernel.func.__name__,
    )(*args, *after)
    return got[0] if single else got


def tail_part(z_in, d_in, c_in, x1, s_own, z, d, c, sems):
    typed, half = c.shape
    rows = z.shape[0] // 2
    head = typed - half
    step = typed // 2
    copies = []
    for i in range(2):
        here = pl.ds(i * step, step)
        tail = (pl.ds(head, half), here)
        copies.append(pltpu.make_async_copy(d_in.at[tail], d.at[tail], sems.at[3 * i]))
        copies.append(pltpu.make_async_copy(c_in.at[here], c.at[here], sems.at[3 * i + 1]))
        copies.append(pltpu.make_async_copy(z_in.at[:, here], z.at[:, here], sems.at[3 * i + 2]))
    rest = pl.ds(0, head)
    copies.append(pltpu.make_async_copy(d_in.at[rest], d.at[rest], sems.at[6]))
    for copy in copies:
        copy.start()
    m = s = 0.0
    for i in range(2):
        here = pl.ds(i * step, step)
        for copy in copies[3 * i : 3 * i + 3]:
            copy.wait()
        tail = d[head:, here]
        m = m - dot(tail, c[here])
        s = s + dot(z[:, here], tail, 1, 1)
    x1[:half] = m
    keep, send = ordered(low_traits(), s[:rows], s[rows:])
    x1[half:] = send
    s_own[...] = keep
    copies[6].wait()


def head_part(z, d, c, x1, s_own, x3, g_own, solved, p):
    half = c.shape[1]
    rows = z.shape[0] // 2
    head = d.shape[0] - half
    first, _, _ = where_am_i()
    p[:head] = dot(d[:head], c[...])
    p[head:] = -x1[:half]
    solved[:, :head] = dot(z[...], d[:head], 1, 1)
    low, high = ordered(low_traits(), s_own[...], x1[half:])
    solved[:rows, head:] = low
    solved[rows:, head:] = high
    g = dot(solved[...], p[...])
    keep, send = ordered(low_traits(), g[:rows], g[rows:])
    x3[:half] = dot(p[...], p[...], 0, 0)
    x3[half:] = send
    g_own[...] = keep


def pair_forward(x1, got1, s_own, x2, n_own, sp_own):
    half = x1.shape[1]
    first, first_pair, _ = where_am_i()
    m0, m1 = ordered(first, x1[:half], got1[:half])
    s0, s1 = ordered(first, s_own[...], got1[half:])
    n = dot(m1, m0)
    n_own[...] = n
    split = coded_rows(half // 2, half)
    x2[:split] = code(jnp.where(first, n[: half // 2], n[half // 2 :]))
    s = dot(s0, m1, 1, 1) + s1
    rows = s.shape[0] // 2
    keep, send = ordered(first_pair, s[:rows], s[rows:])
    x2[split:] = code(send)
    sp_own[...] = keep


def pair_backward(x1, got1, s_own, x3, got3, g_own, x4, gg_own, gp_own):
    half = x1.shape[1]
    first, first_pair, _ = where_am_i()
    m0, _ = ordered(first, x1[:half], got1[:half])
    s0, _ = ordered(first, s_own[...], got1[half:])
    gg0, gg1 = ordered(first, x3[:half], got3[:half])
    g0, g1 = ordered(first, g_own[...], got3[half:])
    both = dot(jnp.concatenate([gg1, g1 - dot(s0, gg1)], axis=0), m0)
    gg = dot(m0, both[:half], 0, 0) + gg0
    gg_own[...] = gg
    split = coded_rows(half // 2, half)
    x4[:split] = code(jnp.where(first, gg[: half // 2], gg[half // 2 :]))
    g = both[half:] + g0
    rows = g.shape[0] // 2
    keep, send = ordered(first_pair, g[:rows], g[rows:])
    x4[split:] = code(send)
    gp_own[...] = keep


def pair_matrices(own, got, got_core):
    first, first_pair, _ = where_am_i()
    other = jnp.concatenate(ordered(first, got_core, got), axis=0)
    return ordered(first_pair, own[...], other)


def pair_vectors(own, got):
    _, first_pair, _ = where_am_i()
    return ordered(first_pair, own[...], got)


def relay(got, out):
    out[...] = got[: out.shape[0]]


def relay_halves(got, low, high):
    rows = low.shape[0] - SCALES
    low[:rows] = got[:rows]
    high[:rows] = got[rows : 2 * rows]
    low[rows:] = got[2 * rows : 2 * rows + SCALES]
    high[rows:] = got[2 * rows : 2 * rows + SCALES]


def group_forward(n_own, got2, got2_core, sp_own, out):
    _, _, group = where_am_i()
    out[...] = jnp.zeros_like(out)

    @pl.when(group == 0)
    def _():
        split = coded_rows(n_own.shape[1] // 2, n_own.shape[1])
        _, n1 = pair_matrices(n_own, decode(got2[:split]), decode(got2_core))
        s0, s1 = pair_vectors(sp_own, decode(got2[split:]))
        out[...] = code(dot(s0, n1, 1, 1) + s1)


def group_map(n_own, got2, got2_core, sp_own, s_group, up, down, n_first, n_second):
    split = coded_rows(n_own.shape[1] // 2, n_own.shape[1])
    n0, n1 = pair_matrices(n_own, decode(got2[:split]), decode(got2_core))
    s0, s1 = pair_vectors(sp_own, decode(got2[split:]))
    s_group[...] = dot(s0, n1, 1, 1) + s1
    n_first[...] = n0
    n_second[...] = n1
    n_group = dot(n1, n0)
    up[...] = ready(n_group.T)
    down[...] = ready(n_group)


def block_map(n_second, x1, got1, d, k):
    half = x1.shape[1]
    first, first_pair, _ = where_am_i()
    rows = lax.broadcasted_iota(jnp.int32, (half, half), 0)
    columns = lax.broadcasted_iota(jnp.int32, (half, half), 1)
    unit = (rows == columns).astype(f32)
    _, m1 = ordered(first, x1[:half], got1[:half])
    above = jnp.where(first_pair, n_second[...], unit)
    above = jnp.where(first, dot(above, m1), above)
    k[...] = ready(dot(above, d[d.shape[0] - half :]))


def group_backward(
    n_first, got2, sp_own, gg_own, got4, got4_low, got4_high, gp_own,
    gg_group, g_group, gg_second, g_second,
):
    half = n_first.shape[1]
    split = coded_rows(half // 2, half)
    n0 = n_first[...]
    s0, _ = pair_vectors(sp_own, decode(got2[split:]))
    rows = got4_low.shape[0] - SCALES
    got4_core = jnp.concatenate([got4_low[:rows], got4_high[...]], axis=0)
    gg0, gg1 = pair_matrices(gg_own, decode(got4[:split]), decode(got4_core))
    g0, g1 = pair_vectors(gp_own, decode(got4[split:]))
    gg_second[...] = gg1
    g_second[...] = g1
    both = dot(jnp.concatenate([gg1, g1 - dot(s0, gg1)], axis=0), n0)
    gg_group[...] = ready(dot(n0, both[:half], 0, 0) + gg0)
    g_group[...] = both[half:] + g0


def forward_hop(step, got, t_in, up, s_group, t_out, out):
    _, _, group = where_am_i()
    t = jnp.where(group == step + 1, decode(got), t_in[...])
    t_out[...] = t
    out[...] = code(dot_ready(t, up) + s_group[...])


def turn(step, got, t_in, gg_group, g_group, t_out, out):
    _, _, group = where_am_i()
    t = jnp.where(group == step + 1, decode(got), t_in[...])
    t_out[...] = t
    out[...] = jnp.zeros_like(out)

    @pl.when(group == step + 1)
    def _():
        out[...] = code(g_group[...] - dot_ready(t, gg_group))


def backward_hop(step, got, u_in, down, local, u_out, out):
    _, _, group = where_am_i()
    u = jnp.where(group == step, decode(got), u_in[...])
    u_out[...] = u
    out[...] = code(dot_ready(u, down) + local[...])


def arrive(step, got, u_in, out):
    _, _, group = where_am_i()
    out[...] = code(jnp.where(group == step, decode(got), u_in[...]))


def spread_forward(
    t_in, n_first, got2, sp_own, gg_second, g_second, gg_group, g_group, x5, kept, rest_own, local
):
    half = n_first.shape[1]
    _, first_pair, _ = where_am_i()
    s0, _ = pair_vectors(sp_own, decode(got2[coded_rows(half // 2, half) :]))
    t_mid = dot(t_in[...], n_first[...], 1, 1) + s0
    rest = g_second[...] - dot(t_mid, gg_second[...])
    keep, send = ordered(first_pair, t_in[...], t_mid)
    x5[...] = code(jnp.concatenate([send, rest], axis=0))
    kept[...] = keep
    rest_own[...] = rest
    local[...] = g_group[...] - dot_ready(t_in[...], gg_group)


def pair_states(kept, rest_own, got5, x1, got1, s_own, x3, got3, g_own, x6, own):
    half = x1.shape[1]
    rows = s_own.shape[0]
    first, first_pair, _ = where_am_i()
    got = decode(got5)
    quarter = kept.shape[0]
    t = jnp.concatenate(ordered(first_pair, kept[...], got[:quarter]), axis=0)
    rest = jnp.concatenate(ordered(first_pair, rest_own[...], got[quarter:]), axis=0)
    m0, m1 = ordered(first, x1[:half], got1[:half])
    s0, _ = ordered(first, s_own[...], got1[half:])
    _, gg1 = ordered(first, x3[:half], got3[:half])
    _, g1 = ordered(first, g_own[...], got3[half:])
    t_mid = dot(t, m0, 1, 1) + s0
    fixed = jnp.where(first_pair, rest, 0.0)
    fixed_mid = dot(fixed, m1) + g1 - dot(t_mid, gg1)
    split = coded_rows(rows, half)
    keep, send = ordered(first, t, t_mid)
    x6[:split] = code(send)
    own[:rows] = keep
    keep, send = ordered(first, fixed_mid, fixed)
    x6[split:] = code(send)
    own[rows:] = keep


def block_parts(solved, p, d, start, maps):
    half = p.shape[1]
    start[...] = dot(solved[...], d[...])
    maps[:half] = dot(p[...], d[...], 0, 0)
    maps[half:] = d[d.shape[0] - half :]


def block_fixed(own, got6, start, maps, fixed_weights):
    rows = own.shape[0] // 2
    split = coded_rows(rows, own.shape[1])
    low = low_traits()
    t = jnp.concatenate(ordered(low, own[:rows], decode(got6[:split])), axis=0)
    above = jnp.concatenate(ordered(low, own[rows:], decode(got6[split:])), axis=0)
    fixed_weights[...] = start[...] - dot(jnp.concatenate([t, above], axis=1), maps[...])


def gather(mine, got_u, both):
    rows = mine.shape[0]
    both[:rows] = mine[...]
    both[rows:] = got_u[...]


def block_weights(both, got_both, fixed_weights, k, xa, xb):
    half = xa.shape[1]
    rows = both.shape[0] // 2
    first, first_pair, _ = where_am_i()
    near = jnp.concatenate(ordered(first_pair, decode(both[:rows]), decode(both[rows:])), axis=0)
    far = jnp.concatenate(
        ordered(first_pair, decode(got_both[:rows]), decode(got_both[rows:])), axis=0
    )
    u = jnp.concatenate(ordered(low_traits(), near, far), axis=0)
    weights = (fixed_weights[...] - dot_ready(u, k)).astype(bf16)
    a, b = ordered(first, weights[:, :half], weights[:, half:])
    xa[...] = a
    xb[...] = b


def contract(values, coefs):
    return lax.dot_general(values, coefs, (((1,), (1,)), ((), ())), preferred_element_type=f32)


def mask_coefs(coefs_in, anchor_in, masked, coefs, anchor, sems):
    untyped, span = coefs.shape
    half = span // 4
    typed = span - 2 * half
    tile = 128
    place = lax.axis_index(AXIS)
    total = lax.axis_size(AXIS) * typed
    copies = [pltpu.make_async_copy(anchor_in, anchor, sems.at[0])]
    for i in range(untyped // tile):
        rows = pl.ds(i * tile, tile)
        copies.append(pltpu.make_async_copy(coefs_in.at[rows], coefs.at[rows], sems.at[i + 1]))
    for copy in copies:
        copy.start()
    copies[0].wait()
    first_column = place * typed - half
    for i in range(untyped // tile):
        rows = pl.ds(i * tile, tile)
        nearest = jnp.broadcast_to(anchor[:, i * tile : (i + 1) * tile], (tile, tile)).T
        copies[i + 1].wait()
        for j in range(span // tile):
            lanes = pl.ds(j * tile, tile)
            columns = first_column + j * tile + lax.broadcasted_iota(jnp.int32, (tile, tile), 1)
            within = (jnp.abs(columns - nearest) <= half) & (columns >= 0) & (columns < total)
            masked[rows, lanes] = jnp.where(within, coefs[rows, lanes].astype(f32), 0.0).astype(bf16)


def impute_own(xa, xb, masked, out):
    first, _, _ = where_am_i()
    half = xa.shape[1]
    span = masked.shape[1]
    weights = jnp.concatenate(ordered(first, xa[...], xb[...]), axis=1)
    out[...] = contract(weights, masked[:, half : span - half])


def impute_edges(acc, got_a, got_b, masked, out):
    first, _, _ = where_am_i()
    half = got_a.shape[1]
    span = masked.shape[1]
    left, right = ordered(first, got_a[...], got_b[...])
    out[...] = acc[...] + contract(left, masked[:, :half]) + contract(right, masked[:, span - half :])


def swap(block, distance):
    n = lax.axis_size(AXIS)
    return lax.ppermute(block, AXIS, [(i, i ^ distance) for i in range(n)])


def hop(block, step):
    pairs = []
    for i in range(lax.axis_size(AXIS)):
        g = i // GROUP
        to = i + GROUP if g == step else i - GROUP if g == step + 1 else i
        pairs.append((i, to ^ 1))
    return lax.ppermute(block, AXIS, pairs)


def swap_chips(block):
    n, segments = lax.axis_size(AXIS), lax.axis_size(SEGMENTS)
    pairs = []
    for seg in range(segments):
        for i in range(n):
            to, to_seg = i + 1 if i % 2 else i - 1, seg
            if not 0 <= to < n:
                to, to_seg = (i, seg ^ 1) if segments % 2 == 0 else (to % n, seg)
            pairs.append((seg * n + i, to_seg * n + to))
    return lax.ppermute(block, (SEGMENTS, AXIS), pairs)


def per_device(z, diag_inverse, coupling, impute_coef, anchor):
    d = diag_inverse[0]
    c = coupling[0]
    typed = d.shape[0]
    half = c.shape[1]
    traits = z.shape[0]
    untyped, span = impute_coef.shape
    assert span == typed + 2 * half and typed == 2 * half
    assert lax.axis_size(AXIS) >= 3 * GROUP
    groups = lax.axis_size(AXIS) // GROUP
    two, four = traits // 2, traits // 4
    square = (half, half)
    sq, h2, h4 = (square, f32), ((two, half), f32), ((four, half), f32)
    x1_shape, x6_shape = ((half + two, half), f32), ((2 * two, half), f32)
    x6_coded = ((2 * coded_rows(two, half), LANES), i16)
    coded = ((coded_rows(four, half), LANES), i16)
    coded_half = ((coded_rows(half // 2, half), LANES), i16)
    mixed = ((coded_rows(half // 2, half) + coded_rows(four, half), LANES), i16)

    solved_shape, p_shape = ((traits, typed), f32), ((typed, half), f32)
    x1, s_own, z, d, c = call(
        tail_part, [x1_shape, h2, solved_shape, ((typed, typed), f32), p_shape], z, d, c,
        hbm=True, scratch=[pltpu.SemaphoreType.DMA((7,))],
    )
    got1 = swap(x1, 1)
    x3, g_own, solved, p = call(
        head_part, [x1_shape, h2, solved_shape, p_shape], z, d, c, x1, s_own
    )
    x2, n_own, sp_own = call(pair_forward, [mixed, sq, h4], x1, got1, s_own, after=(p,))
    got2 = swap(x2, 3)
    got3 = swap(x3, 1)
    masked = call(
        mask_coefs, ((untyped, span), bf16), impute_coef, anchor[None, :], after=(x2,), hbm=True,
        scratch=[
            pltpu.VMEM((untyped, span), bf16),
            pltpu.VMEM((1, untyped), jnp.int32),
            pltpu.SemaphoreType.DMA((untyped // 128 + 1,)),
        ],
    )
    x4, gg_own, gp_own = call(
        pair_backward, [mixed, sq, h4], x1, got1, s_own, x3, got3, g_own, after=(x2,)
    )
    got2_core = swap(call(relay, coded_half, got2, after=(x4, masked)), 1)
    out = call(group_forward, coded, n_own, got2, got2_core, sp_own)
    parts3 = ((3 * half, half), bf16)
    s_group, up, down, n_first, n_second = call(
        group_map, [h4, parts3, parts3, sq, sq], n_own, got2, got2_core, sp_own, after=(out,)
    )
    k = call(block_map, ((3 * half, typed), bf16), n_second, x1, got1, d)
    start, maps = call(
        block_parts, [solved_shape, ((2 * half, typed), f32)], solved, p, d, after=(k,)
    )
    t_in = jnp.zeros((four, half), f32)
    got4 = swap(x4, 3)
    for step in range(groups - 2):
        got = hop(out, step)
        t_in, out = call(
            functools.partial(forward_hop, step), [h4, coded], got, t_in, up, s_group,
            after=(maps,) if step == 0 else (),
        )
        if step == 0:
            pieces = [((half // 2 + SCALES, LANES), i16)] * 2
            low, high = call(relay_halves, pieces, got4, after=(out,))
            got4_low, got4_high = swap(low, 1), swap(high, 1)
    gg_group, g_group, gg_second, g_second = call(
        group_backward, [parts3, h4, sq, h4],
        n_first, got2, sp_own, gg_own, got4, got4_low, got4_high, gp_own, after=(out,),
    )
    last = groups - 2
    got = hop(out, last)
    t_in, out = call(
        functools.partial(turn, last), [h4, coded], got, t_in, gg_group, g_group
    )

    u_in = jnp.zeros((four, half), f32)
    for step in reversed(range(groups - 1)):
        got = hop(out, step)
        if step == last:
            x5, kept, rest_own, local = call(
                spread_forward, [coded_half, h4, h4, h4],
                t_in, n_first, got2, sp_own, gg_second, g_second, gg_group, g_group, after=(out,),
            )
            got5 = swap(x5, 3)
        if step:
            u_in, out = call(
                functools.partial(backward_hop, step), [h4, coded], got, u_in, down, local
            )
        else:
            out = call(functools.partial(arrive, step), coded, got, u_in)
    x6, own = call(
        pair_states, [x6_coded, x6_shape], kept, rest_own, got5, x1, got1, s_own, x3, got3, g_own
    )
    got6 = swap(x6, 1)
    fixed = call(block_fixed, solved_shape, own, got6, start, maps)
    both = call(gather, ((2 * coded[0][0], LANES), i16), out, swap(out, 3))
    got_both = swap(both, 1)
    edge = (square, bf16)
    xa, xb = call(block_weights, [edge, edge], both, got_both, fixed, k)
    got_a = swap_chips(xa)
    got_b = swap(xb, 1)
    acc = call(impute_own, ((traits, untyped), f32), xa, xb, masked)
    return call(
        impute_edges, ((traits, untyped), f32), acc, got_a, got_b, masked, last=True
    )


def solution(mesh):
    in_specs = (
        P(None, (SEGMENTS, AXIS)),
        P((SEGMENTS, AXIS), None, None),
        P((SEGMENTS, AXIS), None, None),
        P((SEGMENTS, AXIS), None),
        P((SEGMENTS, AXIS)),
    )
    return jax.shard_map(
        per_device, mesh=mesh, in_specs=in_specs, out_specs=P(None, (SEGMENTS, AXIS)), check_vma=False
    )
```

```python
import functools

import jax
import jax.numpy as jnp
from jax import lax
from jax.experimental import pallas as pl
from jax.experimental.pallas import tpu as pltpu
from jax.sharding import PartitionSpec as P

AXIS = "genome"
SEGMENTS = "seg"
GROUP = 4
f32 = jnp.float32
bf16 = jnp.bfloat16
i16 = jnp.int16
SCALES = 16
LANES = 128
LIMIT = 32767.0


def parts(x):
    high = x.astype(bf16)
    return high, (x - high.astype(f32)).astype(bf16)


def dot(a, b, ca=1, cb=0):
    ah, al = parts(a)
    bh, bl = parts(b)
    return lax.dot_general(
        jnp.concatenate([al, ah, ah], axis=ca),
        jnp.concatenate([bh, bl, bh], axis=cb),
        (((ca,), (cb,)), ((), ())),
        preferred_element_type=f32,
    )


def code(x):
    top = jnp.maximum(jnp.max(jnp.abs(x), axis=0, keepdims=True), 1e-32)
    power = jnp.ceil(jnp.log2(top) * 4.0)
    root = jnp.exp2(power * -0.125)
    steps = jnp.floor(x * root * (root * LIMIT) + 0.5)
    steps = jnp.clip(steps, -LIMIT, LIMIT)
    tiles = x.shape[1] // LANES
    powers = jnp.broadcast_to(power, (SCALES // tiles, x.shape[1]))
    pieces = [v[:, i * LANES : (i + 1) * LANES] for v in (steps, powers) for i in range(tiles)]
    return jnp.concatenate(pieces, axis=0).astype(jnp.int32).astype(i16)


def decode(coded, tiles=2):
    rows = (coded.shape[0] - SCALES) // tiles
    values = coded[...].astype(jnp.int32).astype(f32)
    columns = []
    for i in range(tiles):
        at = tiles * rows + i * (SCALES // tiles)
        root = jnp.exp2(values[at : at + 1] * 0.125)
        columns.append(values[i * rows : (i + 1) * rows] * (root / LIMIT) * root)
    return jnp.concatenate(columns, axis=1)


def coded_rows(rows, columns):
    return rows * (columns // LANES) + SCALES


def where_am_i():
    place = lax.axis_index(AXIS)
    return place % 2 == 0, (place // 2) % 2 == 0, place // GROUP


def ready(b):
    bh, bl = parts(b)
    return jnp.concatenate([bh, bl, bh], axis=0)


def dot_ready(a, b):
    ah, al = parts(a)
    return jnp.dot(jnp.concatenate([al, ah, ah], axis=1), b[...], preferred_element_type=f32)


def low_traits():
    place = lax.axis_index(AXIS)
    return (place + place // 2 + place // GROUP) % 2 == 0


def ordered(first, own, other):
    return jnp.where(first, own, other), jnp.where(first, other, own)


def call(kernel, outs, *args, after=(), hbm=False, last=False, scratch=()):
    n_in, n_after = len(args), len(after)

    def body(*refs):
        kernel(*refs[:n_in], *refs[n_in + n_after :])

    single = not isinstance(outs, list)
    shapes = [outs] if single else outs
    vmem = pl.BlockSpec(memory_space=pltpu.VMEM)
    anywhere = pl.BlockSpec(memory_space=pl.ANY)
    if hbm:
        args = [pltpu.with_memory_space_constraint(a, pltpu.HBM) for a in args]
    got = pl.pallas_call(
        body,
        out_shape=[jax.ShapeDtypeStruct(s, t) if last else pltpu.VMEM(s, t) for s, t in shapes],
        in_specs=[anywhere if hbm else vmem] * n_in + [anywhere] * n_after,
        out_specs=[vmem] * len(shapes),
        scratch_shapes=scratch,
        compiler_params=pltpu.CompilerParams(vmem_limit_bytes=8 * 2**20),
        name=kernel.__name__ if hasattr(kernel, "__name__") else kernel.func.__name__,
    )(*args, *after)
    return got[0] if single else got


def tail_part(z_in, d_in, c_in, x1, s_own, z, d, c, sems):
    typed, half = c.shape
    rows = z.shape[0] // 2
    head = typed - half
    step = typed // 2
    copies = []
    for i in range(2):
        here = pl.ds(i * step, step)
        tail = (pl.ds(head, half), here)
        copies.append(pltpu.make_async_copy(d_in.at[tail], d.at[tail], sems.at[3 * i]))
        copies.append(pltpu.make_async_copy(c_in.at[here], c.at[here], sems.at[3 * i + 1]))
        copies.append(pltpu.make_async_copy(z_in.at[:, here], z.at[:, here], sems.at[3 * i + 2]))
    rest = pl.ds(0, head)
    copies.append(pltpu.make_async_copy(d_in.at[rest], d.at[rest], sems.at[6]))
    for copy in copies:
        copy.start()
    m = s = 0.0
    for i in range(2):
        here = pl.ds(i * step, step)
        for copy in copies[3 * i : 3 * i + 3]:
            copy.wait()
        tail = d[head:, here]
        m = m - dot(tail, c[here])
        s = s + dot(z[:, here], tail, 1, 1)
    x1[:half] = m
    keep, send = ordered(low_traits(), s[:rows], s[rows:])
    x1[half:] = send
    s_own[...] = keep
    copies[6].wait()


def head_part(z, d, c, x1, s_own, x3, g_own, solved, p):
    half = c.shape[1]
    rows = z.shape[0] // 2
    head = d.shape[0] - half
    first, _, _ = where_am_i()
    p[:head] = dot(d[:head], c[...])
    p[head:] = -x1[:half]
    solved[:, :head] = dot(z[...], d[:head], 1, 1)
    low, high = ordered(low_traits(), s_own[...], x1[half:])
    solved[:rows, head:] = low
    solved[rows:, head:] = high
    g = dot(solved[...], p[...])
    keep, send = ordered(low_traits(), g[:rows], g[rows:])
    x3[:half] = dot(p[...], p[...], 0, 0)
    x3[half:] = send
    g_own[...] = keep


def pair_forward(x1, got1, s_own, x2, n_own, sp_own):
    half = x1.shape[1]
    first, first_pair, _ = where_am_i()
    m0, m1 = ordered(first, x1[:half], got1[:half])
    s0, s1 = ordered(first, s_own[...], got1[half:])
    n = dot(m1, m0)
    n_own[...] = n
    split = coded_rows(half // 2, half)
    x2[:split] = code(jnp.where(first, n[: half // 2], n[half // 2 :]))
    s = dot(s0, m1, 1, 1) + s1
    rows = s.shape[0] // 2
    keep, send = ordered(first_pair, s[:rows], s[rows:])
    x2[split:] = code(send)
    sp_own[...] = keep


def pair_backward(x1, got1, s_own, x3, got3, g_own, x4, gg_own, gp_own):
    half = x1.shape[1]
    first, first_pair, _ = where_am_i()
    m0, _ = ordered(first, x1[:half], got1[:half])
    s0, _ = ordered(first, s_own[...], got1[half:])
    gg0, gg1 = ordered(first, x3[:half], got3[:half])
    g0, g1 = ordered(first, g_own[...], got3[half:])
    both = dot(jnp.concatenate([gg1, g1 - dot(s0, gg1)], axis=0), m0)
    gg = dot(m0, both[:half], 0, 0) + gg0
    gg_own[...] = gg
    split = coded_rows(half // 2, half)
    x4[:split] = code(jnp.where(first, gg[: half // 2], gg[half // 2 :]))
    g = both[half:] + g0
    rows = g.shape[0] // 2
    keep, send = ordered(first_pair, g[:rows], g[rows:])
    x4[split:] = code(send)
    gp_own[...] = keep


def pair_matrices(own, got, got_core):
    first, first_pair, _ = where_am_i()
    other = jnp.concatenate(ordered(first, got_core, got), axis=0)
    return ordered(first_pair, own[...], other)


def pair_vectors(own, got):
    _, first_pair, _ = where_am_i()
    return ordered(first_pair, own[...], got)


def relay(got, out):
    out[...] = got[: out.shape[0]]


def group_forward(n_own, got2, got2_core, sp_own, out):
    _, _, group = where_am_i()
    out[...] = jnp.zeros_like(out)

    @pl.when(group == 0)
    def _():
        split = coded_rows(n_own.shape[1] // 2, n_own.shape[1])
        _, n1 = pair_matrices(n_own, decode(got2[:split]), decode(got2_core))
        s0, s1 = pair_vectors(sp_own, decode(got2[split:]))
        out[...] = code(dot(s0, n1, 1, 1) + s1)


def group_map(n_own, got2, got2_core, sp_own, s_group, up, down, n_first, n_second):
    split = coded_rows(n_own.shape[1] // 2, n_own.shape[1])
    n0, n1 = pair_matrices(n_own, decode(got2[:split]), decode(got2_core))
    s0, s1 = pair_vectors(sp_own, decode(got2[split:]))
    s_group[...] = dot(s0, n1, 1, 1) + s1
    n_first[...] = n0
    n_second[...] = n1
    n_group = dot(n1, n0)
    up[...] = ready(n_group.T)
    down[...] = ready(n_group)


def block_map(n_second, x1, got1, d, k):
    half = x1.shape[1]
    first, first_pair, _ = where_am_i()
    rows = lax.broadcasted_iota(jnp.int32, (half, half), 0)
    columns = lax.broadcasted_iota(jnp.int32, (half, half), 1)
    unit = (rows == columns).astype(f32)
    _, m1 = ordered(first, x1[:half], got1[:half])
    above = jnp.where(first_pair, n_second[...], unit)
    above = jnp.where(first, dot(above, m1), above)
    k[...] = ready(dot(above, d[d.shape[0] - half :]))


def group_backward(
    n_first, got2, sp_own, gg_own, got4, got4_core, gp_own,
    gg_group, g_group, gg_second, g_second,
):
    half = n_first.shape[1]
    split = coded_rows(half // 2, half)
    n0 = n_first[...]
    s0, _ = pair_vectors(sp_own, decode(got2[split:]))
    gg0, gg1 = pair_matrices(gg_own, decode(got4[:split]), decode(got4_core))
    g0, g1 = pair_vectors(gp_own, decode(got4[split:]))
    gg_second[...] = gg1
    g_second[...] = g1
    both = dot(jnp.concatenate([gg1, g1 - dot(s0, gg1)], axis=0), n0)
    gg_group[...] = ready(dot(n0, both[:half], 0, 0) + gg0)
    g_group[...] = both[half:] + g0


def forward_hop(step, got, t_in, up, s_group, t_out, out):
    _, _, group = where_am_i()
    t = jnp.where(group == step + 1, decode(got), t_in[...])
    t_out[...] = t
    out[...] = code(dot_ready(t, up) + s_group[...])


def turn(step, got, t_in, gg_group, g_group, t_out, out):
    _, _, group = where_am_i()
    t = jnp.where(group == step + 1, decode(got), t_in[...])
    t_out[...] = t
    out[...] = jnp.zeros_like(out)

    @pl.when(group == step + 1)
    def _():
        out[...] = code(g_group[...] - dot_ready(t, gg_group))


def backward_hop(step, got, u_in, down, local, u_out, out):
    _, _, group = where_am_i()
    u = jnp.where(group == step, decode(got), u_in[...])
    u_out[...] = u
    out[...] = code(dot_ready(u, down) + local[...])


def arrive(step, got, u_in, out):
    _, _, group = where_am_i()
    out[...] = code(jnp.where(group == step, decode(got), u_in[...]))


def spread_forward(
    t_in, n_first, got2, sp_own, gg_second, g_second, gg_group, g_group, x5, kept, rest_own, local
):
    half = n_first.shape[1]
    _, first_pair, _ = where_am_i()
    s0, _ = pair_vectors(sp_own, decode(got2[coded_rows(half // 2, half) :]))
    t_mid = dot(t_in[...], n_first[...], 1, 1) + s0
    rest = g_second[...] - dot(t_mid, gg_second[...])
    keep, send = ordered(first_pair, t_in[...], t_mid)
    x5[...] = code(jnp.concatenate([send, rest], axis=0))
    kept[...] = keep
    rest_own[...] = rest
    local[...] = g_group[...] - dot_ready(t_in[...], gg_group)


def pair_states(kept, rest_own, got5, x1, got1, s_own, x3, got3, g_own, x6, own):
    half = x1.shape[1]
    rows = s_own.shape[0]
    first, first_pair, _ = where_am_i()
    got = decode(got5)
    quarter = kept.shape[0]
    t = jnp.concatenate(ordered(first_pair, kept[...], got[:quarter]), axis=0)
    rest = jnp.concatenate(ordered(first_pair, rest_own[...], got[quarter:]), axis=0)
    m0, m1 = ordered(first, x1[:half], got1[:half])
    s0, _ = ordered(first, s_own[...], got1[half:])
    _, gg1 = ordered(first, x3[:half], got3[:half])
    _, g1 = ordered(first, g_own[...], got3[half:])
    t_mid = dot(t, m0, 1, 1) + s0
    fixed = jnp.where(first_pair, rest, 0.0)
    fixed_mid = dot(fixed, m1) + g1 - dot(t_mid, gg1)
    split = coded_rows(rows, half)
    keep, send = ordered(first, t, t_mid)
    x6[:split] = code(send)
    own[:rows] = keep
    keep, send = ordered(first, fixed_mid, fixed)
    x6[split:] = code(send)
    own[rows:] = keep


def block_parts(solved, p, d, start, maps):
    half = p.shape[1]
    start[...] = dot(solved[...], d[...])
    maps[:half] = dot(p[...], d[...], 0, 0)
    maps[half:] = d[d.shape[0] - half :]


def block_fixed(own, got6, start, maps, fixed_weights):
    rows = own.shape[0] // 2
    split = coded_rows(rows, own.shape[1])
    low = low_traits()
    t = jnp.concatenate(ordered(low, own[:rows], decode(got6[:split])), axis=0)
    above = jnp.concatenate(ordered(low, own[rows:], decode(got6[split:])), axis=0)
    fixed_weights[...] = start[...] - dot(jnp.concatenate([t, above], axis=1), maps[...])


def gather(mine, got_u, both):
    rows = mine.shape[0]
    both[:rows] = mine[...]
    both[rows:] = got_u[...]


def block_weights(both, got_both, fixed_weights, k, xa, xb):
    half = xa.shape[1]
    rows = both.shape[0] // 2
    first, first_pair, _ = where_am_i()
    near = jnp.concatenate(ordered(first_pair, decode(both[:rows]), decode(both[rows:])), axis=0)
    far = jnp.concatenate(
        ordered(first_pair, decode(got_both[:rows]), decode(got_both[rows:])), axis=0
    )
    u = jnp.concatenate(ordered(low_traits(), near, far), axis=0)
    weights = (fixed_weights[...] - dot_ready(u, k)).astype(bf16)
    a, b = ordered(first, weights[:, :half], weights[:, half:])
    xa[...] = a
    xb[...] = b


def contract(values, coefs):
    return lax.dot_general(values, coefs, (((1,), (1,)), ((), ())), preferred_element_type=f32)


def mask_coefs(coefs_in, anchor_in, masked, coefs, anchor, sems):
    untyped, span = coefs.shape
    half = span // 4
    typed = span - 2 * half
    tile = 128
    place = lax.axis_index(AXIS)
    total = lax.axis_size(AXIS) * typed
    copies = [pltpu.make_async_copy(anchor_in, anchor, sems.at[0])]
    for i in range(untyped // tile):
        rows = pl.ds(i * tile, tile)
        copies.append(pltpu.make_async_copy(coefs_in.at[rows], coefs.at[rows], sems.at[i + 1]))
    for copy in copies:
        copy.start()
    copies[0].wait()
    first_column = place * typed - half
    for i in range(untyped // tile):
        rows = pl.ds(i * tile, tile)
        nearest = jnp.broadcast_to(anchor[:, i * tile : (i + 1) * tile], (tile, tile)).T
        copies[i + 1].wait()
        for j in range(span // tile):
            lanes = pl.ds(j * tile, tile)
            columns = first_column + j * tile + lax.broadcasted_iota(jnp.int32, (tile, tile), 1)
            within = (jnp.abs(columns - nearest) <= half) & (columns >= 0) & (columns < total)
            masked[rows, lanes] = jnp.where(within, coefs[rows, lanes].astype(f32), 0.0).astype(bf16)


def impute_own(xa, xb, masked, out):
    first, _, _ = where_am_i()
    half = xa.shape[1]
    span = masked.shape[1]
    weights = jnp.concatenate(ordered(first, xa[...], xb[...]), axis=1)
    out[...] = contract(weights, masked[:, half : span - half])


def impute_edges(acc, got_a, got_b, masked, out):
    first, _, _ = where_am_i()
    half = got_a.shape[1]
    span = masked.shape[1]
    left, right = ordered(first, got_a[...], got_b[...])
    out[...] = acc[...] + contract(left, masked[:, :half]) + contract(right, masked[:, span - half :])


def swap(block, distance):
    n = lax.axis_size(AXIS)
    return lax.ppermute(block, AXIS, [(i, i ^ distance) for i in range(n)])


def hop(block, step):
    pairs = []
    for i in range(lax.axis_size(AXIS)):
        g = i // GROUP
        to = i + GROUP if g == step else i - GROUP if g == step + 1 else i
        pairs.append((i, to ^ 1))
    return lax.ppermute(block, AXIS, pairs)


def swap_chips(block):
    n, segments = lax.axis_size(AXIS), lax.axis_size(SEGMENTS)
    pairs = []
    for seg in range(segments):
        for i in range(n):
            to, to_seg = i + 1 if i % 2 else i - 1, seg
            if not 0 <= to < n:
                to, to_seg = (i, seg ^ 1) if segments % 2 == 0 else (to % n, seg)
            pairs.append((seg * n + i, to_seg * n + to))
    return lax.ppermute(block, (SEGMENTS, AXIS), pairs)


def per_device(z, diag_inverse, coupling, impute_coef, anchor):
    d = diag_inverse[0]
    c = coupling[0]
    typed = d.shape[0]
    half = c.shape[1]
    traits = z.shape[0]
    untyped, span = impute_coef.shape
    assert span == typed + 2 * half and typed == 2 * half
    assert lax.axis_size(AXIS) >= 3 * GROUP
    groups = lax.axis_size(AXIS) // GROUP
    two, four = traits // 2, traits // 4
    square = (half, half)
    sq, h2, h4 = (square, f32), ((two, half), f32), ((four, half), f32)
    x1_shape, x6_shape = ((half + two, half), f32), ((2 * two, half), f32)
    x6_coded = ((2 * coded_rows(two, half), LANES), i16)
    coded = ((coded_rows(four, half), LANES), i16)
    coded_half = ((coded_rows(half // 2, half), LANES), i16)
    mixed = ((coded_rows(half // 2, half) + coded_rows(four, half), LANES), i16)

    solved_shape, p_shape = ((traits, typed), f32), ((typed, half), f32)
    x1, s_own, z, d, c = call(
        tail_part, [x1_shape, h2, solved_shape, ((typed, typed), f32), p_shape], z, d, c,
        hbm=True, scratch=[pltpu.SemaphoreType.DMA((7,))],
    )
    got1 = swap(x1, 1)
    x3, g_own, solved, p = call(
        head_part, [x1_shape, h2, solved_shape, p_shape], z, d, c, x1, s_own
    )
    x2, n_own, sp_own = call(pair_forward, [mixed, sq, h4], x1, got1, s_own, after=(p,))
    got2 = swap(x2, 3)
    got3 = swap(x3, 1)
    masked = call(
        mask_coefs, ((untyped, span), bf16), impute_coef, anchor[None, :], after=(x2,), hbm=True,
        scratch=[
            pltpu.VMEM((untyped, span), bf16),
            pltpu.VMEM((1, untyped), jnp.int32),
            pltpu.SemaphoreType.DMA((untyped // 128 + 1,)),
        ],
    )
    x4, gg_own, gp_own = call(
        pair_backward, [mixed, sq, h4], x1, got1, s_own, x3, got3, g_own, after=(x2,)
    )
    got2_core = swap(call(relay, coded_half, got2, after=(x4, masked)), 1)
    out = call(group_forward, coded, n_own, got2, got2_core, sp_own)
    parts3 = ((3 * half, half), bf16)
    s_group, up, down, n_first, n_second = call(
        group_map, [h4, parts3, parts3, sq, sq], n_own, got2, got2_core, sp_own, after=(out,)
    )
    k = call(block_map, ((3 * half, typed), bf16), n_second, x1, got1, d)
    start, maps = call(
        block_parts, [solved_shape, ((2 * half, typed), f32)], solved, p, d, after=(k,)
    )
    t_in = jnp.zeros((four, half), f32)
    got4 = swap(x4, 3)
    for step in range(groups - 2):
        got = hop(out, step)
        t_in, out = call(
            functools.partial(forward_hop, step), [h4, coded], got, t_in, up, s_group,
            after=(maps,) if step == 0 else (),
        )
        if step == 0:
            got4_core = swap(call(relay, coded_half, got4, after=(out,)), 1)
    gg_group, g_group, gg_second, g_second = call(
        group_backward, [parts3, h4, sq, h4],
        n_first, got2, sp_own, gg_own, got4, got4_core, gp_own, after=(out,),
    )
    last = groups - 2
    got = hop(out, last)
    t_in, out = call(
        functools.partial(turn, last), [h4, coded], got, t_in, gg_group, g_group
    )

    u_in = jnp.zeros((four, half), f32)
    for step in reversed(range(groups - 1)):
        got = hop(out, step)
        if step == last:
            x5, kept, rest_own, local = call(
                spread_forward, [coded_half, h4, h4, h4],
                t_in, n_first, got2, sp_own, gg_second, g_second, gg_group, g_group, after=(out,),
            )
            got5 = swap(x5, 3)
        if step:
            u_in, out = call(
                functools.partial(backward_hop, step), [h4, coded], got, u_in, down, local
            )
        else:
            out = call(functools.partial(arrive, step), coded, got, u_in)
    x6, own = call(
        pair_states, [x6_coded, x6_shape], kept, rest_own, got5, x1, got1, s_own, x3, got3, g_own
    )
    got6 = swap(x6, 1)
    fixed = call(block_fixed, solved_shape, own, got6, start, maps)
    both = call(gather, ((2 * coded[0][0], LANES), i16), out, swap(out, 3))
    got_both = swap(both, 1)
    edge = (square, bf16)
    xa, xb = call(block_weights, [edge, edge], both, got_both, fixed, k)
    got_a = swap_chips(xa)
    got_b = swap(xb, 1)
    acc = call(impute_own, ((traits, untyped), f32), xa, xb, masked)
    return call(
        impute_edges, ((traits, untyped), f32), acc, got_a, got_b, masked, last=True
    )


def solution(mesh):
    in_specs = (
        P(None, (SEGMENTS, AXIS)),
        P((SEGMENTS, AXIS), None, None),
        P((SEGMENTS, AXIS), None, None),
        P((SEGMENTS, AXIS), None),
        P((SEGMENTS, AXIS)),
    )
    return jax.shard_map(
        per_device, mesh=mesh, in_specs=in_specs, out_specs=P(None, (SEGMENTS, AXIS)), check_vma=False
    )
```

```python
import functools

import jax
import jax.numpy as jnp
from jax import lax
from jax.experimental import pallas as pl
from jax.experimental.pallas import tpu as pltpu
from jax.sharding import PartitionSpec as P

AXIS = "genome"
SEGMENTS = "seg"
GROUP = 4
f32 = jnp.float32
bf16 = jnp.bfloat16
i16 = jnp.int16
SCALES = 16
LANES = 128
LIMIT = 32767.0


def parts(x):
    high = x.astype(bf16)
    return high, (x - high.astype(f32)).astype(bf16)


def dot(a, b, ca=1, cb=0):
    ah, al = parts(a)
    bh, bl = parts(b)
    return lax.dot_general(
        jnp.concatenate([al, ah, ah], axis=ca),
        jnp.concatenate([bh, bl, bh], axis=cb),
        (((ca,), (cb,)), ((), ())),
        preferred_element_type=f32,
    )


def code(x):
    top = jnp.maximum(jnp.max(jnp.abs(x), axis=0, keepdims=True), 1e-32)
    power = jnp.ceil(jnp.log2(top) * 4.0)
    root = jnp.exp2(power * -0.125)
    steps = jnp.floor(x * root * (root * LIMIT) + 0.5)
    steps = jnp.clip(steps, -LIMIT, LIMIT)
    tiles = x.shape[1] // LANES
    powers = jnp.broadcast_to(power, (SCALES // tiles, x.shape[1]))
    pieces = [v[:, i * LANES : (i + 1) * LANES] for v in (steps, powers) for i in range(tiles)]
    return jnp.concatenate(pieces, axis=0).astype(jnp.int32).astype(i16)


def decode(coded, tiles=2):
    rows = (coded.shape[0] - SCALES) // tiles
    values = coded[...].astype(jnp.int32).astype(f32)
    columns = []
    for i in range(tiles):
        at = tiles * rows + i * (SCALES // tiles)
        root = jnp.exp2(values[at : at + 1] * 0.125)
        columns.append(values[i * rows : (i + 1) * rows] * (root / LIMIT) * root)
    return jnp.concatenate(columns, axis=1)


def coded_rows(rows, columns):
    return rows * (columns // LANES) + SCALES


def where_am_i():
    place = lax.axis_index(AXIS)
    return place % 2 == 0, (place // 2) % 2 == 0, place // GROUP


def ready(b):
    bh, bl = parts(b)
    return jnp.concatenate([bh, bl, bh], axis=0)


def dot_ready(a, b):
    ah, al = parts(a)
    return jnp.dot(jnp.concatenate([al, ah, ah], axis=1), b[...], preferred_element_type=f32)


def low_traits():
    place = lax.axis_index(AXIS)
    return (place + place // 2 + place // GROUP) % 2 == 0


def ordered(first, own, other):
    return jnp.where(first, own, other), jnp.where(first, other, own)


def call(kernel, outs, *args, after=(), hbm=False, last=False, scratch=()):
    n_in, n_after = len(args), len(after)

    def body(*refs):
        kernel(*refs[:n_in], *refs[n_in + n_after :])

    single = not isinstance(outs, list)
    shapes = [outs] if single else outs
    vmem = pl.BlockSpec(memory_space=pltpu.VMEM)
    anywhere = pl.BlockSpec(memory_space=pl.ANY)
    if hbm:
        args = [pltpu.with_memory_space_constraint(a, pltpu.HBM) for a in args]
    got = pl.pallas_call(
        body,
        out_shape=[jax.ShapeDtypeStruct(s, t) if last else pltpu.VMEM(s, t) for s, t in shapes],
        in_specs=[anywhere if hbm else vmem] * n_in + [anywhere] * n_after,
        out_specs=[vmem] * len(shapes),
        scratch_shapes=scratch,
        compiler_params=pltpu.CompilerParams(vmem_limit_bytes=8 * 2**20),
        name=kernel.__name__ if hasattr(kernel, "__name__") else kernel.func.__name__,
    )(*args, *after)
    return got[0] if single else got


def tail_part(z_in, d_in, c_in, x1, s_own, z, d, c, sems):
    typed, half = c.shape
    rows = z.shape[0] // 2
    head = typed - half
    step = typed // 2
    copies = []
    for i in range(2):
        here = pl.ds(i * step, step)
        tail = (pl.ds(head, half), here)
        copies.append(pltpu.make_async_copy(d_in.at[tail], d.at[tail], sems.at[3 * i]))
        copies.append(pltpu.make_async_copy(c_in.at[here], c.at[here], sems.at[3 * i + 1]))
        copies.append(pltpu.make_async_copy(z_in.at[:, here], z.at[:, here], sems.at[3 * i + 2]))
    rest = pl.ds(0, head)
    copies.append(pltpu.make_async_copy(d_in.at[rest], d.at[rest], sems.at[6]))
    for copy in copies:
        copy.start()
    m = s = 0.0
    for i in range(2):
        here = pl.ds(i * step, step)
        for copy in copies[3 * i : 3 * i + 3]:
            copy.wait()
        tail = d[head:, here]
        m = m - dot(tail, c[here])
        s = s + dot(z[:, here], tail, 1, 1)
    x1[:half] = m
    keep, send = ordered(low_traits(), s[:rows], s[rows:])
    x1[half:] = send
    s_own[...] = keep
    copies[6].wait()


def head_part(z, d, c, x1, s_own, x3, g_own, solved, p):
    half = c.shape[1]
    rows = z.shape[0] // 2
    head = d.shape[0] - half
    first, _, _ = where_am_i()
    p[:head] = dot(d[:head], c[...])
    p[head:] = -x1[:half]
    solved[:, :head] = dot(z[...], d[:head], 1, 1)
    low, high = ordered(low_traits(), s_own[...], x1[half:])
    solved[:rows, head:] = low
    solved[rows:, head:] = high
    g = dot(solved[...], p[...])
    keep, send = ordered(low_traits(), g[:rows], g[rows:])
    x3[:half] = dot(p[...], p[...], 0, 0)
    x3[half:] = send
    g_own[...] = keep


def pair_forward(x1, got1, s_own, x2, n_own, sp_own):
    half = x1.shape[1]
    first, first_pair, _ = where_am_i()
    m0, m1 = ordered(first, x1[:half], got1[:half])
    s0, s1 = ordered(first, s_own[...], got1[half:])
    n = dot(m1, m0)
    n_own[...] = n
    split = coded_rows(half // 2, half)
    x2[:split] = code(jnp.where(first, n[: half // 2], n[half // 2 :]))
    s = dot(s0, m1, 1, 1) + s1
    rows = s.shape[0] // 2
    keep, send = ordered(first_pair, s[:rows], s[rows:])
    x2[split:] = code(send)
    sp_own[...] = keep


def pair_backward(x1, got1, s_own, x3, got3, g_own, x4, gg_own, gp_own):
    half = x1.shape[1]
    first, first_pair, _ = where_am_i()
    m0, _ = ordered(first, x1[:half], got1[:half])
    s0, _ = ordered(first, s_own[...], got1[half:])
    gg0, gg1 = ordered(first, x3[:half], got3[:half])
    g0, g1 = ordered(first, g_own[...], got3[half:])
    both = dot(jnp.concatenate([gg1, g1 - dot(s0, gg1)], axis=0), m0)
    gg = dot(m0, both[:half], 0, 0) + gg0
    gg_own[...] = gg
    split = coded_rows(half // 2, half)
    x4[:split] = code(jnp.where(first, gg[: half // 2], gg[half // 2 :]))
    g = both[half:] + g0
    rows = g.shape[0] // 2
    keep, send = ordered(first_pair, g[:rows], g[rows:])
    x4[split:] = code(send)
    gp_own[...] = keep


def pair_matrices(own, got, got_core):
    first, first_pair, _ = where_am_i()
    other = jnp.concatenate(ordered(first, got_core, got), axis=0)
    return ordered(first_pair, own[...], other)


def pair_vectors(own, got):
    _, first_pair, _ = where_am_i()
    return ordered(first_pair, own[...], got)


def relay(got, out):
    out[...] = got[: out.shape[0]]


def relay_halves(got, low, high):
    rows = low.shape[0] - SCALES
    low[:rows] = got[:rows]
    high[:rows] = got[rows : 2 * rows]
    low[rows:] = got[2 * rows : 2 * rows + SCALES]
    high[rows:] = got[2 * rows : 2 * rows + SCALES]


def group_forward(n_own, got2, got2_core, sp_own, out):
    _, _, group = where_am_i()
    out[...] = jnp.zeros_like(out)

    @pl.when(group == 0)
    def _():
        split = coded_rows(n_own.shape[1] // 2, n_own.shape[1])
        _, n1 = pair_matrices(n_own, decode(got2[:split]), decode(got2_core))
        s0, s1 = pair_vectors(sp_own, decode(got2[split:]))
        out[...] = code(dot(s0, n1, 1, 1) + s1)


def group_map(n_own, got2, got2_core, sp_own, s_group, up, down, n_first, n_second):
    split = coded_rows(n_own.shape[1] // 2, n_own.shape[1])
    n0, n1 = pair_matrices(n_own, decode(got2[:split]), decode(got2_core))
    s0, s1 = pair_vectors(sp_own, decode(got2[split:]))
    s_group[...] = dot(s0, n1, 1, 1) + s1
    n_first[...] = n0
    n_second[...] = n1
    n_group = dot(n1, n0)
    up[...] = ready(n_group.T)
    down[...] = ready(n_group)


def block_map(n_second, x1, got1, d, k):
    half = x1.shape[1]
    first, first_pair, _ = where_am_i()
    rows = lax.broadcasted_iota(jnp.int32, (half, half), 0)
    columns = lax.broadcasted_iota(jnp.int32, (half, half), 1)
    unit = (rows == columns).astype(f32)
    _, m1 = ordered(first, x1[:half], got1[:half])
    above = jnp.where(first_pair, n_second[...], unit)
    above = jnp.where(first, dot(above, m1), above)
    k[...] = ready(dot(above, d[d.shape[0] - half :]))


def group_backward(
    n_first, got2, sp_own, gg_own, got4, got4_low, got4_high, gp_own,
    gg_group, g_group, gg_second, g_second,
):
    half = n_first.shape[1]
    split = coded_rows(half // 2, half)
    n0 = n_first[...]
    s0, _ = pair_vectors(sp_own, decode(got2[split:]))
    rows = got4_low.shape[0] - SCALES
    got4_core = jnp.concatenate([got4_low[:rows], got4_high[...]], axis=0)
    gg0, gg1 = pair_matrices(gg_own, decode(got4[:split]), decode(got4_core))
    g0, g1 = pair_vectors(gp_own, decode(got4[split:]))
    gg_second[...] = gg1
    g_second[...] = g1
    both = dot(jnp.concatenate([gg1, g1 - dot(s0, gg1)], axis=0), n0)
    gg_group[...] = ready(dot(n0, both[:half], 0, 0) + gg0)
    g_group[...] = both[half:] + g0


def forward_hop(step, got, t_in, up, s_group, t_out, out):
    _, _, group = where_am_i()
    t = jnp.where(group == step + 1, decode(got), t_in[...])
    t_out[...] = t
    out[...] = code(dot_ready(t, up) + s_group[...])


def turn(step, got, t_in, gg_group, g_group, t_out, out):
    _, _, group = where_am_i()
    t = jnp.where(group == step + 1, decode(got), t_in[...])
    t_out[...] = t
    out[...] = jnp.zeros_like(out)

    @pl.when(group == step + 1)
    def _():
        out[...] = code(g_group[...] - dot_ready(t, gg_group))


def backward_hop(step, got, u_in, down, local, u_out, out):
    _, _, group = where_am_i()
    u = jnp.where(group == step, decode(got), u_in[...])
    u_out[...] = u
    out[...] = code(dot_ready(u, down) + local[...])


def arrive(step, got, u_in, out):
    _, _, group = where_am_i()
    out[...] = code(jnp.where(group == step, decode(got), u_in[...]))


def spread_forward(
    t_in, n_first, got2, sp_own, gg_second, g_second, gg_group, g_group, x5, kept, rest_own, local
):
    half = n_first.shape[1]
    _, first_pair, _ = where_am_i()
    s0, _ = pair_vectors(sp_own, decode(got2[coded_rows(half // 2, half) :]))
    t_mid = dot(t_in[...], n_first[...], 1, 1) + s0
    rest = g_second[...] - dot(t_mid, gg_second[...])
    keep, send = ordered(first_pair, t_in[...], t_mid)
    x5[...] = code(jnp.concatenate([send, rest], axis=0))
    kept[...] = keep
    rest_own[...] = rest
    local[...] = g_group[...] - dot_ready(t_in[...], gg_group)


def pair_states(kept, rest_own, got5, x1, got1, s_own, x3, got3, g_own, x6, own):
    half = x1.shape[1]
    rows = s_own.shape[0]
    first, first_pair, _ = where_am_i()
    got = decode(got5)
    quarter = kept.shape[0]
    t = jnp.concatenate(ordered(first_pair, kept[...], got[:quarter]), axis=0)
    rest = jnp.concatenate(ordered(first_pair, rest_own[...], got[quarter:]), axis=0)
    m0, m1 = ordered(first, x1[:half], got1[:half])
    s0, _ = ordered(first, s_own[...], got1[half:])
    _, gg1 = ordered(first, x3[:half], got3[:half])
    _, g1 = ordered(first, g_own[...], got3[half:])
    t_mid = dot(t, m0, 1, 1) + s0
    fixed = jnp.where(first_pair, rest, 0.0)
    fixed_mid = dot(fixed, m1) + g1 - dot(t_mid, gg1)
    split = coded_rows(rows, half)
    keep, send = ordered(first, t, t_mid)
    x6[:split] = code(send)
    own[:rows] = keep
    keep, send = ordered(first, fixed_mid, fixed)
    x6[split:] = code(send)
    own[rows:] = keep


def block_parts(solved, p, d, start, maps):
    half = p.shape[1]
    start[...] = dot(solved[...], d[...])
    maps[:half] = dot(p[...], d[...], 0, 0)
    maps[half:] = d[d.shape[0] - half :]


def block_fixed(own, got6, start, maps, fixed_weights):
    rows = own.shape[0] // 2
    split = coded_rows(rows, own.shape[1])
    low = low_traits()
    t = jnp.concatenate(ordered(low, own[:rows], decode(got6[:split])), axis=0)
    above = jnp.concatenate(ordered(low, own[rows:], decode(got6[split:])), axis=0)
    fixed_weights[...] = start[...] - dot(jnp.concatenate([t, above], axis=1), maps[...])


def gather(mine, got_u, both):
    rows = mine.shape[0]
    both[:rows] = mine[...]
    both[rows:] = got_u[...]


def block_weights(both, got_both, fixed_weights, k, xa, xb):
    half = xa.shape[1]
    rows = both.shape[0] // 2
    first, first_pair, _ = where_am_i()
    near = jnp.concatenate(ordered(first_pair, decode(both[:rows]), decode(both[rows:])), axis=0)
    far = jnp.concatenate(
        ordered(first_pair, decode(got_both[:rows]), decode(got_both[rows:])), axis=0
    )
    u = jnp.concatenate(ordered(low_traits(), near, far), axis=0)
    weights = (fixed_weights[...] - dot_ready(u, k)).astype(bf16)
    a, b = ordered(first, weights[:, :half], weights[:, half:])
    xa[...] = a
    xb[...] = b


def contract(values, coefs):
    return lax.dot_general(values, coefs, (((1,), (1,)), ((), ())), preferred_element_type=f32)


def mask_coefs(coefs_in, anchor_in, masked, coefs, anchor, sems):
    untyped, span = coefs.shape
    half = span // 4
    typed = span - 2 * half
    tile = 128
    place = lax.axis_index(AXIS)
    total = lax.axis_size(AXIS) * typed
    copies = [pltpu.make_async_copy(anchor_in, anchor, sems.at[0])]
    for i in range(untyped // tile):
        rows = pl.ds(i * tile, tile)
        copies.append(pltpu.make_async_copy(coefs_in.at[rows], coefs.at[rows], sems.at[i + 1]))
    for copy in copies:
        copy.start()
    copies[0].wait()
    first_column = place * typed - half
    for i in range(untyped // tile):
        rows = pl.ds(i * tile, tile)
        nearest = jnp.broadcast_to(anchor[:, i * tile : (i + 1) * tile], (tile, tile)).T
        copies[i + 1].wait()
        for j in range(span // tile):
            lanes = pl.ds(j * tile, tile)
            columns = first_column + j * tile + lax.broadcasted_iota(jnp.int32, (tile, tile), 1)
            within = (jnp.abs(columns - nearest) <= half) & (columns >= 0) & (columns < total)
            masked[rows, lanes] = jnp.where(within, coefs[rows, lanes].astype(f32), 0.0).astype(bf16)


def impute_own(xa, xb, masked, out):
    first, _, _ = where_am_i()
    half = xa.shape[1]
    span = masked.shape[1]
    weights = jnp.concatenate(ordered(first, xa[...], xb[...]), axis=1)
    out[...] = contract(weights, masked[:, half : span - half])


def impute_edges(acc, got_a, got_b, masked, out):
    first, _, _ = where_am_i()
    half = got_a.shape[1]
    span = masked.shape[1]
    left, right = ordered(first, got_a[...], got_b[...])
    edges = jnp.concatenate([left, right], axis=1)
    coefs = jnp.concatenate([masked[:, :half], masked[:, span - half :]], axis=1)
    out[...] = acc[...] + contract(edges, coefs)


def swap(block, distance):
    n = lax.axis_size(AXIS)
    return lax.ppermute(block, AXIS, [(i, i ^ distance) for i in range(n)])


def hop(block, step):
    pairs = []
    for i in range(lax.axis_size(AXIS)):
        g = i // GROUP
        to = i + GROUP if g == step else i - GROUP if g == step + 1 else i
        pairs.append((i, to ^ 1))
    return lax.ppermute(block, AXIS, pairs)


def swap_chips(block):
    n, segments = lax.axis_size(AXIS), lax.axis_size(SEGMENTS)
    pairs = []
    for seg in range(segments):
        for i in range(n):
            to, to_seg = i + 1 if i % 2 else i - 1, seg
            if not 0 <= to < n:
                to, to_seg = (i, seg ^ 1) if segments % 2 == 0 else (to % n, seg)
            pairs.append((seg * n + i, to_seg * n + to))
    return lax.ppermute(block, (SEGMENTS, AXIS), pairs)


def per_device(z, diag_inverse, coupling, impute_coef, anchor):
    d = diag_inverse[0]
    c = coupling[0]
    typed = d.shape[0]
    half = c.shape[1]
    traits = z.shape[0]
    untyped, span = impute_coef.shape
    assert span == typed + 2 * half and typed == 2 * half
    assert lax.axis_size(AXIS) >= 3 * GROUP
    groups = lax.axis_size(AXIS) // GROUP
    two, four = traits // 2, traits // 4
    square = (half, half)
    sq, h2, h4 = (square, f32), ((two, half), f32), ((four, half), f32)
    x1_shape, x6_shape = ((half + two, half), f32), ((2 * two, half), f32)
    x6_coded = ((2 * coded_rows(two, half), LANES), i16)
    coded = ((coded_rows(four, half), LANES), i16)
    coded_half = ((coded_rows(half // 2, half), LANES), i16)
    mixed = ((coded_rows(half // 2, half) + coded_rows(four, half), LANES), i16)

    solved_shape, p_shape = ((traits, typed), f32), ((typed, half), f32)
    x1, s_own, z, d, c = call(
        tail_part, [x1_shape, h2, solved_shape, ((typed, typed), f32), p_shape], z, d, c,
        hbm=True, scratch=[pltpu.SemaphoreType.DMA((7,))],
    )
    got1 = swap(x1, 1)
    x3, g_own, solved, p = call(
        head_part, [x1_shape, h2, solved_shape, p_shape], z, d, c, x1, s_own
    )
    x2, n_own, sp_own = call(pair_forward, [mixed, sq, h4], x1, got1, s_own, after=(p,))
    got2 = swap(x2, 3)
    got3 = swap(x3, 1)
    masked = call(
        mask_coefs, ((untyped, span), bf16), impute_coef, anchor[None, :], after=(x2,), hbm=True,
        scratch=[
            pltpu.VMEM((untyped, span), bf16),
            pltpu.VMEM((1, untyped), jnp.int32),
            pltpu.SemaphoreType.DMA((untyped // 128 + 1,)),
        ],
    )
    x4, gg_own, gp_own = call(
        pair_backward, [mixed, sq, h4], x1, got1, s_own, x3, got3, g_own, after=(x2,)
    )
    got2_core = swap(call(relay, coded_half, got2, after=(x4, masked)), 1)
    out = call(group_forward, coded, n_own, got2, got2_core, sp_own)
    parts3 = ((3 * half, half), bf16)
    s_group, up, down, n_first, n_second = call(
        group_map, [h4, parts3, parts3, sq, sq], n_own, got2, got2_core, sp_own, after=(out,)
    )
    k = call(block_map, ((3 * half, typed), bf16), n_second, x1, got1, d)
    start, maps = call(
        block_parts, [solved_shape, ((2 * half, typed), f32)], solved, p, d, after=(k,)
    )
    t_in = jnp.zeros((four, half), f32)
    got4 = swap(x4, 3)
    for step in range(groups - 2):
        got = hop(out, step)
        t_in, out = call(
            functools.partial(forward_hop, step), [h4, coded], got, t_in, up, s_group,
            after=(maps,) if step == 0 else (),
        )
        if step == 0:
            pieces = [((half // 2 + SCALES, LANES), i16)] * 2
            low, high = call(relay_halves, pieces, got4, after=(out,))
            got4_low, got4_high = swap(low, 1), swap(high, 1)
    gg_group, g_group, gg_second, g_second = call(
        group_backward, [parts3, h4, sq, h4],
        n_first, got2, sp_own, gg_own, got4, got4_low, got4_high, gp_own, after=(out,),
    )
    last = groups - 2
    got = hop(out, last)
    t_in, out = call(
        functools.partial(turn, last), [h4, coded], got, t_in, gg_group, g_group
    )

    u_in = jnp.zeros((four, half), f32)
    for step in reversed(range(groups - 1)):
        got = hop(out, step)
        if step == last:
            x5, kept, rest_own, local = call(
                spread_forward, [coded_half, h4, h4, h4],
                t_in, n_first, got2, sp_own, gg_second, g_second, gg_group, g_group, after=(out,),
            )
            got5 = swap(x5, 3)
        if step:
            u_in, out = call(
                functools.partial(backward_hop, step), [h4, coded], got, u_in, down, local
            )
        else:
            out = call(functools.partial(arrive, step), coded, got, u_in)
    x6, own = call(
        pair_states, [x6_coded, x6_shape], kept, rest_own, got5, x1, got1, s_own, x3, got3, g_own
    )
    got6 = swap(x6, 1)
    fixed = call(block_fixed, solved_shape, own, got6, start, maps)
    both = call(gather, ((2 * coded[0][0], LANES), i16), out, swap(out, 3))
    got_both = swap(both, 1)
    edge = (square, bf16)
    xa, xb = call(block_weights, [edge, edge], both, got_both, fixed, k)
    got_a = swap_chips(xa)
    got_b = swap(xb, 1)
    acc = call(impute_own, ((traits, untyped), f32), xa, xb, masked)
    return call(
        impute_edges, ((traits, untyped), f32), acc, got_a, got_b, masked, last=True
    )


def solution(mesh):
    in_specs = (
        P(None, (SEGMENTS, AXIS)),
        P((SEGMENTS, AXIS), None, None),
        P((SEGMENTS, AXIS), None, None),
        P((SEGMENTS, AXIS), None),
        P((SEGMENTS, AXIS)),
    )
    return jax.shard_map(
        per_device, mesh=mesh, in_specs=in_specs, out_specs=P(None, (SEGMENTS, AXIS)), check_vma=False
    )
```
